128 devices in a mesh: ctx: 16 (over x, z), fsdp: 8 (over y, core).
Axes of the slice: x: 4, y: 4, z: 4, core: 2. Of those that a mesh axis runs over, the one named last changes fastest.
Arguments:
- tokens: bfloat16 [8, 4096, 768], P('fsdp', 'ctx'), may hold values from -6 to 6
- segments: int32 [8, 4096], P('fsdp', 'ctx'), may hold values from 0 to 2, as said below
- routes: int32 [8, 4096, 2], P('fsdp', 'ctx'), may hold values from 0 to 15, all different within a row; in each aligned block of 256 rows (0 to 255, 256 to 511, ..., all dimensions but the last counted through in order) at most 48 rows name the same one
- w_qkv: bfloat16 [768, 2304], P(('ctx', 'fsdp')), may hold values from -0.21875 to 0.21875
- w_out: bfloat16 [768, 768], P(('ctx', 'fsdp')), may hold values from -1.75 to 1.75
- w_router: bfloat16 [768, 16], P(('ctx', 'fsdp')), may hold values from -0.21875 to 0.21875
- shared_in: bfloat16 [768, 4096], P(('ctx', 'fsdp')), may hold values from -0.21875 to 0.21875
- shared_down: bfloat16 [2048, 768], P(('ctx', 'fsdp')), may hold values from -0.125 to 0.125
- attn_gain: bfloat16 [768], P(('ctx', 'fsdp')), may hold values from 0.5 to 1.5
- ffn_gain: bfloat16 [768], P(('ctx', 'fsdp')), may hold values from 0.5 to 1.5
- expert_in: bfloat16 [16, 768, 4096], P('ctx', 'fsdp'), may hold values from -0.21875 to 0.21875
- expert_down: bfloat16 [16, 2048, 768], P('ctx', 'fsdp'), may hold values from -0.125 to 0.125
- cotangent: bfloat16 [8, 4096, 768], P('fsdp', 'ctx'), may hold values from -6 to 6
Outputs:
- mixed: bfloat16 [8, 4096, 768], P('fsdp', 'ctx')
- input_grad: float32 [8, 4096, 768], P('fsdp', 'ctx')
- grad_w_qkv: float32 [768, 2304], P(('ctx', 'fsdp'))
- grad_w_out: float32 [768, 768], P(('ctx', 'fsdp'))
- grad_w_router: float32 [768, 16], P(('ctx', 'fsdp'))
- grad_shared_in: float32 [768, 4096], P(('ctx', 'fsdp'))
- grad_shared_down: float32 [2048, 768], P(('ctx', 'fsdp'))
- grad_attn_gain: float32 [768], P(('ctx', 'fsdp'))
- grad_ffn_gain: float32 [768], P(('ctx', 'fsdp'))
- grad_expert_in: float32 [16, 768, 4096], P('ctx', 'fsdp')
- grad_expert_down: float32 [16, 2048, 768], P('ctx', 'fsdp')
The draws below stay inside these ranges and needn't reach their ends.
Inputs may be any that keep to these rules, and one draw needn't show every extreme that they name: `segments`: segment numbers never fall along a sequence; document 1 begins within the first 256 positions and ends within the last 256; documents 0 and 2 are not empty. `routes`: A token's 2 experts differ; among the rows of one device no expert is named more than 48 times, and in some device's rows some expert exactly 48 times.
All inputs are finite; a program needn't handle non-finite values.
Results may differ from the reference program's by a relative error of at most 0.023.
Values may be sent and summed in bfloat16 or wider, within the bound.
No kernel may reach another device: no remote copies, remote signals or barrier semaphores. Data moves between devices by JAX's collectives and lax.ppermute only.
A program may use at most 256 MiB of HBM per device.

```python
import math
import jax
import jax.numpy as jnp
import numpy as np
from jax import lax

D = 768
HEADS = 12
HEAD_DIM = 64
FF = 2048
TOPK = 2
WIN = 1024
TOK_DEV = 256
EXPERTS = 16
CAP = 48
SEQS = 8
SEQ_LEN = 4096


def draw_segments(key, part):
    key = jax.random.fold_in(key, 11)
    key_front, key_back = jax.random.split(key)
    front_cut = jax.random.randint(key_front, (SEQS, 1), 1, TOK_DEV, dtype=jnp.int32)
    back_cut = jax.random.randint(key_back, (SEQS, 1), SEQ_LEN - TOK_DEV + 1, SEQ_LEN, dtype=jnp.int32)
    places = jnp.arange(SEQ_LEN, dtype=jnp.int32)[None, :]
    return (places >= front_cut).astype(jnp.int32) + (places >= back_cut).astype(jnp.int32)


def levels(key, dims, cuts, low, high):
    def one(dim, parts):
        draws = jax.random.uniform(jax.random.fold_in(jax.random.fold_in(key, 6), dim), (parts,), jnp.float32, low / len(cuts), high / len(cuts))
        return jnp.repeat(jnp.exp(draws), dims[dim] // parts).reshape((-1,) + (1,) * (len(dims) - dim - 1))

    gain = one(*cuts[0])
    for cut in cuts[1:]:
        gain = gain * one(*cut)
    return gain


def routed_block(rng, own, number, rows, number_of, top, limit, slope):
    order = jax.random.permutation(rng, number_of)
    heavy_load, usual = shares(number_of, rows * top, limit, slope, True), shares(number_of, rows * top, limit, slope, False)
    places = jnp.arange(number_of)

    def named(tallies, turn):
        used = int((tallies > 0).sum())
        fixed = max(1, used // 4)
        shifted = fixed + (places - fixed + turn * (used - fixed)) % max(1, number_of - fixed)
        return jnp.zeros((number_of,), jnp.int32).at[order[jnp.where(places < fixed, places, shifted)]].set(jnp.asarray(tallies, jnp.int32))

    tallies = jnp.where(number % 4 == 0, named(heavy_load, number // 4), named(usual, number - number // 4 - 1))
    mixed = jax.random.permutation(jax.random.fold_in(own, 3), number_of)
    donor, sink = mixed[0:number_of // 2 * 2:2], mixed[1:number_of // 2 * 2:2]
    slack = jnp.minimum(tallies[donor] - 1, limit - tallies[sink]) // 2
    slack = jnp.where((donor == order[0]) | (sink == order[0]) | (tallies[sink] == 0), 0, jnp.maximum(slack, 0))
    shifted = jax.random.randint(jax.random.fold_in(own, 4), (number_of // 2,), 0, 1 << 20) % (slack + 1)
    tallies = tallies.at[donor].add(-shifted).at[sink].add(shifted)
    labels = jnp.searchsorted(jnp.cumsum(tallies), jnp.arange(rows * top), side="right").astype(jnp.int32)
    grid = labels.reshape(top, rows).T
    grid = grid[jax.random.permutation(jax.random.fold_in(own, 1), rows)]
    turn = jax.random.randint(jax.random.fold_in(own, 2), (rows, 1), 0, top)
    return jnp.take_along_axis(grid, (jnp.arange(top)[None, :] + turn) % top, axis=1)


def shares(count, total, reach, slope, full):
    weights = [(1 << 20) // math.isqrt(grade ** slope) + 1 for grade in range(1, count + 1)]
    largest = reach if full else min(reach, max(-(-total // count), total * weights[0] // sum(weights)))
    least = 1 if total - largest >= count - 1 else 0
    counts, spare = [largest] + [least] * (count - 1), total - largest - least * (count - 1)
    while spare > 0:
        free = [i for i in range(1, count) if counts[i] < largest] or [i for i in range(1, count) if counts[i] < reach]
        mass, remaining = sum([weights[i] for i in free]), spare
        for i in free:
            extra = min(reach - counts[i], max(1, remaining * weights[i] // mass), spare)
            counts[i] = counts[i] + extra
            spare = spare - extra
    return np.array(counts)


def bell_draw(key, dims, scale, reach, shards=(), kind=jnp.bfloat16):
    drawn = jax.random.normal(key, dims, jnp.float32) * scale
    if len(shards) > 0:
        drawn = levels(key, dims, shards, -0.22, 0.18) * drawn
    return jnp.clip(drawn, min=-reach, max=reach).astype(kind)


def setup_inputs(seed: int = 0) -> dict:
    key_list = jax.random.split(jax.random.key(seed), 14)
    tokens = bell_draw(key_list[0], (SEQS, SEQ_LEN, D), 1.0, 6.0, ((0, 8), (1, 16)))
    segments = draw_segments(jax.random.fold_in(key_list[13], 71), 0)
    routes_keys = jax.random.split(jax.random.fold_in(key_list[2], 1), SEQS * SEQ_LEN // TOK_DEV)
    routes_turns = jax.random.permutation(jax.random.fold_in(key_list[2], 3), SEQS * SEQ_LEN // TOK_DEV)
    routes = jax.vmap(lambda own, number: routed_block(jax.random.fold_in(key_list[2], 2), own, number, TOK_DEV, EXPERTS, TOPK, CAP, 1))(routes_keys, routes_turns).reshape((SEQS, SEQ_LEN, TOPK))
    w_qkv = bell_draw(key_list[3], (D, 3 * D), D ** -0.5, 0.21875, ((0, 128),))
    w_out = bell_draw(key_list[4], (D, D), (D // 64) ** -0.5, 1.75, ((0, 128),))
    w_router = bell_draw(key_list[5], (D, EXPERTS), D ** -0.5, 0.21875, ((0, 128),))
    shared_in = bell_draw(key_list[6], (D, 2 * FF), D ** -0.5, 0.21875, ((0, 128),))
    shared_down = bell_draw(key_list[7], (FF, D), FF ** -0.5, 0.125, ((0, 128),))
    attn_gain = jnp.clip(1.0 + 0.1 * jax.random.normal(key_list[8], (D,), jnp.float32), 0.5, 1.5).astype(jnp.bfloat16)
    ffn_gain = jnp.clip(1.0 + 0.1 * jax.random.normal(key_list[9], (D,), jnp.float32), 0.5, 1.5).astype(jnp.bfloat16)
    expert_in = bell_draw(key_list[10], (EXPERTS, D, 2 * FF), D ** -0.5, 0.21875, ((0, 16), (1, 8)))
    expert_down = bell_draw(key_list[11], (EXPERTS, FF, D), FF ** -0.5, 0.125, ((0, 16), (1, 8)))
    cotangent = bell_draw(key_list[12], (SEQS, SEQ_LEN, D), 1.0, 6.0, ((0, 8), (1, 16)))
    return {"tokens": tokens, "segments": segments, "routes": routes, "w_qkv": w_qkv, "w_out": w_out, "w_router": w_router, "shared_in": shared_in, "shared_down": shared_down, "attn_gain": attn_gain, "ffn_gain": ffn_gain, "expert_in": expert_in, "expert_down": expert_down, "cotangent": cotangent}


EPSILON = 1e-06
TOP_ACCURACY = lax.Precision.HIGHEST

@jax.custom_vjp
def low(v):
    return lax.optimization_barrier(v.astype(jnp.bfloat16)).astype(jnp.float32)

@jax.custom_vjp
def reduced_backward(v):
    return v

def low_keep(v):
    return (low(v), None)

def low_pass(kept, grad):
    return (grad,)

def back_keep(v):
    return (v, None)

def back_low(kept, grad):
    return (low(grad),)
low.defvjp(low_keep, low_pass)
reduced_backward.defvjp(back_keep, back_low)

def norm_rows(values, gain_row):
    return values * lax.rsqrt(lax.optimization_barrier(jnp.mean(values * values, axis=-1, keepdims=True)) + EPSILON) * gain_row

def rotary_table(length_all, head_width):
    half_width = head_width // 2
    frequency = jnp.exp(-jnp.log(10000.0) * (2.0 * jnp.arange(half_width, dtype=jnp.float32) / head_width))
    places = jnp.arange(length_all, dtype=jnp.int32).astype(jnp.float32)
    angles = places[:, None] * frequency[None, :]
    return (jnp.cos(angles)[:, None, :], jnp.sin(angles)[:, None, :])

def rotate(values, cosine_table, sine_table):
    half_width = values.shape[-1] // 2
    front_half = values[..., :half_width]
    back_half = values[..., half_width:]
    return jnp.concatenate([front_half * cosine_table - back_half * sine_table, back_half * cosine_table + front_half * sine_table], axis=-1)

def window_attention(queries, key_rows, value_rows, segment_ids):
    block_rows = min(512, SEQ_LEN)
    key_span = block_rows + WIN
    key_padded = jnp.pad(key_rows, ((WIN, 0), (0, 0), (0, 0)))
    value_padded = jnp.pad(value_rows, ((WIN, 0), (0, 0), (0, 0)))
    segment_padded = jnp.pad(segment_ids, (WIN, 0), constant_values=-1)
    score_scale = HEAD_DIM ** (-0.5)

    def one_block(first_row):
        query_block = lax.dynamic_slice_in_dim(queries, first_row, block_rows, 0)
        key_block = lax.dynamic_slice_in_dim(key_padded, first_row, key_span, 0)
        value_block = lax.dynamic_slice_in_dim(value_padded, first_row, key_span, 0)
        query_segs = lax.dynamic_slice_in_dim(segment_ids, first_row, block_rows, 0)
        key_segs = lax.dynamic_slice_in_dim(segment_padded, first_row, key_span, 0)
        query_pos = first_row + jnp.arange(block_rows, dtype=jnp.int32)
        key_pos = first_row - WIN + jnp.arange(key_span, dtype=jnp.int32)
        allowed = (key_pos[None, :] <= query_pos[:, None]) & (query_pos[:, None] - key_pos[None, :] < WIN) & (query_segs[:, None] == key_segs[None, :])
        scores = reduced_backward(jnp.einsum('qhd,khd->hqk', query_block, key_block, precision=TOP_ACCURACY) * score_scale)
        scores = jnp.where(allowed[None], scores, -1e+30)
        largest = lax.optimization_barrier(jnp.max(scores, axis=-1, keepdims=True))
        exponent = jnp.exp(scores - largest)
        weights_soft = low(exponent / lax.optimization_barrier(jnp.sum(exponent, axis=-1, keepdims=True)))
        return jnp.einsum('hqk,khd->qhd', weights_soft, value_block, precision=TOP_ACCURACY)
    starts = jnp.arange(0, SEQ_LEN, block_rows, dtype=jnp.int32)
    pieces = lax.map(jax.checkpoint(one_block), starts)
    return pieces.reshape(SEQ_LEN, HEADS, HEAD_DIM)

def reference(tokens, segments, routes, w_qkv, w_out, w_router, shared_in, shared_down, attn_gain, ffn_gain, expert_in, expert_down, cotangent):
    token_count = SEQS * SEQ_LEN
    route_rows = routes.reshape(token_count, TOPK)
    expert_ids = jnp.arange(EXPERTS, dtype=jnp.int32)
    hits = route_rows[:, :, None] == expert_ids[None, None, :]
    picked = hits.astype(jnp.float32)
    member = lax.optimization_barrier(jnp.sum(hits.astype(jnp.int32), axis=1)).astype(jnp.int32)
    ranking = jnp.cumsum(member.reshape(token_count // TOK_DEV, TOK_DEV, EXPERTS), axis=1, dtype=jnp.int32).reshape(token_count, EXPERTS) - 1
    block_ids = jnp.arange(token_count, dtype=jnp.int32) // TOK_DEV
    spill_row = token_count // TOK_DEV * CAP
    targets = jnp.where(member > 0, block_ids[:, None] * CAP + ranking, spill_row).astype(jnp.int32)
    token_ids = jnp.arange(token_count, dtype=jnp.int32)

    def owners_of(target_col):
        table = jnp.full((spill_row + 1,), token_count, dtype=jnp.int32).at[target_col].set(token_ids)
        return table.at[spill_row].set(token_count)
    owners = jax.vmap(owners_of, in_axes=1)(targets)
    cosine_table, sine_table = rotary_table(SEQ_LEN, HEAD_DIM)

    def forward(input_rows, query_key_value_weight, output_weight, router_weight, shared_up, shared_back, gain_one, gain_two, expert_up, expert_back):
        first_normalized = low(norm_rows(input_rows, gain_one))
        projected_output = reduced_backward(jnp.einsum('xni,if->xnf', first_normalized, query_key_value_weight, precision=TOP_ACCURACY))
        queries = projected_output[..., :D].reshape(SEQS, SEQ_LEN, HEADS, HEAD_DIM)
        key_rows = projected_output[..., D:2 * D].reshape(SEQS, SEQ_LEN, HEADS, HEAD_DIM)
        value_rows = projected_output[..., 2 * D:].reshape(SEQS, SEQ_LEN, HEADS, HEAD_DIM)
        queries = low(rotate(queries, cosine_table, sine_table))
        key_rows = low(rotate(key_rows, cosine_table, sine_table))
        value_rows = low(value_rows)
        attended = lax.map(lambda members: window_attention(members[0], members[1], members[2], members[3]), (queries, key_rows, value_rows, segments))
        combined_heads = low(reduced_backward(attended.reshape(SEQS, SEQ_LEN, D)))
        hidden_state = input_rows + reduced_backward(jnp.einsum('xni,if->xnf', combined_heads, output_weight, precision=TOP_ACCURACY))
        hidden_rows = hidden_state.reshape(token_count, D)
        normed_two = low(norm_rows(hidden_rows, gain_two))
        logits = reduced_backward(jnp.dot(normed_two, router_weight, precision=TOP_ACCURACY))
        chosen = lax.optimization_barrier(jnp.sum(logits[:, None, :] * picked, axis=-1))
        gate_weights = jax.nn.softmax(chosen, axis=-1)
        weight_table = lax.optimization_barrier(jnp.sum(gate_weights[:, :, None] * picked, axis=1))
        padded_rows = jnp.concatenate([normed_two, jnp.zeros((1, D), jnp.float32)], axis=0)

        def one_expert(running, pieces):
            up_weight, down_weight, owner_col, target_col, weight_col = pieces
            expert_rows = reduced_backward(padded_rows[owner_col])
            both = reduced_backward(jnp.dot(expert_rows, up_weight, precision=TOP_ACCURACY))
            expert_hidden = low(jax.nn.silu(both[:, :FF]) * both[:, FF:])
            expert_result = low(reduced_backward(jnp.dot(expert_hidden, down_weight, precision=TOP_ACCURACY)))
            return (running + weight_col[:, None] * expert_result[target_col], None)
        mixture, unused = lax.scan(jax.checkpoint(one_expert), jnp.zeros((token_count, D), jnp.float32), (expert_up, expert_back, owners, targets.T, weight_table.T))
        shared_both = reduced_backward(jnp.dot(normed_two, shared_up, precision=TOP_ACCURACY))
        shared_hidden = low(jax.nn.silu(shared_both[:, :FF]) * shared_both[:, FF:])
        shared_result = reduced_backward(jnp.dot(shared_hidden, shared_back, precision=TOP_ACCURACY))
        return (hidden_rows + mixture + shared_result).reshape(SEQS, SEQ_LEN, D)
    floats = [argument.astype(jnp.float32) for argument in (tokens, w_qkv, w_out, w_router, shared_in, shared_down, attn_gain, ffn_gain, expert_in, expert_down)]
    layer_out, pullback = jax.vjp(forward, floats[0], floats[1], floats[2], floats[3], floats[4], floats[5], floats[6], floats[7], floats[8], floats[9])
    grads = pullback(cotangent.astype(jnp.float32))
    return (layer_out.astype(jnp.bfloat16), grads[0], grads[1], grads[2], grads[3], grads[4], grads[5], grads[6], grads[7], grads[8], grads[9])
```

```python
import jax
import jax.numpy as jnp
from jax import lax
from jax.sharding import PartitionSpec as P

HEADS = 12
HEAD_DIM = 64
TOPK = 2
WIN = 1024


EPSILON = 1e-06


def shifted(value, axis, steps):
    count = lax.axis_size(axis)
    leading, last = (max(0, -steps), min(count, count - steps))
    return lax.ppermute(value, axis, [(source, source + steps) for source in range(leading, last)])


def rms_scale(values):
    return lax.rsqrt(jnp.mean(values * values, axis=-1, keepdims=True) + EPSILON)


def rotary_table(local_rows, offset, head_width):
    half_width = head_width // 2
    frequency = jnp.exp(
        -jnp.log(10000.0) * (2.0 * jnp.arange(half_width, dtype=jnp.float32) / head_width)
    )
    places = (offset + jnp.arange(local_rows, dtype=jnp.int32)).astype(jnp.float32)
    angles = places[:, None] * frequency[None, :]
    return (jnp.cos(angles)[:, None, :], jnp.sin(angles)[:, None, :])


def rotate(values, cosine_table, sine_table):
    half_width = values.shape[-1] // 2
    front_half = values[..., :half_width]
    back_half = values[..., half_width:]
    return jnp.concatenate(
        [
            front_half * cosine_table - back_half * sine_table,
            back_half * cosine_table + front_half * sine_table,
        ],
        axis=-1,
    )


def rotate_back(gradient, cosine_table, sine_table):
    half_width = gradient.shape[-1] // 2
    front_half = gradient[..., :half_width]
    back_half = gradient[..., half_width:]
    return jnp.concatenate(
        [
            front_half * cosine_table + back_half * sine_table,
            back_half * cosine_table - front_half * sine_table,
        ],
        axis=-1,
    )


def silu_slope(values):
    sigmoid_part = jax.nn.sigmoid(values)
    return sigmoid_part * (1.0 + values * (1.0 - sigmoid_part))


def norm_back(dnormed, values, row_scale, gain_row):
    weighted = dnormed * gain_row
    dvalues = row_scale * weighted - values * row_scale**3 * jnp.mean(
        weighted * values, axis=-1, keepdims=True
    )
    dgain = jnp.sum(dnormed * values * row_scale, axis=0)
    return (dvalues, dgain)


def window_scores(queries, key_heads, allowed, score_scale):
    scores = (
        jnp.einsum("qhd,khd->hqk", queries, key_heads, preferred_element_type=jnp.float32)
        * score_scale
    )
    return jnp.where(allowed[None], scores, -1e30)


def sum_to_owners(grads, rows):
    low = grads.astype(jnp.bfloat16).reshape(
        lax.axis_size("ctx"), lax.axis_size("fsdp"), rows, grads.shape[-1]
    )
    part = lax.psum_scatter(low.transpose(1, 0, 2, 3), "fsdp", scatter_dimension=0)
    pieces = lax.all_to_all(part, "ctx", split_axis=0, concat_axis=0, tiled=True)
    return jnp.sum(pieces.astype(jnp.float32), axis=0)


def per_device(
    tokens,
    segments,
    routes,
    w_qkv,
    w_out,
    w_router,
    shared_in,
    shared_down,
    attn_gain,
    ffn_gain,
    expert_in,
    expert_down,
    cotangent,
):
    ctx_count = lax.axis_size("ctx")
    ctx_index = lax.axis_index("ctx")
    local_rows = tokens.shape[1]
    model_width = tokens.shape[2]
    reach_back = max(1, WIN // local_rows)
    capacity = max(2, 3 * local_rows * TOPK // (2 * ctx_count))
    score_scale = HEAD_DIM ** (-0.5)
    bfloat = jnp.bfloat16
    single = jnp.float32
    rows_own = w_qkv.shape[0]
    rows_down = shared_down.shape[0]
    small = jnp.concatenate(
        [
            w_router,
            attn_gain[:, None],
            ffn_gain[:, None],
            jnp.zeros((rows_own, 128 - w_router.shape[1] - 2), w_router.dtype),
        ],
        axis=1,
    )
    packed = jnp.pad(
        jnp.concatenate([w_qkv, w_out, shared_in, small], axis=1), ((0, 8 - rows_own), (0, 0))
    )
    packed = jnp.concatenate([packed, shared_down[:8], shared_down[8:]], axis=1)
    gathered = lax.all_gather(packed, ("ctx", "fsdp"), axis=0, tiled=True)
    device_count = ctx_count * lax.axis_size("fsdp")
    gathered = gathered.reshape(device_count, 8, gathered.shape[1])

    def columns(start, width):
        return gathered[:, :rows_own, start : start + width].reshape(
            device_count * rows_own, width
        )

    place = 0
    full_qkv = columns(place, w_qkv.shape[1])
    place += w_qkv.shape[1]
    full_out = columns(place, w_out.shape[1])
    place += w_out.shape[1]
    full_shared_in = columns(place, shared_in.shape[1])
    place += shared_in.shape[1]
    full_small = columns(place, 128)
    place += 128
    full_shared_down = (
        gathered[:, :, place:]
        .reshape(device_count, 8, 2, model_width)
        .transpose(0, 2, 1, 3)
        .reshape(device_count * rows_down, model_width)
    )
    expert_count = w_router.shape[1]
    full_router = full_small[:, :expert_count]
    gain_attn = full_small[:, expert_count]
    gain_ffn = full_small[:, expert_count + 1]
    expert_full = (
        lax.all_gather(expert_in, "fsdp", axis=1, tiled=True),
        lax.all_gather(expert_down, "fsdp", axis=1, tiled=True),
    )
    expert_up = expert_full[0][0]
    expert_back = expert_full[1][0]
    input_rows = tokens[0].astype(single)
    segment_own = segments[0]
    route_own = routes[0]
    gain_one = gain_attn.astype(single)
    gain_two = gain_ffn.astype(single)
    earlier_rows = []
    earlier_segments = []
    for distance in range(reach_back, 0, -1):
        moved_rows, moved_segment = shifted((tokens[0], segment_own), "ctx", distance)
        earlier_rows.append(moved_rows)
        earlier_segments.append(moved_segment)
    span_rows = jnp.concatenate(earlier_rows + [tokens[0]], axis=0).astype(single)
    all_segments = jnp.concatenate(earlier_segments + [segment_own], axis=0)
    span_scale = rms_scale(span_rows)
    span_normalized = (span_rows * span_scale * gain_one).astype(bfloat)
    scale_one = span_scale[reach_back * local_rows :]
    first_normalized = span_normalized[reach_back * local_rows :]
    key_span = (reach_back + 1) * local_rows
    queries_flat = jnp.dot(
        first_normalized, full_qkv[:, :model_width], preferred_element_type=single
    )
    pairs_flat = jnp.dot(
        span_normalized, full_qkv[:, model_width:], preferred_element_type=single
    )
    span_cosine, span_sine = rotary_table(
        key_span, (ctx_index - reach_back) * local_rows, HEAD_DIM
    )
    cosine_table = span_cosine[reach_back * local_rows :]
    sine_table = span_sine[reach_back * local_rows :]
    queries = rotate(
        queries_flat.reshape(local_rows, HEADS, HEAD_DIM), cosine_table, sine_table
    ).astype(bfloat)
    key_heads = rotate(
        pairs_flat[:, :model_width].reshape(key_span, HEADS, HEAD_DIM), span_cosine, span_sine
    ).astype(bfloat)
    value_heads = pairs_flat[:, model_width:].astype(bfloat).reshape(key_span, HEADS, HEAD_DIM)
    query_pos = ctx_index * local_rows + jnp.arange(local_rows, dtype=jnp.int32)
    key_pos = (ctx_index - reach_back) * local_rows + jnp.arange(key_span, dtype=jnp.int32)
    allowed = (
        (key_pos[None, :] <= query_pos[:, None])
        & (query_pos[:, None] - key_pos[None, :] < WIN)
        & (key_pos[None, :] >= 0)
        & (segment_own[:, None] == all_segments[None, :])
    )
    scores = window_scores(queries, key_heads, allowed, score_scale)
    largest = jnp.max(scores, axis=-1, keepdims=True)
    exponent = jnp.exp(scores - largest)
    row_total = jnp.sum(exponent, axis=-1, keepdims=True)
    log_total = largest + jnp.log(row_total)
    weights_low = (exponent / row_total).astype(bfloat)
    attended = (
        jnp.einsum("hqk,khd->qhd", weights_low, value_heads, preferred_element_type=single)
        .reshape(local_rows, model_width)
        .astype(bfloat)
    )
    hidden_state = input_rows + jnp.dot(attended, full_out, preferred_element_type=single)
    scale_two = rms_scale(hidden_state)
    normed_two = (hidden_state * scale_two * gain_two).astype(bfloat)
    logits = jnp.dot(normed_two, full_router, preferred_element_type=single)
    expert_ids = jnp.arange(ctx_count, dtype=jnp.int32)
    hits = route_own[:, :, None] == expert_ids[None, None, :]
    picked = hits.astype(single)
    chosen = jnp.sum(logits[:, None, :] * picked, axis=-1)
    gate_weights = jax.nn.softmax(chosen, axis=-1)
    member = jnp.sum(hits.astype(jnp.int32), axis=1)
    ranking = jnp.cumsum(member, axis=0, dtype=jnp.int32) - 1
    slot_ids = jnp.arange(capacity, dtype=jnp.int32)
    placed_mask = (member[:, :, None] > 0) & (ranking[:, :, None] == slot_ids[None, None, :])
    selector = (
        (hits[:, :, :, None] & placed_mask[:, None, :, :])
        .astype(bfloat)
        .reshape(local_rows, TOPK, ctx_count * capacity)
    )
    outgoing = jnp.einsum(
        "tec,td->ecd", placed_mask.astype(bfloat), normed_two, preferred_element_type=single
    ).astype(bfloat)
    grad_rows = cotangent[0].astype(single)
    grad_low = grad_rows.astype(bfloat)
    dslot_low = (gate_weights[:, :, None] * grad_rows[:, None, :]).astype(bfloat)
    slot_grads = (
        jnp.einsum("tks,tkd->sd", selector, dslot_low, preferred_element_type=single)
        .astype(bfloat)
        .reshape(ctx_count, capacity, model_width)
    )
    incoming = lax.all_to_all(outgoing, "ctx", split_axis=0, concat_axis=0, tiled=True)
    grad_incoming = lax.all_to_all(slot_grads, "ctx", split_axis=0, concat_axis=0, tiled=True)
    expert_rows = incoming.reshape(ctx_count * capacity, model_width)
    gate_up = jnp.dot(expert_rows, expert_up, preferred_element_type=single)
    hidden_width = gate_up.shape[1] // 2
    expert_gate = gate_up[:, :hidden_width]
    expert_lift = gate_up[:, hidden_width:]
    expert_act = jax.nn.silu(expert_gate)
    expert_hidden = (expert_act * expert_lift).astype(bfloat)
    expert_result = (
        jnp.dot(expert_hidden, expert_back, preferred_element_type=single)
        .astype(bfloat)
        .reshape(ctx_count, capacity, model_width)
    )
    returned = lax.all_to_all(expert_result, "ctx", split_axis=0, concat_axis=0, tiled=True)
    slot_values = jnp.einsum(
        "tks,sd->tkd",
        selector,
        returned.reshape(ctx_count * capacity, model_width),
        preferred_element_type=single,
    )
    mixture = jnp.sum(gate_weights[:, :, None] * slot_values, axis=1)
    shared_both = jnp.dot(normed_two, full_shared_in, preferred_element_type=single)
    shared_gate = shared_both[:, :hidden_width]
    shared_lift = shared_both[:, hidden_width:]
    shared_act = jax.nn.silu(shared_gate)
    shared_hidden = (shared_act * shared_lift).astype(bfloat)
    shared_result = jnp.dot(shared_hidden, full_shared_down, preferred_element_type=single)
    mixed = (hidden_state + mixture + shared_result).astype(bfloat)[None]
    grad_shared_down = jnp.dot(shared_hidden.T, grad_low, preferred_element_type=single)
    dshared_hidden = jnp.dot(grad_low, full_shared_down.T, preferred_element_type=single)
    dshared_both = jnp.concatenate(
        [dshared_hidden * shared_lift * silu_slope(shared_gate), dshared_hidden * shared_act],
        axis=1,
    ).astype(bfloat)
    grad_shared_in = jnp.dot(normed_two.T, dshared_both, preferred_element_type=single)
    dnormed_two = jnp.dot(dshared_both, full_shared_in.T, preferred_element_type=single)
    dgates = jnp.sum(grad_rows[:, None, :] * slot_values, axis=-1)
    dexpert_result = grad_incoming.reshape(ctx_count * capacity, model_width)
    grad_expert_back = jnp.dot(expert_hidden.T, dexpert_result, preferred_element_type=single)
    dexpert_hidden = jnp.dot(dexpert_result, expert_back.T, preferred_element_type=single)
    dgate_up = jnp.concatenate(
        [dexpert_hidden * expert_lift * silu_slope(expert_gate), dexpert_hidden * expert_act],
        axis=1,
    ).astype(bfloat)
    grad_expert_up = jnp.dot(expert_rows.T, dgate_up, preferred_element_type=single)
    dexpert_rows = (
        jnp.dot(dgate_up, expert_up.T, preferred_element_type=single)
        .astype(bfloat)
        .reshape(ctx_count, capacity, model_width)
    )
    grad_returned = lax.all_to_all(dexpert_rows, "ctx", split_axis=0, concat_axis=0, tiled=True)
    dnormed_two = dnormed_two + jnp.einsum(
        "tks,sd->td",
        selector,
        grad_returned.reshape(ctx_count * capacity, model_width),
        preferred_element_type=single,
    )
    dchosen = gate_weights * (dgates - jnp.sum(gate_weights * dgates, axis=-1, keepdims=True))
    dlogits = jnp.sum(dchosen[:, :, None] * picked, axis=1).astype(bfloat)
    grad_router = jnp.dot(normed_two.T, dlogits, preferred_element_type=single)
    dnormed_two = dnormed_two + jnp.dot(dlogits, full_router.T, preferred_element_type=single)
    dhidden_norm, grad_gain_two = norm_back(dnormed_two, hidden_state, scale_two, gain_two)
    dhidden = grad_rows + dhidden_norm
    dhidden_low = dhidden.astype(bfloat)
    grad_out = jnp.dot(attended.T, dhidden_low, preferred_element_type=single)
    dattended = (
        jnp.dot(dhidden_low, full_out.T, preferred_element_type=single)
        .astype(bfloat)
        .reshape(local_rows, HEADS, HEAD_DIM)
    )
    probs = jnp.exp(window_scores(queries, key_heads, allowed, score_scale) - log_total)
    probs_low = probs.astype(bfloat)
    dprobs = jnp.einsum("qhd,khd->hqk", dattended, value_heads, preferred_element_type=single)
    dscores = (probs * (dprobs - jnp.sum(probs * dprobs, axis=-1, keepdims=True))).astype(bfloat)
    dqueries = (
        jnp.einsum("hqk,khd->qhd", dscores, key_heads, preferred_element_type=single) * score_scale
    )
    dkeys = (
        jnp.einsum("hqk,qhd->khd", dscores, queries, preferred_element_type=single) * score_scale
    )
    dvalues = jnp.einsum("hqk,qhd->khd", probs_low, dattended, preferred_element_type=single)
    dquery_low = (
        rotate_back(dqueries, cosine_table, sine_table)
        .reshape(local_rows, model_width)
        .astype(bfloat)
    )
    dkey_low = (
        rotate_back(dkeys, span_cosine, span_sine).reshape(key_span, model_width).astype(bfloat)
    )
    dpairs = jnp.concatenate(
        [dkey_low, dvalues.reshape(key_span, model_width).astype(bfloat)], axis=1
    )
    grad_qkv = jnp.concatenate(
        [
            jnp.dot(first_normalized.T, dquery_low, preferred_element_type=single),
            jnp.dot(span_normalized.T, dpairs, preferred_element_type=single),
        ],
        axis=1,
    )
    dspan_one = jnp.dot(dpairs, full_qkv[:, model_width:].T, preferred_element_type=single)
    dnormed_one = dspan_one[reach_back * local_rows :] + jnp.dot(
        dquery_low, full_qkv[:, :model_width].T, preferred_element_type=single
    )
    for distance in range(1, reach_back + 1):
        lower_edge = (reach_back - distance) * local_rows
        block_grads = dspan_one[lower_edge : lower_edge + local_rows]
        dnormed_one = dnormed_one + shifted(
            block_grads.astype(jnp.bfloat16), "ctx", -distance
        ).astype(single)
    dinput_norm, grad_gain_one = norm_back(dnormed_one, input_rows, scale_one, gain_one)
    input_grad = (dhidden + dinput_norm)[None]
    grad_small = jnp.concatenate(
        [
            grad_router,
            grad_gain_one[:, None],
            grad_gain_two[:, None],
            jnp.zeros((model_width, 128 - expert_count - 2), single),
        ],
        axis=1,
    )
    early_grads = sum_to_owners(grad_shared_in, rows_own)
    down_grads = sum_to_owners(grad_shared_down, rows_down)
    late_grads = sum_to_owners(jnp.concatenate([grad_qkv, grad_out, grad_small], axis=1), rows_own)
    qkv_width = grad_qkv.shape[1]
    last = qkv_width + model_width
    dense_grads = (
        late_grads[:, :qkv_width],
        late_grads[:, qkv_width:last],
        late_grads[:, last : last + expert_count],
        early_grads,
        down_grads,
        late_grads[:, last + expert_count],
        late_grads[:, last + expert_count + 1],
    )
    expert_grads = (
        lax.psum_scatter(
            grad_expert_up[None].astype(jnp.bfloat16), "fsdp", scatter_dimension=1, tiled=True
        ).astype(jnp.float32),
        lax.psum_scatter(
            grad_expert_back[None].astype(jnp.bfloat16), "fsdp", scatter_dimension=1, tiled=True
        ).astype(jnp.float32),
    )
    return (
        mixed,
        input_grad,
        dense_grads[0],
        dense_grads[1],
        dense_grads[2],
        dense_grads[3],
        dense_grads[4],
        dense_grads[5],
        dense_grads[6],
        expert_grads[0],
        expert_grads[1],
    )


def solution(mesh):
    placed = (
        P("fsdp", "ctx", None),
        P("fsdp", "ctx"),
        P("fsdp", "ctx", None),
        P(("ctx", "fsdp"), None),
        P(("ctx", "fsdp"), None),
        P(("ctx", "fsdp"), None),
        P(("ctx", "fsdp"), None),
        P(("ctx", "fsdp"), None),
        P(("ctx", "fsdp")),
        P(("ctx", "fsdp")),
        P("ctx", "fsdp", None),
        P("ctx", "fsdp", None),
        P("fsdp", "ctx", None),
    )
    return jax.shard_map(
        per_device,
        mesh=mesh,
        in_specs=placed,
        out_specs=(
            P("fsdp", "ctx", None),
            P("fsdp", "ctx", None),
            P(("ctx", "fsdp"), None),
            P(("ctx", "fsdp"), None),
            P(("ctx", "fsdp"), None),
            P(("ctx", "fsdp"), None),
            P(("ctx", "fsdp"), None),
            P(("ctx", "fsdp")),
            P(("ctx", "fsdp")),
            P("ctx", "fsdp", None),
            P("ctx", "fsdp", None),
        ),
        check_vma=False,
    )
```

```python
import functools

import jax
import jax.numpy as jnp
from jax import lax
from jax.experimental import pallas as pl
from jax.experimental.pallas import tpu as pltpu
from jax.sharding import PartitionSpec as P

HEADS = 12
HEAD_DIM = 64
TOPK = 2
WIN = 1024
EPSILON = 1e-06

BF = jnp.bfloat16
F32 = jnp.float32
PAD_ROWS = 8
TILE = 256
LANES = 128
KEY_BLOCK = 128
VMEM_MB = 60


def dot(a, b):
    return jnp.dot(a, b, preferred_element_type=F32)


def dot_nt(a, b):
    return lax.dot_general(a, b, (((1,), (1,)), ((), ())), preferred_element_type=F32)


def dot_tn(a, b):
    return lax.dot_general(a, b, (((0,), (0,)), ((), ())), preferred_element_type=F32)


def params(megabytes):
    return pltpu.CompilerParams(vmem_limit_bytes=megabytes * 1024 * 1024)


def cost(microseconds):
    return pl.CostEstimate(
        flops=int(microseconds * 1.0e9), bytes_accessed=int(microseconds * 1.0e6), transcendentals=0
    )


def after(value, *others):
    return lax.optimization_barrier((value, *others))[0]


def whole(array):
    return pl.BlockSpec(array.shape, lambda *_: (0,) * array.ndim)


def shifted(value, axis, steps):
    count = lax.axis_size(axis)
    leading, last = (max(0, -steps), min(count, count - steps))
    return lax.ppermute(value, axis, [(source, source + steps) for source in range(leading, last)])


def split_high_low(values):
    high = values.astype(BF)
    return high, (values - high.astype(F32)).astype(BF)


def rotary_tables(rows, offset):
    half = HEAD_DIM // 2
    frequency = jnp.exp(-jnp.log(10000.0) * (2.0 * jnp.arange(half, dtype=F32) / HEAD_DIM))
    places = (offset + jnp.arange(rows, dtype=jnp.int32)).astype(F32)
    angles = places[:, None] * frequency[None, :]
    cosine, sine = jnp.cos(angles), jnp.sin(angles)
    return (
        jnp.concatenate([cosine] * 4, axis=1),
        jnp.concatenate([-sine, sine, -sine, sine], axis=1),
    )


def swapped_halves(values):
    lane = lax.broadcasted_iota(jnp.int32, (1, LANES), 1)
    half = HEAD_DIM // 2
    return jnp.where(
        lane % HEAD_DIM < half,
        pltpu.roll(values, LANES - half, 1),
        pltpu.roll(values, half, 1),
    )


def head_lanes(values, head):
    lane = lax.broadcasted_iota(jnp.int32, (1, LANES), 1)
    return jnp.where(lane // HEAD_DIM == head, values, jnp.zeros_like(values))


def fold_rows(values, op):
    return op(values.reshape(values.shape[0] // 8, 8, values.shape[1]), axis=0)


def attend_kernel(
    x_ref, scale_ref, small_ref, wq_ref, wk_ref, wv_ref, cos_ref, sin_ref, bias_ref,
    q_ref, k_ref, kt_ref, v_ref, e_ref, rl_ref, rlb_ref, o_ref,
    normed, score, vt,
    *, gain_lane,
):
    span, rows = x_ref.shape[0], q_ref.shape[0]

    @pl.when(pl.program_id(0) == 0)
    def _():
        gain = small_ref[...].astype(F32).T[gain_lane : gain_lane + 1, :]
        for start in range(0, span, TILE):
            part = pl.ds(start, TILE)
            normed[part, :] = (x_ref[part, :].astype(F32) * scale_ref[part, :] * gain).astype(BF)

    pair = dot(normed[...], jnp.concatenate([wk_ref[...], wv_ref[...]], axis=1))
    keys = pair[:, :LANES]
    keys = keys * cos_ref[...] + swapped_halves(keys) * sin_ref[...]
    k_ref[...] = keys.astype(BF)
    kt_ref[...] = keys.T.astype(BF)
    values = pair[:, LANES:]
    v_ref[...] = values.astype(BF)
    vt[...] = values.T.astype(BF)
    queries = dot(normed[span - rows :, :], wq_ref[...])
    queries = queries * cos_ref[span - rows :, :] + swapped_halves(queries) * sin_ref[span - rows :, :]
    queries = (queries.astype(BF).astype(F32) * HEAD_DIM**-0.5).astype(BF)
    q_ref[...] = queries

    outs, sums = [], []
    for head in range(2):
        own = head_lanes(queries, head)
        largest = jnp.full((8, rows), -3e38, F32)
        for start in range(0, span, KEY_BLOCK):
            part = pl.ds(start, KEY_BLOCK)
            block = dot_nt(k_ref[part, :], own) + bias_ref[part, :]
            score[part, :] = block
            largest = jnp.maximum(largest, fold_rows(block, jnp.max))
        largest = jnp.max(largest, axis=0, keepdims=True)
        total = jnp.zeros((8, rows), F32)
        for start in range(0, span, KEY_BLOCK):
            part = pl.ds(start, KEY_BLOCK)
            block = jnp.exp(score[part, :] - largest)
            total = total + fold_rows(block, jnp.sum)
            e_ref[head, part, :] = block.astype(BF)
        inverse = 1.0 / jnp.sum(total, axis=0, keepdims=True)
        rl_ref[0, head : head + 1, :] = inverse
        outs.append(dot(vt[head * HEAD_DIM : (head + 1) * HEAD_DIM, :], e_ref[head]) * inverse)
        sums.append(jnp.broadcast_to(inverse, (HEAD_DIM, rows)))
    o_ref[...] = jnp.concatenate(outs, axis=0).T.astype(BF)
    rlb_ref[...] = jnp.concatenate(sums, axis=0).T


def attend_back_kernel(
    q_ref, k_ref, kt_ref, v_ref, e_ref, rl_ref, rlb_ref, do_ref, cos_ref, sin_ref, xt_ref,
    dq_ref, dk_ref, dv_ref, gq_ref, gk_ref, gv_ref,
    dprob, dscore, dk, dv,
):
    span, rows = k_ref.shape[0], q_ref.shape[0]
    scaled = do_ref[...].astype(F32) * rlb_ref[...]
    dqs = []
    for head in range(2):
        down = head_lanes(scaled, head).astype(BF)
        own = head_lanes(q_ref[...], head)
        inner = jnp.zeros((8, rows), F32)
        for start in range(0, span, KEY_BLOCK):
            part = pl.ds(start, KEY_BLOCK)
            block = dot_nt(v_ref[part, :], down)
            dprob[part, :] = block
            inner = inner + fold_rows(block * e_ref[head, part, :].astype(F32), jnp.sum)
        inner = jnp.sum(inner, axis=0, keepdims=True) * rl_ref[0, head : head + 1, :]
        for start in range(0, span, KEY_BLOCK):
            part = pl.ds(start, KEY_BLOCK)
            weight = e_ref[head, part, :]
            block = (weight.astype(F32) * (dprob[part, :] - inner)).astype(BF)
            dscore[part, :] = block
            dk_part = dot(block, own)
            dv_part = dot(weight, down)
            if head == 0:
                dk[part, :] = dk_part
                dv[part, :] = dv_part
            else:
                dk[part, :] += dk_part
                dv[part, :] += dv_part
        dqs.append(dot(kt_ref[head * HEAD_DIM : (head + 1) * HEAD_DIM, :], dscore[...]))
    dquery = jnp.concatenate(dqs, axis=0).T * HEAD_DIM**-0.5
    dquery = dquery * cos_ref[span - rows :, :] - swapped_halves(dquery) * sin_ref[span - rows :, :]
    dquery = dquery.astype(BF)
    dq_ref[...] = dquery
    dkeys = dk[...]
    dkeys = (dkeys * cos_ref[...] - swapped_halves(dkeys) * sin_ref[...]).astype(BF)
    dvalues = dv[...].astype(BF)
    dk_ref[...] = dkeys
    dv_ref[...] = dvalues
    gq_ref[...] = dot(xt_ref[:, span - rows :], dquery).astype(BF)
    both = dot(xt_ref[...], jnp.concatenate([dkeys, dvalues], axis=1))
    gk_ref[...] = both[:, :LANES].astype(BF)
    gv_ref[...] = both[:, LANES:].astype(BF)


def middle_kernel(
    o_ref, spread_ref, w_ref, small_ref, x_ref, pick_ref, put_ref,
    h_ref, scale_ref, a_ref, at_ref, ap_ref, out_ref, gate_ref, gain_ref,
    *, gain_lane,
):
    spread = spread_ref[...]
    padded = dot(o_ref[...], spread).astype(BF)
    hidden = x_ref[...].astype(F32) + dot(padded, w_ref[...])
    h_ref[...] = hidden
    scale = lax.rsqrt(jnp.mean(hidden * hidden, axis=-1, keepdims=True) + EPSILON)
    scale_ref[...] = scale
    small = small_ref[...]
    rows = small.astype(F32).T[gain_lane // 8 * 8 : gain_lane // 8 * 8 + 8, :].astype(BF)
    gain = dot_nt(rows, spread)[gain_lane % 8 : gain_lane % 8 + 1, :]
    gain_ref[...] = gain
    normed = hidden * scale * gain
    low = normed.astype(BF)
    a_ref[...] = low
    at_ref[...] = low.astype(F32).T.astype(BF)
    low_padded = dot(low, spread).astype(BF)
    ap_ref[...] = low_padded
    logits = dot(low_padded, small)
    first, second = pick_ref[0], pick_ref[1]
    chosen_first = jnp.sum(logits * first, axis=-1, keepdims=True)
    chosen_second = jnp.sum(logits * second, axis=-1, keepdims=True)
    largest = jnp.maximum(chosen_first, chosen_second)
    chosen_first = jnp.exp(chosen_first - largest)
    chosen_second = jnp.exp(chosen_second - largest)
    total = chosen_first + chosen_second
    table = (chosen_first / total) * first + (chosen_second / total) * second
    gate_ref[...] = table
    high, rest = split_high_low(table)
    extra = (high.astype(F32) + pltpu.roll(rest.astype(F32), LANES // 2, 1)).astype(BF)
    put = put_ref[...]
    width = a_ref.shape[1]
    out_ref[:, :width] = dot(put, low).astype(BF)
    out_ref[:, width:] = dot(put, extra).astype(BF)


def gated_forward(x, w_gate, w_lift):
    gate, lift = dot(x, w_gate), dot(x, w_lift)
    sigmoid = 1.0 / (1.0 + jnp.exp(-gate))
    act = gate * sigmoid
    slope = sigmoid * (1.0 + gate * (1.0 - sigmoid))
    return (act * lift).astype(BF), act, lift * slope


def add_up(total_ref, value):
    @pl.when(pl.program_id(0) == 0)
    def _():
        total_ref[...] = value

    @pl.when(pl.program_id(0) != 0)
    def _():
        total_ref[...] += value


def flush(step, steps, copies):
    @pl.when(step >= 2)
    def _():
        for copy in copies(step % 2, step):
            copy.wait()


def send(step, steps, copies):
    for copy in copies(step % 2, step):
        copy.start()

    @pl.when(step == steps - 1)
    def _():
        for copy in copies((step + 1) % 2, step):
            copy.wait()
        for copy in copies(step % 2, step):
            copy.wait()


def shared_kernel(
    xp_ref, xt_ref, dy_ref, wg_ref, wl_ref, wd_ref, y_ref, dx_ref, grads_ref, gin, gdown, sems
):
    step, steps = pl.program_id(0), pl.num_programs(0)
    model, columns = xt_ref.shape[0], gdown.shape[2]
    fsdp, piece = gdown.shape[1], gdown.shape[3] // 2

    def copies(slot, now):
        part = pl.ds(pl.multiple_of(now * 2 * piece, 2 * piece), 2 * piece)
        yield pltpu.make_async_copy(
            gin.at[slot], grads_ref.at[now, pl.ds(0, 2 * model)], sems.at[slot, 0]
        )
        for column in range(columns):
            yield pltpu.make_async_copy(
                gdown.at[slot, :, column],
                grads_ref.at[:, pl.ds(2 * model + column * TILE + part.start, 2 * piece)],
                sems.at[slot, 1 + column],
            )

    flush(step, steps, copies)
    slot = step % 2
    half = wd_ref.shape[1] // 2
    packed = wd_ref[...].astype(F32)
    packed = packed.reshape(packed.shape[0] // 8, 8, packed.shape[1])
    w_down = (
        jnp.concatenate([packed[:, :, :half], packed[:, :, half:]], axis=1)
        .reshape(-1, half)
        .astype(BF)
    )
    w_gate, w_lift, dy, xt = wg_ref[...], wl_ref[...], dy_ref[...], xt_ref[...]
    hidden, act, slope = gated_forward(xp_ref[...], w_gate, w_lift)
    dhidden = dot_nt(dy, w_down)
    dgate, dlift = (dhidden * slope).astype(BF), (dhidden * act).astype(BF)
    add_up(y_ref, dot(hidden, w_down))
    add_up(dx_ref, dot_nt(dgate, w_gate) + dot_nt(dlift, w_lift))
    gin[slot, :model, :] = dot(xt, dgate).astype(BF)
    gin[slot, model:, :] = dot(xt, dlift).astype(BF)
    down = dot_tn(hidden, dy).astype(BF)
    for owner in range(fsdp):
        for part in range(2):
            first = (part * fsdp + owner) * piece
            for column in range(columns):
                gdown[slot, owner, column, part * piece : (part + 1) * piece, :] = down[
                    first : first + piece, column * TILE : (column + 1) * TILE
                ]
    send(step, steps, copies)


def unpack_down(packed, model):
    return jnp.concatenate(
        [packed[start : start + TILE] for start in range(0, model, TILE)], axis=1
    )


def expert_kernel(
    in_ref, g_ref, wg_ref, wl_ref, wd_ref, y_ref, hidden_ref, act_ref, slope_ref, y_sum
):
    model = g_ref.shape[1]
    w_gate = wg_ref[...].reshape(model, TILE)
    w_lift = wl_ref[...].reshape(model, TILE)
    hidden, act, slope = gated_forward(in_ref[:, :model], w_gate, w_lift)
    hidden_ref[...] = hidden
    act_ref[...] = act.astype(BF)
    slope_ref[...] = slope.astype(BF)
    add_up(y_sum, dot(hidden, unpack_down(wd_ref[0], model)))

    @pl.when(pl.program_id(0) == pl.num_programs(0) - 1)
    def _():
        result = y_sum[...].astype(BF)
        y_ref[:, :model] = result
        dgate = jnp.sum(result.astype(F32) * g_ref[...].astype(F32), axis=-1, keepdims=True)
        high, rest = split_high_low(dgate)
        lane = lax.broadcasted_iota(jnp.int32, (1, LANES), 1)
        y_ref[:, model:] = (
            jnp.where(lane == 0, high.astype(F32), 0.0)
            + jnp.where(lane == 1, rest.astype(F32), 0.0)
        ).astype(BF)


def expert_back_kernel(
    in_ref, g_ref, own_ref, wg_ref, wl_ref, wd_ref, hidden_ref, act_ref, slope_ref,
    dx_ref, grads_ref,
    xt, dy, dx_sum, gin, gdown, sems,
):
    model = g_ref.shape[1]
    step, steps = pl.program_id(0), pl.num_programs(0)
    in_rows = gin.shape[3]

    def copies(slot, now):
        for part in range(2):
            first = pl.multiple_of((part * steps + now) * in_rows, in_rows)
            yield pltpu.make_async_copy(
                gin.at[slot, part], grads_ref.at[:, pl.ds(first, in_rows)], sems.at[slot, part]
            )
        yield pltpu.make_async_copy(
            gdown.at[slot], grads_ref.at[now, pl.ds(2 * steps * in_rows, model)], sems.at[slot, 2]
        )

    @pl.when(step == 0)
    def _():
        xt[...] = in_ref[:, :model].astype(F32).T.astype(BF)
        gate = jnp.sum(in_ref[:, model:].astype(F32) * own_ref[...], axis=-1, keepdims=True)
        dy[...] = (g_ref[...].astype(F32) * gate).astype(BF)

    flush(step, steps, copies)
    slot = step % 2
    w_gate = wg_ref[...].reshape(model, TILE)
    w_lift = wl_ref[...].reshape(model, TILE)
    w_down = unpack_down(wd_ref[0], model)
    dhidden = dot_nt(dy[...], w_down)
    dgate = (dhidden * slope_ref[...].astype(F32)).astype(BF)
    dlift = (dhidden * act_ref[...].astype(F32)).astype(BF)
    add_up(dx_sum, dot_nt(dgate, w_gate) + dot_nt(dlift, w_lift))
    shape = (gin.shape[2], in_rows, TILE)
    gin[slot, 0] = dot(xt[...], dgate).astype(BF).reshape(shape)
    gin[slot, 1] = dot(xt[...], dlift).astype(BF).reshape(shape)
    down = dot_tn(hidden_ref[...], dy[...]).astype(BF)
    for column in range(model // TILE):
        part = slice(column * TILE, (column + 1) * TILE)
        gdown[slot, part, :] = down[:, part]
    send(step, steps, copies)

    @pl.when(step == steps - 1)
    def _():
        dx_ref[...] = dx_sum[...].astype(BF)


def combine_kernel(y_ref, first_ref, second_ref, pick_ref, gate_ref, h_ref, shared_ref, out_ref):
    table = gate_ref[...]
    gate_first = jnp.sum(table * pick_ref[0], axis=-1, keepdims=True)
    gate_second = jnp.sum(table * pick_ref[1], axis=-1, keepdims=True)
    mixture = gate_first * dot(first_ref[...], y_ref[...])
    mixture = mixture + gate_second * dot(second_ref[...], y_ref[...])
    out_ref[0] = (h_ref[...] + mixture + shared_ref[...]).astype(BF)


def middle_back_kernel(
    back_ref, extra_ref, take_ref, slot_ref, pick_ref, gate_ref, small_ref, spread_ref, dshared_ref, g_ref,
    h_ref, scale_ref, gain_ref, w_ref,
    dh_ref, dhb_ref, do_ref, dlogits_ref, ggain_ref,
):
    model = g_ref.shape[1]
    take, spread = take_ref[...], spread_ref[...]
    extra = extra_ref[...].astype(F32)
    slots = slot_ref[...]
    lane = lax.broadcasted_iota(jnp.int32, (1, LANES), 1)
    high = jnp.sum(jnp.where(lane == 0, extra, 0.0), axis=-1, keepdims=True)
    rest = jnp.sum(jnp.where(lane == 1, extra, 0.0), axis=-1, keepdims=True)
    dgates = dot(take, (high * slots).astype(BF)) + dot(take, (rest * slots).astype(BF))
    table = gate_ref[...]
    first, second = pick_ref[0], pick_ref[1]
    gated = jnp.sum(table * dgates, axis=-1, keepdims=True)
    dlogits = (table * (dgates - gated)).astype(BF)
    dlogits_ref[...] = dlogits
    padded = dshared_ref[...] + dot_nt(dlogits, small_ref[...])
    high, rest = split_high_low(padded)
    da = dot_nt(high, spread) + dot_nt(rest, spread) + dot(take, back_ref[...])
    hidden, scale = h_ref[...], scale_ref[...]
    ggain_ref[...] = jnp.sum(da * hidden * scale, axis=0, keepdims=True)
    weighted = da * gain_ref[...]
    mean = jnp.mean(weighted * hidden, axis=-1, keepdims=True)
    dhidden = g_ref[...].astype(F32) + scale * weighted - hidden * (scale * scale * scale) * mean
    dh_ref[...] = dhidden
    low = dhidden.astype(BF)
    dhb_ref[...] = low
    do_ref[...] = dot_nt(dot_nt(low, w_ref[...]).astype(BF), spread).astype(BF)


def project_back_kernel(
    dq_ref, dk_ref, dv_ref, wq_ref, wk_ref, wv_ref, spread_ref, halo_ref, own_ref, total
):
    total[...] = dot_nt(dk_ref[...], wk_ref[...]) + dot_nt(dv_ref[...], wv_ref[...])

    @pl.when(pl.program_id(0) == pl.num_programs(0) - 1)
    def _():
        total[...] += dot_nt(dq_ref[...], wq_ref[...])

    high, rest = split_high_low(total[...])
    spread = spread_ref[...]
    da = dot_nt(high, spread) + dot_nt(rest, spread)
    halo_ref[...] = da.astype(BF)
    own_ref[...] = da


def per_device(
    tokens,
    segments,
    routes,
    w_qkv,
    w_out,
    w_router,
    shared_in,
    shared_down,
    attn_gain,
    ffn_gain,
    expert_in,
    expert_down,
    cotangent,
):
    ctx, fsdp = lax.axis_size("ctx"), lax.axis_size("fsdp")
    ctx_index, core = lax.axis_index("ctx"), lax.axis_index("fsdp") % 2
    devices = ctx * fsdp
    rows, model = tokens.shape[1], tokens.shape[2]
    reach = max(1, WIN // rows)
    span = (reach + 1) * rows
    capacity = max(2, 3 * rows * TOPK // (2 * ctx))
    slots = ctx * capacity
    own = w_qkv.shape[0]
    owned_down = shared_down.shape[0]
    experts = w_router.shape[1]
    ff = shared_in.shape[1] // 2
    tiles = ff // TILE
    padded = devices * PAD_ROWS
    width_qkv = w_qkv.shape[1]

    x, g = tokens[0], cotangent[0]
    small = jnp.concatenate(
        [w_router, attn_gain[:, None], ffn_gain[:, None], jnp.zeros((own, LANES - experts - 2), BF)],
        axis=1,
    )
    rows_packed = jnp.pad(
        jnp.concatenate([w_qkv, w_out, shared_in, small], axis=1), ((0, PAD_ROWS - own), (0, 0))
    )
    packed = jnp.concatenate([shared_down[:8], shared_down[8:], rows_packed], axis=1)
    dense = lax.all_gather(packed, ("ctx", "fsdp"), axis=0, tiled=True)
    at_qkv = 2 * model
    at_out = at_qkv + width_qkv
    at_shared = at_out + model
    at_small = at_shared + 2 * ff
    in_rows, down_rows = expert_in.shape[1], expert_down.shape[1]
    expert_packed = jnp.concatenate(
        [
            expert_in[0].reshape(in_rows, 2 * tiles, TILE).transpose(1, 0, 2).reshape(-1, TILE),
            expert_down[0].reshape(down_rows, model // TILE, TILE).transpose(1, 0, 2).reshape(-1, TILE),
        ],
        axis=0,
    )
    expert_full = lax.all_gather(expert_packed, "fsdp", axis=0)

    segment_row = jnp.zeros((16, model), BF).at[0, :rows].set(segments[0].astype(BF))
    carried = jnp.concatenate([x, segment_row], axis=0)
    arrived = [shifted(carried, "ctx", distance) for distance in range(reach, 0, -1)]
    span_x = jnp.concatenate([part[:rows] for part in arrived] + [x], axis=0)
    span_segments = jnp.concatenate(
        [part[rows, :rows] for part in arrived] + [segments[0].astype(BF)], axis=0
    )
    span_float = span_x.astype(F32)
    span_scale = lax.rsqrt(jnp.mean(span_float * span_float, axis=-1, keepdims=True) + EPSILON)
    feature = jnp.arange(model, dtype=jnp.int32)
    spread = (
        (feature // own * PAD_ROWS + feature % own)[:, None]
        == jnp.arange(padded, dtype=jnp.int32)[None, :]
    ).astype(BF)
    span_padded = dot(span_x, spread).astype(BF)
    query_place = jnp.arange(rows, dtype=jnp.int32)[None, :] + reach * rows
    key_place = jnp.arange(span, dtype=jnp.int32)[:, None]
    allowed = (
        (key_place <= query_place)
        & (query_place - key_place < WIN)
        & (key_place + (ctx_index - reach) * rows >= 0)
        & (span_segments[:, None] == segments[0].astype(BF)[None, :])
    )
    bias = jnp.where(allowed, 0.0, -1e30).astype(F32)
    cosine, sine = rotary_tables(span, (ctx_index - reach) * rows)

    route_own = routes[0]
    expert_ids = jnp.arange(experts, dtype=jnp.int32)
    hits = route_own[:, :, None] == expert_ids[None, None, :]
    member = jnp.sum(hits.astype(jnp.int32), axis=1)
    ranking = jnp.cumsum(member, axis=0, dtype=jnp.int32) - 1
    slot_ids = jnp.arange(capacity, dtype=jnp.int32)
    placed = (member[:, :, None] > 0) & (ranking[:, :, None] == slot_ids[None, None, :])
    take = placed.astype(BF).reshape(rows, slots)
    put = take.T
    selector = (
        (hits[:, :, :, None] & placed[:, None, :, :]).astype(BF).reshape(rows, TOPK * slots)
    )
    picked = jnp.pad(
        hits.astype(F32).transpose(1, 0, 2), ((0, 0), (0, 0), (0, LANES - experts))
    )
    slot_expert = (
        (jnp.arange(slots, dtype=jnp.int32) // capacity)[:, None]
        == jnp.arange(LANES, dtype=jnp.int32)[None, :]
    ).astype(F32)
    lane = jnp.arange(LANES, dtype=jnp.int32)[None, :]
    own_lanes = ((lane == ctx_index) | (lane == ctx_index + LANES // 2)).astype(F32)

    def exchange(values):
        return lax.all_to_all(
            values.reshape(ctx, values.shape[0] // ctx, values.shape[1]),
            "ctx",
            split_axis=0,
            concat_axis=0,
            tiled=True,
        ).reshape(values.shape)

    slot_g = exchange(dot(put, g).astype(BF))

    span_padded, slot_g = lax.optimization_barrier((span_padded, slot_g))
    pairs = model // LANES
    at = at_qkv // LANES
    small_spec = pl.BlockSpec((padded, LANES), lambda *_: (0, at_small // LANES))
    pair_spec = lambda height: pl.BlockSpec((height, LANES), lambda j: (0, j))
    q, k, kt, v, e, rl, rlb, attended = pl.pallas_call(
        functools.partial(attend_kernel, gain_lane=experts),
        grid=(pairs,),
        in_specs=[
            whole(span_padded),
            whole(span_scale),
            small_spec,
            pl.BlockSpec((padded, LANES), lambda j: (0, at + j)),
            pl.BlockSpec((padded, LANES), lambda j: (0, at + pairs + j)),
            pl.BlockSpec((padded, LANES), lambda j: (0, at + 2 * pairs + j)),
            whole(cosine),
            whole(sine),
            whole(bias),
        ],
        out_specs=[
            pair_spec(rows),
            pair_spec(span),
            pl.BlockSpec((LANES, span), lambda j: (j, 0)),
            pair_spec(span),
            pl.BlockSpec((2, span, rows), lambda j: (j, 0, 0)),
            pl.BlockSpec((1, 8, rows), lambda j: (j, 0, 0)),
            pair_spec(rows),
            pair_spec(rows),
        ],
        out_shape=[
            jax.ShapeDtypeStruct((rows, model), BF),
            jax.ShapeDtypeStruct((span, model), BF),
            jax.ShapeDtypeStruct((model, span), BF),
            jax.ShapeDtypeStruct((span, model), BF),
            jax.ShapeDtypeStruct((HEADS, span, rows), BF),
            jax.ShapeDtypeStruct((pairs, 8, rows), F32),
            jax.ShapeDtypeStruct((rows, model), F32),
            jax.ShapeDtypeStruct((rows, model), BF),
        ],
        scratch_shapes=[
            pltpu.VMEM((span, padded), BF),
            pltpu.VMEM((span, rows), F32),
            pltpu.VMEM((LANES, span), BF),
        ],
        compiler_params=params(VMEM_MB),
        cost_estimate=cost(20),
        name="attend",
    )(span_padded, span_scale, dense, dense, dense, dense, cosine, sine, bias)

    out_spec = pl.BlockSpec((padded, model), lambda *_: (0, at_out // model))
    hidden, scale_two, normed, normed_t, normed_padded, outgoing, gates, gain_two = pl.pallas_call(
        functools.partial(middle_kernel, gain_lane=experts + 1),
        grid=(1,),
        in_specs=[
            whole(attended),
            whole(spread),
            out_spec,
            small_spec,
            whole(x),
            whole(picked),
            whole(put),
        ],
        out_specs=[
            pl.BlockSpec((rows, model), lambda *_: (0, 0)),
            pl.BlockSpec((rows, 1), lambda *_: (0, 0)),
            pl.BlockSpec((rows, model), lambda *_: (0, 0)),
            pl.BlockSpec((model, rows), lambda *_: (0, 0)),
            pl.BlockSpec((rows, padded), lambda *_: (0, 0)),
            pl.BlockSpec((slots, model + LANES), lambda *_: (0, 0)),
            pl.BlockSpec((rows, LANES), lambda *_: (0, 0)),
            pl.BlockSpec((1, model), lambda *_: (0, 0)),
        ],
        out_shape=[
            jax.ShapeDtypeStruct((rows, model), F32),
            jax.ShapeDtypeStruct((rows, 1), F32),
            jax.ShapeDtypeStruct((rows, model), BF),
            jax.ShapeDtypeStruct((model, rows), BF),
            jax.ShapeDtypeStruct((rows, padded), BF),
            jax.ShapeDtypeStruct((slots, model + LANES), BF),
            jax.ShapeDtypeStruct((rows, LANES), F32),
            jax.ShapeDtypeStruct((1, model), F32),
        ],
        compiler_params=params(VMEM_MB),
        cost_estimate=cost(5),
        name="middle",
    )(attended, spread, dense, dense, x, picked, put)
    incoming = exchange(outgoing)

    columns = model // TILE
    at_gate = at_shared // TILE
    packed_rows = 3 * model
    shared_out, dshared, gshared = pl.pallas_call(
        shared_kernel,
        grid=(tiles,),
        in_specs=[
            whole(normed_padded),
            whole(normed_t),
            whole(g),
            pl.BlockSpec((padded, TILE), lambda t: (0, at_gate + t)),
            pl.BlockSpec((padded, TILE), lambda t: (0, at_gate + tiles + t)),
            pl.BlockSpec((padded // tiles, 2 * model), lambda t: (t, 0)),
        ],
        out_specs=[
            pl.BlockSpec((rows, model), lambda t: (0, 0)),
            pl.BlockSpec((rows, padded), lambda t: (0, 0)),
            pl.BlockSpec(memory_space=pl.ANY),
        ],
        out_shape=[
            jax.ShapeDtypeStruct((rows, model), F32),
            jax.ShapeDtypeStruct((rows, padded), F32),
            jax.ShapeDtypeStruct((fsdp, packed_rows, TILE), BF),
        ],
        scratch_shapes=[
            pltpu.VMEM((2, 2 * model, TILE), BF),
            pltpu.VMEM((2, fsdp, columns, 2 * owned_down, TILE), BF),
            pltpu.SemaphoreType.DMA((2, 1 + columns)),
        ],
        compiler_params=params(VMEM_MB),
        cost_estimate=cost(15),
        name="shared",
    )(normed_padded, normed_t, g, dense, dense, dense)
    shared_sum = lax.psum_scatter(after(gshared, incoming), "fsdp", scatter_dimension=0)

    expert_specs = [
        pl.BlockSpec((fsdp, in_rows, TILE), lambda t: (0, t, 0)),
        pl.BlockSpec((fsdp, in_rows, TILE), lambda t: (0, tiles + t, 0)),
        pl.BlockSpec((1, model, TILE), lambda t: (t, 2 * in_rows * tiles // model, 0)),
    ]
    unit_spec = pl.BlockSpec((slots, TILE), lambda t: (0, t))
    expert_y, *units = pl.pallas_call(
        expert_kernel,
        grid=(tiles,),
        in_specs=[whole(incoming), whole(slot_g), *expert_specs],
        out_specs=[
            pl.BlockSpec((slots, model + LANES), lambda t: (0, 0)),
            unit_spec,
            unit_spec,
            unit_spec,
        ],
        out_shape=[jax.ShapeDtypeStruct((slots, model + LANES), BF)]
        + [jax.ShapeDtypeStruct((slots, ff), BF)] * 3,
        scratch_shapes=[pltpu.VMEM((slots, model), F32)],
        compiler_params=params(VMEM_MB),
        cost_estimate=cost(14),
        name="expert",
    )(incoming, slot_g, expert_full, expert_full, expert_full)
    returned_y = exchange(expert_y)
    back, gexpert = pl.pallas_call(
        expert_back_kernel,
        grid=(tiles,),
        in_specs=[
            whole(incoming),
            whole(slot_g),
            whole(own_lanes),
            *expert_specs,
            unit_spec,
            unit_spec,
            unit_spec,
        ],
        out_specs=[
            pl.BlockSpec((slots, model), lambda t: (0, 0)),
            pl.BlockSpec(memory_space=pl.ANY),
        ],
        out_shape=[
            jax.ShapeDtypeStruct((slots, model), BF),
            jax.ShapeDtypeStruct((fsdp, packed_rows, TILE), BF),
        ],
        scratch_shapes=[
            pltpu.VMEM((model, slots), BF),
            pltpu.VMEM((slots, model), BF),
            pltpu.VMEM((slots, model), F32),
            pltpu.VMEM((2, 2, fsdp, in_rows, TILE), BF),
            pltpu.VMEM((2, model, TILE), BF),
            pltpu.SemaphoreType.DMA((2, 3)),
        ],
        compiler_params=params(VMEM_MB),
        cost_estimate=cost(24),
        name="expert_back",
    )(incoming, slot_g, own_lanes, expert_full, expert_full, expert_full, *units)
    returned = exchange(after(back, returned_y))
    expert_sum = lax.psum_scatter(after(gexpert, returned_y), "fsdp", scatter_dimension=0)

    mixed = pl.pallas_call(
        combine_kernel,
        grid=(1,),
        in_specs=[
            pl.BlockSpec((slots, model), lambda *_: (0, 0)),
            pl.BlockSpec((rows, slots), lambda *_: (0, 0)),
            pl.BlockSpec((rows, slots), lambda *_: (0, 1)),
            whole(picked),
            whole(gates),
            whole(hidden),
            whole(shared_out),
        ],
        out_specs=pl.BlockSpec((1, rows, model), lambda *_: (0, 0, 0)),
        out_shape=jax.ShapeDtypeStruct((1, rows, model), BF),
        compiler_params=params(VMEM_MB),
        cost_estimate=cost(3),
        name="combine",
    )(returned_y, selector, selector, picked, gates, hidden, shared_out)

    dhidden, dhidden_low, dattended, dlogits, ggain_two = pl.pallas_call(
        middle_back_kernel,
        grid=(1,),
        in_specs=[
            whole(returned),
            pl.BlockSpec((slots, LANES), lambda *_: (0, model // LANES)),
            whole(take),
            whole(slot_expert),
            whole(picked),
            whole(gates),
            small_spec,
            whole(spread),
            whole(dshared),
            whole(g),
            whole(hidden),
            whole(scale_two),
            whole(gain_two),
            out_spec,
        ],
        out_specs=[
            pl.BlockSpec((rows, model), lambda *_: (0, 0)),
            pl.BlockSpec((rows, model), lambda *_: (0, 0)),
            pl.BlockSpec((rows, model), lambda *_: (0, 0)),
            pl.BlockSpec((rows, LANES), lambda *_: (0, 0)),
            pl.BlockSpec((1, model), lambda *_: (0, 0)),
        ],
        out_shape=[
            jax.ShapeDtypeStruct((rows, model), F32),
            jax.ShapeDtypeStruct((rows, model), BF),
            jax.ShapeDtypeStruct((rows, model), BF),
            jax.ShapeDtypeStruct((rows, LANES), BF),
            jax.ShapeDtypeStruct((1, model), F32),
        ],
        compiler_params=params(VMEM_MB),
        cost_estimate=cost(6),
        name="middle_back",
    )(
        returned, returned_y, take, slot_expert, picked, gates, dense, spread, dshared, g, hidden, scale_two,
        gain_two, dense,
    )

    def split_ctx(values):
        return lax.all_to_all(
            values.reshape(ctx, model // ctx, values.shape[1]),
            "ctx",
            split_axis=0,
            concat_axis=0,
            tiled=True,
        )

    def core_halves(first, second):
        kept = jnp.where(core == 0, first, second)
        sent = jnp.where(core == 0, second, first)
        partner = lax.ppermute(sent, "fsdp", [(i, i ^ 1) for i in range(fsdp)])
        return (kept.astype(F32) + partner.astype(F32)).astype(BF)

    rows_in = 2 * model
    shared_in_part = shared_sum[:rows_in].reshape(2, ctx, model // ctx, TILE)
    shared_down_part = shared_sum[rows_in:].reshape(columns, ctx, owned_down, TILE)
    half = model // 2
    block = model // ctx
    gout = dot(attended.T, dhidden_low).astype(BF)
    grouter = dot(normed_t, dlogits)
    small_grads = jnp.concatenate(
        [grouter[:, :experts], ggain_two.T, jnp.zeros((model, LANES - experts - 1), F32)], axis=1
    ).astype(BF)
    out_pieces = core_halves(
        jnp.concatenate([gout[:, :half], small_grads], axis=1),
        jnp.concatenate([gout[:, half:], jnp.zeros((model, LANES), BF)], axis=1),
    )
    early_pieces = jnp.concatenate(
        [
            shared_in_part.transpose(1, 0, 2, 3).reshape(ctx, -1, TILE),
            shared_down_part.transpose(1, 0, 2, 3).reshape(ctx, -1, TILE),
            out_pieces[:, :TILE].reshape(ctx, block, TILE),
            out_pieces[:, TILE:].reshape(ctx, block, TILE),
        ],
        axis=1,
    )
    early_own = jnp.sum(
        lax.all_to_all(early_pieces, "ctx", split_axis=0, concat_axis=0, tiled=True).astype(F32),
        axis=0,
    )
    shared_down_end = 2 * block + columns * owned_down

    small_full = dot(spread, dense[:, at_small:])
    first_t = (
        span_x.T.astype(F32) * span_scale.reshape(1, span) * small_full[:, experts : experts + 1]
    ).astype(BF)
    dq, dk, dv, gq, gk, gv = pl.pallas_call(
        attend_back_kernel,
        grid=(pairs,),
        in_specs=[
            pair_spec(rows),
            pair_spec(span),
            pl.BlockSpec((LANES, span), lambda j: (j, 0)),
            pair_spec(span),
            pl.BlockSpec((2, span, rows), lambda j: (j, 0, 0)),
            pl.BlockSpec((1, 8, rows), lambda j: (j, 0, 0)),
            pair_spec(rows),
            pair_spec(rows),
            whole(cosine),
            whole(sine),
            whole(first_t),
        ],
        out_specs=[
            pair_spec(rows),
            pair_spec(span),
            pair_spec(span),
            pair_spec(model),
            pair_spec(model),
            pair_spec(model),
        ],
        out_shape=[
            jax.ShapeDtypeStruct((rows, model), BF),
            jax.ShapeDtypeStruct((span, model), BF),
            jax.ShapeDtypeStruct((span, model), BF),
            jax.ShapeDtypeStruct((model, model), BF),
            jax.ShapeDtypeStruct((model, model), BF),
            jax.ShapeDtypeStruct((model, model), BF),
        ],
        scratch_shapes=[
            pltpu.VMEM((span, rows), F32),
            pltpu.VMEM((span, rows), BF),
            pltpu.VMEM((span, LANES), F32),
            pltpu.VMEM((span, LANES), F32),
        ],
        compiler_params=params(VMEM_MB),
        cost_estimate=cost(22),
        name="attend_back",
    )(q, k, kt, v, e, rl, rlb, dattended, cosine, sine, first_t)
    group_first = jnp.concatenate([gk, gq[:, :half]], axis=1)
    group_second = jnp.concatenate([gv, gq[:, half:]], axis=1)
    late = split_ctx(core_halves(after(group_first, early_own), group_second))
    late_own = jnp.sum(late.astype(F32), axis=0)

    at_model = at_qkv // model
    dspan, down = pl.pallas_call(
        project_back_kernel,
        grid=(reach + 1,),
        in_specs=[
            whole(dq),
            pl.BlockSpec((rows, model), lambda b: (b, 0)),
            pl.BlockSpec((rows, model), lambda b: (b, 0)),
            pl.BlockSpec((padded, model), lambda b: (0, at_model)),
            pl.BlockSpec((padded, model), lambda b: (0, at_model + 1)),
            pl.BlockSpec((padded, model), lambda b: (0, at_model + 2)),
            whole(spread),
        ],
        out_specs=[
            pl.BlockSpec((rows, model), lambda b: (b, 0)),
            pl.BlockSpec((rows, model), lambda b: (0, 0)),
        ],
        out_shape=[
            jax.ShapeDtypeStruct((span, model), BF),
            jax.ShapeDtypeStruct((rows, model), F32),
        ],
        scratch_shapes=[pltpu.VMEM((rows, padded), F32)],
        compiler_params=params(VMEM_MB),
        cost_estimate=cost(10),
        name="project_back",
    )(dq, dk, dv, dense, dense, dense, spread)

    grad_shared_down = (
        early_own[2 * block : shared_down_end]
        .reshape(columns, owned_down, TILE)
        .transpose(1, 0, 2)
        .reshape(owned_down, model)
    )
    last = jnp.concatenate(
        [
            late_own,
            early_own[shared_down_end : shared_down_end + block],
            early_own[shared_down_end + block :],
            early_own[:block],
            early_own[block : 2 * block],
        ],
        axis=1,
    ).reshape(fsdp, own, -1)
    last = lax.all_to_all(last, "fsdp", split_axis=0, concat_axis=0, tiled=True)
    wide = late_own.shape[1] + 2 * TILE
    per_core = jnp.sum(last[:, :, :wide].reshape(fsdp // 2, 2, own, wide), axis=0)
    small_total = per_core[0, :, wide - LANES :]
    grad_qkv = jnp.concatenate(
        [
            per_core[0, :, model : model + half],
            per_core[1, :, model : model + half],
            per_core[0, :, :model],
            per_core[1, :, :model],
        ],
        axis=1,
    )
    at_half = model + half
    grad_out = jnp.concatenate(
        [per_core[0, :, at_half : at_half + half], per_core[1, :, at_half : at_half + half]], axis=1
    )
    grad_gain_one = jnp.sum(grad_qkv * w_qkv.astype(F32), axis=1) / attn_gain.astype(F32)
    shared_last = last[:, :, wide:].reshape(fsdp, own, 2, TILE)
    grad_shared_in = shared_last.transpose(1, 2, 0, 3).reshape(own, 2 * ff)

    total = down
    for distance in range(1, reach + 1):
        lower = (reach - distance) * rows
        total = total + shifted(dspan[lower : lower + rows], "ctx", -distance).astype(F32)
    input_rows = x.astype(F32)
    scale_one = span_scale[reach * rows :]
    weighted = total * small_full[:, experts][None, :]
    input_grad = (
        dhidden
        + scale_one * weighted
        - input_rows
        * scale_one**3
        * jnp.mean(weighted * input_rows, axis=-1, keepdims=True)
    )[None]

    expert_rows = 2 * tiles * in_rows
    grad_expert_in = (
        expert_sum[:expert_rows]
        .astype(F32)
        .reshape(2 * tiles, in_rows, TILE)
        .transpose(1, 0, 2)
        .reshape(1, in_rows, 2 * ff)
    )
    grad_expert_down = (
        expert_sum[expert_rows:]
        .astype(F32)
        .reshape(columns, down_rows, TILE)
        .transpose(1, 0, 2)
        .reshape(1, down_rows, model)
    )
    return (
        mixed,
        input_grad,
        grad_qkv,
        grad_out,
        small_total[:, :experts],
        grad_shared_in,
        grad_shared_down,
        grad_gain_one,
        small_total[:, experts],
        grad_expert_in,
        grad_expert_down,
    )


def solution(mesh):
    placed = (
        P("fsdp", "ctx", None),
        P("fsdp", "ctx"),
        P("fsdp", "ctx", None),
        P(("ctx", "fsdp"), None),
        P(("ctx", "fsdp"), None),
        P(("ctx", "fsdp"), None),
        P(("ctx", "fsdp"), None),
        P(("ctx", "fsdp"), None),
        P(("ctx", "fsdp")),
        P(("ctx", "fsdp")),
        P("ctx", "fsdp", None),
        P("ctx", "fsdp", None),
        P("fsdp", "ctx", None),
    )
    return jax.shard_map(
        per_device,
        mesh=mesh,
        in_specs=placed,
        out_specs=(
            P("fsdp", "ctx", None),
            P("fsdp", "ctx", None),
            P(("ctx", "fsdp"), None),
            P(("ctx", "fsdp"), None),
            P(("ctx", "fsdp"), None),
            P(("ctx", "fsdp"), None),
            P(("ctx", "fsdp"), None),
            P(("ctx", "fsdp")),
            P(("ctx", "fsdp")),
            P("ctx", "fsdp", None),
            P("ctx", "fsdp", None),
        ),
        check_vma=False,
    )
```

```python
import functools

import jax
import jax.numpy as jnp
from jax import lax
from jax.experimental import pallas as pl
from jax.experimental.pallas import tpu as pltpu
from jax.sharding import PartitionSpec as P

HEADS = 12
HEAD_DIM = 64
TOPK = 2
WIN = 1024
EPSILON = 1e-06

BF = jnp.bfloat16
F32 = jnp.float32
TILE = 256
LANES = 128
KEY_BLOCK = 128
ROW = 4
VMEM_MB = 60


def dot(a, b):
    return jnp.dot(a, b, preferred_element_type=F32)


def dot_nt(a, b):
    return lax.dot_general(a, b, (((1,), (1,)), ((), ())), preferred_element_type=F32)


def dot_tn(a, b):
    return lax.dot_general(a, b, (((0,), (0,)), ((), ())), preferred_element_type=F32)


def params(megabytes):
    return pltpu.CompilerParams(vmem_limit_bytes=megabytes * 1024 * 1024)


def cost(microseconds):
    return pl.CostEstimate(
        flops=int(microseconds * 1.0e9), bytes_accessed=int(microseconds * 1.0e6), transcendentals=0
    )


def after(value, *others):
    return lax.optimization_barrier((value, *others))[0]


def whole(array):
    return pl.BlockSpec(array.shape, lambda *_: (0,) * array.ndim)


def shifted(value, axis, steps):
    count = lax.axis_size(axis)
    leading, last = (max(0, -steps), min(count, count - steps))
    return lax.ppermute(value, axis, [(source, source + steps) for source in range(leading, last)])


def split_high_low(values):
    high = values.astype(BF)
    return high, (values - high.astype(F32)).astype(BF)


def rotary_tables(rows, offset):
    half = HEAD_DIM // 2
    frequency = jnp.exp(-jnp.log(10000.0) * (2.0 * jnp.arange(half, dtype=F32) / HEAD_DIM))
    places = (offset + jnp.arange(rows, dtype=jnp.int32)).astype(F32)
    angles = places[:, None] * frequency[None, :]
    cosine, sine = jnp.cos(angles), jnp.sin(angles)
    return (
        jnp.concatenate([cosine] * 4, axis=1),
        jnp.concatenate([-sine, sine, -sine, sine], axis=1),
    )


def swapped_halves(values):
    lane = lax.broadcasted_iota(jnp.int32, (1, LANES), 1)
    half = HEAD_DIM // 2
    return jnp.where(
        lane % HEAD_DIM < half,
        pltpu.roll(values, LANES - half, 1),
        pltpu.roll(values, half, 1),
    )


def head_lanes(values, head):
    lane = lax.broadcasted_iota(jnp.int32, (1, LANES), 1)
    return jnp.where(lane // HEAD_DIM == head, values, jnp.zeros_like(values))


def fold_rows(values, op):
    return op(values.reshape(values.shape[0] // 8, 8, values.shape[1]), axis=0)


def attend_kernel(
    place_ref, *refs, gain_lane, parts
):
    blocks, refs = refs[:parts], refs[parts:]
    (
        small_ref, wq_ref, wk_ref, wv_ref, cos_ref, sin_ref,
        q_ref, k_ref, kt_ref, v_ref, e_ref, rl_ref, rlb_ref, o_ref, scale_ref,
        normed, score, vt, bias_ref,
    ) = refs
    rows, model = q_ref.shape[0], normed.shape[1]
    span = parts * rows

    @pl.when(pl.program_id(0) == 0)
    def _():
        gain = small_ref[...].astype(F32).T[gain_lane : gain_lane + 1, :]
        query_segment = blocks[-1][rows : rows + 1, :rows].astype(F32)
        query_place = lax.broadcasted_iota(jnp.int32, (rows, rows), 1)
        key_place = lax.broadcasted_iota(jnp.int32, (rows, rows), 0)
        for index, block in enumerate(blocks):
            part = pl.ds(index * rows, rows)
            values = block[:rows, :].astype(F32)
            scale = lax.rsqrt(jnp.mean(values * values, axis=-1, keepdims=True) + EPSILON)
            scale_ref[part, :] = scale
            normed[part, :] = (values * scale * gain).astype(BF)
            key_segment = block[rows : rows + 16, :rows].astype(F32).T[:, :1]
            distance = query_place - key_place + (parts - 1 - index) * rows
            allowed = (distance >= 0) & (distance < WIN) & (key_segment == query_segment)
            allowed = allowed & (place_ref[0] >= parts - 1 - index)
            bias_ref[part, :] = jnp.where(allowed, 0.0, -1e30)

    pair = dot(normed[...], jnp.concatenate([wk_ref[0], wv_ref[0]], axis=1))
    keys = pair[:, :LANES]
    keys = keys * cos_ref[...] + swapped_halves(keys) * sin_ref[...]
    k_ref[...] = keys.astype(BF)
    kt_ref[...] = keys.T.astype(BF)
    values = pair[:, LANES:]
    v_ref[...] = values.astype(BF)
    vt[...] = values.T.astype(BF)
    queries = dot(normed[span - rows :, :], wq_ref[0])
    queries = queries * cos_ref[span - rows :, :] + swapped_halves(queries) * sin_ref[span - rows :, :]
    queries = (queries.astype(BF).astype(F32) * HEAD_DIM**-0.5).astype(BF)
    q_ref[...] = queries

    outs, sums = [], []
    for head in range(2):
        own = head_lanes(queries, head)
        largest = jnp.full((8, rows), -3e38, F32)
        for start in range(0, span, KEY_BLOCK):
            part = pl.ds(start, KEY_BLOCK)
            block = dot_nt(k_ref[part, :], own) + bias_ref[part, :]
            score[part, :] = block
            largest = jnp.maximum(largest, fold_rows(block, jnp.max))
        largest = jnp.max(largest, axis=0, keepdims=True)
        total = jnp.zeros((8, rows), F32)
        for start in range(0, span, KEY_BLOCK):
            part = pl.ds(start, KEY_BLOCK)
            block = jnp.exp(score[part, :] - largest)
            total = total + fold_rows(block, jnp.sum)
            e_ref[head, part, :] = block.astype(BF)
        inverse = 1.0 / jnp.sum(total, axis=0, keepdims=True)
        rl_ref[0, head : head + 1, :] = inverse
        outs.append(dot(vt[head * HEAD_DIM : (head + 1) * HEAD_DIM, :], e_ref[head]) * inverse)
        sums.append(jnp.broadcast_to(inverse, (HEAD_DIM, rows)))
    o_ref[...] = jnp.concatenate(outs, axis=0).T.astype(BF)
    rlb_ref[...] = jnp.concatenate(sums, axis=0).T


def attend_back_kernel(
    core_ref, q_ref, k_ref, kt_ref, v_ref, e_ref, rl_ref, rlb_ref, do_ref, cos_ref, sin_ref, xt_ref, ot_ref, dh_ref,
    *refs,
):
    dq_ref, dk_ref, dv_ref, grads_ref, dprob, dscore, dk, dv = refs[-8:]
    span, rows = k_ref.shape[0], q_ref.shape[0]
    scaled = do_ref[...].astype(F32) * rlb_ref[...]
    dqs = []
    for head in range(2):
        down = head_lanes(scaled, head).astype(BF)
        own = head_lanes(q_ref[...], head)
        inner = jnp.zeros((8, rows), F32)
        for start in range(0, span, KEY_BLOCK):
            part = pl.ds(start, KEY_BLOCK)
            block = dot_nt(v_ref[part, :], down)
            dprob[part, :] = block
            inner = inner + fold_rows(block * e_ref[head, part, :].astype(F32), jnp.sum)
        inner = jnp.sum(inner, axis=0, keepdims=True) * rl_ref[0, head : head + 1, :]
        for start in range(0, span, KEY_BLOCK):
            part = pl.ds(start, KEY_BLOCK)
            weight = e_ref[head, part, :]
            block = (weight.astype(F32) * (dprob[part, :] - inner)).astype(BF)
            dscore[part, :] = block
            dk_part = dot(block, own)
            dv_part = dot(weight, down)
            if head == 0:
                dk[part, :] = dk_part
                dv[part, :] = dv_part
            else:
                dk[part, :] += dk_part
                dv[part, :] += dv_part
        dqs.append(dot(kt_ref[head * HEAD_DIM : (head + 1) * HEAD_DIM, :], dscore[...]))
    dquery = jnp.concatenate(dqs, axis=0).T * HEAD_DIM**-0.5
    dquery = dquery * cos_ref[span - rows :, :] - swapped_halves(dquery) * sin_ref[span - rows :, :]
    dquery = dquery.astype(BF)
    dq_ref[...] = dquery
    dkeys = dk[...]
    dkeys = (dkeys * cos_ref[...] - swapped_halves(dkeys) * sin_ref[...]).astype(BF)
    dvalues = dv[...].astype(BF)
    dk_ref[...] = dkeys
    dv_ref[...] = dvalues
    core = core_ref[0]
    grads_ref[core] = dot(xt_ref[...], jnp.concatenate([dkeys, dvalues], axis=1)).astype(BF)
    grads_ref[1 - core, :, :LANES] = dot(xt_ref[:, span - rows :], dquery).astype(BF)
    grads_ref[1 - core, :, LANES:] = dot(ot_ref[...], dh_ref[...]).astype(BF)


def middle_kernel(
    o_ref, w_ref, small_ref, x_ref, pick_ref, put_ref,
    h_ref, scale_ref, a_ref, at_ref, out_ref, gate_ref, gain_ref,
    *, gain_lane,
):
    projected = jnp.concatenate([dot(o_ref[...], w_ref[part]) for part in range(2)], axis=1)
    hidden = x_ref[...].astype(F32) + projected
    h_ref[...] = hidden
    scale = lax.rsqrt(jnp.mean(hidden * hidden, axis=-1, keepdims=True) + EPSILON)
    scale_ref[...] = scale
    small = small_ref[...]
    gain = small.astype(F32).T[gain_lane : gain_lane + 1, :]
    gain_ref[...] = gain
    low = (hidden * scale * gain).astype(BF)
    a_ref[...] = low
    at_ref[...] = low.astype(F32).T.astype(BF)
    logits = dot(low, small)
    first, second = pick_ref[0], pick_ref[1]
    chosen_first = jnp.sum(logits * first, axis=-1, keepdims=True)
    chosen_second = jnp.sum(logits * second, axis=-1, keepdims=True)
    largest = jnp.maximum(chosen_first, chosen_second)
    chosen_first = jnp.exp(chosen_first - largest)
    chosen_second = jnp.exp(chosen_second - largest)
    total = chosen_first + chosen_second
    table = (chosen_first / total) * first + (chosen_second / total) * second
    gate_ref[...] = table
    high, rest = split_high_low(table)
    extra = (high.astype(F32) + pltpu.roll(rest.astype(F32), LANES // 2, 1)).astype(BF)
    put = put_ref[...]
    width = a_ref.shape[1]
    out_ref[:, :width] = dot(put, low).astype(BF)
    out_ref[:, width:] = dot(put, extra).astype(BF)


def gated_forward(x, w_gate, w_lift):
    gate, lift = dot(x, w_gate), dot(x, w_lift)
    sigmoid = 1.0 / (1.0 + jnp.exp(-gate))
    act = gate * sigmoid
    slope = sigmoid * (1.0 + gate * (1.0 - sigmoid))
    return (act * lift).astype(BF), act, lift * slope


def add_up(total_ref, value):
    @pl.when(pl.program_id(0) == 0)
    def _():
        total_ref[...] = value

    @pl.when(pl.program_id(0) != 0)
    def _():
        total_ref[...] += value


def flush(step, steps, copies):
    @pl.when(step >= 2)
    def _():
        for copy in copies(step % 2, step):
            copy.wait()


def send(step, steps, copies):
    for copy in copies(step % 2, step):
        copy.start()

    @pl.when(step == steps - 1)
    def _():
        for copy in copies((step + 1) % 2, step):
            copy.wait()
        for copy in copies(step % 2, step):
            copy.wait()


def shared_kernel(
    x_ref, dy_ref, w_ref, out_ref, pieces_ref, gin_sum, gdown_sum
):
    count, rows, model = x_ref.shape
    block, columns = model // w_ref.shape[0], model // TILE
    piece = (w_ref.shape[1] - 2 * block) // columns
    x, dy = x_ref[...].reshape(count * rows, model), dy_ref[...].reshape(count * rows, model)
    w_gate = w_ref[:, :block, :].reshape(model, TILE)
    w_lift = w_ref[:, block : 2 * block, :].reshape(model, TILE)
    w_down = jnp.concatenate(
        [
            w_ref[:, start : start + piece, :].reshape(-1, TILE)
            for start in range(2 * block, w_ref.shape[1], piece)
        ],
        axis=1,
    )
    hidden, act, slope = gated_forward(x, w_gate, w_lift)
    out_ref[:, :, :model] = dot(hidden, w_down).astype(BF).reshape(count, rows, model)
    dhidden = dot_nt(dy, w_down)
    dgate, dlift = (dhidden * slope).astype(BF), (dhidden * act).astype(BF)
    dx = dot_nt(dgate, w_gate) + dot_nt(dlift, w_lift)
    out_ref[:, :, model:] = dx.astype(BF).reshape(count, rows, model)
    add_up(gin_sum, dot_tn(x, jnp.concatenate([dgate, dlift], axis=1)))
    add_up(gdown_sum, dot_tn(hidden, dy))

    @pl.when(pl.program_id(0) == pl.num_programs(0) - 1)
    def _():
        for owner in range(pieces_ref.shape[0]):
            rows_in = pl.ds(owner * block, block)
            for part in range(2):
                pieces_ref[owner, part * block : (part + 1) * block, :] = gin_sum[
                    rows_in, part * TILE : (part + 1) * TILE
                ].astype(BF)
            rows_down = pl.ds(owner * piece, piece)
            for column in range(columns):
                start = 2 * block + column * piece
                pieces_ref[owner, start : start + piece, :] = gdown_sum[
                    rows_down, column * TILE : (column + 1) * TILE
                ].astype(BF)


def unpack_down(packed, model):
    return jnp.concatenate(
        [packed[start : start + TILE] for start in range(0, model, TILE)], axis=1
    )


def expert_kernel(
    in_ref, wg_ref, wl_ref, wd_ref, y_ref, hidden_ref, act_ref, slope_ref, y_sum
):
    model = y_ref.shape[1]
    w_gate = wg_ref[...].reshape(model, TILE)
    w_lift = wl_ref[...].reshape(model, TILE)
    hidden, act, slope = gated_forward(in_ref[:, :model], w_gate, w_lift)
    hidden_ref[...] = hidden
    act_ref[...] = act.astype(BF)
    slope_ref[...] = slope.astype(BF)
    add_up(y_sum, dot(hidden, unpack_down(wd_ref[0], model)))

    @pl.when(pl.program_id(0) == pl.num_programs(0) - 1)
    def _():
        y_ref[...] = y_sum[...].astype(BF)


def expert_back_kernel(
    in_ref, g_ref, own_ref, wg_ref, wl_ref, wd_ref, hidden_ref, act_ref, slope_ref,
    dx_ref, grads_ref,
    xt, dy, dx_sum, gin, gdown, sems,
):
    model = g_ref.shape[1]
    step, steps = pl.program_id(0), pl.num_programs(0)
    in_rows = gin.shape[3]

    def copies(slot, now):
        for part in range(2):
            first = pl.multiple_of((part * steps + now) * in_rows, in_rows)
            yield pltpu.make_async_copy(
                gin.at[slot, part], grads_ref.at[:, pl.ds(first, in_rows)], sems.at[slot, part]
            )
        yield pltpu.make_async_copy(
            gdown.at[slot], grads_ref.at[now, pl.ds(2 * steps * in_rows, model)], sems.at[slot, 2]
        )

    @pl.when(step == 0)
    def _():
        xt[...] = in_ref[:, :model].astype(F32).T.astype(BF)
        gate = jnp.sum(in_ref[:, model:].astype(F32) * own_ref[...], axis=-1, keepdims=True)
        dy[...] = (g_ref[...].astype(F32) * gate).astype(BF)

    flush(step, steps, copies)
    slot = step % 2
    w_gate = wg_ref[...].reshape(model, TILE)
    w_lift = wl_ref[...].reshape(model, TILE)
    w_down = unpack_down(wd_ref[0], model)
    dhidden = dot_nt(dy[...], w_down)
    dgate = (dhidden * slope_ref[...].astype(F32)).astype(BF)
    dlift = (dhidden * act_ref[...].astype(F32)).astype(BF)
    add_up(dx_sum, dot_nt(dgate, w_gate) + dot_nt(dlift, w_lift))
    shape = (gin.shape[2], in_rows, TILE)
    gin[slot, 0] = dot(xt[...], dgate).astype(BF).reshape(shape)
    gin[slot, 1] = dot(xt[...], dlift).astype(BF).reshape(shape)
    down = dot_tn(hidden_ref[...], dy[...]).astype(BF)
    for column in range(model // TILE):
        part = slice(column * TILE, (column + 1) * TILE)
        gdown[slot, part, :] = down[:, part]
    send(step, steps, copies)

    @pl.when(step == steps - 1)
    def _():
        dx_ref[...] = dx_sum[...].astype(BF)


def combine_kernel(
    y_ref, first_ref, second_ref, pick_ref, gate_ref, h_ref, shared_ref, g_ref, out_ref, dgate_ref
):
    table = gate_ref[...]
    y_first, y_second = dot(first_ref[...], y_ref[...]), dot(second_ref[...], y_ref[...])
    gate_first = jnp.sum(table * pick_ref[0], axis=-1, keepdims=True)
    gate_second = jnp.sum(table * pick_ref[1], axis=-1, keepdims=True)
    mixture = gate_first * y_first + gate_second * y_second
    out_ref[0] = (h_ref[...] + mixture + shared_ref[...].astype(F32)).astype(BF)
    g = g_ref[...].astype(F32)
    dgate_ref[...] = (
        jnp.sum(g * y_first, axis=-1, keepdims=True) * pick_ref[0]
        + jnp.sum(g * y_second, axis=-1, keepdims=True) * pick_ref[1]
    )


def middle_back_kernel(
    back_ref, dgate_ref, take_ref, gate_ref, small_ref, dshared_ref, g_ref, h_ref, scale_ref, gain_ref, w_ref,
    dh_ref, dhb_ref, do_ref, dlogits_ref, ggain_ref,
):
    take = take_ref[...]
    dgates = dgate_ref[...]
    table = gate_ref[...]
    gated = jnp.sum(table * dgates, axis=-1, keepdims=True)
    dlogits = (table * (dgates - gated)).astype(BF)
    dlogits_ref[...] = dlogits
    da = dshared_ref[...].astype(F32) + dot_nt(dlogits, small_ref[...]) + dot(take, back_ref[...])
    hidden, scale = h_ref[...], scale_ref[...]
    ggain_ref[...] = jnp.sum(da * hidden * scale, axis=0, keepdims=True)
    weighted = da * gain_ref[...]
    mean = jnp.mean(weighted * hidden, axis=-1, keepdims=True)
    dhidden = g_ref[...].astype(F32) + scale * weighted - hidden * (scale * scale * scale) * mean
    dh_ref[...] = dhidden
    low = dhidden.astype(BF)
    dhb_ref[...] = low
    width = w_ref.shape[2]
    do = dot_nt(low[:, :width], w_ref[0]) + dot_nt(low[:, width:], w_ref[1])
    do_ref[...] = do.astype(BF)


def project_back_kernel(dq_ref, dk_ref, dv_ref, w_ref, halo_ref, own_ref):
    width = w_ref.shape[2]
    parts = dk_ref.shape[1] // width

    def back(grads_ref, which):
        return sum(
            dot_nt(grads_ref[:, part * width : (part + 1) * width], w_ref[which * parts + part])
            for part in range(parts)
        )

    da = back(dk_ref, 1) + back(dv_ref, 2)
    halo_ref[...] = da.astype(BF)

    @pl.when(pl.program_id(0) == pl.num_programs(0) - 1)
    def _():
        own_ref[...] = da + back(dq_ref, 0)


def per_device(
    tokens,
    segments,
    routes,
    w_qkv,
    w_out,
    w_router,
    shared_in,
    shared_down,
    attn_gain,
    ffn_gain,
    expert_in,
    expert_down,
    cotangent,
):
    ctx, fsdp = lax.axis_size("ctx"), lax.axis_size("fsdp")
    ctx_index, core = lax.axis_index("ctx"), lax.axis_index("fsdp") % 2
    rows, model = tokens.shape[1], tokens.shape[2]
    reach = max(1, WIN // rows)
    span = (reach + 1) * rows
    capacity = max(2, 3 * rows * TOPK // (2 * ctx))
    slots = ctx * capacity
    own = w_qkv.shape[0]
    owned_down = shared_down.shape[0]
    experts = w_router.shape[1]
    ff = shared_in.shape[1] // 2
    tiles = ff // TILE

    x, g = tokens[0], cotangent[0]
    segment_row = jnp.zeros((16, model), BF).at[0, :rows].set(segments[0].astype(BF))
    carried = jnp.concatenate([x, segment_row], axis=0)
    place_z = ctx_index % ROW
    lines = range(0, ctx, ROW)
    previous = shifted(carried, "ctx", ROW)
    arrived = [previous]
    for distance in range(reach - 1, 0, -1):
        arrived.append(
            lax.ppermute(
                jnp.where(place_z + distance < ROW, carried, previous),
                "ctx",
                [(line + z, line + (z + distance) % ROW) for line in lines for z in range(ROW)],
            )
        )

    small = jnp.concatenate(
        [w_router, attn_gain[:, None], ffn_gain[:, None], jnp.zeros((own, LANES - experts - 2), BF)],
        axis=1,
    )
    projections = jnp.concatenate([w_qkv, w_out], axis=1)
    width = projections.shape[1] // fsdp
    cosine, sine = rotary_tables(span, (ctx_index - reach) * rows)
    near = lax.all_to_all(
        jnp.concatenate(
            [
                projections.reshape(own, fsdp, width).transpose(1, 0, 2),
                jnp.broadcast_to(small, (fsdp, own, LANES)),
                shared_in.reshape(own, 2, ctx, fsdp, owned_down)
                .transpose(3, 0, 1, 2, 4)
                .reshape(fsdp, own, 2 * TILE),
            ],
            axis=2,
        ),
        "fsdp",
        split_axis=0,
        concat_axis=0,
        tiled=True,
    ).reshape(fsdp * own, -1)

    def to_ctx(values):
        return lax.all_to_all(
            jnp.broadcast_to(values, (ctx, *values.shape)), "ctx", split_axis=0, concat_axis=0, tiled=True
        )

    g_all = lax.all_gather(g, "fsdp", axis=0)
    columns = model // TILE
    dense = to_ctx(after(near[:, : width + LANES], previous)).reshape(model, width + LANES)
    w_full = lax.all_gather(after(dense[:, :width], g_all, *arrived), "fsdp", axis=0)
    down_own = shared_down.reshape(owned_down, columns, TILE).transpose(1, 0, 2).reshape(-1, TILE)
    shared_own_w = jnp.concatenate(
        [near[:, width + LANES : -TILE], near[:, -TILE:], down_own], axis=0
    )
    shared_full = to_ctx(after(shared_own_w, dense, cosine, sine, *arrived))
    place = ctx_index.astype(jnp.int32).reshape(1)
    place_spec = pl.BlockSpec(memory_space=pltpu.SMEM)
    in_rows, down_rows = expert_in.shape[1], expert_down.shape[1]
    expert_packed = jnp.concatenate(
        [
            expert_in[0].reshape(in_rows, 2 * tiles, TILE).transpose(1, 0, 2).reshape(-1, TILE),
            expert_down[0].reshape(down_rows, model // TILE, TILE).transpose(1, 0, 2).reshape(-1, TILE),
        ],
        axis=0,
    )
    expert_full = lax.all_gather(after(expert_packed, w_full, shared_full), "fsdp", axis=0)


    route_own = routes[0]
    expert_ids = jnp.arange(experts, dtype=jnp.int32)
    hits = route_own[:, :, None] == expert_ids[None, None, :]
    member = jnp.sum(hits.astype(jnp.int32), axis=1)
    ranking = jnp.cumsum(member, axis=0, dtype=jnp.int32) - 1
    slot_ids = jnp.arange(capacity, dtype=jnp.int32)
    placed = (member[:, :, None] > 0) & (ranking[:, :, None] == slot_ids[None, None, :])
    take = placed.astype(BF).reshape(rows, slots)
    put = take.T
    selector = (
        (hits[:, :, :, None] & placed[:, None, :, :]).astype(BF).reshape(rows, TOPK * slots)
    )
    picked = jnp.pad(
        hits.astype(F32).transpose(1, 0, 2), ((0, 0), (0, 0), (0, LANES - experts))
    )
    lane = jnp.arange(LANES, dtype=jnp.int32)[None, :]
    own_lanes = ((lane == ctx_index) | (lane == ctx_index + LANES // 2)).astype(F32)

    def exchange(values):
        return lax.all_to_all(
            values.reshape(ctx, values.shape[0] // ctx, values.shape[1]),
            "ctx",
            split_axis=0,
            concat_axis=0,
            tiled=True,
        ).reshape(values.shape)

    g_to_slots = dot(put, g).astype(BF)

    pairs = model // LANES
    small_spec = pl.BlockSpec((model, LANES), lambda *_: (0, width // LANES))
    per, parts = width // LANES, model // width

    def columns_of(which):
        return pl.BlockSpec((1, model, LANES), lambda j: (which * parts + j // per, 0, j % per))

    blocks = [*arrived, carried]
    pair_spec = lambda height: pl.BlockSpec((height, LANES), lambda j: (0, j))
    q, k, kt, v, e, rl, rlb, attended, span_scale = pl.pallas_call(
        functools.partial(attend_kernel, gain_lane=experts, parts=reach + 1),
        grid=(pairs,),
        in_specs=[
            place_spec,
            *[whole(block) for block in blocks],
            small_spec,
            columns_of(0),
            columns_of(1),
            columns_of(2),
            whole(cosine),
            whole(sine),
        ],
        out_specs=[
            pair_spec(rows),
            pair_spec(span),
            pl.BlockSpec((LANES, span), lambda j: (j, 0)),
            pair_spec(span),
            pl.BlockSpec((2, span, rows), lambda j: (j, 0, 0)),
            pl.BlockSpec((1, 8, rows), lambda j: (j, 0, 0)),
            pair_spec(rows),
            pair_spec(rows),
            pl.BlockSpec((span, 1), lambda j: (0, 0)),
        ],
        out_shape=[
            jax.ShapeDtypeStruct((rows, model), BF),
            jax.ShapeDtypeStruct((span, model), BF),
            jax.ShapeDtypeStruct((model, span), BF),
            jax.ShapeDtypeStruct((span, model), BF),
            jax.ShapeDtypeStruct((HEADS, span, rows), BF),
            jax.ShapeDtypeStruct((pairs, 8, rows), F32),
            jax.ShapeDtypeStruct((rows, model), F32),
            jax.ShapeDtypeStruct((rows, model), BF),
            jax.ShapeDtypeStruct((span, 1), F32),
        ],
        scratch_shapes=[
            pltpu.VMEM((span, model), BF),
            pltpu.VMEM((span, rows), F32),
            pltpu.VMEM((LANES, span), BF),
            pltpu.VMEM((span, rows), F32),
        ],
        compiler_params=params(VMEM_MB),
        cost_estimate=cost(20),
        name="attend",
    )(place, *blocks, dense, w_full, w_full, w_full, cosine, sine)

    out_spec = pl.BlockSpec((parts, model, width), lambda *_: (3, 0, 0))
    hidden, scale_two, normed, normed_t, outgoing, gates, gain_two = pl.pallas_call(
        functools.partial(middle_kernel, gain_lane=experts + 1),
        grid=(1,),
        in_specs=[
            whole(attended),
            out_spec,
            small_spec,
            whole(x),
            whole(picked),
            whole(put),
        ],
        out_specs=[
            pl.BlockSpec((rows, model), lambda *_: (0, 0)),
            pl.BlockSpec((rows, 1), lambda *_: (0, 0)),
            pl.BlockSpec((rows, model), lambda *_: (0, 0)),
            pl.BlockSpec((model, rows), lambda *_: (0, 0)),
            pl.BlockSpec((slots, model + LANES), lambda *_: (0, 0)),
            pl.BlockSpec((rows, LANES), lambda *_: (0, 0)),
            pl.BlockSpec((1, model), lambda *_: (0, 0)),
        ],
        out_shape=[
            jax.ShapeDtypeStruct((rows, model), F32),
            jax.ShapeDtypeStruct((rows, 1), F32),
            jax.ShapeDtypeStruct((rows, model), BF),
            jax.ShapeDtypeStruct((model, rows), BF),
            jax.ShapeDtypeStruct((slots, model + LANES), BF),
            jax.ShapeDtypeStruct((rows, LANES), F32),
            jax.ShapeDtypeStruct((1, model), F32),
        ],
        compiler_params=params(VMEM_MB),
        cost_estimate=cost(5),
        name="middle",
    )(attended, w_full, dense, x, picked, put)
    normed_all = lax.all_gather(normed, "fsdp", axis=0)
    incoming = exchange(outgoing)
    gain_one = dense[:, width + experts : width + experts + 1].astype(F32)
    span_x = jnp.concatenate([block[:rows] for block in blocks], axis=0)
    first_t = (span_x.T.astype(F32) * span_scale.reshape(1, span) * gain_one).astype(BF)
    incoming = after(incoming, first_t)

    packed_rows = 3 * model

    expert_specs = [
        pl.BlockSpec((fsdp, in_rows, TILE), lambda t: (0, t, 0)),
        pl.BlockSpec((fsdp, in_rows, TILE), lambda t: (0, tiles + t, 0)),
        pl.BlockSpec((1, model, TILE), lambda t: (t, 2 * in_rows * tiles // model, 0)),
    ]
    unit_spec = pl.BlockSpec((slots, TILE), lambda t: (0, t))
    expert_y, *units = pl.pallas_call(
        expert_kernel,
        grid=(tiles,),
        in_specs=[whole(incoming), *expert_specs],
        out_specs=[
            pl.BlockSpec((slots, model), lambda t: (0, 0)),
            unit_spec,
            unit_spec,
            unit_spec,
        ],
        out_shape=[jax.ShapeDtypeStruct((slots, model), BF)]
        + [jax.ShapeDtypeStruct((slots, ff), BF)] * 3,
        scratch_shapes=[pltpu.VMEM((slots, model), F32)],
        compiler_params=params(VMEM_MB),
        cost_estimate=cost(14),
        name="expert",
    )(incoming, expert_full, expert_full, expert_full)
    slot_g = exchange(after(g_to_slots, incoming))
    returned_y = exchange(after(expert_y, slot_g))

    at_once = 2
    block = model // ctx
    shared_part, shared_pieces = pl.pallas_call(
        shared_kernel,
        grid=(fsdp // at_once,),
        in_specs=[
            pl.BlockSpec((at_once, rows, model), lambda t: (t, 0, 0)),
            pl.BlockSpec((at_once, rows, model), lambda t: (t, 0, 0)),
            whole(shared_full),
        ],
        out_specs=[
            pl.BlockSpec((at_once, rows, 2 * model), lambda t: (t, 0, 0)),
            whole(shared_full),
        ],
        out_shape=[
            jax.ShapeDtypeStruct((fsdp, rows, 2 * model), BF),
            jax.ShapeDtypeStruct(shared_full.shape, BF),
        ],
        scratch_shapes=[pltpu.VMEM((model, 2 * TILE), F32), pltpu.VMEM((TILE, model), F32)],
        compiler_params=params(VMEM_MB),
        cost_estimate=cost(18),
        name="shared",
    )(after(normed_all, expert_y), g_all, shared_full)
    shared_both = lax.psum_scatter(after(shared_part, returned_y), "fsdp", scatter_dimension=0)
    shared_own = jnp.sum(
        lax.all_to_all(
            after(shared_pieces, returned_y), "ctx", split_axis=0, concat_axis=0, tiled=True
        ).astype(F32),
        axis=0,
    )
    back, gexpert = pl.pallas_call(
        expert_back_kernel,
        grid=(tiles,),
        in_specs=[
            whole(incoming),
            whole(slot_g),
            whole(own_lanes),
            *expert_specs,
            unit_spec,
            unit_spec,
            unit_spec,
        ],
        out_specs=[
            pl.BlockSpec((slots, model), lambda t: (0, 0)),
            pl.BlockSpec(memory_space=pl.ANY),
        ],
        out_shape=[
            jax.ShapeDtypeStruct((slots, model), BF),
            jax.ShapeDtypeStruct((fsdp, packed_rows, TILE), BF),
        ],
        scratch_shapes=[
            pltpu.VMEM((model, slots), BF),
            pltpu.VMEM((slots, model), BF),
            pltpu.VMEM((slots, model), F32),
            pltpu.VMEM((2, 2, fsdp, in_rows, TILE), BF),
            pltpu.VMEM((2, model, TILE), BF),
            pltpu.SemaphoreType.DMA((2, 3)),
        ],
        compiler_params=params(VMEM_MB),
        cost_estimate=cost(24),
        name="expert_back",
    )(after(incoming, shared_part, returned_y), slot_g, own_lanes, expert_full, expert_full, expert_full, *units)
    returned = exchange(after(back, shared_own))
    expert_sum = lax.psum_scatter(after(gexpert, shared_own), "fsdp", scatter_dimension=0)

    mixed, dgates = pl.pallas_call(
        combine_kernel,
        grid=(1,),
        in_specs=[
            pl.BlockSpec((slots, model), lambda *_: (0, 0)),
            pl.BlockSpec((rows, slots), lambda *_: (0, 0)),
            pl.BlockSpec((rows, slots), lambda *_: (0, 1)),
            whole(picked),
            whole(gates),
            whole(hidden),
            pl.BlockSpec((rows, model), lambda *_: (0, 0)),
            whole(g),
        ],
        out_specs=[
            pl.BlockSpec((1, rows, model), lambda *_: (0, 0, 0)),
            pl.BlockSpec((rows, LANES), lambda *_: (0, 0)),
        ],
        out_shape=[
            jax.ShapeDtypeStruct((1, rows, model), BF),
            jax.ShapeDtypeStruct((rows, LANES), F32),
        ],
        compiler_params=params(VMEM_MB),
        cost_estimate=cost(3),
        name="combine",
    )(returned_y, selector, selector, picked, gates, hidden, shared_both, g)

    returned = after(returned, dgates)

    dhidden, dhidden_low, dattended, dlogits, ggain_two = pl.pallas_call(
        middle_back_kernel,
        grid=(1,),
        in_specs=[
            whole(returned),
            whole(dgates),
            whole(take),
            whole(gates),
            small_spec,
            pl.BlockSpec((rows, model), lambda *_: (0, 1)),
            whole(g),
            whole(hidden),
            whole(scale_two),
            whole(gain_two),
            out_spec,
        ],
        out_specs=[
            pl.BlockSpec((rows, model), lambda *_: (0, 0)),
            pl.BlockSpec((rows, model), lambda *_: (0, 0)),
            pl.BlockSpec((rows, model), lambda *_: (0, 0)),
            pl.BlockSpec((rows, LANES), lambda *_: (0, 0)),
            pl.BlockSpec((1, model), lambda *_: (0, 0)),
        ],
        out_shape=[
            jax.ShapeDtypeStruct((rows, model), F32),
            jax.ShapeDtypeStruct((rows, model), BF),
            jax.ShapeDtypeStruct((rows, model), BF),
            jax.ShapeDtypeStruct((rows, LANES), BF),
            jax.ShapeDtypeStruct((1, model), F32),
        ],
        compiler_params=params(VMEM_MB),
        cost_estimate=cost(6),
        name="middle_back",
    )(
        returned, dgates, take, gates, dense, shared_both, g, hidden, scale_two, gain_two, w_full
    )

    grouter = dot(normed_t, dlogits)
    small_grads = jnp.concatenate(
        [grouter[:, :experts], ggain_two.T, jnp.zeros((model, LANES - experts - 1), F32)], axis=1
    ).astype(BF)
    attended_t = attended.T
    core_scalar = core.astype(jnp.int32).reshape(1)

    def attend_back(first, count, down, *filled):
        pair_from = lambda height: pl.BlockSpec((height, LANES), lambda j: (0, first + j))
        operands = (
            core_scalar, q, k, kt, v, e, rl, rlb, down, cosine, sine, first_t, attended_t, dhidden_low, *filled,
        )
        return pl.pallas_call(
            attend_back_kernel,
            grid=(count,),
            in_specs=[
                place_spec,
                pair_from(rows),
                pair_from(span),
                pl.BlockSpec((LANES, span), lambda j: (first + j, 0)),
                pair_from(span),
                pl.BlockSpec((2, span, rows), lambda j: (first + j, 0, 0)),
                pl.BlockSpec((1, 8, rows), lambda j: (first + j, 0, 0)),
                pair_from(rows),
                pair_from(rows),
                whole(cosine),
                whole(sine),
                whole(first_t),
                whole(attended_t),
                pair_from(rows),
            ]
            + [pl.BlockSpec(memory_space=pl.ANY)] * len(filled),
            out_specs=[
                pair_from(rows),
                pair_from(span),
                pair_from(span),
                pl.BlockSpec((2, model, 2 * LANES), lambda j: (0, 0, j)),
            ],
            out_shape=[
                jax.ShapeDtypeStruct((rows, model), BF),
                jax.ShapeDtypeStruct((span, model), BF),
                jax.ShapeDtypeStruct((span, model), BF),
                jax.ShapeDtypeStruct((2, model, count * 2 * LANES), BF),
            ],
            input_output_aliases={
                len(operands) - len(filled) + index: index for index in range(len(filled))
            },
            scratch_shapes=[
                pltpu.VMEM((span, rows), F32),
                pltpu.VMEM((span, rows), BF),
                pltpu.VMEM((span, LANES), F32),
                pltpu.VMEM((span, LANES), F32),
            ],
            compiler_params=params(VMEM_MB),
            cost_estimate=cost(4 * count),
            name=f"attend_back_{first}",
        )(*operands)

    def rows_to_owners(values):
        return lax.all_to_all(
            values.reshape(fsdp, own, -1), "fsdp", split_axis=0, concat_axis=0, tiled=True
        )


    chips = fsdp // 2

    def paired_columns(grads, *others):
        kept, sent = grads[0], grads[1]
        if others:
            sent = after(sent, *others)
        partner = lax.ppermute(sent, "fsdp", [(i, i ^ 1) for i in range(fsdp)])
        paired = (kept.astype(F32) + partner.astype(F32)).astype(BF)
        return paired.reshape(model, chips, -1).transpose(1, 0, 2)

    def along_y(paired):
        pieces = lax.all_to_all(
            paired,
            "fsdp",
            split_axis=0,
            concat_axis=0,
            axis_index_groups=[list(range(start, fsdp, 2)) for start in range(2)],
            tiled=True,
        )
        return jnp.sum(pieces.astype(F32), axis=0).astype(BF)

    early_pairs = pairs // 3
    *grads_a, group_a = attend_back(0, early_pairs, dattended)
    paired_a = paired_columns(group_a)
    late_a = along_y(paired_a)
    dq, dk, dv, group_b = attend_back(
        early_pairs, pairs - early_pairs, after(dattended, paired_a), *grads_a
    )
    paired_b = paired_columns(group_b, late_a)
    late_b = along_y(paired_b)

    dspan, down = pl.pallas_call(
        project_back_kernel,
        grid=(reach + 1,),
        in_specs=[
            whole(dq),
            pl.BlockSpec((rows, model), lambda b: (b, 0)),
            pl.BlockSpec((rows, model), lambda b: (b, 0)),
            pl.BlockSpec((3 * parts, model, width), lambda b: (0, 0, 0)),
        ],
        out_specs=[
            pl.BlockSpec((rows, model), lambda b: (b, 0)),
            pl.BlockSpec((rows, model), lambda b: (0, 0)),
        ],
        out_shape=[
            jax.ShapeDtypeStruct((span, model), BF),
            jax.ShapeDtypeStruct((rows, model), F32),
        ],
        compiler_params=params(VMEM_MB),
        cost_estimate=cost(8),
        name="project_back",
    )(dq, dk, dv, w_full)
    late = jnp.concatenate([late_a, late_b, small_grads], axis=1).reshape(ctx, block, -1)
    late_own = jnp.sum(
        lax.all_to_all(late, "ctx", split_axis=0, concat_axis=0, tiled=True).astype(F32), axis=0
    )

    grad_shared_down = (
        shared_own[2 * block :]
        .reshape(columns, owned_down, TILE)
        .transpose(1, 0, 2)
        .reshape(owned_down, model)
    )
    expert_rows = 2 * tiles * in_rows
    grad_expert_in = (
        expert_sum[:expert_rows]
        .astype(F32)
        .reshape(2 * tiles, in_rows, TILE)
        .transpose(1, 0, 2)
        .reshape(1, in_rows, 2 * ff)
    )
    grad_expert_down = (
        expert_sum[expert_rows:]
        .astype(F32)
        .reshape(columns, down_rows, TILE)
        .transpose(1, 0, 2)
        .reshape(1, down_rows, model)
    )
    wide_a, wide = late_a.shape[1], late_a.shape[1] + late_b.shape[1]
    last = rows_to_owners(
        after(
            jnp.concatenate([late_own, shared_own[:block], shared_own[block : 2 * block]], axis=1),
            grad_expert_in,
            grad_expert_down,
        )
    )
    small_total = jnp.sum(last[:, :, wide : wide + LANES], axis=0)
    shared_last = last[:, :, wide + LANES :]

    def by_core(values):
        values = values.reshape(chips, 2, own, -1).transpose(1, 2, 0, 3).reshape(2, own, -1, 2, LANES)
        return values.transpose(0, 3, 1, 2, 4).reshape(2, 2, own, -1)

    late_total = jnp.concatenate([by_core(last[:, :, :wide_a]), by_core(last[:, :, wide_a:wide])], axis=3)
    grad_qkv = jnp.concatenate([late_total[1, 0], late_total[0, 0], late_total[0, 1]], axis=1)
    grad_out = late_total[1, 1]
    grad_gain_one = jnp.sum(grad_qkv * w_qkv.astype(F32), axis=1) / attn_gain.astype(F32)
    grad_shared_in = (
        shared_last.reshape(fsdp, own, 2, ctx, owned_down)
        .transpose(1, 2, 3, 0, 4)
        .reshape(own, 2 * ff)
    )

    total, passed = down, dspan[:rows].astype(F32)
    for distance in range(1, reach):
        lower = (reach - distance) * rows
        moved = lax.ppermute(
            dspan[lower : lower + rows],
            "ctx",
            [(line + z, line + (z - distance) % ROW) for line in lines for z in range(ROW)],
        ).astype(F32)
        here = place_z + distance < ROW
        total = total + jnp.where(here, moved, 0.0)
        passed = passed + jnp.where(here, 0.0, moved)
    total = total + shifted(passed.astype(BF), "ctx", -ROW).astype(F32)
    input_rows = x.astype(F32)
    scale_one = span_scale[reach * rows :]
    weighted = total * gain_one.reshape(1, model)
    input_grad = (
        dhidden
        + scale_one * weighted
        - input_rows
        * scale_one**3
        * jnp.mean(weighted * input_rows, axis=-1, keepdims=True)
    )[None]

    return (
        mixed,
        input_grad,
        grad_qkv,
        grad_out,
        small_total[:, :experts],
        grad_shared_in,
        grad_shared_down,
        grad_gain_one,
        small_total[:, experts],
        grad_expert_in,
        grad_expert_down,
    )


def solution(mesh):
    placed = (
        P("fsdp", "ctx", None),
        P("fsdp", "ctx"),
        P("fsdp", "ctx", None),
        P(("ctx", "fsdp"), None),
        P(("ctx", "fsdp"), None),
        P(("ctx", "fsdp"), None),
        P(("ctx", "fsdp"), None),
        P(("ctx", "fsdp"), None),
        P(("ctx", "fsdp")),
        P(("ctx", "fsdp")),
        P("ctx", "fsdp", None),
        P("ctx", "fsdp", None),
        P("fsdp", "ctx", None),
    )
    return jax.shard_map(
        per_device,
        mesh=mesh,
        in_specs=placed,
        out_specs=(
            P("fsdp", "ctx", None),
            P("fsdp", "ctx", None),
            P(("ctx", "fsdp"), None),
            P(("ctx", "fsdp"), None),
            P(("ctx", "fsdp"), None),
            P(("ctx", "fsdp"), None),
            P(("ctx", "fsdp"), None),
            P(("ctx", "fsdp")),
            P(("ctx", "fsdp")),
            P("ctx", "fsdp", None),
            P("ctx", "fsdp", None),
        ),
        check_vma=False,
    )
```

```python
import functools

import jax
import jax.numpy as jnp
from jax import lax
from jax.experimental import pallas as pl
from jax.experimental.pallas import tpu as pltpu
from jax.sharding import PartitionSpec as P

HEADS = 12
HEAD_DIM = 64
TOPK = 2
WIN = 1024
EPSILON = 1e-06

BF = jnp.bfloat16
F32 = jnp.float32
TILE = 256
LANES = 128
IN_ROWS = 96
AT_ONCE = 2
KEY_BLOCK = 128
ROW = 4
VMEM_MB = 60


def dot(a, b):
    return jnp.dot(a, b, preferred_element_type=F32)


def dot_nt(a, b):
    return lax.dot_general(a, b, (((1,), (1,)), ((), ())), preferred_element_type=F32)


def dot_tn(a, b):
    return lax.dot_general(a, b, (((0,), (0,)), ((), ())), preferred_element_type=F32)


def params(megabytes):
    return pltpu.CompilerParams(vmem_limit_bytes=megabytes * 1024 * 1024)


def cost(microseconds):
    return pl.CostEstimate(
        flops=int(microseconds * 1.0e9), bytes_accessed=int(microseconds * 1.0e6), transcendentals=0
    )


def after(value, *others):
    return lax.optimization_barrier((value, *others))[0]


def whole(array):
    return pl.BlockSpec(array.shape, lambda *_: (0,) * array.ndim)


def shifted(value, axis, steps):
    count = lax.axis_size(axis)
    leading, last = (max(0, -steps), min(count, count - steps))
    return lax.ppermute(value, axis, [(source, source + steps) for source in range(leading, last)])


def split_high_low(values):
    high = values.astype(BF)
    return high, (values - high.astype(F32)).astype(BF)


def rotary_tables(rows, offset):
    half = HEAD_DIM // 2
    frequency = jnp.exp(-jnp.log(10000.0) * (2.0 * jnp.arange(half, dtype=F32) / HEAD_DIM))
    places = (offset + jnp.arange(rows, dtype=jnp.int32)).astype(F32)
    angles = places[:, None] * frequency[None, :]
    cosine, sine = jnp.cos(angles), jnp.sin(angles)
    return (
        jnp.concatenate([cosine] * 4, axis=1),
        jnp.concatenate([-sine, sine, -sine, sine], axis=1),
    )


def swapped_halves(values):
    lane = lax.broadcasted_iota(jnp.int32, (1, LANES), 1)
    half = HEAD_DIM // 2
    return jnp.where(
        lane % HEAD_DIM < half,
        pltpu.roll(values, LANES - half, 1),
        pltpu.roll(values, half, 1),
    )


def head_lanes(values, head):
    lane = lax.broadcasted_iota(jnp.int32, (1, LANES), 1)
    return jnp.where(lane // HEAD_DIM == head, values, jnp.zeros_like(values))


def fold_rows(values, op):
    return op(values.reshape(values.shape[0] // 8, 8, values.shape[1]), axis=0)


def attend_kernel(
    place_ref, *refs, gain_lane, parts
):
    blocks, refs = refs[:parts], refs[parts:]
    (
        small_ref, wq_ref, wk_ref, wv_ref, cos_ref, sin_ref,
        q_ref, k_ref, kt_ref, v_ref, e_ref, rl_ref, rlb_ref, o_ref, scale_ref,
        normed, score, vt, bias_ref,
    ) = refs
    rows, model = q_ref.shape[0], normed.shape[1]
    span = parts * rows

    @pl.when(pl.program_id(0) == 0)
    def _():
        gain = small_ref[...].astype(F32).T[gain_lane : gain_lane + 1, :]
        query_segment = blocks[-1][rows : rows + 1, :rows].astype(F32)
        query_place = lax.broadcasted_iota(jnp.int32, (rows, rows), 1)
        key_place = lax.broadcasted_iota(jnp.int32, (rows, rows), 0)
        for index, block in enumerate(blocks):
            part = pl.ds(index * rows, rows)
            values = block[:rows, :].astype(F32)
            scale = lax.rsqrt(jnp.mean(values * values, axis=-1, keepdims=True) + EPSILON)
            scale_ref[part, :] = scale
            normed[part, :] = (values * scale * gain).astype(BF)
            key_segment = block[rows : rows + 16, :rows].astype(F32).T[:, :1]
            distance = query_place - key_place + (parts - 1 - index) * rows
            allowed = (distance >= 0) & (distance < WIN) & (key_segment == query_segment)
            allowed = allowed & (place_ref[0] >= parts - 1 - index)
            bias_ref[part, :] = jnp.where(allowed, 0.0, -1e30)

    pair = dot(normed[...], jnp.concatenate([wk_ref[0], wv_ref[0]], axis=1))
    keys = pair[:, :LANES]
    keys = keys * cos_ref[...] + swapped_halves(keys) * sin_ref[...]
    k_ref[...] = keys.astype(BF)
    kt_ref[...] = keys.T.astype(BF)
    values = pair[:, LANES:]
    v_ref[...] = values.astype(BF)
    vt[...] = values.T.astype(BF)
    queries = dot(normed[span - rows :, :], wq_ref[0])
    queries = queries * cos_ref[span - rows :, :] + swapped_halves(queries) * sin_ref[span - rows :, :]
    queries = (queries.astype(BF).astype(F32) * HEAD_DIM**-0.5).astype(BF)
    q_ref[...] = queries

    heads = range(2)
    own = [head_lanes(queries, head) for head in heads]
    largest = [jnp.full((8, rows), -3e38, F32) for _ in heads]
    for start in range(0, span, KEY_BLOCK):
        part = pl.ds(start, KEY_BLOCK)
        for head in heads:
            block = dot_nt(k_ref[part, :], own[head]) + bias_ref[part, :]
            score[head, part, :] = block
            largest[head] = jnp.maximum(largest[head], fold_rows(block, jnp.max))
    largest = [jnp.max(value, axis=0, keepdims=True) for value in largest]
    total = [jnp.zeros((8, rows), F32) for _ in heads]
    for start in range(0, span, KEY_BLOCK):
        part = pl.ds(start, KEY_BLOCK)
        for head in heads:
            block = jnp.exp(score[head, part, :] - largest[head])
            total[head] = total[head] + fold_rows(block, jnp.sum)
            e_ref[head, part, :] = block.astype(BF)
    outs, sums = [], []
    for head in heads:
        inverse = 1.0 / jnp.sum(total[head], axis=0, keepdims=True)
        rl_ref[0, head : head + 1, :] = inverse
        outs.append(dot(vt[head * HEAD_DIM : (head + 1) * HEAD_DIM, :], e_ref[head]) * inverse)
        sums.append(jnp.broadcast_to(inverse, (HEAD_DIM, rows)))
    o_ref[...] = jnp.concatenate(outs, axis=0).T.astype(BF)
    rlb_ref[...] = jnp.concatenate(sums, axis=0).T


def attend_back_kernel(
    core_ref, q_ref, k_ref, kt_ref, v_ref, e_ref, rl_ref, rlb_ref, do_ref, cos_ref, sin_ref, xt_ref, ot_ref, dh_ref,
    *refs,
):
    dq_ref, dk_ref, dv_ref, grads_ref, dprob, dscore, dk, dv = refs[-8:]
    span, rows = k_ref.shape[0], q_ref.shape[0]
    scaled = do_ref[...].astype(F32) * rlb_ref[...]
    heads = range(2)
    down = [head_lanes(scaled, head).astype(BF) for head in heads]
    own = [head_lanes(q_ref[...], head) for head in heads]
    own_both, down_both = jnp.concatenate(own, axis=0), jnp.concatenate(down, axis=0)
    inner = [jnp.zeros((8, rows), F32) for _ in heads]
    for start in range(0, span, KEY_BLOCK):
        part = pl.ds(start, KEY_BLOCK)
        for head in heads:
            block = dot_nt(v_ref[part, :], down[head])
            dprob[head, part, :] = block
            inner[head] = inner[head] + fold_rows(block * e_ref[head, part, :].astype(F32), jnp.sum)
    inner = [
        jnp.sum(inner[head], axis=0, keepdims=True) * rl_ref[0, head : head + 1, :]
        for head in heads
    ]
    for start in range(0, span, KEY_BLOCK):
        part = pl.ds(start, KEY_BLOCK)
        for head in heads:
            weight = e_ref[head, part, :]
            block = (weight.astype(F32) * (dprob[head, part, :] - inner[head])).astype(BF)
            dscore[head, part, :] = block
        dk[part, :] = dot(
            jnp.concatenate([dscore[head, part, :] for head in heads], axis=1), own_both
        )
        dv[part, :] = dot(
            jnp.concatenate([e_ref[head, part, :] for head in heads], axis=1), down_both
        )
    dqs = [
        dot(kt_ref[head * HEAD_DIM : (head + 1) * HEAD_DIM, :], dscore[head]) for head in heads
    ]
    dquery = jnp.concatenate(dqs, axis=0).T * HEAD_DIM**-0.5
    dquery = dquery * cos_ref[span - rows :, :] - swapped_halves(dquery) * sin_ref[span - rows :, :]
    dquery = dquery.astype(BF)
    dq_ref[...] = dquery
    dkeys = dk[...]
    dkeys = (dkeys * cos_ref[...] - swapped_halves(dkeys) * sin_ref[...]).astype(BF)
    dvalues = dv[...].astype(BF)
    dk_ref[...] = dkeys
    dv_ref[...] = dvalues
    core = core_ref[0]
    grads_ref[core] = dot(xt_ref[...], jnp.concatenate([dkeys, dvalues], axis=1)).astype(BF)
    grads_ref[1 - core, :, :LANES] = dot(xt_ref[:, span - rows :], dquery).astype(BF)
    grads_ref[1 - core, :, LANES:] = dot(ot_ref[...], dh_ref[...]).astype(BF)


def middle_kernel(
    o_ref, w_ref, small_ref, x_ref, pick_ref, put_ref,
    h_ref, scale_ref, a_ref, at_ref, out_ref, gate_ref, gain_ref,
    *, gain_lane,
):
    projected = jnp.concatenate([dot(o_ref[...], w_ref[part]) for part in range(2)], axis=1)
    hidden = x_ref[...].astype(F32) + projected
    h_ref[...] = hidden
    scale = lax.rsqrt(jnp.mean(hidden * hidden, axis=-1, keepdims=True) + EPSILON)
    scale_ref[...] = scale
    small = small_ref[...]
    gain = small.astype(F32).T[gain_lane : gain_lane + 1, :]
    gain_ref[...] = gain
    low = (hidden * scale * gain).astype(BF)
    a_ref[...] = low
    at_ref[...] = low.astype(F32).T.astype(BF)
    logits = dot(low, small)
    first, second = pick_ref[0], pick_ref[1]
    chosen_first = jnp.sum(logits * first, axis=-1, keepdims=True)
    chosen_second = jnp.sum(logits * second, axis=-1, keepdims=True)
    largest = jnp.maximum(chosen_first, chosen_second)
    chosen_first = jnp.exp(chosen_first - largest)
    chosen_second = jnp.exp(chosen_second - largest)
    total = chosen_first + chosen_second
    table = (chosen_first / total) * first + (chosen_second / total) * second
    gate_ref[...] = table
    high, rest = split_high_low(table)
    extra = (high.astype(F32) + pltpu.roll(rest.astype(F32), LANES // 2, 1)).astype(BF)
    put = put_ref[...]
    width = a_ref.shape[1]
    out_ref[:, :width] = dot(put, low).astype(BF)
    out_ref[:, width:] = dot(put, extra).astype(BF)


def gated_forward(x, w_gate, w_lift):
    gate, lift = dot(x, w_gate), dot(x, w_lift)
    sigmoid = 0.5 * jnp.tanh(0.5 * gate) + 0.5
    act = gate * sigmoid
    slope = sigmoid + (act - act * sigmoid)
    return (act * lift).astype(BF), act, lift * slope


def add_up(total_ref, value):
    first = pl.program_id(0) == 0
    total_ref[...] = value + jnp.where(first, 0.0, total_ref[...])


def flush(step, steps, copies):
    @pl.when(step >= 2)
    def _():
        for copy in copies(step % 2, step):
            copy.wait()


def send(step, steps, copies):
    for copy in copies(step % 2, step):
        copy.start()

    @pl.when(step == steps - 1)
    def _():
        for copy in copies((step + 1) % 2, step):
            copy.wait()
        for copy in copies(step % 2, step):
            copy.wait()


def shared_kernel(
    x_ref, dy_ref, w_ref, out_ref, pieces_ref, gin_sum, gdown_sum
):
    count, rows, model = x_ref.shape
    block, columns = model // w_ref.shape[0], model // TILE
    piece = (w_ref.shape[1] - 2 * block) // columns
    x, dy = x_ref[...].reshape(count * rows, model), dy_ref[...].reshape(count * rows, model)
    w_gate = w_ref[:, :block, :].reshape(model, TILE)
    w_lift = w_ref[:, block : 2 * block, :].reshape(model, TILE)
    w_down = jnp.concatenate(
        [
            w_ref[:, start : start + piece, :].reshape(-1, TILE)
            for start in range(2 * block, w_ref.shape[1], piece)
        ],
        axis=1,
    )
    hidden, act, slope = gated_forward(x, w_gate, w_lift)
    out_ref[:, :, :model] = dot(hidden, w_down).astype(BF).reshape(count, rows, model)
    dhidden = dot_nt(dy, w_down)
    both = jnp.concatenate([dhidden * slope, dhidden * act], axis=1).astype(BF)
    dx = dot_nt(both, jnp.concatenate([w_gate, w_lift], axis=1))
    out_ref[:, :, model:] = dx.astype(BF).reshape(count, rows, model)
    add_up(gin_sum, dot_tn(x, both))
    add_up(gdown_sum, dot_tn(hidden, dy))

    @pl.when(pl.program_id(0) == pl.num_programs(0) - 1)
    def _():
        for owner in range(pieces_ref.shape[0]):
            rows_in = pl.ds(owner * block, block)
            for part in range(2):
                pieces_ref[owner, part * block : (part + 1) * block, :] = gin_sum[
                    rows_in, part * TILE : (part + 1) * TILE
                ].astype(BF)
            rows_down = pl.ds(owner * piece, piece)
            for column in range(columns):
                start = 2 * block + column * piece
                pieces_ref[owner, start : start + piece, :] = gdown_sum[
                    rows_down, column * TILE : (column + 1) * TILE
                ].astype(BF)


def side_by_side(blocks):
    count = blocks.shape[1] // IN_ROWS
    return jnp.concatenate(
        [
            blocks[:, part * IN_ROWS : (part + 1) * IN_ROWS].reshape(-1, TILE)
            for part in range(count)
        ],
        axis=1,
    )


def unpack_down(packed, model):
    return jnp.concatenate(
        [
            jnp.concatenate(
                [packed[tile, start : start + TILE] for start in range(0, model, TILE)], axis=1
            )
            for tile in range(packed.shape[0])
        ],
        axis=0,
    )


def expert_kernel(
    in_ref, wg_ref, wl_ref, wd_ref, y_ref, hidden_ref, act_ref, slope_ref, y_sum
):
    model = y_ref.shape[1]
    w_gate, w_lift = side_by_side(wg_ref[...]), side_by_side(wl_ref[...])
    hidden, act, slope = gated_forward(in_ref[:, :model], w_gate, w_lift)
    hidden_ref[0] = hidden
    act_ref[0] = act.astype(BF)
    slope_ref[0] = slope.astype(BF)
    add_up(y_sum, dot(hidden, unpack_down(wd_ref[...], model)))

    @pl.when(pl.program_id(0) == pl.num_programs(0) - 1)
    def _():
        y_ref[...] = y_sum[...].astype(BF)


def expert_back_kernel(
    in_ref, g_ref, own_ref, wg_ref, wl_ref, wd_ref, hidden_ref, act_ref, slope_ref,
    dx_ref, grads_ref,
    xt, dy, dx_sum, gin, gdown, sems,
):
    model = g_ref.shape[1]
    step, steps = pl.program_id(0), pl.num_programs(0)
    in_rows, tiles = gin.shape[3], gdown.shape[1]

    def copies(slot, now):
        for part in range(2):
            first = pl.multiple_of((part * steps + now) * in_rows, in_rows)
            yield pltpu.make_async_copy(
                gin.at[slot, part], grads_ref.at[:, pl.ds(first, in_rows)], sems.at[slot, part]
            )
        yield pltpu.make_async_copy(
            gdown.at[slot],
            grads_ref.at[pl.ds(now * tiles, tiles), pl.ds(2 * steps * in_rows, model)],
            sems.at[slot, 2],
        )

    @pl.when(step == 0)
    def _():
        xt[...] = in_ref[:, :model].astype(F32).T.astype(BF)
        gate = jnp.sum(in_ref[:, model:].astype(F32) * own_ref[...], axis=-1, keepdims=True)
        dy[...] = (g_ref[...].astype(F32) * gate).astype(BF)

    flush(step, steps, copies)
    slot = step % 2
    w_gate, w_lift = side_by_side(wg_ref[...]), side_by_side(wl_ref[...])
    dhidden = dot_nt(dy[...], unpack_down(wd_ref[...], model)).astype(BF)
    both = jnp.concatenate([dhidden * slope_ref[0], dhidden * act_ref[0]], axis=1)
    add_up(dx_sum, dot_nt(both, jnp.concatenate([w_gate, w_lift], axis=1)))
    into = dot(xt[...], both).astype(BF)
    shape = (gin.shape[2], IN_ROWS, TILE)
    for part in range(2):
        for tile in range(tiles):
            column = (part * tiles + tile) * TILE
            gin[slot, part, :, tile * IN_ROWS : (tile + 1) * IN_ROWS, :] = into[
                :, column : column + TILE
            ].reshape(shape)
    down = dot_tn(hidden_ref[0], dy[...]).astype(BF)
    for tile in range(tiles):
        for column in range(model // TILE):
            part = slice(column * TILE, (column + 1) * TILE)
            gdown[slot, tile, part, :] = down[tile * TILE : (tile + 1) * TILE, part]
    send(step, steps, copies)

    @pl.when(step == steps - 1)
    def _():
        dx_ref[...] = dx_sum[...].astype(BF)


def combine_kernel(
    y_ref, first_ref, second_ref, pick_ref, gate_ref, h_ref, shared_ref, g_ref, out_ref, dgate_ref
):
    table = gate_ref[...]
    y_first, y_second = dot(first_ref[...], y_ref[...]), dot(second_ref[...], y_ref[...])
    gate_first = jnp.sum(table * pick_ref[0], axis=-1, keepdims=True)
    gate_second = jnp.sum(table * pick_ref[1], axis=-1, keepdims=True)
    mixture = gate_first * y_first + gate_second * y_second
    out_ref[0] = (h_ref[...] + mixture + shared_ref[...].astype(F32)).astype(BF)
    g = g_ref[...].astype(F32)
    dgate_ref[...] = (
        jnp.sum(g * y_first, axis=-1, keepdims=True) * pick_ref[0]
        + jnp.sum(g * y_second, axis=-1, keepdims=True) * pick_ref[1]
    )


def middle_back_kernel(
    back_ref, dgate_ref, take_ref, gate_ref, small_ref, dshared_ref, g_ref, h_ref, scale_ref, gain_ref, w_ref,
    dh_ref, dhb_ref, do_ref, dlogits_ref, ggain_ref,
):
    take = take_ref[...]
    dgates = dgate_ref[...]
    table = gate_ref[...]
    gated = jnp.sum(table * dgates, axis=-1, keepdims=True)
    dlogits = (table * (dgates - gated)).astype(BF)
    dlogits_ref[...] = dlogits
    da = dshared_ref[...].astype(F32) + dot_nt(dlogits, small_ref[...]) + dot(take, back_ref[...])
    hidden, scale = h_ref[...], scale_ref[...]
    ggain_ref[...] = jnp.sum(da * hidden * scale, axis=0, keepdims=True)
    weighted = da * gain_ref[...]
    mean = jnp.mean(weighted * hidden, axis=-1, keepdims=True)
    dhidden = g_ref[...].astype(F32) + scale * weighted - hidden * (scale * scale * scale) * mean
    dh_ref[...] = dhidden
    low = dhidden.astype(BF)
    dhb_ref[...] = low
    width = w_ref.shape[2]
    do = dot_nt(low[:, :width], w_ref[0]) + dot_nt(low[:, width:], w_ref[1])
    do_ref[...] = do.astype(BF)


def project_back_kernel(dq_ref, dk_ref, dv_ref, w_ref, halo_ref, own_ref, w_back):
    width, model = w_ref.shape[2], w_ref.shape[1]
    parts = model // width
    rows = dq_ref.shape[0]

    @pl.when(pl.program_id(0) == 0)
    def _():
        for part in range(3 * parts):
            w_back[:, part * width : (part + 1) * width] = w_ref[part]

    da = dot_nt(
        jnp.concatenate([dk_ref[...], dv_ref[...]], axis=1), w_back[:, model:]
    )
    halo_ref[...] = da.astype(BF)

    @pl.when(pl.program_id(0) == pl.num_programs(0) - 1)
    def _():
        own_ref[...] = da[da.shape[0] - rows :] + dot_nt(dq_ref[...], w_back[:, :model])


def pack_kernel(late_ref, shared_ref, out_ref, *, block):
    late = late_ref[0].astype(F32)
    for source in range(1, late_ref.shape[0]):
        late = late + late_ref[source].astype(F32)
    width, own = late.shape[1], out_ref.shape[1]
    for owner in range(out_ref.shape[0]):
        part = slice(owner * own, (owner + 1) * own)
        out_ref[owner, :, :width] = late[part]
        for half in range(2):
            columns = pl.ds(width + half * TILE, TILE)
            out_ref[owner, :, columns] = shared_ref[half * block + owner * own : half * block + (owner + 1) * own, :]


def unpack_kernel(
    in_ref, w_ref, gain_ref, qkv_ref, out_ref, small_ref, dgain_ref, shared_ref, *, wide_a, piece
):
    sources, own = in_ref.shape[0], in_ref.shape[1]
    model = out_ref.shape[1]
    early = sources // 2

    def take(source, start):
        return in_ref[source, :, start : start + LANES]

    small = take(0, wide_a + LANES)
    for source in range(1, sources):
        small = small + take(source, wide_a + LANES)
    small_ref[...] = small
    dgain = jnp.zeros((own, LANES), F32)
    for pair in range(model // LANES):
        if pair < early:
            k, v = take(2 * pair, 0), take(2 * pair, LANES)
            q, o = take(2 * pair + 1, 0), take(2 * pair + 1, LANES)
        else:
            first = 4 * (pair - early)
            k, q, v, o = (take(first + index, wide_a) for index in range(4))
        for which, value in enumerate((q, k, v)):
            part = slice(which * model + pair * LANES, which * model + (pair + 1) * LANES)
            qkv_ref[:, part] = value
            dgain = dgain + value * w_ref[:, part].astype(F32)
        out_ref[:, pair * LANES : (pair + 1) * LANES] = o
    dgain_ref[...] = jnp.sum(dgain, axis=-1, keepdims=True) / gain_ref[...]
    lane = lax.broadcasted_iota(jnp.int32, (own, LANES), 1)
    per = LANES // piece
    for column in range(shared_ref.shape[1] // LANES):
        start = wide_a + 2 * LANES + column // per * LANES
        total = jnp.zeros((own, LANES), F32)
        for source in range(sources):
            turn = (source - column % per) * piece % LANES
            value = take(source, start)
            value = pltpu.roll(value, turn, 1) if turn else value
            total = jnp.where(lane // piece == source, value, total)
        shared_ref[:, column * LANES : (column + 1) * LANES] = total


def per_device(
    tokens,
    segments,
    routes,
    w_qkv,
    w_out,
    w_router,
    shared_in,
    shared_down,
    attn_gain,
    ffn_gain,
    expert_in,
    expert_down,
    cotangent,
):
    ctx, fsdp = lax.axis_size("ctx"), lax.axis_size("fsdp")
    ctx_index, core = lax.axis_index("ctx"), lax.axis_index("fsdp") % 2
    rows, model = tokens.shape[1], tokens.shape[2]
    reach = max(1, WIN // rows)
    span = (reach + 1) * rows
    capacity = max(2, 3 * rows * TOPK // (2 * ctx))
    slots = ctx * capacity
    own = w_qkv.shape[0]
    owned_down = shared_down.shape[0]
    experts = w_router.shape[1]
    ff = shared_in.shape[1] // 2
    tiles = ff // TILE

    x, g = tokens[0], cotangent[0]
    segment_row = jnp.zeros((16, model), BF).at[0, :rows].set(segments[0].astype(BF))
    carried = jnp.concatenate([x, segment_row], axis=0)
    place_z = ctx_index % ROW
    lines = range(0, ctx, ROW)
    previous = shifted(carried, "ctx", ROW)
    arrived = [previous]
    for distance in range(reach - 1, 0, -1):
        arrived.append(
            lax.ppermute(
                jnp.where(place_z + distance < ROW, carried, previous),
                "ctx",
                [(line + z, line + (z + distance) % ROW) for line in lines for z in range(ROW)],
            )
        )

    cosine, sine = rotary_tables(span, (ctx_index - reach) * rows)
    route_own = routes[0]
    expert_ids = jnp.arange(experts, dtype=jnp.int32)
    hits = route_own[:, :, None] == expert_ids[None, None, :]
    member = jnp.sum(hits.astype(jnp.int32), axis=1)
    ranking = jnp.cumsum(member, axis=0, dtype=jnp.int32) - 1
    slot_ids = jnp.arange(capacity, dtype=jnp.int32)
    placed = (member[:, :, None] > 0) & (ranking[:, :, None] == slot_ids[None, None, :])
    take = placed.astype(BF).reshape(rows, slots)
    put = take.T
    selector = (
        (hits[:, :, :, None] & placed[:, None, :, :]).astype(BF).reshape(rows, TOPK * slots)
    )
    picked = jnp.pad(
        hits.astype(F32).transpose(1, 0, 2), ((0, 0), (0, 0), (0, LANES - experts))
    )
    lane = jnp.arange(LANES, dtype=jnp.int32)[None, :]
    own_lanes = ((lane == ctx_index) | (lane == ctx_index + LANES // 2)).astype(F32)
    g_to_slots = dot(put, g).astype(BF)

    small = jnp.concatenate(
        [w_router, attn_gain[:, None], ffn_gain[:, None], jnp.zeros((own, LANES - experts - 2), BF)],
        axis=1,
    )
    projections = jnp.concatenate([w_qkv, w_out], axis=1)
    width = projections.shape[1] // fsdp
    near = lax.all_to_all(
        jnp.concatenate(
            [
                projections.reshape(own, fsdp, width).transpose(1, 0, 2),
                jnp.broadcast_to(small, (fsdp, own, LANES)),
                shared_in.reshape(own, 2, ctx, fsdp, owned_down)
                .transpose(3, 0, 1, 2, 4)
                .reshape(fsdp, own, 2 * TILE),
            ],
            axis=2,
        ),
        "fsdp",
        split_axis=0,
        concat_axis=0,
        tiled=True,
    ).reshape(fsdp * own, -1)

    def to_ctx(values):
        return lax.all_to_all(
            jnp.broadcast_to(values, (ctx, *values.shape)), "ctx", split_axis=0, concat_axis=0, tiled=True
        )

    g_all = lax.all_gather(g, "fsdp", axis=0)
    columns = model // TILE
    dense = to_ctx(after(near[:, : width + LANES], previous)).reshape(model, width + LANES)
    w_full = lax.all_gather(after(dense[:, :width], g_all, cosine, sine, g_to_slots, picked), "fsdp", axis=0)
    down_own = shared_down.reshape(owned_down, columns, TILE).transpose(1, 0, 2).reshape(-1, TILE)
    shared_own_w = jnp.concatenate(
        [near[:, width + LANES : -TILE], near[:, -TILE:], down_own], axis=0
    )
    place = ctx_index.astype(jnp.int32).reshape(1)
    place_spec = pl.BlockSpec(memory_space=pltpu.SMEM)
    in_rows, down_rows = expert_in.shape[1], expert_down.shape[1]
    expert_packed = jnp.concatenate(
        [
            expert_in[0].reshape(in_rows, 2 * tiles, TILE).transpose(1, 0, 2).reshape(-1, TILE),
            expert_down[0].reshape(down_rows, model // TILE, TILE).transpose(1, 0, 2).reshape(-1, TILE),
        ],
        axis=0,
    )
    expert_full = lax.all_gather(after(expert_packed, w_full, *arrived), "fsdp", axis=0)

    def exchange(values):
        return lax.all_to_all(
            values.reshape(ctx, values.shape[0] // ctx, values.shape[1]),
            "ctx",
            split_axis=0,
            concat_axis=0,
            tiled=True,
        ).reshape(values.shape)

    slot_g = exchange(after(g_to_slots, *arrived))

    pairs = model // LANES
    small_spec = pl.BlockSpec((model, LANES), lambda *_: (0, width // LANES))
    per, parts = width // LANES, model // width

    def columns_of(which):
        return pl.BlockSpec((1, model, LANES), lambda j: (which * parts + j // per, 0, j % per))

    blocks = [*arrived, carried]
    pair_spec = lambda height: pl.BlockSpec((height, LANES), lambda j: (0, j))
    q, k, kt, v, e, rl, rlb, attended, span_scale = pl.pallas_call(
        functools.partial(attend_kernel, gain_lane=experts, parts=reach + 1),
        grid=(pairs,),
        in_specs=[
            place_spec,
            *[whole(block) for block in blocks],
            small_spec,
            columns_of(0),
            columns_of(1),
            columns_of(2),
            whole(cosine),
            whole(sine),
        ],
        out_specs=[
            pair_spec(rows),
            pair_spec(span),
            pl.BlockSpec((LANES, span), lambda j: (j, 0)),
            pair_spec(span),
            pl.BlockSpec((2, span, rows), lambda j: (j, 0, 0)),
            pl.BlockSpec((1, 8, rows), lambda j: (j, 0, 0)),
            pair_spec(rows),
            pair_spec(rows),
            pl.BlockSpec((span, 1), lambda j: (0, 0)),
        ],
        out_shape=[
            jax.ShapeDtypeStruct((rows, model), BF),
            jax.ShapeDtypeStruct((span, model), BF),
            jax.ShapeDtypeStruct((model, span), BF),
            jax.ShapeDtypeStruct((span, model), BF),
            jax.ShapeDtypeStruct((HEADS, span, rows), BF),
            jax.ShapeDtypeStruct((pairs, 8, rows), F32),
            jax.ShapeDtypeStruct((rows, model), F32),
            jax.ShapeDtypeStruct((rows, model), BF),
            jax.ShapeDtypeStruct((span, 1), F32),
        ],
        scratch_shapes=[
            pltpu.VMEM((span, model), BF),
            pltpu.VMEM((2, span, rows), F32),
            pltpu.VMEM((LANES, span), BF),
            pltpu.VMEM((span, rows), F32),
        ],
        compiler_params=params(VMEM_MB),
        cost_estimate=cost(20),
        name="attend",
    )(place, *blocks, dense, w_full, w_full, w_full, cosine, sine)

    out_spec = pl.BlockSpec((parts, model, width), lambda *_: (3, 0, 0))
    hidden, scale_two, normed, normed_t, outgoing, gates, gain_two = pl.pallas_call(
        functools.partial(middle_kernel, gain_lane=experts + 1),
        grid=(1,),
        in_specs=[
            whole(attended),
            out_spec,
            small_spec,
            whole(x),
            whole(picked),
            whole(put),
        ],
        out_specs=[
            pl.BlockSpec((rows, model), lambda *_: (0, 0)),
            pl.BlockSpec((rows, 1), lambda *_: (0, 0)),
            pl.BlockSpec((rows, model), lambda *_: (0, 0)),
            pl.BlockSpec((model, rows), lambda *_: (0, 0)),
            pl.BlockSpec((slots, model + LANES), lambda *_: (0, 0)),
            pl.BlockSpec((rows, LANES), lambda *_: (0, 0)),
            pl.BlockSpec((1, model), lambda *_: (0, 0)),
        ],
        out_shape=[
            jax.ShapeDtypeStruct((rows, model), F32),
            jax.ShapeDtypeStruct((rows, 1), F32),
            jax.ShapeDtypeStruct((rows, model), BF),
            jax.ShapeDtypeStruct((model, rows), BF),
            jax.ShapeDtypeStruct((slots, model + LANES), BF),
            jax.ShapeDtypeStruct((rows, LANES), F32),
            jax.ShapeDtypeStruct((1, model), F32),
        ],
        compiler_params=params(VMEM_MB),
        cost_estimate=cost(5),
        name="middle",
    )(attended, w_full, dense, x, picked, put)
    normed_all = lax.all_gather(normed, "fsdp", axis=0)
    incoming = exchange(after(outgoing, slot_g))
    shared_full = to_ctx(after(shared_own_w, incoming))
    gain_one = dense[:, width + experts : width + experts + 1].astype(F32)
    span_x = jnp.concatenate([block[:rows] for block in blocks], axis=0)
    first_t = (span_x.T.astype(F32) * span_scale.reshape(1, span) * gain_one).astype(BF)
    incoming = after(incoming, first_t)

    packed_rows = 3 * model

    steps = tiles // AT_ONCE
    expert_specs = [
        pl.BlockSpec((fsdp, AT_ONCE * in_rows, TILE), lambda t: (0, t, 0)),
        pl.BlockSpec((fsdp, AT_ONCE * in_rows, TILE), lambda t: (0, steps + t, 0)),
        pl.BlockSpec((AT_ONCE, model, TILE), lambda t: (t, 2 * in_rows * tiles // model, 0)),
    ]
    unit_spec = pl.BlockSpec((1, slots, AT_ONCE * TILE), lambda t: (t, 0, 0))
    expert_y, *units = pl.pallas_call(
        expert_kernel,
        grid=(steps,),
        in_specs=[whole(incoming), *expert_specs],
        out_specs=[
            pl.BlockSpec((slots, model), lambda t: (0, 0)),
            unit_spec,
            unit_spec,
            unit_spec,
        ],
        out_shape=[jax.ShapeDtypeStruct((slots, model), BF)]
        + [jax.ShapeDtypeStruct((steps, slots, AT_ONCE * TILE), BF)] * 3,
        scratch_shapes=[pltpu.VMEM((slots, model), F32)],
        compiler_params=params(VMEM_MB),
        cost_estimate=cost(60),
        name="expert",
    )(incoming, expert_full, expert_full, expert_full)
    returned_y = exchange(after(expert_y, shared_full))

    at_once = 2
    block = model // ctx
    shared_part, shared_pieces = pl.pallas_call(
        shared_kernel,
        grid=(fsdp // at_once,),
        in_specs=[
            pl.BlockSpec((at_once, rows, model), lambda t: (t, 0, 0)),
            pl.BlockSpec((at_once, rows, model), lambda t: (t, 0, 0)),
            whole(shared_full),
        ],
        out_specs=[
            pl.BlockSpec((at_once, rows, 2 * model), lambda t: (t, 0, 0)),
            whole(shared_full),
        ],
        out_shape=[
            jax.ShapeDtypeStruct((fsdp, rows, 2 * model), BF),
            jax.ShapeDtypeStruct(shared_full.shape, BF),
        ],
        scratch_shapes=[pltpu.VMEM((model, 2 * TILE), F32), pltpu.VMEM((TILE, model), F32)],
        compiler_params=params(VMEM_MB),
        cost_estimate=cost(18),
        name="shared",
    )(after(normed_all, expert_y), g_all, shared_full)
    shared_both = lax.psum_scatter(after(shared_part, returned_y), "fsdp", scatter_dimension=0)
    shared_own = jnp.sum(
        lax.all_to_all(
            after(shared_pieces, returned_y), "ctx", split_axis=0, concat_axis=0, tiled=True
        ).astype(F32),
        axis=0,
    )
    back, gexpert = pl.pallas_call(
        expert_back_kernel,
        grid=(steps,),
        in_specs=[
            whole(incoming),
            whole(slot_g),
            whole(own_lanes),
            *expert_specs,
            unit_spec,
            unit_spec,
            unit_spec,
        ],
        out_specs=[
            pl.BlockSpec((slots, model), lambda t: (0, 0)),
            pl.BlockSpec(memory_space=pl.ANY),
        ],
        out_shape=[
            jax.ShapeDtypeStruct((slots, model), BF),
            jax.ShapeDtypeStruct((fsdp, packed_rows, TILE), BF),
        ],
        scratch_shapes=[
            pltpu.VMEM((model, slots), BF),
            pltpu.VMEM((slots, model), BF),
            pltpu.VMEM((slots, model), F32),
            pltpu.VMEM((2, 2, fsdp, AT_ONCE * in_rows, TILE), BF),
            pltpu.VMEM((2, AT_ONCE, model, TILE), BF),
            pltpu.SemaphoreType.DMA((2, 3)),
        ],
        compiler_params=params(VMEM_MB),
        cost_estimate=cost(22),
        name="expert_back",
    )(after(incoming, shared_part, returned_y), slot_g, own_lanes, expert_full, expert_full, expert_full, *units)
    returned = exchange(after(back, shared_own))
    expert_sum = lax.psum_scatter(after(gexpert, shared_own), "fsdp", scatter_dimension=0)

    mixed, dgates = pl.pallas_call(
        combine_kernel,
        grid=(1,),
        in_specs=[
            pl.BlockSpec((slots, model), lambda *_: (0, 0)),
            pl.BlockSpec((rows, slots), lambda *_: (0, 0)),
            pl.BlockSpec((rows, slots), lambda *_: (0, 1)),
            whole(picked),
            whole(gates),
            whole(hidden),
            pl.BlockSpec((rows, model), lambda *_: (0, 0)),
            whole(g),
        ],
        out_specs=[
            pl.BlockSpec((1, rows, model), lambda *_: (0, 0, 0)),
            pl.BlockSpec((rows, LANES), lambda *_: (0, 0)),
        ],
        out_shape=[
            jax.ShapeDtypeStruct((1, rows, model), BF),
            jax.ShapeDtypeStruct((rows, LANES), F32),
        ],
        compiler_params=params(VMEM_MB),
        cost_estimate=cost(3),
        name="combine",
    )(returned_y, selector, selector, picked, gates, hidden, shared_both, g)

    returned = after(returned, dgates)

    dhidden, dhidden_low, dattended, dlogits, ggain_two = pl.pallas_call(
        middle_back_kernel,
        grid=(1,),
        in_specs=[
            whole(returned),
            whole(dgates),
            whole(take),
            whole(gates),
            small_spec,
            pl.BlockSpec((rows, model), lambda *_: (0, 1)),
            whole(g),
            whole(hidden),
            whole(scale_two),
            whole(gain_two),
            out_spec,
        ],
        out_specs=[
            pl.BlockSpec((rows, model), lambda *_: (0, 0)),
            pl.BlockSpec((rows, model), lambda *_: (0, 0)),
            pl.BlockSpec((rows, model), lambda *_: (0, 0)),
            pl.BlockSpec((rows, LANES), lambda *_: (0, 0)),
            pl.BlockSpec((1, model), lambda *_: (0, 0)),
        ],
        out_shape=[
            jax.ShapeDtypeStruct((rows, model), F32),
            jax.ShapeDtypeStruct((rows, model), BF),
            jax.ShapeDtypeStruct((rows, model), BF),
            jax.ShapeDtypeStruct((rows, LANES), BF),
            jax.ShapeDtypeStruct((1, model), F32),
        ],
        compiler_params=params(VMEM_MB),
        cost_estimate=cost(6),
        name="middle_back",
    )(
        returned, dgates, take, gates, dense, shared_both, g, hidden, scale_two, gain_two, w_full
    )

    grouter = dot(normed_t, dlogits)
    small_grads = jnp.concatenate(
        [grouter[:, :experts], ggain_two.T, jnp.zeros((model, LANES - experts - 1), F32)], axis=1
    ).astype(BF)
    attended_t = attended.T
    core_scalar = core.astype(jnp.int32).reshape(1)

    def attend_back(first, count, down, *filled):
        pair_from = lambda height: pl.BlockSpec((height, LANES), lambda j: (0, first + j))
        operands = (
            core_scalar, q, k, kt, v, e, rl, rlb, down, cosine, sine, first_t, attended_t, dhidden_low, *filled,
        )
        return pl.pallas_call(
            attend_back_kernel,
            grid=(count,),
            in_specs=[
                place_spec,
                pair_from(rows),
                pair_from(span),
                pl.BlockSpec((LANES, span), lambda j: (first + j, 0)),
                pair_from(span),
                pl.BlockSpec((2, span, rows), lambda j: (first + j, 0, 0)),
                pl.BlockSpec((1, 8, rows), lambda j: (first + j, 0, 0)),
                pair_from(rows),
                pair_from(rows),
                whole(cosine),
                whole(sine),
                whole(first_t),
                whole(attended_t),
                pair_from(rows),
            ]
            + [pl.BlockSpec(memory_space=pl.ANY)] * len(filled),
            out_specs=[
                pair_from(rows),
                pair_from(span),
                pair_from(span),
                pl.BlockSpec((2, model, 2 * LANES), lambda j: (0, 0, j)),
            ],
            out_shape=[
                jax.ShapeDtypeStruct((rows, model), BF),
                jax.ShapeDtypeStruct((span, model), BF),
                jax.ShapeDtypeStruct((span, model), BF),
                jax.ShapeDtypeStruct((2, model, count * 2 * LANES), BF),
            ],
            input_output_aliases={
                len(operands) - len(filled) + index: index for index in range(len(filled))
            },
            scratch_shapes=[
                pltpu.VMEM((2, span, rows), F32),
                pltpu.VMEM((2, span, rows), BF),
                pltpu.VMEM((span, LANES), F32),
                pltpu.VMEM((span, LANES), F32),
            ],
            compiler_params=params(VMEM_MB),
            cost_estimate=cost(4 * count),
            name=f"attend_back_{first}",
        )(*operands)

    chips = fsdp // 2

    def paired_columns(grads, *others):
        kept, sent = grads[0], grads[1]
        if others:
            sent = after(sent, *others)
        partner = lax.ppermute(sent, "fsdp", [(i, i ^ 1) for i in range(fsdp)])
        paired = (kept.astype(F32) + partner.astype(F32)).astype(BF)
        return paired.reshape(model, chips, -1).transpose(1, 0, 2)

    def along_y(paired):
        pieces = lax.all_to_all(
            paired,
            "fsdp",
            split_axis=0,
            concat_axis=0,
            axis_index_groups=[list(range(start, fsdp, 2)) for start in range(2)],
            tiled=True,
        )
        return jnp.sum(pieces.astype(F32), axis=0).astype(BF)

    early_pairs = 2 * pairs // 3
    *grads_a, group_a = attend_back(0, early_pairs, dattended)
    paired_a = paired_columns(group_a)
    late_a = along_y(paired_a)
    dq, dk, dv, group_b = attend_back(
        early_pairs, pairs - early_pairs, after(dattended, paired_a), *grads_a
    )
    paired_b = paired_columns(group_b)

    dspan, down = pl.pallas_call(
        project_back_kernel,
        grid=(2,),
        in_specs=[
            whole(dq),
            pl.BlockSpec((span // 2, model), lambda b: (b, 0)),
            pl.BlockSpec((span // 2, model), lambda b: (b, 0)),
            pl.BlockSpec((3 * parts, model, width), lambda b: (0, 0, 0)),
        ],
        out_specs=[
            pl.BlockSpec((span // 2, model), lambda b: (b, 0)),
            pl.BlockSpec((rows, model), lambda b: (0, 0)),
        ],
        out_shape=[
            jax.ShapeDtypeStruct((span, model), BF),
            jax.ShapeDtypeStruct((rows, model), F32),
        ],
        compiler_params=params(VMEM_MB),
        scratch_shapes=[pltpu.VMEM((model, 3 * model), BF)],
        cost_estimate=cost(8),
        name="project_back",
    )(dq, dk, dv, w_full)
    total, passed = down, dspan[:rows].astype(F32)
    for distance in range(1, reach):
        lower = (reach - distance) * rows
        moved = lax.ppermute(
            dspan[lower : lower + rows],
            "ctx",
            [(line + z, line + (z - distance) % ROW) for line in lines for z in range(ROW)],
        ).astype(F32)
        here = place_z + distance < ROW
        total = total + jnp.where(here, moved, 0.0)
        passed = passed + jnp.where(here, 0.0, moved)
    expert_rows = 2 * tiles * in_rows
    grad_expert_in = (
        expert_sum[:expert_rows]
        .astype(F32)
        .reshape(2 * tiles, in_rows, TILE)
        .transpose(1, 0, 2)
        .reshape(1, in_rows, 2 * ff)
    )
    grad_expert_down = (
        expert_sum[expert_rows:]
        .astype(F32)
        .reshape(columns, down_rows, TILE)
        .transpose(1, 0, 2)
        .reshape(1, down_rows, model)
    )
    late_b = along_y(after(paired_b, down, late_a))
    passed = after(passed.astype(BF), grad_expert_in, grad_expert_down, late_b)
    late = jnp.concatenate([late_a, late_b, small_grads], axis=1).reshape(ctx, block, -1)
    late = lax.all_to_all(after(late, passed), "ctx", split_axis=0, concat_axis=0, tiled=True)

    grad_shared_down = (
        shared_own[2 * block :]
        .reshape(columns, owned_down, TILE)
        .transpose(1, 0, 2)
        .reshape(owned_down, model)
    )
    wide_a = late_a.shape[1]
    late_width = late.shape[2]
    last = pl.pallas_call(
        functools.partial(pack_kernel, block=block),
        grid=(1,),
        in_specs=[whole(late), pl.BlockSpec((2 * block, TILE), lambda *_: (0, 0))],
        out_specs=pl.BlockSpec((fsdp, own, late_width + 2 * TILE), lambda *_: (0, 0, 0)),
        out_shape=jax.ShapeDtypeStruct((fsdp, own, late_width + 2 * TILE), F32),
        compiler_params=params(VMEM_MB),
        cost_estimate=cost(2),
        name="pack",
    )(late, shared_own)
    last = lax.all_to_all(last, "fsdp", split_axis=0, concat_axis=0, tiled=True)
    wanted = [
        jax.ShapeDtypeStruct((own, 3 * model), F32),
        jax.ShapeDtypeStruct((own, model), F32),
        jax.ShapeDtypeStruct((own, LANES), F32),
        jax.ShapeDtypeStruct((own, 1), F32),
        jax.ShapeDtypeStruct((own, 2 * ff), F32),
    ]
    gain_own = attn_gain.astype(F32)[:, None]
    grad_qkv, grad_out, small_total, grad_gain_one, grad_shared_in = pl.pallas_call(
        functools.partial(unpack_kernel, wide_a=wide_a, piece=owned_down),
        grid=(1,),
        in_specs=[whole(last), whole(w_qkv), whole(gain_own)],
        out_specs=[whole(array) for array in wanted],
        out_shape=wanted,
        compiler_params=params(VMEM_MB),
        cost_estimate=cost(2),
        name="unpack",
    )(last, w_qkv, gain_own)

    total = total + shifted(passed, "ctx", -ROW).astype(F32)
    input_rows = x.astype(F32)
    scale_one = span_scale[reach * rows :]
    weighted = total * gain_one.reshape(1, model)
    input_grad = (
        dhidden
        + scale_one * weighted
        - input_rows
        * scale_one**3
        * jnp.mean(weighted * input_rows, axis=-1, keepdims=True)
    )[None]

    return (
        mixed,
        input_grad,
        grad_qkv,
        grad_out,
        small_total[:, :experts],
        grad_shared_in,
        grad_shared_down,
        grad_gain_one[:, 0],
        small_total[:, experts],
        grad_expert_in,
        grad_expert_down,
    )


def solution(mesh):
    placed = (
        P("fsdp", "ctx", None),
        P("fsdp", "ctx"),
        P("fsdp", "ctx", None),
        P(("ctx", "fsdp"), None),
        P(("ctx", "fsdp"), None),
        P(("ctx", "fsdp"), None),
        P(("ctx", "fsdp"), None),
        P(("ctx", "fsdp"), None),
        P(("ctx", "fsdp")),
        P(("ctx", "fsdp")),
        P("ctx", "fsdp", None),
        P("ctx", "fsdp", None),
        P("fsdp", "ctx", None),
    )
    return jax.shard_map(
        per_device,
        mesh=mesh,
        in_specs=placed,
        out_specs=(
            P("fsdp", "ctx", None),
            P("fsdp", "ctx", None),
            P(("ctx", "fsdp"), None),
            P(("ctx", "fsdp"), None),
            P(("ctx", "fsdp"), None),
            P(("ctx", "fsdp"), None),
            P(("ctx", "fsdp"), None),
            P(("ctx", "fsdp")),
            P(("ctx", "fsdp")),
            P("ctx", "fsdp", None),
            P("ctx", "fsdp", None),
        ),
        check_vma=False,
    )
```

```python
import functools

import jax
import jax.numpy as jnp
from jax import lax
from jax.experimental import pallas as pl
from jax.experimental.pallas import tpu as pltpu
from jax.sharding import PartitionSpec as P

HEADS = 12
HEAD_DIM = 64
TOPK = 2
WIN = 1024
EPSILON = 1e-06

BF = jnp.bfloat16
F32 = jnp.float32
TILE = 256
LANES = 128
IN_ROWS = 96
AT_ONCE = 2
KEY_BLOCK = 128
ROW = 4
VMEM_MB = 60


def dot(a, b):
    return jnp.dot(a, b, preferred_element_type=F32)


def dot_nt(a, b):
    return lax.dot_general(a, b, (((1,), (1,)), ((), ())), preferred_element_type=F32)


def dot_tn(a, b):
    return lax.dot_general(a, b, (((0,), (0,)), ((), ())), preferred_element_type=F32)


def params(megabytes):
    return pltpu.CompilerParams(vmem_limit_bytes=megabytes * 1024 * 1024)


def cost(microseconds):
    return pl.CostEstimate(
        flops=int(microseconds * 1.0e9), bytes_accessed=int(microseconds * 1.0e6), transcendentals=0
    )


def after(value, *others):
    return lax.optimization_barrier((value, *others))[0]


def whole(array):
    return pl.BlockSpec(array.shape, lambda *_: (0,) * array.ndim)


def shifted(value, axis, steps):
    count = lax.axis_size(axis)
    leading, last = (max(0, -steps), min(count, count - steps))
    return lax.ppermute(value, axis, [(source, source + steps) for source in range(leading, last)])


def split_high_low(values):
    high = values.astype(BF)
    return high, (values - high.astype(F32)).astype(BF)


def rotary_tables(rows, offset):
    half = HEAD_DIM // 2
    frequency = jnp.exp(-jnp.log(10000.0) * (2.0 * jnp.arange(half, dtype=F32) / HEAD_DIM))
    places = (offset + jnp.arange(rows, dtype=jnp.int32)).astype(F32)
    angles = places[:, None] * frequency[None, :]
    cosine, sine = jnp.cos(angles), jnp.sin(angles)
    return (
        jnp.concatenate([cosine] * 4, axis=1),
        jnp.concatenate([-sine, sine, -sine, sine], axis=1),
    )


def swapped_halves(values):
    lane = lax.broadcasted_iota(jnp.int32, (1, LANES), 1)
    half = HEAD_DIM // 2
    return jnp.where(
        lane % HEAD_DIM < half,
        pltpu.roll(values, LANES - half, 1),
        pltpu.roll(values, half, 1),
    )


def head_lanes(values, head):
    lane = lax.broadcasted_iota(jnp.int32, (1, LANES), 1)
    return jnp.where(lane // HEAD_DIM == head, values, jnp.zeros_like(values))


def fold_rows(values, op):
    return op(values.reshape(values.shape[0] // 8, 8, values.shape[1]), axis=0)


def attend_kernel(
    place_ref, *refs, gain_lane, parts
):
    blocks, refs = refs[:parts], refs[parts:]
    (
        small_ref, wq_ref, wk_ref, wv_ref, cos_ref, sin_ref,
        q_ref, k_ref, kt_ref, v_ref, e_ref, rl_ref, rlb_ref, o_ref, scale_ref,
        normed, score, vt, bias_ref,
    ) = refs
    rows, model = q_ref.shape[0], normed.shape[1]
    span = parts * rows

    @pl.when(pl.program_id(0) == 0)
    def _():
        gain = small_ref[...].astype(F32).T[gain_lane : gain_lane + 1, :]
        query_segment = blocks[-1][rows : rows + 1, :rows].astype(F32)
        query_place = lax.broadcasted_iota(jnp.int32, (rows, rows), 1)
        key_place = lax.broadcasted_iota(jnp.int32, (rows, rows), 0)
        for index, block in enumerate(blocks):
            part = pl.ds(index * rows, rows)
            values = block[:rows, :].astype(F32)
            scale = lax.rsqrt(jnp.mean(values * values, axis=-1, keepdims=True) + EPSILON)
            scale_ref[part, :] = scale
            normed[part, :] = (values * scale * gain).astype(BF)
            key_segment = block[rows : rows + 16, :rows].astype(F32).T[:, :1]
            distance = query_place - key_place + (parts - 1 - index) * rows
            allowed = (distance >= 0) & (distance < WIN) & (key_segment == query_segment)
            allowed = allowed & (place_ref[0] >= parts - 1 - index)
            bias_ref[part, :] = jnp.where(allowed, 0.0, -1e30)

    pair = dot(normed[...], jnp.concatenate([wk_ref[0], wv_ref[0]], axis=1))
    keys = pair[:, :LANES]
    keys = keys * cos_ref[...] + swapped_halves(keys) * sin_ref[...]
    k_ref[...] = keys.astype(BF)
    kt_ref[...] = keys.T.astype(BF)
    values = pair[:, LANES:]
    v_ref[...] = values.astype(BF)
    vt[...] = values.T.astype(BF)
    queries = dot(normed[span - rows :, :], wq_ref[0])
    queries = queries * cos_ref[span - rows :, :] + swapped_halves(queries) * sin_ref[span - rows :, :]
    queries = (queries.astype(BF).astype(F32) * HEAD_DIM**-0.5).astype(BF)
    q_ref[...] = queries

    heads = range(2)
    own = [head_lanes(queries, head) for head in heads]
    largest = [jnp.full((8, rows), -3e38, F32) for _ in heads]
    for start in range(0, span, KEY_BLOCK):
        part = pl.ds(start, KEY_BLOCK)
        for head in heads:
            block = dot_nt(k_ref[part, :], own[head]) + bias_ref[part, :]
            score[head, part, :] = block
            largest[head] = jnp.maximum(largest[head], fold_rows(block, jnp.max))
    largest = [jnp.max(value, axis=0, keepdims=True) for value in largest]
    total = [jnp.zeros((8, rows), F32) for _ in heads]
    for start in range(0, span, KEY_BLOCK):
        part = pl.ds(start, KEY_BLOCK)
        for head in heads:
            block = jnp.exp(score[head, part, :] - largest[head])
            total[head] = total[head] + fold_rows(block, jnp.sum)
            e_ref[head, part, :] = block.astype(BF)
    outs, sums = [], []
    for head in heads:
        inverse = 1.0 / jnp.sum(total[head], axis=0, keepdims=True)
        rl_ref[0, head : head + 1, :] = inverse
        outs.append(dot(vt[head * HEAD_DIM : (head + 1) * HEAD_DIM, :], e_ref[head]) * inverse)
        sums.append(jnp.broadcast_to(inverse, (HEAD_DIM, rows)))
    o_ref[...] = jnp.concatenate(outs, axis=0).T.astype(BF)
    rlb_ref[...] = jnp.concatenate(sums, axis=0).T


def attend_back_kernel(
    core_ref, q_ref, k_ref, kt_ref, v_ref, e_ref, rl_ref, rlb_ref, do_ref, cos_ref, sin_ref, xt_ref, ot_ref, dh_ref,
    *refs,
):
    dq_ref, dk_ref, dv_ref, grads_ref, dprob, dscore, dk, dv = refs[-8:]
    span, rows = k_ref.shape[0], q_ref.shape[0]
    scaled = do_ref[...].astype(F32) * rlb_ref[...]
    heads = range(2)
    down = [head_lanes(scaled, head).astype(BF) for head in heads]
    own = [head_lanes(q_ref[...], head) for head in heads]
    own_both, down_both = jnp.concatenate(own, axis=0), jnp.concatenate(down, axis=0)
    inner = [jnp.zeros((8, rows), F32) for _ in heads]
    for start in range(0, span, KEY_BLOCK):
        part = pl.ds(start, KEY_BLOCK)
        for head in heads:
            block = dot_nt(v_ref[part, :], down[head])
            dprob[head, part, :] = block
            inner[head] = inner[head] + fold_rows(block * e_ref[head, part, :].astype(F32), jnp.sum)
    inner = [
        jnp.sum(inner[head], axis=0, keepdims=True) * rl_ref[0, head : head + 1, :]
        for head in heads
    ]
    for start in range(0, span, KEY_BLOCK):
        part = pl.ds(start, KEY_BLOCK)
        for head in heads:
            weight = e_ref[head, part, :]
            block = (weight.astype(F32) * (dprob[head, part, :] - inner[head])).astype(BF)
            dscore[head, part, :] = block
        dk[part, :] = dot(
            jnp.concatenate([dscore[head, part, :] for head in heads], axis=1), own_both
        )
        dv[part, :] = dot(
            jnp.concatenate([e_ref[head, part, :] for head in heads], axis=1), down_both
        )
    dqs = [
        dot(kt_ref[head * HEAD_DIM : (head + 1) * HEAD_DIM, :], dscore[head]) for head in heads
    ]
    dquery = jnp.concatenate(dqs, axis=0).T * HEAD_DIM**-0.5
    dquery = dquery * cos_ref[span - rows :, :] - swapped_halves(dquery) * sin_ref[span - rows :, :]
    dquery = dquery.astype(BF)
    dq_ref[...] = dquery
    dkeys = dk[...]
    dkeys = (dkeys * cos_ref[...] - swapped_halves(dkeys) * sin_ref[...]).astype(BF)
    dvalues = dv[...].astype(BF)
    dk_ref[...] = dkeys
    dv_ref[...] = dvalues
    core = core_ref[0]
    grads_ref[core] = dot(xt_ref[...], jnp.concatenate([dkeys, dvalues], axis=1)).astype(BF)
    grads_ref[1 - core, :, :LANES] = dot(xt_ref[:, span - rows :], dquery).astype(BF)
    grads_ref[1 - core, :, LANES:] = dot(ot_ref[...], dh_ref[...]).astype(BF)


def middle_kernel(
    o_ref, w_ref, small_ref, x_ref, pick_ref, put_ref,
    h_ref, scale_ref, a_ref, at_ref, out_ref, gate_ref, gain_ref,
    *, gain_lane,
):
    projected = jnp.concatenate([dot(o_ref[...], w_ref[part]) for part in range(2)], axis=1)
    hidden = x_ref[...].astype(F32) + projected
    h_ref[...] = hidden
    scale = lax.rsqrt(jnp.mean(hidden * hidden, axis=-1, keepdims=True) + EPSILON)
    scale_ref[...] = scale
    small = small_ref[...]
    gain = small.astype(F32).T[gain_lane : gain_lane + 1, :]
    gain_ref[...] = gain
    low = (hidden * scale * gain).astype(BF)
    a_ref[...] = low
    at_ref[...] = low.astype(F32).T.astype(BF)
    logits = dot(low, small)
    first, second = pick_ref[0], pick_ref[1]
    chosen_first = jnp.sum(logits * first, axis=-1, keepdims=True)
    chosen_second = jnp.sum(logits * second, axis=-1, keepdims=True)
    largest = jnp.maximum(chosen_first, chosen_second)
    chosen_first = jnp.exp(chosen_first - largest)
    chosen_second = jnp.exp(chosen_second - largest)
    total = chosen_first + chosen_second
    table = (chosen_first / total) * first + (chosen_second / total) * second
    gate_ref[...] = table
    high, rest = split_high_low(table)
    extra = (high.astype(F32) + pltpu.roll(rest.astype(F32), LANES // 2, 1)).astype(BF)
    put = put_ref[...]
    width = a_ref.shape[1]
    out_ref[:, :width] = dot(put, low).astype(BF)
    out_ref[:, width:] = dot(put, extra).astype(BF)


def gated_forward(x, w_gate, w_lift):
    gate, lift = dot(x, w_gate), dot(x, w_lift)
    sigmoid = 0.5 * jnp.tanh(0.5 * gate) + 0.5
    act = gate * sigmoid
    slope = sigmoid + (act - act * sigmoid)
    return (act * lift).astype(BF), act, lift * slope


def add_up(total_ref, value):
    first = pl.program_id(0) == 0
    total_ref[...] = value + jnp.where(first, 0.0, total_ref[...])


def flush(step, steps, copies):
    @pl.when(step >= 2)
    def _():
        for copy in copies(step % 2, step):
            copy.wait()


def send(step, steps, copies):
    for copy in copies(step % 2, step):
        copy.start()

    @pl.when(step == steps - 1)
    def _():
        for copy in copies((step + 1) % 2, step):
            copy.wait()
        for copy in copies(step % 2, step):
            copy.wait()


def shared_kernel(
    x_ref, dy_ref, w_ref, out_ref, pieces_ref, gin_sum, gdown_sum
):
    count, rows, model = x_ref.shape
    block, columns = model // w_ref.shape[0], model // TILE
    piece = (w_ref.shape[1] - 2 * block) // columns
    x, dy = x_ref[...].reshape(count * rows, model), dy_ref[...].reshape(count * rows, model)
    w_gate = w_ref[:, :block, :].reshape(model, TILE)
    w_lift = w_ref[:, block : 2 * block, :].reshape(model, TILE)
    w_down = jnp.concatenate(
        [
            w_ref[:, start : start + piece, :].reshape(-1, TILE)
            for start in range(2 * block, w_ref.shape[1], piece)
        ],
        axis=1,
    )
    hidden, act, slope = gated_forward(x, w_gate, w_lift)
    out_ref[:, :, :model] = dot(hidden, w_down).astype(BF).reshape(count, rows, model)
    dhidden = dot_nt(dy, w_down)
    both = jnp.concatenate([dhidden * slope, dhidden * act], axis=1).astype(BF)
    dx = dot_nt(both, jnp.concatenate([w_gate, w_lift], axis=1))
    out_ref[:, :, model:] = dx.astype(BF).reshape(count, rows, model)
    add_up(gin_sum, dot_tn(x, both))
    add_up(gdown_sum, dot_tn(hidden, dy))

    @pl.when(pl.program_id(0) == pl.num_programs(0) - 1)
    def _():
        for owner in range(pieces_ref.shape[0]):
            rows_in = pl.ds(owner * block, block)
            for part in range(2):
                pieces_ref[owner, part * block : (part + 1) * block, :] = gin_sum[
                    rows_in, part * TILE : (part + 1) * TILE
                ].astype(BF)
            rows_down = pl.ds(owner * piece, piece)
            for column in range(columns):
                start = 2 * block + column * piece
                pieces_ref[owner, start : start + piece, :] = gdown_sum[
                    rows_down, column * TILE : (column + 1) * TILE
                ].astype(BF)


def side_by_side(blocks):
    count = blocks.shape[1] // IN_ROWS
    return jnp.concatenate(
        [
            blocks[:, part * IN_ROWS : (part + 1) * IN_ROWS].reshape(-1, TILE)
            for part in range(count)
        ],
        axis=1,
    )


def unpack_down(packed, model):
    return jnp.concatenate(
        [
            jnp.concatenate(
                [packed[tile, start : start + TILE] for start in range(0, model, TILE)], axis=1
            )
            for tile in range(packed.shape[0])
        ],
        axis=0,
    )


def expert_kernel(
    in_ref, wg_ref, wl_ref, wd_ref, y_ref, hidden_ref, act_ref, slope_ref, y_sum
):
    model = y_ref.shape[1]
    w_gate, w_lift = side_by_side(wg_ref[...]), side_by_side(wl_ref[...])
    hidden, act, slope = gated_forward(in_ref[:, :model], w_gate, w_lift)
    hidden_ref[0] = hidden
    act_ref[0] = act.astype(BF)
    slope_ref[0] = slope.astype(BF)
    add_up(y_sum, dot(hidden, unpack_down(wd_ref[...], model)))

    @pl.when(pl.program_id(0) == pl.num_programs(0) - 1)
    def _():
        y_ref[...] = y_sum[...].astype(BF)


def expert_back_kernel(
    in_ref, g_ref, own_ref, wg_ref, wl_ref, wd_ref, hidden_ref, act_ref, slope_ref,
    dx_ref, grads_ref,
    xt, dy, dx_sum, gin, gdown, sems,
):
    model = g_ref.shape[1]
    step, steps = pl.program_id(0), pl.num_programs(0)
    in_rows, tiles = gin.shape[3], gdown.shape[1]

    def copies(slot, now):
        for part in range(2):
            first = pl.multiple_of((part * steps + now) * in_rows, in_rows)
            yield pltpu.make_async_copy(
                gin.at[slot, part], grads_ref.at[:, pl.ds(first, in_rows)], sems.at[slot, part]
            )
        yield pltpu.make_async_copy(
            gdown.at[slot],
            grads_ref.at[pl.ds(now * tiles, tiles), pl.ds(2 * steps * in_rows, model)],
            sems.at[slot, 2],
        )

    @pl.when(step == 0)
    def _():
        xt[...] = in_ref[:, :model].astype(F32).T.astype(BF)
        gate = jnp.sum(in_ref[:, model:].astype(F32) * own_ref[...], axis=-1, keepdims=True)
        dy[...] = (g_ref[...].astype(F32) * gate).astype(BF)

    flush(step, steps, copies)
    slot = step % 2
    w_gate, w_lift = side_by_side(wg_ref[...]), side_by_side(wl_ref[...])
    dhidden = dot_nt(dy[...], unpack_down(wd_ref[...], model)).astype(BF)
    both = jnp.concatenate([dhidden * slope_ref[0], dhidden * act_ref[0]], axis=1)
    add_up(dx_sum, dot_nt(both, jnp.concatenate([w_gate, w_lift], axis=1)))
    into = dot(xt[...], both).astype(BF)
    shape = (gin.shape[2], IN_ROWS, TILE)
    for part in range(2):
        for tile in range(tiles):
            column = (part * tiles + tile) * TILE
            gin[slot, part, :, tile * IN_ROWS : (tile + 1) * IN_ROWS, :] = into[
                :, column : column + TILE
            ].reshape(shape)
    down = dot_tn(hidden_ref[0], dy[...]).astype(BF)
    for tile in range(tiles):
        for column in range(model // TILE):
            part = slice(column * TILE, (column + 1) * TILE)
            gdown[slot, tile, part, :] = down[tile * TILE : (tile + 1) * TILE, part]
    send(step, steps, copies)

    @pl.when(step == steps - 1)
    def _():
        dx_ref[...] = dx_sum[...].astype(BF)


def combine_kernel(
    y_ref, first_ref, second_ref, pick_ref, gate_ref, h_ref, shared_ref, g_ref, out_ref, dgate_ref
):
    table = gate_ref[...]
    y_first, y_second = dot(first_ref[...], y_ref[...]), dot(second_ref[...], y_ref[...])
    gate_first = jnp.sum(table * pick_ref[0], axis=-1, keepdims=True)
    gate_second = jnp.sum(table * pick_ref[1], axis=-1, keepdims=True)
    mixture = gate_first * y_first + gate_second * y_second
    out_ref[0] = (h_ref[...] + mixture + shared_ref[...].astype(F32)).astype(BF)
    g = g_ref[...].astype(F32)
    dgate_ref[...] = (
        jnp.sum(g * y_first, axis=-1, keepdims=True) * pick_ref[0]
        + jnp.sum(g * y_second, axis=-1, keepdims=True) * pick_ref[1]
    )


def middle_back_kernel(
    back_ref, dgate_ref, take_ref, gate_ref, small_ref, dshared_ref, g_ref, h_ref, scale_ref, gain_ref, w_ref,
    dh_ref, dhb_ref, do_ref, dlogits_ref, ggain_ref,
):
    take = take_ref[...]
    dgates = dgate_ref[...]
    table = gate_ref[...]
    gated = jnp.sum(table * dgates, axis=-1, keepdims=True)
    dlogits = (table * (dgates - gated)).astype(BF)
    dlogits_ref[...] = dlogits
    da = dshared_ref[...].astype(F32) + dot_nt(dlogits, small_ref[...]) + dot(take, back_ref[...])
    hidden, scale = h_ref[...], scale_ref[...]
    ggain_ref[...] = jnp.sum(da * hidden * scale, axis=0, keepdims=True)
    weighted = da * gain_ref[...]
    mean = jnp.mean(weighted * hidden, axis=-1, keepdims=True)
    dhidden = g_ref[...].astype(F32) + scale * weighted - hidden * (scale * scale * scale) * mean
    dh_ref[...] = dhidden
    low = dhidden.astype(BF)
    dhb_ref[...] = low
    width = w_ref.shape[2]
    do = dot_nt(low[:, :width], w_ref[0]) + dot_nt(low[:, width:], w_ref[1])
    do_ref[...] = do.astype(BF)


def project_back_kernel(dq_ref, dk_ref, dv_ref, w_ref, halo_ref, own_ref, w_back):
    width, model = w_ref.shape[2], w_ref.shape[1]
    parts = model // width
    rows = dq_ref.shape[0]

    @pl.when(pl.program_id(0) == 0)
    def _():
        for part in range(3 * parts):
            w_back[:, part * width : (part + 1) * width] = w_ref[part]

    da = dot_nt(
        jnp.concatenate([dk_ref[...], dv_ref[...]], axis=1), w_back[:, model:]
    )
    halo_ref[...] = da.astype(BF)

    @pl.when(pl.program_id(0) == pl.num_programs(0) - 1)
    def _():
        own_ref[...] = da[da.shape[0] - rows :] + dot_nt(dq_ref[...], w_back[:, :model])


def pack_kernel(early_ref, late_ref, shared_ref, out_ref, *, block):
    late = late_ref[0].astype(F32)
    for source in range(1, late_ref.shape[0]):
        late = late + late_ref[source].astype(F32)
    early, own = early_ref[...], out_ref.shape[1]
    for owner in range(out_ref.shape[0]):
        part = slice(owner * own, (owner + 1) * own)
        first = early.shape[1]
        out_ref[owner, :, :first] = early[part].astype(BF)
        out_ref[owner, :, first : first + late.shape[1]] = late[part].astype(BF)
        first = first + late.shape[1]
        for half in range(2):
            out_ref[owner, :, first + half * TILE : first + (half + 1) * TILE] = shared_ref[
                half * block + owner * own : half * block + (owner + 1) * own, :
            ].astype(BF)


def unpack_kernel(
    in_ref, w_ref, gain_ref, qkv_ref, out_ref, small_ref, dgain_ref, second_ref, shared_ref, *, piece
):
    sources, own = in_ref.shape[0], in_ref.shape[1]
    model = out_ref.shape[1]

    def take(start, some):
        total = in_ref[some[0], :, start : start + LANES].astype(F32)
        for source in some[1:]:
            total = total + in_ref[source, :, start : start + LANES].astype(F32)
        return total

    dgain = jnp.zeros((own, LANES), F32)
    first_core, second_core = range(0, sources, 2), range(1, sources, 2)
    early = 2 * model - 2 * LANES * (sources // 4)
    for pair in range(model // LANES):
        start = pair * 2 * LANES
        if start < early:
            k, v = take(start, first_core), take(start + LANES, first_core)
            q, o = take(start, second_core), take(start + LANES, second_core)
        else:
            source = (start - early) // LANES * 2
            k, q = take(early, (source,)), take(early, (source + 1,))
            v, o = take(early, (source + 2,)), take(early, (source + 3,))
        for which, value in enumerate((q, k, v)):
            part = slice(which * model + pair * LANES, which * model + (pair + 1) * LANES)
            qkv_ref[:, part] = value
            dgain = dgain + value * w_ref[:, part].astype(F32)
        out_ref[:, pair * LANES : (pair + 1) * LANES] = o
    dgain = jnp.sum(dgain, axis=-1, keepdims=True) / gain_ref[...]
    lane = lax.broadcasted_iota(jnp.int32, (own, LANES), 1)
    row = lax.broadcasted_iota(jnp.int32, (own, LANES), 0)

    def as_row(column):
        return jnp.sum(jnp.where(lane == row, column, 0.0), axis=0, keepdims=True)[:, :own]

    dgain_ref[...] = as_row(dgain)
    small = take(early + LANES, range(sources))
    experts = small_ref.shape[1]
    small_ref[...] = small[:, :experts]
    second = jnp.sum(jnp.where(lane == experts, small, 0.0), axis=-1, keepdims=True)
    second_ref[...] = as_row(second)
    per = LANES // piece
    for column in range(shared_ref.shape[1] // LANES):
        start = early + 2 * LANES + column // per * LANES
        total = jnp.zeros((own, LANES), F32)
        for source in range(sources):
            turn = (source - column % per) * piece % LANES
            value = take(start, (source,))
            value = pltpu.roll(value, turn, 1) if turn else value
            total = jnp.where(lane // piece == source, value, total)
        shared_ref[:, column * LANES : (column + 1) * LANES] = total


def per_device(
    tokens,
    segments,
    routes,
    w_qkv,
    w_out,
    w_router,
    shared_in,
    shared_down,
    attn_gain,
    ffn_gain,
    expert_in,
    expert_down,
    cotangent,
):
    ctx, fsdp = lax.axis_size("ctx"), lax.axis_size("fsdp")
    ctx_index, core = lax.axis_index("ctx"), lax.axis_index("fsdp") % 2
    rows, model = tokens.shape[1], tokens.shape[2]
    reach = max(1, WIN // rows)
    span = (reach + 1) * rows
    capacity = max(2, 3 * rows * TOPK // (2 * ctx))
    slots = ctx * capacity
    own = w_qkv.shape[0]
    owned_down = shared_down.shape[0]
    experts = w_router.shape[1]
    ff = shared_in.shape[1] // 2
    tiles = ff // TILE

    x, g = tokens[0], cotangent[0]
    segment_row = jnp.zeros((16, model), BF).at[0, :rows].set(segments[0].astype(BF))
    carried = jnp.concatenate([x, segment_row], axis=0)
    place_z = ctx_index % ROW
    lines = range(0, ctx, ROW)
    previous = shifted(carried, "ctx", ROW)
    arrived = [previous]
    for distance in range(reach - 1, 0, -1):
        arrived.append(
            lax.ppermute(
                jnp.where(place_z + distance < ROW, carried, previous),
                "ctx",
                [(line + z, line + (z + distance) % ROW) for line in lines for z in range(ROW)],
            )
        )

    cosine, sine = rotary_tables(span, (ctx_index - reach) * rows)
    route_own = routes[0]
    expert_ids = jnp.arange(experts, dtype=jnp.int32)
    hits = route_own[:, :, None] == expert_ids[None, None, :]
    member = jnp.sum(hits.astype(jnp.int32), axis=1)
    ranking = jnp.cumsum(member, axis=0, dtype=jnp.int32) - 1
    slot_ids = jnp.arange(capacity, dtype=jnp.int32)
    placed = (member[:, :, None] > 0) & (ranking[:, :, None] == slot_ids[None, None, :])
    take = placed.astype(BF).reshape(rows, slots)
    put = take.T
    selector = (
        (hits[:, :, :, None] & placed[:, None, :, :]).astype(BF).reshape(rows, TOPK * slots)
    )
    picked = jnp.pad(
        hits.astype(F32).transpose(1, 0, 2), ((0, 0), (0, 0), (0, LANES - experts))
    )
    lane = jnp.arange(LANES, dtype=jnp.int32)[None, :]
    own_lanes = ((lane == ctx_index) | (lane == ctx_index + LANES // 2)).astype(F32)
    g_to_slots = dot(put, g).astype(BF)

    small = jnp.concatenate(
        [w_router, attn_gain[:, None], ffn_gain[:, None], jnp.zeros((own, LANES - experts - 2), BF)],
        axis=1,
    )
    projections = jnp.concatenate([w_qkv, w_out], axis=1)
    width = projections.shape[1] // fsdp
    near = lax.all_to_all(
        jnp.concatenate(
            [
                projections.reshape(own, fsdp, width).transpose(1, 0, 2),
                jnp.broadcast_to(small, (fsdp, own, LANES)),
                shared_in.reshape(own, 2, ctx, fsdp, owned_down)
                .transpose(3, 0, 1, 2, 4)
                .reshape(fsdp, own, 2 * TILE),
            ],
            axis=2,
        ),
        "fsdp",
        split_axis=0,
        concat_axis=0,
        tiled=True,
    ).reshape(fsdp * own, -1)

    def to_ctx(values):
        return lax.all_to_all(
            jnp.broadcast_to(values, (ctx, *values.shape)), "ctx", split_axis=0, concat_axis=0, tiled=True
        )

    g_all = lax.all_gather(g, "fsdp", axis=0)
    columns = model // TILE
    dense = to_ctx(after(near[:, :width], previous)).reshape(model, width)
    w_full = lax.all_gather(after(dense, g_all, cosine, sine, g_to_slots, picked), "fsdp", axis=0)
    small_full = to_ctx(after(near[:, width : width + LANES], dense)).reshape(model, LANES)
    down_own = shared_down.reshape(owned_down, columns, TILE).transpose(1, 0, 2).reshape(-1, TILE)
    shared_own_w = jnp.concatenate(
        [near[:, width + LANES : -TILE], near[:, -TILE:], down_own], axis=0
    )
    place = ctx_index.astype(jnp.int32).reshape(1)
    place_spec = pl.BlockSpec(memory_space=pltpu.SMEM)
    in_rows, down_rows = expert_in.shape[1], expert_down.shape[1]
    expert_packed = jnp.concatenate(
        [
            expert_in[0].reshape(in_rows, 2 * tiles, TILE).transpose(1, 0, 2).reshape(-1, TILE),
            expert_down[0].reshape(down_rows, model // TILE, TILE).transpose(1, 0, 2).reshape(-1, TILE),
        ],
        axis=0,
    )
    expert_full = lax.all_gather(after(expert_packed, w_full, small_full, *arrived), "fsdp", axis=0)

    def exchange(values):
        return lax.all_to_all(
            values.reshape(ctx, values.shape[0] // ctx, values.shape[1]),
            "ctx",
            split_axis=0,
            concat_axis=0,
            tiled=True,
        ).reshape(values.shape)


    slot_g = exchange(after(g_to_slots, *arrived))

    pairs = model // LANES
    small_spec = whole(small_full)
    per, parts = width // LANES, model // width

    def columns_of(which):
        return pl.BlockSpec((1, model, LANES), lambda j: (which * parts + j // per, 0, j % per))

    blocks = [*arrived, carried]
    pair_spec = lambda height: pl.BlockSpec((height, LANES), lambda j: (0, j))
    q, k, kt, v, e, rl, rlb, attended, span_scale = pl.pallas_call(
        functools.partial(attend_kernel, gain_lane=experts, parts=reach + 1),
        grid=(pairs,),
        in_specs=[
            place_spec,
            *[whole(block) for block in blocks],
            small_spec,
            columns_of(0),
            columns_of(1),
            columns_of(2),
            whole(cosine),
            whole(sine),
        ],
        out_specs=[
            pair_spec(rows),
            pair_spec(span),
            pl.BlockSpec((LANES, span), lambda j: (j, 0)),
            pair_spec(span),
            pl.BlockSpec((2, span, rows), lambda j: (j, 0, 0)),
            pl.BlockSpec((1, 8, rows), lambda j: (j, 0, 0)),
            pair_spec(rows),
            pair_spec(rows),
            pl.BlockSpec((span, 1), lambda j: (0, 0)),
        ],
        out_shape=[
            jax.ShapeDtypeStruct((rows, model), BF),
            jax.ShapeDtypeStruct((span, model), BF),
            jax.ShapeDtypeStruct((model, span), BF),
            jax.ShapeDtypeStruct((span, model), BF),
            jax.ShapeDtypeStruct((HEADS, span, rows), BF),
            jax.ShapeDtypeStruct((pairs, 8, rows), F32),
            jax.ShapeDtypeStruct((rows, model), F32),
            jax.ShapeDtypeStruct((rows, model), BF),
            jax.ShapeDtypeStruct((span, 1), F32),
        ],
        scratch_shapes=[
            pltpu.VMEM((span, model), BF),
            pltpu.VMEM((2, span, rows), F32),
            pltpu.VMEM((LANES, span), BF),
            pltpu.VMEM((span, rows), F32),
        ],
        compiler_params=params(VMEM_MB),
        cost_estimate=cost(20),
        name="attend",
    )(place, *blocks, small_full, w_full, w_full, w_full, cosine, sine)

    out_spec = pl.BlockSpec((parts, model, width), lambda *_: (3, 0, 0))
    hidden, scale_two, normed, normed_t, outgoing, gates, gain_two = pl.pallas_call(
        functools.partial(middle_kernel, gain_lane=experts + 1),
        grid=(1,),
        in_specs=[
            whole(attended),
            out_spec,
            small_spec,
            whole(x),
            whole(picked),
            whole(put),
        ],
        out_specs=[
            pl.BlockSpec((rows, model), lambda *_: (0, 0)),
            pl.BlockSpec((rows, 1), lambda *_: (0, 0)),
            pl.BlockSpec((rows, model), lambda *_: (0, 0)),
            pl.BlockSpec((model, rows), lambda *_: (0, 0)),
            pl.BlockSpec((slots, model + LANES), lambda *_: (0, 0)),
            pl.BlockSpec((rows, LANES), lambda *_: (0, 0)),
            pl.BlockSpec((1, model), lambda *_: (0, 0)),
        ],
        out_shape=[
            jax.ShapeDtypeStruct((rows, model), F32),
            jax.ShapeDtypeStruct((rows, 1), F32),
            jax.ShapeDtypeStruct((rows, model), BF),
            jax.ShapeDtypeStruct((model, rows), BF),
            jax.ShapeDtypeStruct((slots, model + LANES), BF),
            jax.ShapeDtypeStruct((rows, LANES), F32),
            jax.ShapeDtypeStruct((1, model), F32),
        ],
        compiler_params=params(VMEM_MB),
        cost_estimate=cost(5),
        name="middle",
    )(attended, w_full, small_full, x, picked, put)
    normed_all = lax.all_gather(normed, "fsdp", axis=0)
    incoming = exchange(after(outgoing, slot_g))
    shared_full = to_ctx(after(shared_own_w, incoming))
    gain_one = small_full[:, experts : experts + 1].astype(F32)
    span_x = jnp.concatenate([block[:rows] for block in blocks], axis=0)
    first_t = (span_x.T.astype(F32) * span_scale.reshape(1, span) * gain_one).astype(BF)
    incoming = after(incoming, first_t)

    packed_rows = 3 * model

    steps = tiles // AT_ONCE
    expert_specs = [
        pl.BlockSpec((fsdp, AT_ONCE * in_rows, TILE), lambda t: (0, t, 0)),
        pl.BlockSpec((fsdp, AT_ONCE * in_rows, TILE), lambda t: (0, steps + t, 0)),
        pl.BlockSpec((AT_ONCE, model, TILE), lambda t: (t, 2 * in_rows * tiles // model, 0)),
    ]
    unit_spec = pl.BlockSpec((1, slots, AT_ONCE * TILE), lambda t: (t, 0, 0))
    expert_y, *units = pl.pallas_call(
        expert_kernel,
        grid=(steps,),
        in_specs=[whole(incoming), *expert_specs],
        out_specs=[
            pl.BlockSpec((slots, model), lambda t: (0, 0)),
            unit_spec,
            unit_spec,
            unit_spec,
        ],
        out_shape=[jax.ShapeDtypeStruct((slots, model), BF)]
        + [jax.ShapeDtypeStruct((steps, slots, AT_ONCE * TILE), BF)] * 3,
        scratch_shapes=[pltpu.VMEM((slots, model), F32)],
        compiler_params=params(VMEM_MB),
        cost_estimate=cost(60),
        name="expert",
    )(incoming, expert_full, expert_full, expert_full)
    returned_y = exchange(after(expert_y, shared_full))

    at_once = 2
    block = model // ctx
    shared_part, shared_pieces = pl.pallas_call(
        shared_kernel,
        grid=(fsdp // at_once,),
        in_specs=[
            pl.BlockSpec((at_once, rows, model), lambda t: (t, 0, 0)),
            pl.BlockSpec((at_once, rows, model), lambda t: (t, 0, 0)),
            whole(shared_full),
        ],
        out_specs=[
            pl.BlockSpec((at_once, rows, 2 * model), lambda t: (t, 0, 0)),
            whole(shared_full),
        ],
        out_shape=[
            jax.ShapeDtypeStruct((fsdp, rows, 2 * model), BF),
            jax.ShapeDtypeStruct(shared_full.shape, BF),
        ],
        scratch_shapes=[pltpu.VMEM((model, 2 * TILE), F32), pltpu.VMEM((TILE, model), F32)],
        compiler_params=params(VMEM_MB),
        cost_estimate=cost(18),
        name="shared",
    )(after(normed_all, expert_y), g_all, shared_full)
    shared_both = lax.psum_scatter(after(shared_part, returned_y), "fsdp", scatter_dimension=0)
    shared_own = jnp.sum(
        lax.all_to_all(
            after(shared_pieces, returned_y), "ctx", split_axis=0, concat_axis=0, tiled=True
        ).astype(F32),
        axis=0,
    )
    back, gexpert = pl.pallas_call(
        expert_back_kernel,
        grid=(steps,),
        in_specs=[
            whole(incoming),
            whole(slot_g),
            whole(own_lanes),
            *expert_specs,
            unit_spec,
            unit_spec,
            unit_spec,
        ],
        out_specs=[
            pl.BlockSpec((slots, model), lambda t: (0, 0)),
            pl.BlockSpec(memory_space=pl.ANY),
        ],
        out_shape=[
            jax.ShapeDtypeStruct((slots, model), BF),
            jax.ShapeDtypeStruct((fsdp, packed_rows, TILE), BF),
        ],
        scratch_shapes=[
            pltpu.VMEM((model, slots), BF),
            pltpu.VMEM((slots, model), BF),
            pltpu.VMEM((slots, model), F32),
            pltpu.VMEM((2, 2, fsdp, AT_ONCE * in_rows, TILE), BF),
            pltpu.VMEM((2, AT_ONCE, model, TILE), BF),
            pltpu.SemaphoreType.DMA((2, 3)),
        ],
        compiler_params=params(VMEM_MB),
        cost_estimate=cost(22),
        name="expert_back",
    )(after(incoming, shared_part, returned_y), slot_g, own_lanes, expert_full, expert_full, expert_full, *units)
    returned = exchange(after(back, shared_own))
    expert_sum = lax.psum_scatter(after(gexpert, shared_own), "fsdp", scatter_dimension=0)

    mixed, dgates = pl.pallas_call(
        combine_kernel,
        grid=(1,),
        in_specs=[
            pl.BlockSpec((slots, model), lambda *_: (0, 0)),
            pl.BlockSpec((rows, slots), lambda *_: (0, 0)),
            pl.BlockSpec((rows, slots), lambda *_: (0, 1)),
            whole(picked),
            whole(gates),
            whole(hidden),
            pl.BlockSpec((rows, model), lambda *_: (0, 0)),
            whole(g),
        ],
        out_specs=[
            pl.BlockSpec((1, rows, model), lambda *_: (0, 0, 0)),
            pl.BlockSpec((rows, LANES), lambda *_: (0, 0)),
        ],
        out_shape=[
            jax.ShapeDtypeStruct((1, rows, model), BF),
            jax.ShapeDtypeStruct((rows, LANES), F32),
        ],
        compiler_params=params(VMEM_MB),
        cost_estimate=cost(3),
        name="combine",
    )(returned_y, selector, selector, picked, gates, hidden, shared_both, g)

    returned = after(returned, dgates)

    dhidden, dhidden_low, dattended, dlogits, ggain_two = pl.pallas_call(
        middle_back_kernel,
        grid=(1,),
        in_specs=[
            whole(returned),
            whole(dgates),
            whole(take),
            whole(gates),
            small_spec,
            pl.BlockSpec((rows, model), lambda *_: (0, 1)),
            whole(g),
            whole(hidden),
            whole(scale_two),
            whole(gain_two),
            out_spec,
        ],
        out_specs=[
            pl.BlockSpec((rows, model), lambda *_: (0, 0)),
            pl.BlockSpec((rows, model), lambda *_: (0, 0)),
            pl.BlockSpec((rows, model), lambda *_: (0, 0)),
            pl.BlockSpec((rows, LANES), lambda *_: (0, 0)),
            pl.BlockSpec((1, model), lambda *_: (0, 0)),
        ],
        out_shape=[
            jax.ShapeDtypeStruct((rows, model), F32),
            jax.ShapeDtypeStruct((rows, model), BF),
            jax.ShapeDtypeStruct((rows, model), BF),
            jax.ShapeDtypeStruct((rows, LANES), BF),
            jax.ShapeDtypeStruct((1, model), F32),
        ],
        compiler_params=params(VMEM_MB),
        cost_estimate=cost(6),
        name="middle_back",
    )(
        returned, dgates, take, gates, small_full, shared_both, g, hidden, scale_two, gain_two, w_full
    )

    grouter = dot(normed_t, dlogits)
    small_grads = jnp.concatenate(
        [grouter[:, :experts], ggain_two.T, jnp.zeros((model, LANES - experts - 1), F32)], axis=1
    ).astype(BF)
    attended_t = attended.T
    core_scalar = core.astype(jnp.int32).reshape(1)

    def attend_back(first, count, down, *filled):
        pair_from = lambda height: pl.BlockSpec((height, LANES), lambda j: (0, first + j))
        operands = (
            core_scalar, q, k, kt, v, e, rl, rlb, down, cosine, sine, first_t, attended_t, dhidden_low, *filled,
        )
        return pl.pallas_call(
            attend_back_kernel,
            grid=(count,),
            in_specs=[
                place_spec,
                pair_from(rows),
                pair_from(span),
                pl.BlockSpec((LANES, span), lambda j: (first + j, 0)),
                pair_from(span),
                pl.BlockSpec((2, span, rows), lambda j: (first + j, 0, 0)),
                pl.BlockSpec((1, 8, rows), lambda j: (first + j, 0, 0)),
                pair_from(rows),
                pair_from(rows),
                whole(cosine),
                whole(sine),
                whole(first_t),
                whole(attended_t),
                pair_from(rows),
            ]
            + [pl.BlockSpec(memory_space=pl.ANY)] * len(filled),
            out_specs=[
                pair_from(rows),
                pair_from(span),
                pair_from(span),
                pl.BlockSpec((2, model, 2 * LANES), lambda j: (0, 0, j)),
            ],
            out_shape=[
                jax.ShapeDtypeStruct((rows, model), BF),
                jax.ShapeDtypeStruct((span, model), BF),
                jax.ShapeDtypeStruct((span, model), BF),
                jax.ShapeDtypeStruct((2, model, count * 2 * LANES), BF),
            ],
            input_output_aliases={
                len(operands) - len(filled) + index: index for index in range(len(filled))
            },
            scratch_shapes=[
                pltpu.VMEM((2, span, rows), F32),
                pltpu.VMEM((2, span, rows), BF),
                pltpu.VMEM((span, LANES), F32),
                pltpu.VMEM((span, LANES), F32),
            ],
            compiler_params=params(VMEM_MB),
            cost_estimate=cost(4 * count),
            name=f"attend_back_{first}",
        )(*operands)


    def paired_columns(grads):
        partner = lax.ppermute(grads[1], "fsdp", [(i, i ^ 1) for i in range(fsdp)])
        return (grads[0].astype(F32) + partner.astype(F32)).astype(BF)

    def along_ctx(pieces):
        return lax.all_to_all(pieces, "ctx", split_axis=0, concat_axis=0, tiled=True)

    early_pairs = 2 * pairs // 3
    *grads_a, group_a = attend_back(0, early_pairs, dattended)
    paired_a = paired_columns(group_a)
    late_a = along_ctx(paired_a.reshape(ctx, block, -1))
    dq, dk, dv, group_b = attend_back(
        early_pairs, pairs - early_pairs, after(dattended, paired_a), *grads_a
    )
    paired_b = paired_columns(group_b)

    dspan, down = pl.pallas_call(
        project_back_kernel,
        grid=(2,),
        in_specs=[
            whole(dq),
            pl.BlockSpec((span // 2, model), lambda b: (b, 0)),
            pl.BlockSpec((span // 2, model), lambda b: (b, 0)),
            pl.BlockSpec((3 * parts, model, width), lambda b: (0, 0, 0)),
        ],
        out_specs=[
            pl.BlockSpec((span // 2, model), lambda b: (b, 0)),
            pl.BlockSpec((rows, model), lambda b: (0, 0)),
        ],
        out_shape=[
            jax.ShapeDtypeStruct((span, model), BF),
            jax.ShapeDtypeStruct((rows, model), F32),
        ],
        compiler_params=params(VMEM_MB),
        scratch_shapes=[pltpu.VMEM((model, 3 * model), BF)],
        cost_estimate=cost(8),
        name="project_back",
    )(dq, dk, dv, w_full)
    total, passed = down, dspan[:rows].astype(F32)
    for distance in range(1, reach):
        lower = (reach - distance) * rows
        moved = lax.ppermute(
            dspan[lower : lower + rows],
            "ctx",
            [(line + z, line + (z - distance) % ROW) for line in lines for z in range(ROW)],
        )
        moved = moved.astype(F32)
        here = place_z + distance < ROW
        total = total + jnp.where(here, moved, 0.0)
        passed = passed + jnp.where(here, 0.0, moved)
    expert_rows = 2 * tiles * in_rows
    grad_expert_in = (
        expert_sum[:expert_rows]
        .astype(F32)
        .reshape(2 * tiles, in_rows, TILE)
        .transpose(1, 0, 2)
        .reshape(1, in_rows, 2 * ff)
    )
    grad_expert_down = (
        expert_sum[expert_rows:]
        .astype(F32)
        .reshape(columns, down_rows, TILE)
        .transpose(1, 0, 2)
        .reshape(1, down_rows, model)
    )
    late_a = jnp.sum(late_a.astype(F32), axis=0)
    quarter = paired_b.shape[1] // (fsdp // 2)
    late_b = lax.all_to_all(
        after(paired_b.reshape(model, fsdp // 2, quarter).transpose(1, 0, 2), down, late_a),
        "fsdp",
        split_axis=0,
        concat_axis=0,
        axis_index_groups=[list(range(start, fsdp, 2)) for start in range(2)],
        tiled=True,
    )
    late_b = jnp.sum(late_b.astype(F32), axis=0).astype(BF)
    received = shifted(after(passed.astype(BF), late_b), "ctx", -ROW)
    late_b = along_ctx(jnp.concatenate([late_b, small_grads], axis=1).reshape(ctx, block, -1))

    grad_shared_down = (
        shared_own[2 * block :]
        .reshape(columns, owned_down, TILE)
        .transpose(1, 0, 2)
        .reshape(owned_down, model)
    )
    packed_width = late_a.shape[1] + late_b.shape[2] + 2 * TILE
    last = pl.pallas_call(
        functools.partial(pack_kernel, block=block),
        grid=(1,),
        in_specs=[
            whole(late_a),
            whole(late_b),
            pl.BlockSpec((2 * block, TILE), lambda *_: (0, 0)),
        ],
        out_specs=pl.BlockSpec((fsdp, own, packed_width), lambda *_: (0, 0, 0)),
        out_shape=jax.ShapeDtypeStruct((fsdp, own, packed_width), BF),
        compiler_params=params(VMEM_MB),
        cost_estimate=cost(2),
        name="pack",
    )(late_a, late_b, shared_own)
    last = lax.all_to_all(last, "fsdp", split_axis=0, concat_axis=0, tiled=True)
    last = after(last, received, grad_expert_in, grad_expert_down)
    wanted = [
        jax.ShapeDtypeStruct((own, 3 * model), F32),
        jax.ShapeDtypeStruct((own, model), F32),
        jax.ShapeDtypeStruct((own, experts), F32),
        jax.ShapeDtypeStruct((1, own), F32),
        jax.ShapeDtypeStruct((1, own), F32),
        jax.ShapeDtypeStruct((own, 2 * ff), F32),
    ]
    gain_own = attn_gain.astype(F32)[:, None]
    grad_qkv, grad_out, grad_router, grad_gain_one, grad_gain_two, grad_shared_in = pl.pallas_call(
        functools.partial(unpack_kernel, piece=owned_down),
        grid=(1,),
        in_specs=[whole(last), whole(w_qkv), whole(gain_own)],
        out_specs=[whole(array) for array in wanted],
        out_shape=wanted,
        compiler_params=params(VMEM_MB),
        cost_estimate=cost(2),
        name="unpack",
    )(last, w_qkv, gain_own)

    total = total + received.astype(F32)
    input_rows = x.astype(F32)
    scale_one = span_scale[reach * rows :]
    weighted = total * gain_one.reshape(1, model)
    input_grad = (
        dhidden
        + scale_one * weighted
        - input_rows
        * scale_one**3
        * jnp.mean(weighted * input_rows, axis=-1, keepdims=True)
    )[None]

    return (
        mixed,
        input_grad,
        grad_qkv,
        grad_out,
        grad_router,
        grad_shared_in,
        grad_shared_down,
        grad_gain_one.reshape(own),
        grad_gain_two.reshape(own),
        grad_expert_in,
        grad_expert_down,
    )


def solution(mesh):
    placed = (
        P("fsdp", "ctx", None),
        P("fsdp", "ctx"),
        P("fsdp", "ctx", None),
        P(("ctx", "fsdp"), None),
        P(("ctx", "fsdp"), None),
        P(("ctx", "fsdp"), None),
        P(("ctx", "fsdp"), None),
        P(("ctx", "fsdp"), None),
        P(("ctx", "fsdp")),
        P(("ctx", "fsdp")),
        P("ctx", "fsdp", None),
        P("ctx", "fsdp", None),
        P("fsdp", "ctx", None),
    )
    return jax.shard_map(
        per_device,
        mesh=mesh,
        in_specs=placed,
        out_specs=(
            P("fsdp", "ctx", None),
            P("fsdp", "ctx", None),
            P(("ctx", "fsdp"), None),
            P(("ctx", "fsdp"), None),
            P(("ctx", "fsdp"), None),
            P(("ctx", "fsdp"), None),
            P(("ctx", "fsdp"), None),
            P(("ctx", "fsdp")),
            P(("ctx", "fsdp")),
            P("ctx", "fsdp", None),
            P("ctx", "fsdp", None),
        ),
        check_vma=False,
    )
```

```python
import functools

import jax
import jax.numpy as jnp
from jax import lax
from jax.experimental import pallas as pl
from jax.experimental.pallas import tpu as pltpu
from jax.sharding import PartitionSpec as P

HEADS = 12
HEAD_DIM = 64
TOPK = 2
WIN = 1024
EPSILON = 1e-06

BF = jnp.bfloat16
F32 = jnp.float32
TILE = 256
LANES = 128
IN_ROWS = 96
AT_ONCE = 2
KEY_BLOCK = 128
ROW = 4
VMEM_MB = 60


def dot(a, b):
    return jnp.dot(a, b, preferred_element_type=F32)


def dot_nt(a, b):
    return lax.dot_general(a, b, (((1,), (1,)), ((), ())), preferred_element_type=F32)


def dot_tn(a, b):
    return lax.dot_general(a, b, (((0,), (0,)), ((), ())), preferred_element_type=F32)


def params(megabytes):
    return pltpu.CompilerParams(vmem_limit_bytes=megabytes * 1024 * 1024)


def cost(microseconds):
    return pl.CostEstimate(
        flops=int(microseconds * 1.0e9), bytes_accessed=int(microseconds * 1.0e6), transcendentals=0
    )


def after(value, *others):
    return lax.optimization_barrier((value, *others))[0]


def whole(array):
    return pl.BlockSpec(array.shape, lambda *_: (0,) * array.ndim)


def shifted(value, axis, steps):
    count = lax.axis_size(axis)
    leading, last = (max(0, -steps), min(count, count - steps))
    return lax.ppermute(value, axis, [(source, source + steps) for source in range(leading, last)])


def split_high_low(values):
    high = values.astype(BF)
    return high, (values - high.astype(F32)).astype(BF)


def rotary_tables(rows, offset):
    half = HEAD_DIM // 2
    frequency = jnp.exp(-jnp.log(10000.0) * (2.0 * jnp.arange(half, dtype=F32) / HEAD_DIM))
    places = (offset + jnp.arange(rows, dtype=jnp.int32)).astype(F32)
    angles = places[:, None] * frequency[None, :]
    cosine, sine = jnp.cos(angles), jnp.sin(angles)
    return (
        jnp.concatenate([cosine] * 4, axis=1),
        jnp.concatenate([-sine, sine, -sine, sine], axis=1),
    )


def swapped_halves(values):
    width, half = values.shape[1], HEAD_DIM // 2
    lane = lax.broadcasted_iota(jnp.int32, (1, width), 1)
    return jnp.where(
        lane % HEAD_DIM < half,
        pltpu.roll(values, width - half, 1),
        pltpu.roll(values, half, 1),
    )


def head_lanes(values, head):
    lane = lax.broadcasted_iota(jnp.int32, (1, LANES), 1)
    return jnp.where(lane // HEAD_DIM == head, values, jnp.zeros_like(values))


def fold_rows(values, op):
    return op(values.reshape(values.shape[0] // 8, 8, values.shape[1]), axis=0)


def attend_kernel(
    place_ref, *refs, gain_lane, parts
):
    blocks, refs = refs[:parts], refs[parts:]
    (
        small_ref, wq_ref, wk_ref, wv_ref, cos_ref, sin_ref,
        q_ref, k_ref, kt_ref, v_ref, e_ref, rl_ref, rlb_ref, o_ref, scale_ref,
        normed, score, vt, bias_ref,
    ) = refs
    rows, model = q_ref.shape[0], normed.shape[1]
    span = parts * rows

    @pl.when(pl.program_id(0) == 0)
    def _():
        gain = small_ref[...].astype(F32).T[gain_lane : gain_lane + 1, :]
        query_segment = blocks[-1][rows : rows + 1, :rows].astype(F32)
        query_place = lax.broadcasted_iota(jnp.int32, (rows, rows), 1)
        key_place = lax.broadcasted_iota(jnp.int32, (rows, rows), 0)
        for index, block in enumerate(blocks):
            part = pl.ds(index * rows, rows)
            values = block[:rows, :].astype(F32)
            scale = lax.rsqrt(jnp.mean(values * values, axis=-1, keepdims=True) + EPSILON)
            scale_ref[part, :] = scale
            normed[part, :] = (values * scale * gain).astype(BF)
            key_segment = block[rows : rows + 16, :rows].astype(F32).T[:, :1]
            distance = query_place - key_place + (parts - 1 - index) * rows
            allowed = (distance >= 0) & (distance < WIN) & (key_segment == query_segment)
            allowed = allowed & (place_ref[0] >= parts - 1 - index)
            bias_ref[part, :] = jnp.where(allowed, 0.0, -1e30)

    wide = q_ref.shape[1]
    cosine = jnp.concatenate([cos_ref[...]] * (wide // LANES), axis=1)
    sine = jnp.concatenate([sin_ref[...]] * (wide // LANES), axis=1)
    pair = dot(normed[...], jnp.concatenate([wk_ref[0], wv_ref[0]], axis=1))
    keys = pair[:, :wide]
    keys = keys * cosine + swapped_halves(keys) * sine
    k_ref[...] = keys.astype(BF)
    kt_ref[...] = keys.T.astype(BF)
    queries = dot(normed[span - rows :, :], wq_ref[0])
    queries = queries * cosine[span - rows :] + swapped_halves(queries) * sine[span - rows :]
    queries = (queries.astype(BF).astype(F32) * HEAD_DIM**-0.5).astype(BF)
    q_ref[...] = queries
    heads = wide // HEAD_DIM

    def chunk(head):
        return slice(head // 2 * LANES, (head // 2 + 1) * LANES)

    own = [head_lanes(queries[:, chunk(head)], head % 2) for head in range(heads)]
    largest = [jnp.full((8, rows), -3e38, F32) for _ in range(heads)]
    total = [jnp.zeros((8, rows), F32) for _ in range(heads)]

    def scores(head, part):
        block = dot_nt(k_ref[part, chunk(head)], own[head]) + bias_ref[part, :]
        score[head % 2, part, :] = block
        largest[head] = jnp.maximum(largest[head], fold_rows(block, jnp.max))

    def weights(head, part):
        block = jnp.exp(score[head % 2, part, :] - largest[head])
        total[head] = total[head] + fold_rows(block, jnp.sum)
        e_ref[head, part, :] = block.astype(BF)

    blocks_of_keys = [pl.ds(start, KEY_BLOCK) for start in range(0, span, KEY_BLOCK)]
    for part in blocks_of_keys:
        scores(0, part)
    values = pair[:, wide:]
    v_ref[...] = values.astype(BF)
    vt[...] = values.T.astype(BF)
    outs, sums = [], []
    for head in range(heads):
        largest[head] = jnp.max(largest[head], axis=0, keepdims=True)
        for part in blocks_of_keys:
            weights(head, part)
            if head + 1 < heads:
                scores(head + 1, part)
        inverse = 1.0 / jnp.sum(total[head], axis=0, keepdims=True)
        rl_ref[head // 2, head % 2 : head % 2 + 1, :] = inverse
        outs.append(dot(vt[head * HEAD_DIM : (head + 1) * HEAD_DIM, :], e_ref[head]) * inverse)
        sums.append(jnp.broadcast_to(inverse, (HEAD_DIM, rows)))
    o_ref[...] = jnp.concatenate(outs, axis=0).T.astype(BF)
    rlb_ref[...] = jnp.concatenate(sums, axis=0).T


def attend_back_kernel(
    core_ref, q_ref, k_ref, kt_ref, v_ref, e_ref, rl_ref, rlb_ref, do_ref, cos_ref, sin_ref, xt_ref, ot_ref, dh_ref,
    *refs,
):
    dq_ref, dk_ref, dv_ref, kept_ref, sent_ref, dprob, dscore, dk, dv = refs[-9:]
    span, rows = k_ref.shape[0], q_ref.shape[0]
    scaled = do_ref[...].astype(F32) * rlb_ref[...]
    heads = range(2)
    down = [head_lanes(scaled, head).astype(BF) for head in heads]
    own = [head_lanes(q_ref[...], head) for head in heads]
    own_both, down_both = jnp.concatenate(own, axis=0), jnp.concatenate(down, axis=0)
    inner = [jnp.zeros((8, rows), F32) for _ in heads]
    for start in range(0, span, KEY_BLOCK):
        part = pl.ds(start, KEY_BLOCK)
        for head in heads:
            block = dot_nt(v_ref[part, :], down[head])
            dprob[head, part, :] = block
            inner[head] = inner[head] + fold_rows(block * e_ref[head, part, :].astype(F32), jnp.sum)
    inner = [
        jnp.sum(inner[head], axis=0, keepdims=True) * rl_ref[0, head : head + 1, :]
        for head in heads
    ]
    for start in range(0, span, KEY_BLOCK):
        part = pl.ds(start, KEY_BLOCK)
        for head in heads:
            weight = e_ref[head, part, :]
            block = (weight.astype(F32) * (dprob[head, part, :] - inner[head])).astype(BF)
            dscore[head, part, :] = block
        dk[part, :] = dot(
            jnp.concatenate([dscore[head, part, :] for head in heads], axis=1), own_both
        )
        dv[part, :] = dot(
            jnp.concatenate([e_ref[head, part, :] for head in heads], axis=1), down_both
        )
    dqs = [
        dot(kt_ref[head * HEAD_DIM : (head + 1) * HEAD_DIM, :], dscore[head]) for head in heads
    ]
    dquery = jnp.concatenate(dqs, axis=0).T * HEAD_DIM**-0.5
    dquery = dquery * cos_ref[span - rows :, :] - swapped_halves(dquery) * sin_ref[span - rows :, :]
    dquery = dquery.astype(BF)
    dq_ref[...] = dquery
    dkeys = dk[...]
    dkeys = (dkeys * cos_ref[...] - swapped_halves(dkeys) * sin_ref[...]).astype(BF)
    dvalues = dv[...].astype(BF)
    dk_ref[...] = dkeys
    dv_ref[...] = dvalues
    first = dot(xt_ref[...], jnp.concatenate([dkeys, dvalues], axis=1)).astype(BF)
    second = jnp.concatenate(
        [dot(xt_ref[:, span - rows :], dquery), dot(ot_ref[...], dh_ref[...])], axis=1
    ).astype(BF)
    kept_ref[...] = jnp.where(core_ref[0] == 0, first, second)
    sent_ref[...] = jnp.where(core_ref[0] == 0, second, first)


def middle_kernel(
    o_ref, w_ref, small_ref, x_ref, pick_ref, put_ref,
    h_ref, scale_ref, a_ref, at_ref, out_ref, gate_ref, gain_ref,
    *, gain_lane,
):
    projected = jnp.concatenate([dot(o_ref[...], w_ref[part]) for part in range(2)], axis=1)
    hidden = x_ref[...].astype(F32) + projected
    h_ref[...] = hidden
    scale = lax.rsqrt(jnp.mean(hidden * hidden, axis=-1, keepdims=True) + EPSILON)
    scale_ref[...] = scale
    small = small_ref[...]
    gain = small.astype(F32).T[gain_lane : gain_lane + 1, :]
    gain_ref[...] = gain
    low = (hidden * scale * gain).astype(BF)
    a_ref[...] = low
    at_ref[...] = low.astype(F32).T.astype(BF)
    logits = dot(low, small)
    first, second = pick_ref[0], pick_ref[1]
    chosen_first = jnp.sum(logits * first, axis=-1, keepdims=True)
    chosen_second = jnp.sum(logits * second, axis=-1, keepdims=True)
    largest = jnp.maximum(chosen_first, chosen_second)
    chosen_first = jnp.exp(chosen_first - largest)
    chosen_second = jnp.exp(chosen_second - largest)
    total = chosen_first + chosen_second
    table = (chosen_first / total) * first + (chosen_second / total) * second
    gate_ref[...] = table
    high, rest = split_high_low(table)
    extra = (high.astype(F32) + pltpu.roll(rest.astype(F32), LANES // 2, 1)).astype(BF)
    put = put_ref[...]
    width = a_ref.shape[1]
    out_ref[:, :width] = dot(put, low).astype(BF)
    out_ref[:, width:] = dot(put, extra).astype(BF)


def gated_forward(x, w_gate, w_lift):
    gate, lift = dot(x, w_gate), dot(x, w_lift)
    sigmoid = 0.5 * jnp.tanh(0.5 * gate) + 0.5
    act = gate * sigmoid
    slope = sigmoid + (act - act * sigmoid)
    return (act * lift).astype(BF), act, lift * slope


def add_up(total_ref, value):
    first = pl.program_id(0) == 0
    total_ref[...] = value + jnp.where(first, 0.0, total_ref[...])


def flush(step, steps, copies):
    @pl.when(step >= 2)
    def _():
        for copy in copies(step % 2, step):
            copy.wait()


def send(step, steps, copies):
    for copy in copies(step % 2, step):
        copy.start()

    @pl.when(step == steps - 1)
    def _():
        for copy in copies((step + 1) % 2, step):
            copy.wait()
        for copy in copies(step % 2, step):
            copy.wait()


def shared_kernel(
    x_ref, dy_ref, w_ref, out_ref, pieces_ref, gin_sum, gdown_sum
):
    count, rows, model = x_ref.shape
    block, columns = model // w_ref.shape[0], model // TILE
    piece = (w_ref.shape[1] - 2 * block) // columns
    x, dy = x_ref[...].reshape(count * rows, model), dy_ref[...].reshape(count * rows, model)
    w_gate = w_ref[:, :block, :].reshape(model, TILE)
    w_lift = w_ref[:, block : 2 * block, :].reshape(model, TILE)
    w_down = jnp.concatenate(
        [
            w_ref[:, start : start + piece, :].reshape(-1, TILE)
            for start in range(2 * block, w_ref.shape[1], piece)
        ],
        axis=1,
    )
    hidden, act, slope = gated_forward(x, w_gate, w_lift)
    out_ref[:, :, :model] = dot(hidden, w_down).astype(BF).reshape(count, rows, model)
    dhidden = dot_nt(dy, w_down)
    both = jnp.concatenate([dhidden * slope, dhidden * act], axis=1).astype(BF)
    dx = dot_nt(both, jnp.concatenate([w_gate, w_lift], axis=1))
    out_ref[:, :, model:] = dx.astype(BF).reshape(count, rows, model)
    add_up(gin_sum, dot_tn(x, both))
    add_up(gdown_sum, dot_tn(hidden, dy))

    @pl.when(pl.program_id(0) == pl.num_programs(0) - 1)
    def _():
        for owner in range(pieces_ref.shape[0]):
            rows_in = pl.ds(owner * block, block)
            for part in range(2):
                pieces_ref[owner, part * block : (part + 1) * block, :] = gin_sum[
                    rows_in, part * TILE : (part + 1) * TILE
                ].astype(BF)
            rows_down = pl.ds(owner * piece, piece)
            for column in range(columns):
                start = 2 * block + column * piece
                pieces_ref[owner, start : start + piece, :] = gdown_sum[
                    rows_down, column * TILE : (column + 1) * TILE
                ].astype(BF)


def side_by_side(blocks):
    count = blocks.shape[1] // IN_ROWS
    return jnp.concatenate(
        [
            blocks[:, part * IN_ROWS : (part + 1) * IN_ROWS].reshape(-1, TILE)
            for part in range(count)
        ],
        axis=1,
    )


def unpack_down(packed, model):
    return jnp.concatenate(
        [
            jnp.concatenate(
                [packed[tile, start : start + TILE] for start in range(0, model, TILE)], axis=1
            )
            for tile in range(packed.shape[0])
        ],
        axis=0,
    )


def expert_kernel(
    in_ref, wg_ref, wl_ref, wd_ref, y_ref, hidden_ref, act_ref, slope_ref, y_sum
):
    model = y_ref.shape[1]
    w_gate, w_lift = side_by_side(wg_ref[...]), side_by_side(wl_ref[...])
    hidden, act, slope = gated_forward(in_ref[:, :model], w_gate, w_lift)
    hidden_ref[0] = hidden
    act_ref[0] = act.astype(BF)
    slope_ref[0] = slope.astype(BF)
    add_up(y_sum, dot(hidden, unpack_down(wd_ref[...], model)))

    @pl.when(pl.program_id(0) == pl.num_programs(0) - 1)
    def _():
        y_ref[...] = y_sum[...].astype(BF)


def expert_back_kernel(
    in_ref, g_ref, own_ref, wg_ref, wl_ref, wd_ref, hidden_ref, act_ref, slope_ref,
    dx_ref, grads_ref,
    xt, dy, dx_sum, gin, gdown, sems,
):
    model = g_ref.shape[1]
    step, steps = pl.program_id(0), pl.num_programs(0)
    in_rows, tiles = gin.shape[3], gdown.shape[1]

    def copies(slot, now):
        for part in range(2):
            first = pl.multiple_of((part * steps + now) * in_rows, in_rows)
            yield pltpu.make_async_copy(
                gin.at[slot, part], grads_ref.at[:, pl.ds(first, in_rows)], sems.at[slot, part]
            )
        yield pltpu.make_async_copy(
            gdown.at[slot],
            grads_ref.at[pl.ds(now * tiles, tiles), pl.ds(2 * steps * in_rows, model)],
            sems.at[slot, 2],
        )

    @pl.when(step == 0)
    def _():
        xt[...] = in_ref[:, :model].astype(F32).T.astype(BF)
        gate = jnp.sum(in_ref[:, model:].astype(F32) * own_ref[...], axis=-1, keepdims=True)
        dy[...] = (g_ref[...].astype(F32) * gate).astype(BF)

    flush(step, steps, copies)
    slot = step % 2
    w_gate, w_lift = side_by_side(wg_ref[...]), side_by_side(wl_ref[...])
    dhidden = dot_nt(dy[...], unpack_down(wd_ref[...], model)).astype(BF)
    both = jnp.concatenate([dhidden * slope_ref[0], dhidden * act_ref[0]], axis=1)
    add_up(dx_sum, dot_nt(both, jnp.concatenate([w_gate, w_lift], axis=1)))
    into = dot(xt[...], both).astype(BF)
    shape = (gin.shape[2], IN_ROWS, TILE)
    for part in range(2):
        for tile in range(tiles):
            column = (part * tiles + tile) * TILE
            gin[slot, part, :, tile * IN_ROWS : (tile + 1) * IN_ROWS, :] = into[
                :, column : column + TILE
            ].reshape(shape)
    down = dot_tn(hidden_ref[0], dy[...]).astype(BF)
    for tile in range(tiles):
        for column in range(model // TILE):
            part = slice(column * TILE, (column + 1) * TILE)
            gdown[slot, tile, part, :] = down[tile * TILE : (tile + 1) * TILE, part]
    send(step, steps, copies)

    @pl.when(step == steps - 1)
    def _():
        dx_ref[...] = dx_sum[...].astype(BF)


def combine_kernel(
    y_ref, first_ref, second_ref, pick_ref, gate_ref, h_ref, shared_ref, g_ref, out_ref, dgate_ref
):
    table = gate_ref[...]
    y_first, y_second = dot(first_ref[...], y_ref[...]), dot(second_ref[...], y_ref[...])
    gate_first = jnp.sum(table * pick_ref[0], axis=-1, keepdims=True)
    gate_second = jnp.sum(table * pick_ref[1], axis=-1, keepdims=True)
    mixture = gate_first * y_first + gate_second * y_second
    out_ref[0] = (h_ref[...] + mixture + shared_ref[...].astype(F32)).astype(BF)
    g = g_ref[...].astype(F32)
    dgate_ref[...] = (
        jnp.sum(g * y_first, axis=-1, keepdims=True) * pick_ref[0]
        + jnp.sum(g * y_second, axis=-1, keepdims=True) * pick_ref[1]
    )


def middle_back_kernel(
    back_ref, dgate_ref, take_ref, gate_ref, small_ref, dshared_ref, g_ref, h_ref, scale_ref, gain_ref, w_ref,
    dh_ref, dhb_ref, do_ref, dlogits_ref, ggain_ref,
):
    take = take_ref[...]
    dgates = dgate_ref[...]
    table = gate_ref[...]
    gated = jnp.sum(table * dgates, axis=-1, keepdims=True)
    dlogits = (table * (dgates - gated)).astype(BF)
    dlogits_ref[...] = dlogits
    da = dshared_ref[...].astype(F32) + dot_nt(dlogits, small_ref[...]) + dot(take, back_ref[...])
    hidden, scale = h_ref[...], scale_ref[...]
    ggain_ref[...] = jnp.sum(da * hidden * scale, axis=0, keepdims=True)
    weighted = da * gain_ref[...]
    mean = jnp.mean(weighted * hidden, axis=-1, keepdims=True)
    dhidden = g_ref[...].astype(F32) + scale * weighted - hidden * (scale * scale * scale) * mean
    dh_ref[...] = dhidden
    low = dhidden.astype(BF)
    dhb_ref[...] = low
    width = w_ref.shape[2]
    do = dot_nt(low[:, :width], w_ref[0]) + dot_nt(low[:, width:], w_ref[1])
    do_ref[...] = do.astype(BF)


def project_back_kernel(dq_ref, dk_ref, dv_ref, w_ref, halo_ref, own_ref, w_back):
    width, model = w_ref.shape[2], w_ref.shape[1]
    parts = model // width
    rows = dq_ref.shape[0]

    @pl.when(pl.program_id(0) == 0)
    def _():
        for part in range(3 * parts):
            w_back[:, part * width : (part + 1) * width] = w_ref[part]

    da = dot_nt(
        jnp.concatenate([dk_ref[...], dv_ref[...]], axis=1), w_back[:, model:]
    )
    halo_ref[...] = da.astype(BF)

    @pl.when(pl.program_id(0) == pl.num_programs(0) - 1)
    def _():
        own_ref[...] = da[da.shape[0] - rows :] + dot_nt(dq_ref[...], w_back[:, :model])


def widen_kernel(in_ref, in_out_ref, down_out_ref):
    in_rows, down_rows = in_out_ref.shape[1], down_out_ref.shape[1]
    columns = in_out_ref.shape[2] // TILE
    for column in range(columns):
        in_out_ref[0, :, column * TILE : (column + 1) * TILE] = in_ref[
            column * in_rows : (column + 1) * in_rows, :
        ].astype(F32)
    for column in range(down_out_ref.shape[2] // TILE):
        first = columns * in_rows + column * down_rows
        down_out_ref[0, :, column * TILE : (column + 1) * TILE] = in_ref[
            first : first + down_rows, :
        ].astype(F32)


def pack_kernel(early_ref, late_ref, shared_ref, out_ref, *, block):
    late = late_ref[0].astype(F32)
    for source in range(1, late_ref.shape[0]):
        late = late + late_ref[source].astype(F32)
    early, own = early_ref[...], out_ref.shape[1]
    for owner in range(out_ref.shape[0]):
        part = slice(owner * own, (owner + 1) * own)
        first = early.shape[1]
        out_ref[owner, :, :first] = early[part].astype(BF)
        out_ref[owner, :, first : first + late.shape[1]] = late[part].astype(BF)
        first = first + late.shape[1]
        for half in range(2):
            out_ref[owner, :, first + half * TILE : first + (half + 1) * TILE] = shared_ref[
                half * block + owner * own : half * block + (owner + 1) * own, :
            ].astype(BF)


def unpack_kernel(
    in_ref, w_ref, gain_ref, qkv_ref, out_ref, small_ref, dgain_ref, second_ref, shared_ref, *, piece
):
    sources, own = in_ref.shape[0], in_ref.shape[1]
    model = out_ref.shape[1]

    def take(start, some):
        total = in_ref[some[0], :, start : start + LANES].astype(F32)
        for source in some[1:]:
            total = total + in_ref[source, :, start : start + LANES].astype(F32)
        return total

    dgain = jnp.zeros((own, LANES), F32)
    first_core, second_core = range(0, sources, 2), range(1, sources, 2)
    early = 2 * model - 2 * LANES * (sources // 4)
    for pair in range(model // LANES):
        start = pair * 2 * LANES
        if start < early:
            k, v = take(start, first_core), take(start + LANES, first_core)
            q, o = take(start, second_core), take(start + LANES, second_core)
        else:
            source = (start - early) // LANES * 2
            k, q = take(early, (source,)), take(early, (source + 1,))
            v, o = take(early, (source + 2,)), take(early, (source + 3,))
        for which, value in enumerate((q, k, v)):
            part = slice(which * model + pair * LANES, which * model + (pair + 1) * LANES)
            qkv_ref[:, part] = value
            dgain = dgain + value * w_ref[:, part].astype(F32)
        out_ref[:, pair * LANES : (pair + 1) * LANES] = o
    dgain = jnp.sum(dgain, axis=-1, keepdims=True) / gain_ref[...]
    lane = lax.broadcasted_iota(jnp.int32, (own, LANES), 1)
    row = lax.broadcasted_iota(jnp.int32, (own, LANES), 0)

    def as_row(column):
        return jnp.sum(jnp.where(lane == row, column, 0.0), axis=0, keepdims=True)[:, :own]

    dgain_ref[...] = as_row(dgain)
    small = take(early + LANES, range(sources))
    experts = small_ref.shape[1]
    small_ref[...] = small[:, :experts]
    second = jnp.sum(jnp.where(lane == experts, small, 0.0), axis=-1, keepdims=True)
    second_ref[...] = as_row(second)
    per = LANES // piece
    for column in range(shared_ref.shape[1] // LANES):
        start = early + 2 * LANES + column // per * LANES
        total = jnp.zeros((own, LANES), F32)
        for source in range(sources):
            turn = (source - column % per) * piece % LANES
            value = take(start, (source,))
            value = pltpu.roll(value, turn, 1) if turn else value
            total = jnp.where(lane // piece == source, value, total)
        shared_ref[:, column * LANES : (column + 1) * LANES] = total


def per_device(
    tokens,
    segments,
    routes,
    w_qkv,
    w_out,
    w_router,
    shared_in,
    shared_down,
    attn_gain,
    ffn_gain,
    expert_in,
    expert_down,
    cotangent,
):
    ctx, fsdp = lax.axis_size("ctx"), lax.axis_size("fsdp")
    ctx_index, core = lax.axis_index("ctx"), lax.axis_index("fsdp") % 2
    rows, model = tokens.shape[1], tokens.shape[2]
    reach = max(1, WIN // rows)
    span = (reach + 1) * rows
    capacity = max(2, 3 * rows * TOPK // (2 * ctx))
    slots = ctx * capacity
    own = w_qkv.shape[0]
    owned_down = shared_down.shape[0]
    experts = w_router.shape[1]
    ff = shared_in.shape[1] // 2
    tiles = ff // TILE

    x, g = tokens[0], cotangent[0]
    segment_row = jnp.zeros((16, model), BF).at[0, :rows].set(segments[0].astype(BF))
    carried = jnp.concatenate([x, segment_row], axis=0)
    place_z = ctx_index % ROW
    lines = range(0, ctx, ROW)
    previous = shifted(carried, "ctx", ROW)
    arrived = [previous]
    for distance in range(reach - 1, 0, -1):
        arrived.append(
            lax.ppermute(
                jnp.where(place_z + distance < ROW, carried, previous),
                "ctx",
                [(line + z, line + (z + distance) % ROW) for line in lines for z in range(ROW)],
            )
        )

    cosine, sine = rotary_tables(span, (ctx_index - reach) * rows)
    route_own = routes[0]
    expert_ids = jnp.arange(experts, dtype=jnp.int32)
    hits = route_own[:, :, None] == expert_ids[None, None, :]
    member = jnp.sum(hits.astype(jnp.int32), axis=1)
    ranking = jnp.cumsum(member, axis=0, dtype=jnp.int32) - 1
    slot_ids = jnp.arange(capacity, dtype=jnp.int32)
    placed = (member[:, :, None] > 0) & (ranking[:, :, None] == slot_ids[None, None, :])
    take = placed.astype(BF).reshape(rows, slots)
    put = take.T
    selector = (
        (hits[:, :, :, None] & placed[:, None, :, :]).astype(BF).reshape(rows, TOPK * slots)
    )
    picked = jnp.pad(
        hits.astype(F32).transpose(1, 0, 2), ((0, 0), (0, 0), (0, LANES - experts))
    )
    lane = jnp.arange(LANES, dtype=jnp.int32)[None, :]
    own_lanes = ((lane == ctx_index) | (lane == ctx_index + LANES // 2)).astype(F32)
    g_to_slots = dot(put, g).astype(BF)

    small = jnp.concatenate(
        [w_router, attn_gain[:, None], ffn_gain[:, None], jnp.zeros((own, LANES - experts - 2), BF)],
        axis=1,
    )
    projections = jnp.concatenate([w_qkv, w_out], axis=1)
    width = projections.shape[1] // fsdp
    near = lax.all_to_all(
        jnp.concatenate(
            [
                projections.reshape(own, fsdp, width).transpose(1, 0, 2),
                jnp.broadcast_to(small, (fsdp, own, LANES)),
                shared_in.reshape(own, 2, ctx, fsdp, owned_down)
                .transpose(3, 0, 1, 2, 4)
                .reshape(fsdp, own, 2 * TILE),
            ],
            axis=2,
        ),
        "fsdp",
        split_axis=0,
        concat_axis=0,
        tiled=True,
    ).reshape(fsdp * own, -1)

    def to_ctx(values):
        return lax.all_to_all(
            jnp.broadcast_to(values, (ctx, *values.shape)), "ctx", split_axis=0, concat_axis=0, tiled=True
        )

    g_all = lax.all_gather(g, "fsdp", axis=0)
    columns = model // TILE
    dense = to_ctx(near[:, :width]).reshape(model, width)
    w_full = lax.all_gather(after(dense, g_all, cosine, sine, g_to_slots, picked, previous), "fsdp", axis=0)
    small_full = to_ctx(after(near[:, width : width + LANES], dense)).reshape(model, LANES)
    down_own = shared_down.reshape(owned_down, columns, TILE).transpose(1, 0, 2).reshape(-1, TILE)
    shared_own_w = jnp.concatenate(
        [near[:, width + LANES : -TILE], near[:, -TILE:], down_own], axis=0
    )
    place = ctx_index.astype(jnp.int32).reshape(1)
    place_spec = pl.BlockSpec(memory_space=pltpu.SMEM)
    in_rows, down_rows = expert_in.shape[1], expert_down.shape[1]
    expert_packed = jnp.concatenate(
        [
            expert_in[0].reshape(in_rows, 2 * tiles, TILE).transpose(1, 0, 2).reshape(-1, TILE),
            expert_down[0].reshape(down_rows, model // TILE, TILE).transpose(1, 0, 2).reshape(-1, TILE),
        ],
        axis=0,
    )
    expert_full = lax.all_gather(after(expert_packed, w_full, small_full, *arrived), "fsdp", axis=0)

    def exchange(values):
        return lax.all_to_all(
            values.reshape(ctx, values.shape[0] // ctx, values.shape[1]),
            "ctx",
            split_axis=0,
            concat_axis=0,
            tiled=True,
        ).reshape(values.shape)


    slot_g = exchange(after(g_to_slots, *arrived))

    pairs = model // LANES
    small_spec = whole(small_full)
    parts = model // width
    at_a_time = width // LANES

    def columns_of(which):
        return pl.BlockSpec((1, model, width), lambda j: (which * parts + j, 0, 0))

    def wide_spec(height):
        return pl.BlockSpec((height, width), lambda j: (0, j))

    blocks = [*arrived, carried]
    pair_spec = lambda height: pl.BlockSpec((height, LANES), lambda j: (0, j))
    q, k, kt, v, e, rl, rlb, attended, span_scale = pl.pallas_call(
        functools.partial(attend_kernel, gain_lane=experts, parts=reach + 1),
        grid=(parts,),
        in_specs=[
            place_spec,
            *[whole(block) for block in blocks],
            small_spec,
            columns_of(0),
            columns_of(1),
            columns_of(2),
            whole(cosine),
            whole(sine),
        ],
        out_specs=[
            wide_spec(rows),
            wide_spec(span),
            pl.BlockSpec((width, span), lambda j: (j, 0)),
            wide_spec(span),
            pl.BlockSpec((2 * at_a_time, span, rows), lambda j: (j, 0, 0)),
            pl.BlockSpec((at_a_time, 8, rows), lambda j: (j, 0, 0)),
            wide_spec(rows),
            wide_spec(rows),
            pl.BlockSpec((span, 1), lambda j: (0, 0)),
        ],
        out_shape=[
            jax.ShapeDtypeStruct((rows, model), BF),
            jax.ShapeDtypeStruct((span, model), BF),
            jax.ShapeDtypeStruct((model, span), BF),
            jax.ShapeDtypeStruct((span, model), BF),
            jax.ShapeDtypeStruct((HEADS, span, rows), BF),
            jax.ShapeDtypeStruct((pairs, 8, rows), F32),
            jax.ShapeDtypeStruct((rows, model), F32),
            jax.ShapeDtypeStruct((rows, model), BF),
            jax.ShapeDtypeStruct((span, 1), F32),
        ],
        scratch_shapes=[
            pltpu.VMEM((span, model), BF),
            pltpu.VMEM((2, span, rows), F32),
            pltpu.VMEM((width, span), BF),
            pltpu.VMEM((span, rows), F32),
        ],
        compiler_params=params(VMEM_MB),
        cost_estimate=cost(20),
        name="attend",
    )(place, *blocks, small_full, w_full, w_full, w_full, cosine, sine)

    out_spec = pl.BlockSpec((parts, model, width), lambda *_: (3, 0, 0))
    hidden, scale_two, normed, normed_t, outgoing, gates, gain_two = pl.pallas_call(
        functools.partial(middle_kernel, gain_lane=experts + 1),
        grid=(1,),
        in_specs=[
            whole(attended),
            out_spec,
            small_spec,
            whole(x),
            whole(picked),
            whole(put),
        ],
        out_specs=[
            pl.BlockSpec((rows, model), lambda *_: (0, 0)),
            pl.BlockSpec((rows, 1), lambda *_: (0, 0)),
            pl.BlockSpec((rows, model), lambda *_: (0, 0)),
            pl.BlockSpec((model, rows), lambda *_: (0, 0)),
            pl.BlockSpec((slots, model + LANES), lambda *_: (0, 0)),
            pl.BlockSpec((rows, LANES), lambda *_: (0, 0)),
            pl.BlockSpec((1, model), lambda *_: (0, 0)),
        ],
        out_shape=[
            jax.ShapeDtypeStruct((rows, model), F32),
            jax.ShapeDtypeStruct((rows, 1), F32),
            jax.ShapeDtypeStruct((rows, model), BF),
            jax.ShapeDtypeStruct((model, rows), BF),
            jax.ShapeDtypeStruct((slots, model + LANES), BF),
            jax.ShapeDtypeStruct((rows, LANES), F32),
            jax.ShapeDtypeStruct((1, model), F32),
        ],
        compiler_params=params(VMEM_MB),
        cost_estimate=cost(5),
        name="middle",
    )(attended, w_full, small_full, x, picked, put)
    normed_all = lax.all_gather(normed, "fsdp", axis=0)
    incoming = exchange(after(outgoing, slot_g))
    shared_full = to_ctx(after(shared_own_w, incoming))
    gain_one = small_full[:, experts : experts + 1].astype(F32)
    span_x = jnp.concatenate([block[:rows] for block in blocks], axis=0)
    first_t = (span_x.T.astype(F32) * span_scale.reshape(1, span) * gain_one).astype(BF)
    incoming = after(incoming, first_t)

    packed_rows = 3 * model

    steps = tiles // AT_ONCE
    expert_specs = [
        pl.BlockSpec((fsdp, AT_ONCE * in_rows, TILE), lambda t: (0, t, 0)),
        pl.BlockSpec((fsdp, AT_ONCE * in_rows, TILE), lambda t: (0, steps + t, 0)),
        pl.BlockSpec((AT_ONCE, model, TILE), lambda t: (t, 2 * in_rows * tiles // model, 0)),
    ]
    unit_spec = pl.BlockSpec((1, slots, AT_ONCE * TILE), lambda t: (t, 0, 0))
    expert_y, *units = pl.pallas_call(
        expert_kernel,
        grid=(steps,),
        in_specs=[whole(incoming), *expert_specs],
        out_specs=[
            pl.BlockSpec((slots, model), lambda t: (0, 0)),
            unit_spec,
            unit_spec,
            unit_spec,
        ],
        out_shape=[jax.ShapeDtypeStruct((slots, model), BF)]
        + [jax.ShapeDtypeStruct((steps, slots, AT_ONCE * TILE), BF)] * 3,
        scratch_shapes=[pltpu.VMEM((slots, model), F32)],
        compiler_params=params(VMEM_MB),
        cost_estimate=cost(60),
        name="expert",
    )(incoming, expert_full, expert_full, expert_full)
    returned_y = exchange(after(expert_y, shared_full))

    at_once = 2
    block = model // ctx
    shared_part, shared_pieces = pl.pallas_call(
        shared_kernel,
        grid=(fsdp // at_once,),
        in_specs=[
            pl.BlockSpec((at_once, rows, model), lambda t: (t, 0, 0)),
            pl.BlockSpec((at_once, rows, model), lambda t: (t, 0, 0)),
            whole(shared_full),
        ],
        out_specs=[
            pl.BlockSpec((at_once, rows, 2 * model), lambda t: (t, 0, 0)),
            whole(shared_full),
        ],
        out_shape=[
            jax.ShapeDtypeStruct((fsdp, rows, 2 * model), BF),
            jax.ShapeDtypeStruct(shared_full.shape, BF),
        ],
        scratch_shapes=[pltpu.VMEM((model, 2 * TILE), F32), pltpu.VMEM((TILE, model), F32)],
        compiler_params=params(VMEM_MB),
        cost_estimate=cost(18),
        name="shared",
    )(after(normed_all, expert_y), g_all, shared_full)
    shared_both = lax.psum_scatter(after(shared_part, returned_y), "fsdp", scatter_dimension=0)
    shared_own = jnp.sum(
        lax.all_to_all(
            after(shared_pieces, returned_y), "ctx", split_axis=0, concat_axis=0, tiled=True
        ).astype(F32),
        axis=0,
    )
    back, gexpert = pl.pallas_call(
        expert_back_kernel,
        grid=(steps,),
        in_specs=[
            whole(incoming),
            whole(slot_g),
            whole(own_lanes),
            *expert_specs,
            unit_spec,
            unit_spec,
            unit_spec,
        ],
        out_specs=[
            pl.BlockSpec((slots, model), lambda t: (0, 0)),
            pl.BlockSpec(memory_space=pl.ANY),
        ],
        out_shape=[
            jax.ShapeDtypeStruct((slots, model), BF),
            jax.ShapeDtypeStruct((fsdp, packed_rows, TILE), BF),
        ],
        scratch_shapes=[
            pltpu.VMEM((model, slots), BF),
            pltpu.VMEM((slots, model), BF),
            pltpu.VMEM((slots, model), F32),
            pltpu.VMEM((2, 2, fsdp, AT_ONCE * in_rows, TILE), BF),
            pltpu.VMEM((2, AT_ONCE, model, TILE), BF),
            pltpu.SemaphoreType.DMA((2, 3)),
        ],
        compiler_params=params(VMEM_MB),
        cost_estimate=cost(22),
        name="expert_back",
    )(after(incoming, shared_part, returned_y), slot_g, own_lanes, expert_full, expert_full, expert_full, *units)
    returned = exchange(after(back, shared_own))
    expert_sum = lax.psum_scatter(after(gexpert, shared_own), "fsdp", scatter_dimension=0)

    mixed, dgates = pl.pallas_call(
        combine_kernel,
        grid=(1,),
        in_specs=[
            pl.BlockSpec((slots, model), lambda *_: (0, 0)),
            pl.BlockSpec((rows, slots), lambda *_: (0, 0)),
            pl.BlockSpec((rows, slots), lambda *_: (0, 1)),
            whole(picked),
            whole(gates),
            whole(hidden),
            pl.BlockSpec((rows, model), lambda *_: (0, 0)),
            whole(g),
        ],
        out_specs=[
            pl.BlockSpec((1, rows, model), lambda *_: (0, 0, 0)),
            pl.BlockSpec((rows, LANES), lambda *_: (0, 0)),
        ],
        out_shape=[
            jax.ShapeDtypeStruct((1, rows, model), BF),
            jax.ShapeDtypeStruct((rows, LANES), F32),
        ],
        compiler_params=params(VMEM_MB),
        cost_estimate=cost(3),
        name="combine",
    )(returned_y, selector, selector, picked, gates, hidden, shared_both, g)

    returned = after(returned, dgates)

    dhidden, dhidden_low, dattended, dlogits, ggain_two = pl.pallas_call(
        middle_back_kernel,
        grid=(1,),
        in_specs=[
            whole(returned),
            whole(dgates),
            whole(take),
            whole(gates),
            small_spec,
            pl.BlockSpec((rows, model), lambda *_: (0, 1)),
            whole(g),
            whole(hidden),
            whole(scale_two),
            whole(gain_two),
            out_spec,
        ],
        out_specs=[
            pl.BlockSpec((rows, model), lambda *_: (0, 0)),
            pl.BlockSpec((rows, model), lambda *_: (0, 0)),
            pl.BlockSpec((rows, model), lambda *_: (0, 0)),
            pl.BlockSpec((rows, LANES), lambda *_: (0, 0)),
            pl.BlockSpec((1, model), lambda *_: (0, 0)),
        ],
        out_shape=[
            jax.ShapeDtypeStruct((rows, model), F32),
            jax.ShapeDtypeStruct((rows, model), BF),
            jax.ShapeDtypeStruct((rows, model), BF),
            jax.ShapeDtypeStruct((rows, LANES), BF),
            jax.ShapeDtypeStruct((1, model), F32),
        ],
        compiler_params=params(VMEM_MB),
        cost_estimate=cost(6),
        name="middle_back",
    )(
        returned, dgates, take, gates, small_full, shared_both, g, hidden, scale_two, gain_two, w_full
    )

    grouter = dot(normed_t, dlogits)
    small_grads = jnp.concatenate(
        [grouter[:, :experts], ggain_two.T, jnp.zeros((model, LANES - experts - 1), F32)], axis=1
    ).astype(BF)
    attended_t = attended.T
    core_scalar = core.astype(jnp.int32).reshape(1)

    def attend_back(first, count, down, *filled):
        pair_from = lambda height: pl.BlockSpec((height, LANES), lambda j: (0, first + j))
        operands = (
            core_scalar, q, k, kt, v, e, rl, rlb, down, cosine, sine, first_t, attended_t, dhidden_low, *filled,
        )
        return pl.pallas_call(
            attend_back_kernel,
            grid=(count,),
            in_specs=[
                place_spec,
                pair_from(rows),
                pair_from(span),
                pl.BlockSpec((LANES, span), lambda j: (first + j, 0)),
                pair_from(span),
                pl.BlockSpec((2, span, rows), lambda j: (first + j, 0, 0)),
                pl.BlockSpec((1, 8, rows), lambda j: (first + j, 0, 0)),
                pair_from(rows),
                pair_from(rows),
                whole(cosine),
                whole(sine),
                whole(first_t),
                whole(attended_t),
                pair_from(rows),
            ]
            + [pl.BlockSpec(memory_space=pl.ANY)] * len(filled),
            out_specs=[
                pair_from(rows),
                pair_from(span),
                pair_from(span),
                pl.BlockSpec((model, 2 * LANES), lambda j: (0, j)),
                pl.BlockSpec((model, 2 * LANES), lambda j: (0, j)),
            ],
            out_shape=[
                jax.ShapeDtypeStruct((rows, model), BF),
                jax.ShapeDtypeStruct((span, model), BF),
                jax.ShapeDtypeStruct((span, model), BF),
                jax.ShapeDtypeStruct((model, count * 2 * LANES), BF),
                jax.ShapeDtypeStruct((model, count * 2 * LANES), BF),
            ],
            input_output_aliases={
                len(operands) - len(filled) + index: index for index in range(len(filled))
            },
            scratch_shapes=[
                pltpu.VMEM((2, span, rows), F32),
                pltpu.VMEM((2, span, rows), BF),
                pltpu.VMEM((span, LANES), F32),
                pltpu.VMEM((span, LANES), F32),
            ],
            compiler_params=params(VMEM_MB),
            cost_estimate=cost(12 * count),
            name=f"attend_back_{first}",
        )(*operands)


    def paired_columns(kept, sent):
        partner = lax.ppermute(sent, "fsdp", [(i, i ^ 1) for i in range(fsdp)])
        return (kept.astype(F32) + partner.astype(F32)).astype(BF)

    def along_ctx(pieces):
        return lax.all_to_all(pieces, "ctx", split_axis=0, concat_axis=0, tiled=True)

    early_pairs = 2 * pairs // 3
    *grads_a, kept_a, sent_a = attend_back(0, early_pairs, dattended)
    paired_a = paired_columns(kept_a, sent_a)
    late_a = along_ctx(paired_a.reshape(ctx, block, -1))
    dq, dk, dv, kept_b, sent_b = attend_back(
        early_pairs, pairs - early_pairs, after(dattended, paired_a), *grads_a
    )
    paired_b = paired_columns(kept_b, sent_b)

    dspan, down = pl.pallas_call(
        project_back_kernel,
        grid=(2,),
        in_specs=[
            whole(dq),
            pl.BlockSpec((span // 2, model), lambda b: (b, 0)),
            pl.BlockSpec((span // 2, model), lambda b: (b, 0)),
            pl.BlockSpec((3 * parts, model, width), lambda b: (0, 0, 0)),
        ],
        out_specs=[
            pl.BlockSpec((span // 2, model), lambda b: (b, 0)),
            pl.BlockSpec((rows, model), lambda b: (0, 0)),
        ],
        out_shape=[
            jax.ShapeDtypeStruct((span, model), BF),
            jax.ShapeDtypeStruct((rows, model), F32),
        ],
        compiler_params=params(VMEM_MB),
        scratch_shapes=[pltpu.VMEM((model, 3 * model), BF)],
        cost_estimate=cost(8),
        name="project_back",
    )(dq, dk, dv, w_full)
    total, passed = down, dspan[:rows].astype(F32)
    for distance in range(1, reach):
        lower = (reach - distance) * rows
        moved = lax.ppermute(
            dspan[lower : lower + rows],
            "ctx",
            [(line + z, line + (z - distance) % ROW) for line in lines for z in range(ROW)],
        )
        moved = moved.astype(F32)
        here = place_z + distance < ROW
        total = total + jnp.where(here, moved, 0.0)
        passed = passed + jnp.where(here, 0.0, moved)
    grad_expert_in, grad_expert_down = pl.pallas_call(
        widen_kernel,
        grid=(1,),
        in_specs=[whole(expert_sum)],
        out_specs=[
            pl.BlockSpec((1, in_rows, 2 * ff), lambda *_: (0, 0, 0)),
            pl.BlockSpec((1, down_rows, model), lambda *_: (0, 0, 0)),
        ],
        out_shape=[
            jax.ShapeDtypeStruct((1, in_rows, 2 * ff), F32),
            jax.ShapeDtypeStruct((1, down_rows, model), F32),
        ],
        compiler_params=params(VMEM_MB),
        cost_estimate=cost(2),
        name="widen",
    )(expert_sum)
    late_a = jnp.sum(late_a.astype(F32), axis=0)
    quarter = paired_b.shape[1] // (fsdp // 2)
    late_b = lax.all_to_all(
        after(paired_b.reshape(model, fsdp // 2, quarter).transpose(1, 0, 2), down, late_a),
        "fsdp",
        split_axis=0,
        concat_axis=0,
        axis_index_groups=[list(range(start, fsdp, 2)) for start in range(2)],
        tiled=True,
    )
    late_b = jnp.sum(late_b.astype(F32), axis=0).astype(BF)
    received = shifted(after(passed.astype(BF), late_b), "ctx", -ROW)
    late_b = along_ctx(jnp.concatenate([late_b, small_grads], axis=1).reshape(ctx, block, -1))

    grad_shared_down = (
        shared_own[2 * block :]
        .reshape(columns, owned_down, TILE)
        .transpose(1, 0, 2)
        .reshape(owned_down, model)
    )
    packed_width = late_a.shape[1] + late_b.shape[2] + 2 * TILE
    last = pl.pallas_call(
        functools.partial(pack_kernel, block=block),
        grid=(1,),
        in_specs=[
            whole(late_a),
            whole(late_b),
            pl.BlockSpec((2 * block, TILE), lambda *_: (0, 0)),
        ],
        out_specs=pl.BlockSpec((fsdp, own, packed_width), lambda *_: (0, 0, 0)),
        out_shape=jax.ShapeDtypeStruct((fsdp, own, packed_width), BF),
        compiler_params=params(VMEM_MB),
        cost_estimate=cost(2),
        name="pack",
    )(late_a, late_b, shared_own)
    last = lax.all_to_all(last, "fsdp", split_axis=0, concat_axis=0, tiled=True)
    last = after(last, received, grad_expert_in, grad_expert_down)
    wanted = [
        jax.ShapeDtypeStruct((own, 3 * model), F32),
        jax.ShapeDtypeStruct((own, model), F32),
        jax.ShapeDtypeStruct((own, experts), F32),
        jax.ShapeDtypeStruct((1, own), F32),
        jax.ShapeDtypeStruct((1, own), F32),
        jax.ShapeDtypeStruct((own, 2 * ff), F32),
    ]
    gain_own = attn_gain.astype(F32)[:, None]
    grad_qkv, grad_out, grad_router, grad_gain_one, grad_gain_two, grad_shared_in = pl.pallas_call(
        functools.partial(unpack_kernel, piece=owned_down),
        grid=(1,),
        in_specs=[whole(last), whole(w_qkv), whole(gain_own)],
        out_specs=[whole(array) for array in wanted],
        out_shape=wanted,
        compiler_params=params(VMEM_MB),
        cost_estimate=cost(2),
        name="unpack",
    )(last, w_qkv, gain_own)

    total = total + received.astype(F32)
    input_rows = x.astype(F32)
    scale_one = span_scale[reach * rows :]
    weighted = total * gain_one.reshape(1, model)
    input_grad = (
        dhidden
        + scale_one * weighted
        - input_rows
        * scale_one**3
        * jnp.mean(weighted * input_rows, axis=-1, keepdims=True)
    )[None]

    return (
        mixed,
        input_grad,
        grad_qkv,
        grad_out,
        grad_router,
        grad_shared_in,
        grad_shared_down,
        grad_gain_one.reshape(own),
        grad_gain_two.reshape(own),
        grad_expert_in,
        grad_expert_down,
    )


def solution(mesh):
    placed = (
        P("fsdp", "ctx", None),
        P("fsdp", "ctx"),
        P("fsdp", "ctx", None),
        P(("ctx", "fsdp"), None),
        P(("ctx", "fsdp"), None),
        P(("ctx", "fsdp"), None),
        P(("ctx", "fsdp"), None),
        P(("ctx", "fsdp"), None),
        P(("ctx", "fsdp")),
        P(("ctx", "fsdp")),
        P("ctx", "fsdp", None),
        P("ctx", "fsdp", None),
        P("fsdp", "ctx", None),
    )
    return jax.shard_map(
        per_device,
        mesh=mesh,
        in_specs=placed,
        out_specs=(
            P("fsdp", "ctx", None),
            P("fsdp", "ctx", None),
            P(("ctx", "fsdp"), None),
            P(("ctx", "fsdp"), None),
            P(("ctx", "fsdp"), None),
            P(("ctx", "fsdp"), None),
            P(("ctx", "fsdp"), None),
            P(("ctx", "fsdp")),
            P(("ctx", "fsdp")),
            P("ctx", "fsdp", None),
            P("ctx", "fsdp", None),
        ),
        check_vma=False,
    )
```

```python
import functools

import jax
import jax.numpy as jnp
from jax import lax
from jax.experimental import pallas as pl
from jax.experimental.pallas import tpu as pltpu
from jax.sharding import PartitionSpec as P

HEADS = 12
HEAD_DIM = 64
TOPK = 2
WIN = 1024
EPSILON = 1e-06

BF = jnp.bfloat16
F32 = jnp.float32
TILE = 256
LANES = 128
IN_ROWS = 96
AT_ONCE = 2
KEY_BLOCK = 128
ROW = 4
VMEM_MB = 60


def dot(a, b):
    return jnp.dot(a, b, preferred_element_type=F32)


def dot_nt(a, b):
    return lax.dot_general(a, b, (((1,), (1,)), ((), ())), preferred_element_type=F32)


def dot_tn(a, b):
    return lax.dot_general(a, b, (((0,), (0,)), ((), ())), preferred_element_type=F32)


def params(megabytes):
    return pltpu.CompilerParams(vmem_limit_bytes=megabytes * 1024 * 1024)


def cost(microseconds):
    return pl.CostEstimate(
        flops=int(microseconds * 1.0e9), bytes_accessed=int(microseconds * 1.0e6), transcendentals=0
    )


def after(value, *others):
    return lax.optimization_barrier((value, *others))[0]


def whole(array):
    return pl.BlockSpec(array.shape, lambda *_: (0,) * array.ndim)


def shifted(value, axis, steps):
    count = lax.axis_size(axis)
    leading, last = (max(0, -steps), min(count, count - steps))
    return lax.ppermute(value, axis, [(source, source + steps) for source in range(leading, last)])


def split_high_low(values):
    high = values.astype(BF)
    return high, (values - high.astype(F32)).astype(BF)


def rotary_tables(rows, offset):
    half = HEAD_DIM // 2
    frequency = jnp.exp(-jnp.log(10000.0) * (2.0 * jnp.arange(half, dtype=F32) / HEAD_DIM))
    places = (offset + jnp.arange(rows, dtype=jnp.int32)).astype(F32)
    angles = places[:, None] * frequency[None, :]
    cosine, sine = jnp.cos(angles), jnp.sin(angles)
    return (
        jnp.concatenate([cosine] * 4, axis=1),
        jnp.concatenate([-sine, sine, -sine, sine], axis=1),
    )


def swapped_halves(values):
    width, half = values.shape[1], HEAD_DIM // 2
    lane = lax.broadcasted_iota(jnp.int32, (1, width), 1)
    return jnp.where(
        lane % HEAD_DIM < half,
        pltpu.roll(values, width - half, 1),
        pltpu.roll(values, half, 1),
    )


def head_lanes(values, head):
    lane = lax.broadcasted_iota(jnp.int32, (1, LANES), 1)
    return jnp.where(lane // HEAD_DIM == head, values, jnp.zeros_like(values))


def fold_rows(values, op):
    return op(values.reshape(values.shape[0] // 8, 8, values.shape[1]), axis=0)


def attend_kernel(
    place_ref, *refs, gain_lane, parts
):
    blocks, refs = refs[:parts], refs[parts:]
    (
        small_ref, wq_ref, wk_ref, wv_ref, cos_ref, sin_ref,
        q_ref, k_ref, kt_ref, v_ref, e_ref, rl_ref, rlb_ref, o_ref, scale_ref,
        normed, score, vt, bias_ref,
    ) = refs
    rows, model = q_ref.shape[0], normed.shape[1]
    span = parts * rows

    @pl.when(pl.program_id(0) == 0)
    def _():
        gain = small_ref[...].astype(F32).T[gain_lane : gain_lane + 1, :]
        query_segment = blocks[-1][rows : rows + 1, :rows].astype(F32)
        query_place = lax.broadcasted_iota(jnp.int32, (rows, rows), 1)
        key_place = lax.broadcasted_iota(jnp.int32, (rows, rows), 0)
        for index, block in enumerate(blocks):
            part = pl.ds(index * rows, rows)
            values = block[:rows, :].astype(F32)
            scale = lax.rsqrt(jnp.mean(values * values, axis=-1, keepdims=True) + EPSILON)
            scale_ref[part, :] = scale
            normed[part, :] = (values * scale * gain).astype(BF)
            key_segment = block[rows : rows + 16, :rows].astype(F32).T[:, :1]
            distance = query_place - key_place + (parts - 1 - index) * rows
            allowed = (distance >= 0) & (distance < WIN) & (key_segment == query_segment)
            allowed = allowed & (place_ref[0] >= parts - 1 - index)
            bias_ref[part, :] = jnp.where(allowed, 0.0, -1e30)

    wide = q_ref.shape[1]
    cosine = jnp.concatenate([cos_ref[...]] * (wide // LANES), axis=1)
    sine = jnp.concatenate([sin_ref[...]] * (wide // LANES), axis=1)
    pair = dot(normed[...], jnp.concatenate([wk_ref[0], wv_ref[0]], axis=1))
    keys = pair[:, :wide]
    keys = keys * cosine + swapped_halves(keys) * sine
    k_ref[...] = keys.astype(BF)
    kt_ref[...] = keys.T.astype(BF)
    queries = dot(normed[span - rows :, :], wq_ref[0])
    queries = queries * cosine[span - rows :] + swapped_halves(queries) * sine[span - rows :]
    queries = (queries.astype(BF).astype(F32) * HEAD_DIM**-0.5).astype(BF)
    q_ref[...] = queries
    heads = wide // HEAD_DIM

    def chunk(head):
        return slice(head // 2 * LANES, (head // 2 + 1) * LANES)

    own = [head_lanes(queries[:, chunk(head)], head % 2) for head in range(heads)]
    largest = [jnp.full((8, rows), -3e38, F32) for _ in range(heads)]
    total = [jnp.zeros((8, rows), F32) for _ in range(heads)]

    def scores(head, part):
        block = dot_nt(k_ref[part, chunk(head)], own[head]) + bias_ref[part, :]
        score[head % 2, part, :] = block
        largest[head] = jnp.maximum(largest[head], fold_rows(block, jnp.max))

    def weights(head, part):
        block = jnp.exp(score[head % 2, part, :] - largest[head])
        total[head] = total[head] + fold_rows(block, jnp.sum)
        e_ref[head, part, :] = block.astype(BF)

    blocks_of_keys = [pl.ds(start, KEY_BLOCK) for start in range(0, span, KEY_BLOCK)]
    for part in blocks_of_keys:
        scores(0, part)
    values = pair[:, wide:]
    v_ref[...] = values.astype(BF)
    vt[...] = values.T.astype(BF)
    outs, sums = [], []
    for head in range(heads):
        largest[head] = jnp.max(largest[head], axis=0, keepdims=True)
        for part in blocks_of_keys:
            weights(head, part)
            if head + 1 < heads:
                scores(head + 1, part)
        inverse = 1.0 / jnp.sum(total[head], axis=0, keepdims=True)
        rl_ref[head // 2, head % 2 : head % 2 + 1, :] = inverse
        outs.append(dot(vt[head * HEAD_DIM : (head + 1) * HEAD_DIM, :], e_ref[head]) * inverse)
        sums.append(jnp.broadcast_to(inverse, (HEAD_DIM, rows)))
    o_ref[...] = jnp.concatenate(outs, axis=0).T.astype(BF)
    rlb_ref[...] = jnp.concatenate(sums, axis=0).T


def attend_back_kernel(
    core_ref, q_ref, k_ref, kt_ref, v_ref, e_ref, rl_ref, rlb_ref, do_ref, cos_ref, sin_ref, xt_ref, ot_ref, dh_ref,
    *refs,
):
    dq_ref, dk_ref, dv_ref, kept_ref, sent_ref, dprob, dscore, dk, dv = refs[-9:]
    span, rows = k_ref.shape[0], q_ref.shape[0]
    scaled = do_ref[...].astype(F32) * rlb_ref[...]
    heads = range(2)
    down = [head_lanes(scaled, head).astype(BF) for head in heads]
    own = [head_lanes(q_ref[...], head) for head in heads]
    own_both, down_both = jnp.concatenate(own, axis=0), jnp.concatenate(down, axis=0)
    inner = [jnp.zeros((8, rows), F32) for _ in heads]
    for start in range(0, span, KEY_BLOCK):
        part = pl.ds(start, KEY_BLOCK)
        for head in heads:
            block = dot_nt(v_ref[part, :], down[head])
            dprob[head, part, :] = block
            inner[head] = inner[head] + fold_rows(block * e_ref[head, part, :].astype(F32), jnp.sum)
    inner = [
        jnp.sum(inner[head], axis=0, keepdims=True) * rl_ref[0, head : head + 1, :]
        for head in heads
    ]
    for start in range(0, span, KEY_BLOCK):
        part = pl.ds(start, KEY_BLOCK)
        for head in heads:
            weight = e_ref[head, part, :]
            block = (weight.astype(F32) * (dprob[head, part, :] - inner[head])).astype(BF)
            dscore[head, part, :] = block
        dk[part, :] = dot(
            jnp.concatenate([dscore[head, part, :] for head in heads], axis=1), own_both
        )
        dv[part, :] = dot(
            jnp.concatenate([e_ref[head, part, :] for head in heads], axis=1), down_both
        )
    dqs = [
        dot(kt_ref[head * HEAD_DIM : (head + 1) * HEAD_DIM, :], dscore[head]) for head in heads
    ]
    dquery = jnp.concatenate(dqs, axis=0).T * HEAD_DIM**-0.5
    dquery = dquery * cos_ref[span - rows :, :] - swapped_halves(dquery) * sin_ref[span - rows :, :]
    dquery = dquery.astype(BF)
    dq_ref[...] = dquery
    dkeys = dk[...]
    dkeys = (dkeys * cos_ref[...] - swapped_halves(dkeys) * sin_ref[...]).astype(BF)
    dvalues = dv[...].astype(BF)
    dk_ref[...] = dkeys
    dv_ref[...] = dvalues
    first = dot(xt_ref[...], jnp.concatenate([dkeys, dvalues], axis=1)).astype(BF)
    second = jnp.concatenate(
        [dot(xt_ref[:, span - rows :], dquery), dot(ot_ref[...], dh_ref[...])], axis=1
    ).astype(BF)
    kept_ref[...] = jnp.where(core_ref[0] == 0, first, second)
    sent_ref[...] = jnp.where(core_ref[0] == 0, second, first)


def middle_kernel(
    o_ref, w_ref, small_ref, x_ref, pick_ref, put_ref,
    h_ref, scale_ref, a_ref, at_ref, out_ref, gate_ref, gain_ref,
    *, gain_lane,
):
    projected = jnp.concatenate([dot(o_ref[...], w_ref[part]) for part in range(2)], axis=1)
    hidden = x_ref[...].astype(F32) + projected
    h_ref[...] = hidden
    scale = lax.rsqrt(jnp.mean(hidden * hidden, axis=-1, keepdims=True) + EPSILON)
    scale_ref[...] = scale
    small = small_ref[...]
    gain = small.astype(F32).T[gain_lane : gain_lane + 1, :]
    gain_ref[...] = gain
    low = (hidden * scale * gain).astype(BF)
    a_ref[...] = low
    at_ref[...] = low.astype(F32).T.astype(BF)
    logits = dot(low, small)
    first, second = pick_ref[0], pick_ref[1]
    chosen_first = jnp.sum(logits * first, axis=-1, keepdims=True)
    chosen_second = jnp.sum(logits * second, axis=-1, keepdims=True)
    largest = jnp.maximum(chosen_first, chosen_second)
    chosen_first = jnp.exp(chosen_first - largest)
    chosen_second = jnp.exp(chosen_second - largest)
    total = chosen_first + chosen_second
    table = (chosen_first / total) * first + (chosen_second / total) * second
    gate_ref[...] = table
    high, rest = split_high_low(table)
    extra = (high.astype(F32) + pltpu.roll(rest.astype(F32), LANES // 2, 1)).astype(BF)
    put = put_ref[...]
    width = a_ref.shape[1]
    out_ref[:, :width] = dot(put, low).astype(BF)
    out_ref[:, width:] = dot(put, extra).astype(BF)


def gated_forward(x, w_gate, w_lift):
    gate, lift = dot(x, w_gate), dot(x, w_lift)
    sigmoid = 1.0 / (1.0 + jnp.exp(-gate))
    act = gate * sigmoid
    slope = sigmoid + (act - act * sigmoid)
    return (act * lift).astype(BF), act, lift * slope


def add_up(total_ref, value):
    first = pl.program_id(0) == 0
    total_ref[...] = value + jnp.where(first, 0.0, total_ref[...])


def flush(step, steps, copies):
    @pl.when(step >= 2)
    def _():
        for copy in copies(step % 2, step):
            copy.wait()


def send(step, steps, copies):
    for copy in copies(step % 2, step):
        copy.start()

    @pl.when(step == steps - 1)
    def _():
        for copy in copies((step + 1) % 2, step):
            copy.wait()
        for copy in copies(step % 2, step):
            copy.wait()


def shared_kernel(
    x_ref, dy_ref, w_ref, out_ref, pieces_ref, gin_sum, gdown_sum
):
    count, rows, model = x_ref.shape
    block, columns = model // w_ref.shape[0], model // TILE
    piece = (w_ref.shape[1] - 2 * block) // columns
    x, dy = x_ref[...].reshape(count * rows, model), dy_ref[...].reshape(count * rows, model)
    w_gate = w_ref[:, :block, :].reshape(model, TILE)
    w_lift = w_ref[:, block : 2 * block, :].reshape(model, TILE)
    w_down = jnp.concatenate(
        [
            w_ref[:, start : start + piece, :].reshape(-1, TILE)
            for start in range(2 * block, w_ref.shape[1], piece)
        ],
        axis=1,
    )
    hidden, act, slope = gated_forward(x, w_gate, w_lift)
    out_ref[:, :, :model] = dot(hidden, w_down).astype(BF).reshape(count, rows, model)
    dhidden = dot_nt(dy, w_down)
    both = jnp.concatenate([dhidden * slope, dhidden * act], axis=1).astype(BF)
    dx = dot_nt(both, jnp.concatenate([w_gate, w_lift], axis=1))
    out_ref[:, :, model:] = dx.astype(BF).reshape(count, rows, model)
    add_up(gin_sum, dot_tn(x, both))
    add_up(gdown_sum, dot_tn(hidden, dy))

    @pl.when(pl.program_id(0) == pl.num_programs(0) - 1)
    def _():
        for owner in range(pieces_ref.shape[0]):
            rows_in = pl.ds(owner * block, block)
            for part in range(2):
                pieces_ref[owner, part * block : (part + 1) * block, :] = gin_sum[
                    rows_in, part * TILE : (part + 1) * TILE
                ].astype(BF)
            rows_down = pl.ds(owner * piece, piece)
            for column in range(columns):
                start = 2 * block + column * piece
                pieces_ref[owner, start : start + piece, :] = gdown_sum[
                    rows_down, column * TILE : (column + 1) * TILE
                ].astype(BF)


def side_by_side(blocks):
    count = blocks.shape[1] // IN_ROWS
    return jnp.concatenate(
        [
            blocks[:, part * IN_ROWS : (part + 1) * IN_ROWS].reshape(-1, TILE)
            for part in range(count)
        ],
        axis=1,
    )


def unpack_down(packed, model):
    return jnp.concatenate(
        [
            jnp.concatenate(
                [packed[tile, start : start + TILE] for start in range(0, model, TILE)], axis=1
            )
            for tile in range(packed.shape[0])
        ],
        axis=0,
    )


def expert_kernel(
    in_ref, wg_ref, wl_ref, wd_ref, y_ref, hidden_ref, act_ref, slope_ref, y_sum
):
    model = y_ref.shape[1]
    w_gate, w_lift = side_by_side(wg_ref[...]), side_by_side(wl_ref[...])
    hidden, act, slope = gated_forward(in_ref[:, :model], w_gate, w_lift)
    hidden_ref[0] = hidden
    act_ref[0] = act.astype(BF)
    slope_ref[0] = slope.astype(BF)
    add_up(y_sum, dot(hidden, unpack_down(wd_ref[...], model)))

    @pl.when(pl.program_id(0) == pl.num_programs(0) - 1)
    def _():
        y_ref[...] = y_sum[...].astype(BF)


def expert_back_kernel(
    in_ref, g_ref, own_ref, wg_ref, wl_ref, wd_ref, hidden_ref, act_ref, slope_ref,
    dx_ref, grads_ref,
    xt, dy, dx_sum, gin, gdown, sems,
):
    model = g_ref.shape[1]
    step, steps = pl.program_id(0), pl.num_programs(0)
    in_rows, tiles = gin.shape[3], gdown.shape[1]

    def copies(slot, now):
        for part in range(2):
            first = pl.multiple_of((part * steps + now) * in_rows, in_rows)
            yield pltpu.make_async_copy(
                gin.at[slot, part], grads_ref.at[:, pl.ds(first, in_rows)], sems.at[slot, part]
            )
        yield pltpu.make_async_copy(
            gdown.at[slot],
            grads_ref.at[pl.ds(now * tiles, tiles), pl.ds(2 * steps * in_rows, model)],
            sems.at[slot, 2],
        )

    @pl.when(step == 0)
    def _():
        xt[...] = in_ref[:, :model].astype(F32).T.astype(BF)
        gate = jnp.sum(in_ref[:, model:].astype(F32) * own_ref[...], axis=-1, keepdims=True)
        dy[...] = (g_ref[...].astype(F32) * gate).astype(BF)

    flush(step, steps, copies)
    slot = step % 2
    w_gate, w_lift = side_by_side(wg_ref[...]), side_by_side(wl_ref[...])
    dhidden = dot_nt(dy[...], unpack_down(wd_ref[...], model)).astype(BF)
    both = jnp.concatenate([dhidden * slope_ref[0], dhidden * act_ref[0]], axis=1)
    add_up(dx_sum, dot_nt(both, jnp.concatenate([w_gate, w_lift], axis=1)))
    into = dot(xt[...], both).astype(BF)
    shape = (gin.shape[2], IN_ROWS, TILE)
    for part in range(2):
        for tile in range(tiles):
            column = (part * tiles + tile) * TILE
            gin[slot, part, :, tile * IN_ROWS : (tile + 1) * IN_ROWS, :] = into[
                :, column : column + TILE
            ].reshape(shape)
    down = dot_tn(hidden_ref[0], dy[...]).astype(BF)
    for tile in range(tiles):
        for column in range(model // TILE):
            part = slice(column * TILE, (column + 1) * TILE)
            gdown[slot, tile, part, :] = down[tile * TILE : (tile + 1) * TILE, part]
    send(step, steps, copies)

    @pl.when(step == steps - 1)
    def _():
        dx_ref[...] = dx_sum[...].astype(BF)


def combine_kernel(
    y_ref, first_ref, second_ref, pick_ref, gate_ref, h_ref, shared_ref, g_ref, out_ref, dgate_ref
):
    table = gate_ref[...]
    y_first, y_second = dot(first_ref[...], y_ref[...]), dot(second_ref[...], y_ref[...])
    gate_first = jnp.sum(table * pick_ref[0], axis=-1, keepdims=True)
    gate_second = jnp.sum(table * pick_ref[1], axis=-1, keepdims=True)
    mixture = gate_first * y_first + gate_second * y_second
    out_ref[0] = (h_ref[...] + mixture + shared_ref[...].astype(F32)).astype(BF)
    g = g_ref[...].astype(F32)
    dgate_ref[...] = (
        jnp.sum(g * y_first, axis=-1, keepdims=True) * pick_ref[0]
        + jnp.sum(g * y_second, axis=-1, keepdims=True) * pick_ref[1]
    )


def middle_back_kernel(
    back_ref, dgate_ref, take_ref, gate_ref, small_ref, dshared_ref, g_ref, h_ref, scale_ref, gain_ref, w_ref,
    dh_ref, dhb_ref, do_ref, dlogits_ref, ggain_ref,
):
    take = take_ref[...]
    dgates = dgate_ref[...]
    table = gate_ref[...]
    gated = jnp.sum(table * dgates, axis=-1, keepdims=True)
    dlogits = (table * (dgates - gated)).astype(BF)
    dlogits_ref[...] = dlogits
    da = dshared_ref[...].astype(F32) + dot_nt(dlogits, small_ref[...]) + dot(take, back_ref[...])
    hidden, scale = h_ref[...], scale_ref[...]
    ggain_ref[...] = jnp.sum(da * hidden * scale, axis=0, keepdims=True)
    weighted = da * gain_ref[...]
    mean = jnp.mean(weighted * hidden, axis=-1, keepdims=True)
    dhidden = g_ref[...].astype(F32) + scale * weighted - hidden * (scale * scale * scale) * mean
    dh_ref[...] = dhidden
    low = dhidden.astype(BF)
    dhb_ref[...] = low
    width = w_ref.shape[2]
    do = dot_nt(low[:, :width], w_ref[0]) + dot_nt(low[:, width:], w_ref[1])
    do_ref[...] = do.astype(BF)


def project_back_kernel(dq_ref, dk_ref, dv_ref, w_ref, halo_ref, own_ref, w_back):
    width, model = w_ref.shape[2], w_ref.shape[1]
    parts = model // width
    rows = dq_ref.shape[0]

    @pl.when(pl.program_id(0) == 0)
    def _():
        for part in range(3 * parts):
            w_back[:, part * width : (part + 1) * width] = w_ref[part]

    da = dot_nt(
        jnp.concatenate([dk_ref[...], dv_ref[...]], axis=1), w_back[:, model:]
    )
    halo_ref[...] = da.astype(BF)

    @pl.when(pl.program_id(0) == pl.num_programs(0) - 1)
    def _():
        own_ref[...] = da[da.shape[0] - rows :] + dot_nt(dq_ref[...], w_back[:, :model])


def widen_kernel(in_ref, in_out_ref, down_out_ref):
    in_rows, down_rows = in_out_ref.shape[1], down_out_ref.shape[1]
    columns = in_out_ref.shape[2] // TILE
    for column in range(columns):
        in_out_ref[0, :, column * TILE : (column + 1) * TILE] = in_ref[
            column * in_rows : (column + 1) * in_rows, :
        ].astype(F32)
    for column in range(down_out_ref.shape[2] // TILE):
        first = columns * in_rows + column * down_rows
        down_out_ref[0, :, column * TILE : (column + 1) * TILE] = in_ref[
            first : first + down_rows, :
        ].astype(F32)


def pack_kernel(early_ref, late_ref, shared_ref, out_ref, *, block):
    late = late_ref[0].astype(F32)
    for source in range(1, late_ref.shape[0]):
        late = late + late_ref[source].astype(F32)
    early, own = early_ref[...], out_ref.shape[1]
    for owner in range(out_ref.shape[0]):
        part = slice(owner * own, (owner + 1) * own)
        first = early.shape[1]
        out_ref[owner, :, :first] = early[part].astype(BF)
        out_ref[owner, :, first : first + late.shape[1]] = late[part].astype(BF)
        first = first + late.shape[1]
        for half in range(2):
            out_ref[owner, :, first + half * TILE : first + (half + 1) * TILE] = shared_ref[
                half * block + owner * own : half * block + (owner + 1) * own, :
            ].astype(BF)


def unpack_kernel(
    in_ref, w_ref, gain_ref, qkv_ref, out_ref, small_ref, dgain_ref, second_ref, shared_ref, *, piece
):
    sources, own = in_ref.shape[0], in_ref.shape[1]
    model = out_ref.shape[1]

    def take(start, some):
        total = in_ref[some[0], :, start : start + LANES].astype(F32)
        for source in some[1:]:
            total = total + in_ref[source, :, start : start + LANES].astype(F32)
        return total

    dgain = jnp.zeros((own, LANES), F32)
    first_core, second_core = range(0, sources, 2), range(1, sources, 2)
    early = 2 * model - 2 * LANES * (sources // 4)
    for pair in range(model // LANES):
        start = pair * 2 * LANES
        if start < early:
            k, v = take(start, first_core), take(start + LANES, first_core)
            q, o = take(start, second_core), take(start + LANES, second_core)
        else:
            source = (start - early) // LANES * 2
            k, q = take(early, (source,)), take(early, (source + 1,))
            v, o = take(early, (source + 2,)), take(early, (source + 3,))
        for which, value in enumerate((q, k, v)):
            part = slice(which * model + pair * LANES, which * model + (pair + 1) * LANES)
            qkv_ref[:, part] = value
            dgain = dgain + value * w_ref[:, part].astype(F32)
        out_ref[:, pair * LANES : (pair + 1) * LANES] = o
    dgain = jnp.sum(dgain, axis=-1, keepdims=True) / gain_ref[...]
    lane = lax.broadcasted_iota(jnp.int32, (own, LANES), 1)
    row = lax.broadcasted_iota(jnp.int32, (own, LANES), 0)

    def as_row(column):
        return jnp.sum(jnp.where(lane == row, column, 0.0), axis=0, keepdims=True)[:, :own]

    dgain_ref[...] = as_row(dgain)
    small = take(early + LANES, range(sources))
    experts = small_ref.shape[1]
    small_ref[...] = small[:, :experts]
    second = jnp.sum(jnp.where(lane == experts, small, 0.0), axis=-1, keepdims=True)
    second_ref[...] = as_row(second)
    per = LANES // piece
    for column in range(shared_ref.shape[1] // LANES):
        start = early + 2 * LANES + column // per * LANES
        total = jnp.zeros((own, LANES), F32)
        for source in range(sources):
            turn = (source - column % per) * piece % LANES
            value = take(start, (source,))
            value = pltpu.roll(value, turn, 1) if turn else value
            total = jnp.where(lane // piece == source, value, total)
        shared_ref[:, column * LANES : (column + 1) * LANES] = total


def per_device(
    tokens,
    segments,
    routes,
    w_qkv,
    w_out,
    w_router,
    shared_in,
    shared_down,
    attn_gain,
    ffn_gain,
    expert_in,
    expert_down,
    cotangent,
):
    ctx, fsdp = lax.axis_size("ctx"), lax.axis_size("fsdp")
    ctx_index, core = lax.axis_index("ctx"), lax.axis_index("fsdp") % 2
    rows, model = tokens.shape[1], tokens.shape[2]
    reach = max(1, WIN // rows)
    span = (reach + 1) * rows
    capacity = max(2, 3 * rows * TOPK // (2 * ctx))
    slots = ctx * capacity
    own = w_qkv.shape[0]
    owned_down = shared_down.shape[0]
    experts = w_router.shape[1]
    ff = shared_in.shape[1] // 2
    tiles = ff // TILE

    x, g = tokens[0], cotangent[0]
    segment_row = jnp.zeros((16, model), BF).at[0, :rows].set(segments[0].astype(BF))
    carried = jnp.concatenate([x, segment_row], axis=0)
    place_z = ctx_index % ROW
    lines = range(0, ctx, ROW)
    previous = shifted(carried, "ctx", ROW)
    arrived = [previous]
    for distance in range(reach - 1, 0, -1):
        arrived.append(
            lax.ppermute(
                jnp.where(place_z + distance < ROW, carried, previous),
                "ctx",
                [(line + z, line + (z + distance) % ROW) for line in lines for z in range(ROW)],
            )
        )

    cosine, sine = rotary_tables(span, (ctx_index - reach) * rows)
    route_own = routes[0]
    expert_ids = jnp.arange(experts, dtype=jnp.int32)
    hits = route_own[:, :, None] == expert_ids[None, None, :]
    member = jnp.sum(hits.astype(jnp.int32), axis=1)
    ranking = jnp.cumsum(member, axis=0, dtype=jnp.int32) - 1
    slot_ids = jnp.arange(capacity, dtype=jnp.int32)
    placed = (member[:, :, None] > 0) & (ranking[:, :, None] == slot_ids[None, None, :])
    take = placed.astype(BF).reshape(rows, slots)
    put = take.T
    selector = (
        (hits[:, :, :, None] & placed[:, None, :, :]).astype(BF).reshape(rows, TOPK * slots)
    )
    picked = jnp.pad(
        hits.astype(F32).transpose(1, 0, 2), ((0, 0), (0, 0), (0, LANES - experts))
    )
    lane = jnp.arange(LANES, dtype=jnp.int32)[None, :]
    own_lanes = ((lane == ctx_index) | (lane == ctx_index + LANES // 2)).astype(F32)
    g_to_slots = dot(put, g).astype(BF)

    small = jnp.concatenate(
        [w_router, attn_gain[:, None], ffn_gain[:, None], jnp.zeros((own, LANES - experts - 2), BF)],
        axis=1,
    )
    projections = jnp.concatenate([w_qkv, w_out], axis=1)
    width = projections.shape[1] // fsdp
    near = lax.all_to_all(
        jnp.concatenate(
            [
                projections.reshape(own, fsdp, width).transpose(1, 0, 2),
                jnp.broadcast_to(small, (fsdp, own, LANES)),
                shared_in.reshape(own, 2, ctx, fsdp, owned_down)
                .transpose(3, 0, 1, 2, 4)
                .reshape(fsdp, own, 2 * TILE),
            ],
            axis=2,
        ),
        "fsdp",
        split_axis=0,
        concat_axis=0,
        tiled=True,
    ).reshape(fsdp * own, -1)

    def to_ctx(values):
        return lax.all_to_all(
            jnp.broadcast_to(values, (ctx, *values.shape)), "ctx", split_axis=0, concat_axis=0, tiled=True
        )

    g_all = lax.all_gather(g, "fsdp", axis=0)
    columns = model // TILE
    dense = to_ctx(near[:, :width]).reshape(model, width)
    w_full = lax.all_gather(after(dense, g_all, cosine, sine, g_to_slots, picked, previous), "fsdp", axis=0)
    small_full = to_ctx(after(near[:, width : width + LANES], dense)).reshape(model, LANES)
    down_own = shared_down.reshape(owned_down, columns, TILE).transpose(1, 0, 2).reshape(-1, TILE)
    place = ctx_index.astype(jnp.int32).reshape(1)
    place_spec = pl.BlockSpec(memory_space=pltpu.SMEM)
    in_rows, down_rows = expert_in.shape[1], expert_down.shape[1]
    expert_packed = jnp.concatenate(
        [
            expert_in[0].reshape(in_rows, 2 * tiles, TILE).transpose(1, 0, 2).reshape(-1, TILE),
            expert_down[0].reshape(down_rows, model // TILE, TILE).transpose(1, 0, 2).reshape(-1, TILE),
        ],
        axis=0,
    )
    expert_full = lax.all_gather(after(expert_packed, w_full, small_full, *arrived), "fsdp", axis=0)

    def exchange(values):
        return lax.all_to_all(
            values.reshape(ctx, values.shape[0] // ctx, values.shape[1]),
            "ctx",
            split_axis=0,
            concat_axis=0,
            tiled=True,
        ).reshape(values.shape)


    slot_g = exchange(after(g_to_slots, *arrived))

    pairs = model // LANES
    small_spec = whole(small_full)
    parts = model // width
    at_a_time = width // LANES

    def columns_of(which):
        return pl.BlockSpec((1, model, width), lambda j: (which * parts + j, 0, 0))

    def wide_spec(height):
        return pl.BlockSpec((height, width), lambda j: (0, j))

    blocks = [*arrived, carried]
    pair_spec = lambda height: pl.BlockSpec((height, LANES), lambda j: (0, j))
    q, k, kt, v, e, rl, rlb, attended, span_scale = pl.pallas_call(
        functools.partial(attend_kernel, gain_lane=experts, parts=reach + 1),
        grid=(parts,),
        in_specs=[
            place_spec,
            *[whole(block) for block in blocks],
            small_spec,
            columns_of(0),
            columns_of(1),
            columns_of(2),
            whole(cosine),
            whole(sine),
        ],
        out_specs=[
            wide_spec(rows),
            wide_spec(span),
            pl.BlockSpec((width, span), lambda j: (j, 0)),
            wide_spec(span),
            pl.BlockSpec((2 * at_a_time, span, rows), lambda j: (j, 0, 0)),
            pl.BlockSpec((at_a_time, 8, rows), lambda j: (j, 0, 0)),
            wide_spec(rows),
            wide_spec(rows),
            pl.BlockSpec((span, 1), lambda j: (0, 0)),
        ],
        out_shape=[
            jax.ShapeDtypeStruct((rows, model), BF),
            jax.ShapeDtypeStruct((span, model), BF),
            jax.ShapeDtypeStruct((model, span), BF),
            jax.ShapeDtypeStruct((span, model), BF),
            jax.ShapeDtypeStruct((HEADS, span, rows), BF),
            jax.ShapeDtypeStruct((pairs, 8, rows), F32),
            jax.ShapeDtypeStruct((rows, model), F32),
            jax.ShapeDtypeStruct((rows, model), BF),
            jax.ShapeDtypeStruct((span, 1), F32),
        ],
        scratch_shapes=[
            pltpu.VMEM((span, model), BF),
            pltpu.VMEM((2, span, rows), F32),
            pltpu.VMEM((width, span), BF),
            pltpu.VMEM((span, rows), F32),
        ],
        compiler_params=params(VMEM_MB),
        cost_estimate=cost(20),
        name="attend",
    )(place, *blocks, small_full, w_full, w_full, w_full, cosine, sine)

    out_spec = pl.BlockSpec((parts, model, width), lambda *_: (3, 0, 0))
    hidden, scale_two, normed, normed_t, outgoing, gates, gain_two = pl.pallas_call(
        functools.partial(middle_kernel, gain_lane=experts + 1),
        grid=(1,),
        in_specs=[
            whole(attended),
            out_spec,
            small_spec,
            whole(x),
            whole(picked),
            whole(put),
        ],
        out_specs=[
            pl.BlockSpec((rows, model), lambda *_: (0, 0)),
            pl.BlockSpec((rows, 1), lambda *_: (0, 0)),
            pl.BlockSpec((rows, model), lambda *_: (0, 0)),
            pl.BlockSpec((model, rows), lambda *_: (0, 0)),
            pl.BlockSpec((slots, model + LANES), lambda *_: (0, 0)),
            pl.BlockSpec((rows, LANES), lambda *_: (0, 0)),
            pl.BlockSpec((1, model), lambda *_: (0, 0)),
        ],
        out_shape=[
            jax.ShapeDtypeStruct((rows, model), F32),
            jax.ShapeDtypeStruct((rows, 1), F32),
            jax.ShapeDtypeStruct((rows, model), BF),
            jax.ShapeDtypeStruct((model, rows), BF),
            jax.ShapeDtypeStruct((slots, model + LANES), BF),
            jax.ShapeDtypeStruct((rows, LANES), F32),
            jax.ShapeDtypeStruct((1, model), F32),
        ],
        compiler_params=params(VMEM_MB),
        cost_estimate=cost(5),
        name="middle",
    )(attended, w_full, small_full, x, picked, put)
    normed_all = lax.all_gather(normed, "fsdp", axis=0)
    incoming = exchange(after(outgoing, slot_g))
    narrow = after(near, outgoing)
    shared_own_w = jnp.concatenate(
        [narrow[:, width + LANES : -TILE], narrow[:, -TILE:], down_own], axis=0
    )
    shared_full = to_ctx(after(shared_own_w, incoming))
    gain_one = small_full[:, experts : experts + 1].astype(F32)
    span_x = jnp.concatenate(
        [block[:rows] for block in lax.optimization_barrier((*blocks, outgoing))[:-1]], axis=0
    )
    first_t = (span_x.T.astype(F32) * span_scale.reshape(1, span) * gain_one).astype(BF)
    incoming = after(incoming, first_t)

    packed_rows = 3 * model

    steps = tiles // AT_ONCE
    expert_specs = [
        pl.BlockSpec((fsdp, AT_ONCE * in_rows, TILE), lambda t: (0, t, 0)),
        pl.BlockSpec((fsdp, AT_ONCE * in_rows, TILE), lambda t: (0, steps + t, 0)),
        pl.BlockSpec((AT_ONCE, model, TILE), lambda t: (t, 2 * in_rows * tiles // model, 0)),
    ]
    unit_spec = pl.BlockSpec((1, slots, AT_ONCE * TILE), lambda t: (t, 0, 0))
    expert_y, *units = pl.pallas_call(
        expert_kernel,
        grid=(steps,),
        in_specs=[whole(incoming), *expert_specs],
        out_specs=[
            pl.BlockSpec((slots, model), lambda t: (0, 0)),
            unit_spec,
            unit_spec,
            unit_spec,
        ],
        out_shape=[jax.ShapeDtypeStruct((slots, model), BF)]
        + [jax.ShapeDtypeStruct((steps, slots, AT_ONCE * TILE), BF)] * 3,
        scratch_shapes=[pltpu.VMEM((slots, model), F32)],
        compiler_params=params(VMEM_MB),
        cost_estimate=cost(60),
        name="expert",
    )(incoming, expert_full, expert_full, expert_full)
    returned_y = exchange(after(expert_y, shared_full))

    at_once = 2
    block = model // ctx
    shared_part, shared_pieces = pl.pallas_call(
        shared_kernel,
        grid=(fsdp // at_once,),
        in_specs=[
            pl.BlockSpec((at_once, rows, model), lambda t: (t, 0, 0)),
            pl.BlockSpec((at_once, rows, model), lambda t: (t, 0, 0)),
            whole(shared_full),
        ],
        out_specs=[
            pl.BlockSpec((at_once, rows, 2 * model), lambda t: (t, 0, 0)),
            whole(shared_full),
        ],
        out_shape=[
            jax.ShapeDtypeStruct((fsdp, rows, 2 * model), BF),
            jax.ShapeDtypeStruct(shared_full.shape, BF),
        ],
        scratch_shapes=[pltpu.VMEM((model, 2 * TILE), F32), pltpu.VMEM((TILE, model), F32)],
        compiler_params=params(VMEM_MB),
        cost_estimate=cost(18),
        name="shared",
    )(after(normed_all, expert_y), g_all, shared_full)
    shared_both = lax.psum_scatter(after(shared_part, returned_y), "fsdp", scatter_dimension=0)
    shared_own = jnp.sum(
        lax.all_to_all(
            after(shared_pieces, returned_y), "ctx", split_axis=0, concat_axis=0, tiled=True
        ).astype(F32),
        axis=0,
    )
    back, gexpert = pl.pallas_call(
        expert_back_kernel,
        grid=(steps,),
        in_specs=[
            whole(incoming),
            whole(slot_g),
            whole(own_lanes),
            *expert_specs,
            unit_spec,
            unit_spec,
            unit_spec,
        ],
        out_specs=[
            pl.BlockSpec((slots, model), lambda t: (0, 0)),
            pl.BlockSpec(memory_space=pl.ANY),
        ],
        out_shape=[
            jax.ShapeDtypeStruct((slots, model), BF),
            jax.ShapeDtypeStruct((fsdp, packed_rows, TILE), BF),
        ],
        scratch_shapes=[
            pltpu.VMEM((model, slots), BF),
            pltpu.VMEM((slots, model), BF),
            pltpu.VMEM((slots, model), F32),
            pltpu.VMEM((2, 2, fsdp, AT_ONCE * in_rows, TILE), BF),
            pltpu.VMEM((2, AT_ONCE, model, TILE), BF),
            pltpu.SemaphoreType.DMA((2, 3)),
        ],
        compiler_params=params(VMEM_MB),
        cost_estimate=cost(22),
        name="expert_back",
    )(after(incoming, shared_part, returned_y), slot_g, own_lanes, expert_full, expert_full, expert_full, *units)
    returned = exchange(after(back, shared_own))
    expert_sum = lax.psum_scatter(after(gexpert, shared_own), "fsdp", scatter_dimension=0)

    mixed, dgates = pl.pallas_call(
        combine_kernel,
        grid=(1,),
        in_specs=[
            pl.BlockSpec((slots, model), lambda *_: (0, 0)),
            pl.BlockSpec((rows, slots), lambda *_: (0, 0)),
            pl.BlockSpec((rows, slots), lambda *_: (0, 1)),
            whole(picked),
            whole(gates),
            whole(hidden),
            pl.BlockSpec((rows, model), lambda *_: (0, 0)),
            whole(g),
        ],
        out_specs=[
            pl.BlockSpec((1, rows, model), lambda *_: (0, 0, 0)),
            pl.BlockSpec((rows, LANES), lambda *_: (0, 0)),
        ],
        out_shape=[
            jax.ShapeDtypeStruct((1, rows, model), BF),
            jax.ShapeDtypeStruct((rows, LANES), F32),
        ],
        compiler_params=params(VMEM_MB),
        cost_estimate=cost(3),
        name="combine",
    )(returned_y, selector, selector, picked, gates, hidden, shared_both, g)

    returned = after(returned, dgates)

    dhidden, dhidden_low, dattended, dlogits, ggain_two = pl.pallas_call(
        middle_back_kernel,
        grid=(1,),
        in_specs=[
            whole(returned),
            whole(dgates),
            whole(take),
            whole(gates),
            small_spec,
            pl.BlockSpec((rows, model), lambda *_: (0, 1)),
            whole(g),
            whole(hidden),
            whole(scale_two),
            whole(gain_two),
            out_spec,
        ],
        out_specs=[
            pl.BlockSpec((rows, model), lambda *_: (0, 0)),
            pl.BlockSpec((rows, model), lambda *_: (0, 0)),
            pl.BlockSpec((rows, model), lambda *_: (0, 0)),
            pl.BlockSpec((rows, LANES), lambda *_: (0, 0)),
            pl.BlockSpec((1, model), lambda *_: (0, 0)),
        ],
        out_shape=[
            jax.ShapeDtypeStruct((rows, model), F32),
            jax.ShapeDtypeStruct((rows, model), BF),
            jax.ShapeDtypeStruct((rows, model), BF),
            jax.ShapeDtypeStruct((rows, LANES), BF),
            jax.ShapeDtypeStruct((1, model), F32),
        ],
        compiler_params=params(VMEM_MB),
        cost_estimate=cost(6),
        name="middle_back",
    )(
        returned, dgates, take, gates, small_full, shared_both, g, hidden, scale_two, gain_two, w_full
    )

    grouter = dot(normed_t, dlogits)
    small_grads = jnp.concatenate(
        [grouter[:, :experts], ggain_two.T, jnp.zeros((model, LANES - experts - 1), F32)], axis=1
    ).astype(BF)
    attended_t = attended.T
    core_scalar = core.astype(jnp.int32).reshape(1)

    def attend_back(first, count, down, *filled):
        pair_from = lambda height: pl.BlockSpec((height, LANES), lambda j: (0, first + j))
        operands = (
            core_scalar, q, k, kt, v, e, rl, rlb, down, cosine, sine, first_t, attended_t, dhidden_low, *filled,
        )
        return pl.pallas_call(
            attend_back_kernel,
            grid=(count,),
            in_specs=[
                place_spec,
                pair_from(rows),
                pair_from(span),
                pl.BlockSpec((LANES, span), lambda j: (first + j, 0)),
                pair_from(span),
                pl.BlockSpec((2, span, rows), lambda j: (first + j, 0, 0)),
                pl.BlockSpec((1, 8, rows), lambda j: (first + j, 0, 0)),
                pair_from(rows),
                pair_from(rows),
                whole(cosine),
                whole(sine),
                whole(first_t),
                whole(attended_t),
                pair_from(rows),
            ]
            + [pl.BlockSpec(memory_space=pl.ANY)] * len(filled),
            out_specs=[
                pair_from(rows),
                pair_from(span),
                pair_from(span),
                pl.BlockSpec((model, 2 * LANES), lambda j: (0, j)),
                pl.BlockSpec((model, 2 * LANES), lambda j: (0, j)),
            ],
            out_shape=[
                jax.ShapeDtypeStruct((rows, model), BF),
                jax.ShapeDtypeStruct((span, model), BF),
                jax.ShapeDtypeStruct((span, model), BF),
                jax.ShapeDtypeStruct((model, count * 2 * LANES), BF),
                jax.ShapeDtypeStruct((model, count * 2 * LANES), BF),
            ],
            input_output_aliases={
                len(operands) - len(filled) + index: index for index in range(len(filled))
            },
            scratch_shapes=[
                pltpu.VMEM((2, span, rows), F32),
                pltpu.VMEM((2, span, rows), BF),
                pltpu.VMEM((span, LANES), F32),
                pltpu.VMEM((span, LANES), F32),
            ],
            compiler_params=params(VMEM_MB),
            cost_estimate=cost(12 * count),
            name=f"attend_back_{first}",
        )(*operands)


    def paired_columns(kept, sent):
        partner = lax.ppermute(sent, "fsdp", [(i, i ^ 1) for i in range(fsdp)])
        return (kept.astype(F32) + partner.astype(F32)).astype(BF)

    def along_ctx(pieces):
        return lax.all_to_all(pieces, "ctx", split_axis=0, concat_axis=0, tiled=True)

    early_pairs = 2 * pairs // 3
    *grads_a, kept_a, sent_a = attend_back(0, early_pairs, dattended)
    paired_a = paired_columns(kept_a, sent_a)
    late_a = along_ctx(paired_a.reshape(ctx, block, -1))
    dq, dk, dv, kept_b, sent_b = attend_back(
        early_pairs, pairs - early_pairs, after(dattended, paired_a), *grads_a
    )
    paired_b = paired_columns(kept_b, sent_b)

    dspan, down = pl.pallas_call(
        project_back_kernel,
        grid=(2,),
        in_specs=[
            whole(dq),
            pl.BlockSpec((span // 2, model), lambda b: (b, 0)),
            pl.BlockSpec((span // 2, model), lambda b: (b, 0)),
            pl.BlockSpec((3 * parts, model, width), lambda b: (0, 0, 0)),
        ],
        out_specs=[
            pl.BlockSpec((span // 2, model), lambda b: (b, 0)),
            pl.BlockSpec((rows, model), lambda b: (0, 0)),
        ],
        out_shape=[
            jax.ShapeDtypeStruct((span, model), BF),
            jax.ShapeDtypeStruct((rows, model), F32),
        ],
        compiler_params=params(VMEM_MB),
        scratch_shapes=[pltpu.VMEM((model, 3 * model), BF)],
        cost_estimate=cost(8),
        name="project_back",
    )(dq, dk, dv, w_full)
    total, passed = down, dspan[:rows].astype(F32)
    for distance in range(1, reach):
        lower = (reach - distance) * rows
        moved = lax.ppermute(
            dspan[lower : lower + rows],
            "ctx",
            [(line + z, line + (z - distance) % ROW) for line in lines for z in range(ROW)],
        )
        moved = moved.astype(F32)
        here = place_z + distance < ROW
        total = total + jnp.where(here, moved, 0.0)
        passed = passed + jnp.where(here, 0.0, moved)
    grad_expert_in, grad_expert_down = pl.pallas_call(
        widen_kernel,
        grid=(1,),
        in_specs=[whole(expert_sum)],
        out_specs=[
            pl.BlockSpec((1, in_rows, 2 * ff), lambda *_: (0, 0, 0)),
            pl.BlockSpec((1, down_rows, model), lambda *_: (0, 0, 0)),
        ],
        out_shape=[
            jax.ShapeDtypeStruct((1, in_rows, 2 * ff), F32),
            jax.ShapeDtypeStruct((1, down_rows, model), F32),
        ],
        compiler_params=params(VMEM_MB),
        cost_estimate=cost(2),
        name="widen",
    )(expert_sum)
    late_a = jnp.sum(late_a.astype(F32), axis=0)
    quarter = paired_b.shape[1] // (fsdp // 2)
    late_b = lax.all_to_all(
        after(
            paired_b.reshape(model, fsdp // 2, quarter).transpose(1, 0, 2),
            down, late_a,
        ),
        "fsdp",
        split_axis=0,
        concat_axis=0,
        axis_index_groups=[list(range(start, fsdp, 2)) for start in range(2)],
        tiled=True,
    )
    late_b = jnp.sum(late_b.astype(F32), axis=0).astype(BF)
    received = shifted(after(passed.astype(BF), late_b), "ctx", -ROW)
    late_b = along_ctx(jnp.concatenate([late_b, small_grads], axis=1).reshape(ctx, block, -1))

    grad_shared_down = (
        shared_own[2 * block :]
        .reshape(columns, owned_down, TILE)
        .transpose(1, 0, 2)
        .reshape(owned_down, model)
    )
    packed_width = late_a.shape[1] + late_b.shape[2] + 2 * TILE
    last = pl.pallas_call(
        functools.partial(pack_kernel, block=block),
        grid=(1,),
        in_specs=[
            whole(late_a),
            whole(late_b),
            pl.BlockSpec((2 * block, TILE), lambda *_: (0, 0)),
        ],
        out_specs=pl.BlockSpec((fsdp, own, packed_width), lambda *_: (0, 0, 0)),
        out_shape=jax.ShapeDtypeStruct((fsdp, own, packed_width), BF),
        compiler_params=params(VMEM_MB),
        cost_estimate=cost(2),
        name="pack",
    )(late_a, late_b, shared_own)
    last = lax.all_to_all(last, "fsdp", split_axis=0, concat_axis=0, tiled=True)
    last = after(last, received, grad_expert_in, grad_expert_down)
    wanted = [
        jax.ShapeDtypeStruct((own, 3 * model), F32),
        jax.ShapeDtypeStruct((own, model), F32),
        jax.ShapeDtypeStruct((own, experts), F32),
        jax.ShapeDtypeStruct((1, own), F32),
        jax.ShapeDtypeStruct((1, own), F32),
        jax.ShapeDtypeStruct((own, 2 * ff), F32),
    ]
    gain_own = attn_gain.astype(F32)[:, None]
    grad_qkv, grad_out, grad_router, grad_gain_one, grad_gain_two, grad_shared_in = pl.pallas_call(
        functools.partial(unpack_kernel, piece=owned_down),
        grid=(1,),
        in_specs=[whole(last), whole(w_qkv), whole(gain_own)],
        out_specs=[whole(array) for array in wanted],
        out_shape=wanted,
        compiler_params=params(VMEM_MB),
        cost_estimate=cost(2),
        name="unpack",
    )(last, w_qkv, gain_own)

    total = total + received.astype(F32)
    input_rows = x.astype(F32)
    scale_one = span_scale[reach * rows :]
    weighted = total * gain_one.reshape(1, model)
    input_grad = (
        dhidden
        + scale_one * weighted
        - input_rows
        * scale_one**3
        * jnp.mean(weighted * input_rows, axis=-1, keepdims=True)
    )[None]

    return (
        mixed,
        input_grad,
        grad_qkv,
        grad_out,
        grad_router,
        grad_shared_in,
        grad_shared_down,
        grad_gain_one.reshape(own),
        grad_gain_two.reshape(own),
        grad_expert_in,
        grad_expert_down,
    )


def solution(mesh):
    placed = (
        P("fsdp", "ctx", None),
        P("fsdp", "ctx"),
        P("fsdp", "ctx", None),
        P(("ctx", "fsdp"), None),
        P(("ctx", "fsdp"), None),
        P(("ctx", "fsdp"), None),
        P(("ctx", "fsdp"), None),
        P(("ctx", "fsdp"), None),
        P(("ctx", "fsdp")),
        P(("ctx", "fsdp")),
        P("ctx", "fsdp", None),
        P("ctx", "fsdp", None),
        P("fsdp", "ctx", None),
    )
    return jax.shard_map(
        per_device,
        mesh=mesh,
        in_specs=placed,
        out_specs=(
            P("fsdp", "ctx", None),
            P("fsdp", "ctx", None),
            P(("ctx", "fsdp"), None),
            P(("ctx", "fsdp"), None),
            P(("ctx", "fsdp"), None),
            P(("ctx", "fsdp"), None),
            P(("ctx", "fsdp"), None),
            P(("ctx", "fsdp")),
            P(("ctx", "fsdp")),
            P("ctx", "fsdp", None),
            P("ctx", "fsdp", None),
        ),
        check_vma=False,
    )
```

```python
import functools

import jax
import jax.numpy as jnp
from jax import lax
from jax.experimental import pallas as pl
from jax.experimental.pallas import tpu as pltpu
from jax.sharding import PartitionSpec as P

HEADS = 12
HEAD_DIM = 64
TOPK = 2
WIN = 1024
EPSILON = 1e-06

BF = jnp.bfloat16
F32 = jnp.float32
TILE = 256
LANES = 128
IN_ROWS = 96
AT_ONCE = 2
KEY_BLOCK = 128
ROW = 4
VMEM_MB = 60


def dot(a, b):
    return jnp.dot(a, b, preferred_element_type=F32)


def dot_nt(a, b):
    return lax.dot_general(a, b, (((1,), (1,)), ((), ())), preferred_element_type=F32)


def dot_tn(a, b):
    return lax.dot_general(a, b, (((0,), (0,)), ((), ())), preferred_element_type=F32)


def params(megabytes):
    return pltpu.CompilerParams(vmem_limit_bytes=megabytes * 1024 * 1024)


def cost(microseconds):
    return pl.CostEstimate(
        flops=int(microseconds * 1.0e9), bytes_accessed=int(microseconds * 1.0e6), transcendentals=0
    )


def after(value, *others):
    return lax.optimization_barrier((value, *others))[0]


def whole(array):
    return pl.BlockSpec(array.shape, lambda *_: (0,) * array.ndim)


def shifted(value, axis, steps):
    count = lax.axis_size(axis)
    leading, last = (max(0, -steps), min(count, count - steps))
    return lax.ppermute(value, axis, [(source, source + steps) for source in range(leading, last)])


def split_high_low(values):
    high = values.astype(BF)
    return high, (values - high.astype(F32)).astype(BF)


def rotary_tables(rows, offset):
    half = HEAD_DIM // 2
    frequency = jnp.exp(-jnp.log(10000.0) * (2.0 * jnp.arange(half, dtype=F32) / HEAD_DIM))
    places = (offset + jnp.arange(rows, dtype=jnp.int32)).astype(F32)
    angles = places[:, None] * frequency[None, :]
    cosine, sine = jnp.cos(angles), jnp.sin(angles)
    return (
        jnp.concatenate([cosine] * 4, axis=1),
        jnp.concatenate([-sine, sine, -sine, sine], axis=1),
    )


def swapped_halves(values):
    width, half = values.shape[1], HEAD_DIM // 2
    lane = lax.broadcasted_iota(jnp.int32, (1, width), 1)
    return jnp.where(
        lane % HEAD_DIM < half,
        pltpu.roll(values, width - half, 1),
        pltpu.roll(values, half, 1),
    )


def head_lanes(values, head):
    lane = lax.broadcasted_iota(jnp.int32, (1, LANES), 1)
    return jnp.where(lane // HEAD_DIM == head, values, jnp.zeros_like(values))


def fold_rows(values, op):
    return op(values.reshape(values.shape[0] // 8, 8, values.shape[1]), axis=0)


def attend_kernel(
    place_ref, *refs, gain_lane, parts
):
    blocks, refs = refs[:parts], refs[parts:]
    (
        small_ref, wq_ref, wk_ref, wv_ref, cos_ref, sin_ref,
        q_ref, k_ref, kt_ref, v_ref, e_ref, rl_ref, rlb_ref, o_ref, scale_ref,
        normed, score, vt, bias_ref,
    ) = refs
    rows, model = q_ref.shape[0], normed.shape[1]
    span = parts * rows

    @pl.when(pl.program_id(0) == 0)
    def _():
        gain = small_ref[...].astype(F32).T[gain_lane : gain_lane + 1, :]
        query_segment = blocks[-1][rows : rows + 1, :rows].astype(F32)
        query_place = lax.broadcasted_iota(jnp.int32, (rows, rows), 1)
        key_place = lax.broadcasted_iota(jnp.int32, (rows, rows), 0)
        for index, block in enumerate(blocks):
            part = pl.ds(index * rows, rows)
            values = block[:rows, :].astype(F32)
            scale = lax.rsqrt(jnp.mean(values * values, axis=-1, keepdims=True) + EPSILON)
            scale_ref[part, :] = scale
            normed[part, :] = (values * scale * gain).astype(BF)
            key_segment = block[rows : rows + 16, :rows].astype(F32).T[:, :1]
            distance = query_place - key_place + (parts - 1 - index) * rows
            allowed = (distance >= 0) & (distance < WIN) & (key_segment == query_segment)
            allowed = allowed & (place_ref[0] >= parts - 1 - index)
            bias_ref[part, :] = jnp.where(allowed, 0.0, -1e30)

    wide = q_ref.shape[1]
    cosine = jnp.concatenate([cos_ref[...]] * (wide // LANES), axis=1)
    sine = jnp.concatenate([sin_ref[...]] * (wide // LANES), axis=1)
    pair = dot(normed[...], jnp.concatenate([wk_ref[0], wv_ref[0]], axis=1))
    keys = pair[:, :wide]
    keys = keys * cosine + swapped_halves(keys) * sine
    k_ref[...] = keys.astype(BF)
    kt_ref[...] = keys.T.astype(BF)
    queries = dot(normed[span - rows :, :], wq_ref[0])
    queries = queries * cosine[span - rows :] + swapped_halves(queries) * sine[span - rows :]
    queries = (queries.astype(BF).astype(F32) * HEAD_DIM**-0.5).astype(BF)
    q_ref[...] = queries
    heads = wide // HEAD_DIM

    def chunk(head):
        return slice(head // 2 * LANES, (head // 2 + 1) * LANES)

    own = [head_lanes(queries[:, chunk(head)], head % 2) for head in range(heads)]
    largest = [jnp.full((8, rows), -3e38, F32) for _ in range(heads)]
    total = [jnp.zeros((8, rows), F32) for _ in range(heads)]

    def scores(head, part):
        block = dot_nt(k_ref[part, chunk(head)], own[head]) + bias_ref[part, :]
        score[head % 2, part, :] = block
        largest[head] = jnp.maximum(largest[head], fold_rows(block, jnp.max))

    def weights(head, part):
        block = jnp.exp(score[head % 2, part, :] - largest[head])
        total[head] = total[head] + fold_rows(block, jnp.sum)
        e_ref[head, part, :] = block.astype(BF)

    blocks_of_keys = [pl.ds(start, KEY_BLOCK) for start in range(0, span, KEY_BLOCK)]
    for part in blocks_of_keys:
        scores(0, part)
    values = pair[:, wide:]
    v_ref[...] = values.astype(BF)
    vt[...] = values.T.astype(BF)
    outs, sums = [], []
    for head in range(heads):
        largest[head] = jnp.max(largest[head], axis=0, keepdims=True)
        for part in blocks_of_keys:
            weights(head, part)
            if head + 1 < heads:
                scores(head + 1, part)
        inverse = 1.0 / jnp.sum(total[head], axis=0, keepdims=True)
        rl_ref[head // 2, head % 2 : head % 2 + 1, :] = inverse
        outs.append(dot(vt[head * HEAD_DIM : (head + 1) * HEAD_DIM, :], e_ref[head]) * inverse)
        sums.append(jnp.broadcast_to(inverse, (HEAD_DIM, rows)))
    o_ref[...] = jnp.concatenate(outs, axis=0).T.astype(BF)
    rlb_ref[...] = jnp.concatenate(sums, axis=0).T


def attend_back_kernel(
    core_ref, q_ref, k_ref, kt_ref, v_ref, e_ref, rl_ref, rlb_ref, do_ref, cos_ref, sin_ref, xt_ref, ot_ref, dh_ref,
    *refs,
):
    dq_ref, dk_ref, dv_ref, kept_ref, sent_ref, dprob, dscore, dk, dv = refs[-9:]
    span, rows = k_ref.shape[0], q_ref.shape[0]
    scaled = do_ref[...].astype(F32) * rlb_ref[...]
    heads = range(2)
    down = [head_lanes(scaled, head).astype(BF) for head in heads]
    own = [head_lanes(q_ref[...], head) for head in heads]
    own_both, down_both = jnp.concatenate(own, axis=0), jnp.concatenate(down, axis=0)
    inner = [jnp.zeros((8, rows), F32) for _ in heads]
    for start in range(0, span, KEY_BLOCK):
        part = pl.ds(start, KEY_BLOCK)
        for head in heads:
            block = dot_nt(v_ref[part, :], down[head])
            dprob[head, part, :] = block
            inner[head] = inner[head] + fold_rows(block * e_ref[head, part, :].astype(F32), jnp.sum)
    inner = [
        jnp.sum(inner[head], axis=0, keepdims=True) * rl_ref[0, head : head + 1, :]
        for head in heads
    ]
    for start in range(0, span, KEY_BLOCK):
        part = pl.ds(start, KEY_BLOCK)
        for head in heads:
            weight = e_ref[head, part, :]
            block = (weight.astype(F32) * (dprob[head, part, :] - inner[head])).astype(BF)
            dscore[head, part, :] = block
        dk[part, :] = dot(
            jnp.concatenate([dscore[head, part, :] for head in heads], axis=1), own_both
        )
        dv[part, :] = dot(
            jnp.concatenate([e_ref[head, part, :] for head in heads], axis=1), down_both
        )
    dqs = [
        dot(kt_ref[head * HEAD_DIM : (head + 1) * HEAD_DIM, :], dscore[head]) for head in heads
    ]
    dquery = jnp.concatenate(dqs, axis=0).T * HEAD_DIM**-0.5
    dquery = dquery * cos_ref[span - rows :, :] - swapped_halves(dquery) * sin_ref[span - rows :, :]
    dquery = dquery.astype(BF)
    dq_ref[...] = dquery
    dkeys = dk[...]
    dkeys = (dkeys * cos_ref[...] - swapped_halves(dkeys) * sin_ref[...]).astype(BF)
    dvalues = dv[...].astype(BF)
    dk_ref[...] = dkeys
    dv_ref[...] = dvalues
    first = dot(xt_ref[...], jnp.concatenate([dkeys, dvalues], axis=1)).astype(BF)
    second = jnp.concatenate(
        [dot(xt_ref[:, span - rows :], dquery), dot(ot_ref[...], dh_ref[...])], axis=1
    ).astype(BF)
    kept_ref[...] = jnp.where(core_ref[0] == 0, first, second)
    sent_ref[...] = jnp.where(core_ref[0] == 0, second, first)


def middle_kernel(
    o_ref, w_ref, small_ref, x_ref, pick_ref, put_ref,
    h_ref, scale_ref, a_ref, at_ref, out_ref, gate_ref, gain_ref,
    *, gain_lane,
):
    projected = jnp.concatenate([dot(o_ref[...], w_ref[part]) for part in range(2)], axis=1)
    hidden = x_ref[...].astype(F32) + projected
    h_ref[...] = hidden
    scale = lax.rsqrt(jnp.mean(hidden * hidden, axis=-1, keepdims=True) + EPSILON)
    scale_ref[...] = scale
    small = small_ref[...]
    gain = small.astype(F32).T[gain_lane : gain_lane + 1, :]
    gain_ref[...] = gain
    low = (hidden * scale * gain).astype(BF)
    a_ref[...] = low
    at_ref[...] = low.astype(F32).T.astype(BF)
    logits = dot(low, small)
    first, second = pick_ref[0], pick_ref[1]
    chosen_first = jnp.sum(logits * first, axis=-1, keepdims=True)
    chosen_second = jnp.sum(logits * second, axis=-1, keepdims=True)
    largest = jnp.maximum(chosen_first, chosen_second)
    chosen_first = jnp.exp(chosen_first - largest)
    chosen_second = jnp.exp(chosen_second - largest)
    total = chosen_first + chosen_second
    table = (chosen_first / total) * first + (chosen_second / total) * second
    gate_ref[...] = table
    high, rest = split_high_low(table)
    extra = (high.astype(F32) + pltpu.roll(rest.astype(F32), LANES // 2, 1)).astype(BF)
    put = put_ref[...]
    width = a_ref.shape[1]
    out_ref[:, :width] = dot(put, low).astype(BF)
    out_ref[:, width:] = dot(put, extra).astype(BF)


def gated_forward(x, w_gate, w_lift):
    gate, lift = dot(x, w_gate), dot(x, w_lift)
    sigmoid = 1.0 / (1.0 + jnp.exp(-gate))
    act = gate * sigmoid
    slope = sigmoid + (act - act * sigmoid)
    return (act * lift).astype(BF), act, lift * slope


def add_up(total_ref, value):
    first = pl.program_id(0) == 0
    total_ref[...] = value + jnp.where(first, 0.0, total_ref[...])


def flush(step, steps, copies):
    @pl.when(step >= 2)
    def _():
        for copy in copies(step % 2, step):
            copy.wait()


def send(step, steps, copies):
    for copy in copies(step % 2, step):
        copy.start()

    @pl.when(step == steps - 1)
    def _():
        for copy in copies((step + 1) % 2, step):
            copy.wait()
        for copy in copies(step % 2, step):
            copy.wait()


def shared_kernel(
    x_ref, dy_ref, w_ref, out_ref, pieces_ref, gin_sum, gdown_sum
):
    count, rows, model = x_ref.shape
    block, columns = model // w_ref.shape[0], model // TILE
    piece = (w_ref.shape[1] - 2 * block) // columns
    x, dy = x_ref[...].reshape(count * rows, model), dy_ref[...].reshape(count * rows, model)
    w_gate = w_ref[:, :block, :].reshape(model, TILE)
    w_lift = w_ref[:, block : 2 * block, :].reshape(model, TILE)
    w_down = jnp.concatenate(
        [
            w_ref[:, start : start + piece, :].reshape(-1, TILE)
            for start in range(2 * block, w_ref.shape[1], piece)
        ],
        axis=1,
    )
    hidden, act, slope = gated_forward(x, w_gate, w_lift)
    out_ref[:, :, :model] = dot(hidden, w_down).astype(BF).reshape(count, rows, model)
    dhidden = dot_nt(dy, w_down)
    both = jnp.concatenate([dhidden * slope, dhidden * act], axis=1).astype(BF)
    dx = dot_nt(both, jnp.concatenate([w_gate, w_lift], axis=1))
    out_ref[:, :, model:] = dx.astype(BF).reshape(count, rows, model)
    add_up(gin_sum, dot_tn(x, both))
    add_up(gdown_sum, dot_tn(hidden, dy))

    @pl.when(pl.program_id(0) == pl.num_programs(0) - 1)
    def _():
        for owner in range(pieces_ref.shape[0]):
            rows_in = pl.ds(owner * block, block)
            for part in range(2):
                pieces_ref[owner, part * block : (part + 1) * block, :] = gin_sum[
                    rows_in, part * TILE : (part + 1) * TILE
                ].astype(BF)
            rows_down = pl.ds(owner * piece, piece)
            for column in range(columns):
                start = 2 * block + column * piece
                pieces_ref[owner, start : start + piece, :] = gdown_sum[
                    rows_down, column * TILE : (column + 1) * TILE
                ].astype(BF)


def side_by_side(blocks):
    count = blocks.shape[1] // IN_ROWS
    return jnp.concatenate(
        [
            blocks[:, part * IN_ROWS : (part + 1) * IN_ROWS].reshape(-1, TILE)
            for part in range(count)
        ],
        axis=1,
    )


def unpack_down(packed, model):
    return jnp.concatenate(
        [
            jnp.concatenate(
                [packed[tile, start : start + TILE] for start in range(0, model, TILE)], axis=1
            )
            for tile in range(packed.shape[0])
        ],
        axis=0,
    )


def expert_kernel(
    in_ref, wg_ref, wl_ref, wd_ref, y_ref, hidden_ref, act_ref, slope_ref, y_sum
):
    model = y_ref.shape[1]
    w_gate, w_lift = side_by_side(wg_ref[...]), side_by_side(wl_ref[...])
    hidden, act, slope = gated_forward(in_ref[:, :model], w_gate, w_lift)
    hidden_ref[0] = hidden
    act_ref[0] = act.astype(BF)
    slope_ref[0] = slope.astype(BF)
    add_up(y_sum, dot(hidden, unpack_down(wd_ref[...], model)))

    @pl.when(pl.program_id(0) == pl.num_programs(0) - 1)
    def _():
        y_ref[...] = y_sum[...].astype(BF)


def expert_back_kernel(
    in_ref, g_ref, own_ref, wg_ref, wl_ref, wd_ref, hidden_ref, act_ref, slope_ref,
    dx_ref, grads_ref,
    xt, dy, dx_sum, gin, gdown, sems,
):
    model = g_ref.shape[1]
    step, steps = pl.program_id(0), pl.num_programs(0)
    in_rows, tiles = gin.shape[3], gdown.shape[1]

    def copies(slot, now):
        for part in range(2):
            first = pl.multiple_of((part * steps + now) * in_rows, in_rows)
            yield pltpu.make_async_copy(
                gin.at[slot, part], grads_ref.at[:, pl.ds(first, in_rows)], sems.at[slot, part]
            )
        yield pltpu.make_async_copy(
            gdown.at[slot],
            grads_ref.at[pl.ds(now * tiles, tiles), pl.ds(2 * steps * in_rows, model)],
            sems.at[slot, 2],
        )

    @pl.when(step == 0)
    def _():
        xt[...] = in_ref[:, :model].astype(F32).T.astype(BF)
        gate = jnp.sum(in_ref[:, model:].astype(F32) * own_ref[...], axis=-1, keepdims=True)
        dy[...] = (g_ref[...].astype(F32) * gate).astype(BF)

    flush(step, steps, copies)
    slot = step % 2
    w_gate, w_lift = side_by_side(wg_ref[...]), side_by_side(wl_ref[...])
    dhidden = dot_nt(dy[...], unpack_down(wd_ref[...], model)).astype(BF)
    both = jnp.concatenate([dhidden * slope_ref[0], dhidden * act_ref[0]], axis=1)
    add_up(dx_sum, dot_nt(both, jnp.concatenate([w_gate, w_lift], axis=1)))
    into = dot(xt[...], both).astype(BF)
    shape = (gin.shape[2], IN_ROWS, TILE)
    for part in range(2):
        for tile in range(tiles):
            column = (part * tiles + tile) * TILE
            gin[slot, part, :, tile * IN_ROWS : (tile + 1) * IN_ROWS, :] = into[
                :, column : column + TILE
            ].reshape(shape)
    down = dot_tn(hidden_ref[0], dy[...]).astype(BF)
    for tile in range(tiles):
        for column in range(model // TILE):
            part = slice(column * TILE, (column + 1) * TILE)
            gdown[slot, tile, part, :] = down[tile * TILE : (tile + 1) * TILE, part]
    send(step, steps, copies)

    @pl.when(step == steps - 1)
    def _():
        dx_ref[...] = dx_sum[...].astype(BF)


def combine_kernel(
    y_ref, first_ref, second_ref, pick_ref, gate_ref, h_ref, shared_ref, g_ref, out_ref, dgate_ref
):
    table = gate_ref[...]
    y_first, y_second = dot(first_ref[...], y_ref[...]), dot(second_ref[...], y_ref[...])
    gate_first = jnp.sum(table * pick_ref[0], axis=-1, keepdims=True)
    gate_second = jnp.sum(table * pick_ref[1], axis=-1, keepdims=True)
    mixture = gate_first * y_first + gate_second * y_second
    out_ref[0] = (h_ref[...] + mixture + shared_ref[...].astype(F32)).astype(BF)
    g = g_ref[...].astype(F32)
    dgate_ref[...] = (
        jnp.sum(g * y_first, axis=-1, keepdims=True) * pick_ref[0]
        + jnp.sum(g * y_second, axis=-1, keepdims=True) * pick_ref[1]
    )


def middle_back_kernel(
    back_ref, dgate_ref, take_ref, gate_ref, small_ref, dshared_ref, g_ref, h_ref, scale_ref, gain_ref, w_ref,
    dh_ref, dhb_ref, do_ref, dlogits_ref, ggain_ref,
):
    take = take_ref[...]
    dgates = dgate_ref[...]
    table = gate_ref[...]
    gated = jnp.sum(table * dgates, axis=-1, keepdims=True)
    dlogits = (table * (dgates - gated)).astype(BF)
    dlogits_ref[...] = dlogits
    da = dshared_ref[...].astype(F32) + dot_nt(dlogits, small_ref[...]) + dot(take, back_ref[...])
    hidden, scale = h_ref[...], scale_ref[...]
    ggain_ref[...] = jnp.sum(da * hidden * scale, axis=0, keepdims=True)
    weighted = da * gain_ref[...]
    mean = jnp.mean(weighted * hidden, axis=-1, keepdims=True)
    dhidden = g_ref[...].astype(F32) + scale * weighted - hidden * (scale * scale * scale) * mean
    dh_ref[...] = dhidden
    low = dhidden.astype(BF)
    dhb_ref[...] = low
    width = w_ref.shape[2]
    do = dot_nt(low[:, :width], w_ref[0]) + dot_nt(low[:, width:], w_ref[1])
    do_ref[...] = do.astype(BF)


def project_back_kernel(dq_ref, dk_ref, dv_ref, w_ref, halo_ref, own_ref, w_back):
    width, model = w_ref.shape[2], w_ref.shape[1]
    parts = model // width
    rows = dq_ref.shape[0]

    @pl.when(pl.program_id(0) == 0)
    def _():
        for part in range(3 * parts):
            w_back[:, part * width : (part + 1) * width] = w_ref[part]

    da = dot_nt(
        jnp.concatenate([dk_ref[...], dv_ref[...]], axis=1), w_back[:, model:]
    )
    halo_ref[...] = da.astype(BF)

    @pl.when(pl.program_id(0) == pl.num_programs(0) - 1)
    def _():
        own_ref[...] = da[da.shape[0] - rows :] + dot_nt(dq_ref[...], w_back[:, :model])


def widen_kernel(in_ref, in_out_ref, down_out_ref):
    in_rows, down_rows = in_out_ref.shape[1], down_out_ref.shape[1]
    columns = in_out_ref.shape[2] // TILE
    for column in range(columns):
        in_out_ref[0, :, column * TILE : (column + 1) * TILE] = in_ref[
            column * in_rows : (column + 1) * in_rows, :
        ].astype(F32)
    for column in range(down_out_ref.shape[2] // TILE):
        first = columns * in_rows + column * down_rows
        down_out_ref[0, :, column * TILE : (column + 1) * TILE] = in_ref[
            first : first + down_rows, :
        ].astype(F32)


def pack_kernel(early_ref, late_ref, shared_ref, out_ref, *, block):
    late = late_ref[0].astype(F32)
    for source in range(1, late_ref.shape[0]):
        late = late + late_ref[source].astype(F32)
    early, own = early_ref[...], out_ref.shape[1]
    for owner in range(out_ref.shape[0]):
        part = slice(owner * own, (owner + 1) * own)
        first = early.shape[1]
        out_ref[owner, :, :first] = early[part].astype(BF)
        out_ref[owner, :, first : first + late.shape[1]] = late[part].astype(BF)
        first = first + late.shape[1]
        for half in range(2):
            out_ref[owner, :, first + half * TILE : first + (half + 1) * TILE] = shared_ref[
                half * block + owner * own : half * block + (owner + 1) * own, :
            ].astype(BF)


def unpack_kernel(
    in_ref, w_ref, gain_ref, qkv_ref, out_ref, small_ref, dgain_ref, second_ref, shared_ref, *, piece
):
    sources, own = in_ref.shape[0], in_ref.shape[1]
    model = out_ref.shape[1]

    def take(start, some):
        total = in_ref[some[0], :, start : start + LANES].astype(F32)
        for source in some[1:]:
            total = total + in_ref[source, :, start : start + LANES].astype(F32)
        return total

    dgain = jnp.zeros((own, LANES), F32)
    first_core, second_core = range(0, sources, 2), range(1, sources, 2)
    early = 2 * model - 2 * LANES * (sources // 4)
    for pair in range(model // LANES):
        start = pair * 2 * LANES
        if start < early:
            k, v = take(start, first_core), take(start + LANES, first_core)
            q, o = take(start, second_core), take(start + LANES, second_core)
        else:
            source = (start - early) // LANES * 2
            k, q = take(early, (source,)), take(early, (source + 1,))
            v, o = take(early, (source + 2,)), take(early, (source + 3,))
        for which, value in enumerate((q, k, v)):
            part = slice(which * model + pair * LANES, which * model + (pair + 1) * LANES)
            qkv_ref[:, part] = value
            dgain = dgain + value * w_ref[:, part].astype(F32)
        out_ref[:, pair * LANES : (pair + 1) * LANES] = o
    dgain = jnp.sum(dgain, axis=-1, keepdims=True) / gain_ref[...]
    lane = lax.broadcasted_iota(jnp.int32, (own, LANES), 1)
    row = lax.broadcasted_iota(jnp.int32, (own, LANES), 0)

    def as_row(column):
        return jnp.sum(jnp.where(lane == row, column, 0.0), axis=0, keepdims=True)[:, :own]

    dgain_ref[...] = as_row(dgain)
    small = take(early + LANES, range(sources))
    experts = small_ref.shape[1]
    small_ref[...] = small[:, :experts]
    second = jnp.sum(jnp.where(lane == experts, small, 0.0), axis=-1, keepdims=True)
    second_ref[...] = as_row(second)
    per = LANES // piece
    for column in range(shared_ref.shape[1] // LANES):
        start = early + 2 * LANES + column // per * LANES
        total = jnp.zeros((own, LANES), F32)
        for source in range(sources):
            turn = (source - column % per) * piece % LANES
            value = take(start, (source,))
            value = pltpu.roll(value, turn, 1) if turn else value
            total = jnp.where(lane // piece == source, value, total)
        shared_ref[:, column * LANES : (column + 1) * LANES] = total


def per_device(
    tokens,
    segments,
    routes,
    w_qkv,
    w_out,
    w_router,
    shared_in,
    shared_down,
    attn_gain,
    ffn_gain,
    expert_in,
    expert_down,
    cotangent,
):
    ctx, fsdp = lax.axis_size("ctx"), lax.axis_size("fsdp")
    ctx_index, core = lax.axis_index("ctx"), lax.axis_index("fsdp") % 2
    rows, model = tokens.shape[1], tokens.shape[2]
    reach = max(1, WIN // rows)
    span = (reach + 1) * rows
    capacity = max(2, 3 * rows * TOPK // (2 * ctx))
    slots = ctx * capacity
    own = w_qkv.shape[0]
    owned_down = shared_down.shape[0]
    experts = w_router.shape[1]
    ff = shared_in.shape[1] // 2
    tiles = ff // TILE

    x, g = tokens[0], cotangent[0]
    cosine, sine = rotary_tables(span, (ctx_index - reach) * rows)
    route_own = routes[0]
    expert_ids = jnp.arange(experts, dtype=jnp.int32)
    hits = route_own[:, :, None] == expert_ids[None, None, :]
    member = jnp.sum(hits.astype(jnp.int32), axis=1)
    ranking = jnp.cumsum(member, axis=0, dtype=jnp.int32) - 1
    slot_ids = jnp.arange(capacity, dtype=jnp.int32)
    placed = (member[:, :, None] > 0) & (ranking[:, :, None] == slot_ids[None, None, :])
    take = placed.astype(BF).reshape(rows, slots)
    put = take.T
    selector = (
        (hits[:, :, :, None] & placed[:, None, :, :]).astype(BF).reshape(rows, TOPK * slots)
    )
    picked = jnp.pad(
        hits.astype(F32).transpose(1, 0, 2), ((0, 0), (0, 0), (0, LANES - experts))
    )
    lane = jnp.arange(LANES, dtype=jnp.int32)[None, :]
    own_lanes = ((lane == ctx_index) | (lane == ctx_index + LANES // 2)).astype(F32)
    g_to_slots = dot(put, g).astype(BF)

    small = jnp.concatenate(
        [w_router, attn_gain[:, None], ffn_gain[:, None], jnp.zeros((own, LANES - experts - 2), BF)],
        axis=1,
    )
    projections = jnp.concatenate([w_qkv, w_out], axis=1)
    width = projections.shape[1] // fsdp
    near = lax.all_to_all(
        jnp.concatenate(
            [
                projections.reshape(own, fsdp, width).transpose(1, 0, 2),
                jnp.broadcast_to(small, (fsdp, own, LANES)),
                shared_in.reshape(own, 2, ctx, fsdp, owned_down)
                .transpose(3, 0, 1, 2, 4)
                .reshape(fsdp, own, 2 * TILE),
            ],
            axis=2,
        ),
        "fsdp",
        split_axis=0,
        concat_axis=0,
        tiled=True,
    ).reshape(fsdp * own, -1)

    segment_row = jnp.zeros((16, model), BF).at[0, :rows].set(segments[0].astype(BF))
    carried = jnp.concatenate([x, segment_row], axis=0)
    place_z = ctx_index % ROW
    lines = range(0, ctx, ROW)
    previous = shifted(after(carried, near, cosine, picked), "ctx", ROW)
    arrived = [previous]
    for distance in range(reach - 1, 0, -1):
        arrived.append(
            lax.ppermute(
                jnp.where(place_z + distance < ROW, carried, previous),
                "ctx",
                [(line + z, line + (z + distance) % ROW) for line in lines for z in range(ROW)],
            )
        )

    def to_ctx(values):
        return lax.all_to_all(
            jnp.broadcast_to(values, (ctx, *values.shape)), "ctx", split_axis=0, concat_axis=0, tiled=True
        )

    g_all = lax.all_gather(g, "fsdp", axis=0)
    columns = model // TILE
    dense = to_ctx(near[:, :width]).reshape(model, width)
    w_full = lax.all_gather(after(dense, g_all, cosine, sine, g_to_slots, picked, previous), "fsdp", axis=0)
    small_full = to_ctx(after(near[:, width : width + LANES], dense)).reshape(model, LANES)
    down_own = shared_down.reshape(owned_down, columns, TILE).transpose(1, 0, 2).reshape(-1, TILE)
    place = ctx_index.astype(jnp.int32).reshape(1)
    place_spec = pl.BlockSpec(memory_space=pltpu.SMEM)
    in_rows, down_rows = expert_in.shape[1], expert_down.shape[1]
    expert_packed = jnp.concatenate(
        [
            expert_in[0].reshape(in_rows, 2 * tiles, TILE).transpose(1, 0, 2).reshape(-1, TILE),
            expert_down[0].reshape(down_rows, model // TILE, TILE).transpose(1, 0, 2).reshape(-1, TILE),
        ],
        axis=0,
    )
    expert_full = lax.all_gather(after(expert_packed, w_full, small_full, *arrived), "fsdp", axis=0)

    def exchange(values):
        return lax.all_to_all(
            values.reshape(ctx, values.shape[0] // ctx, values.shape[1]),
            "ctx",
            split_axis=0,
            concat_axis=0,
            tiled=True,
        ).reshape(values.shape)


    slot_g = exchange(after(g_to_slots, *arrived))

    pairs = model // LANES
    small_spec = whole(small_full)
    parts = model // width
    at_a_time = width // LANES

    def columns_of(which):
        return pl.BlockSpec((1, model, width), lambda j: (which * parts + j, 0, 0))

    def wide_spec(height):
        return pl.BlockSpec((height, width), lambda j: (0, j))

    blocks = [*arrived, carried]
    pair_spec = lambda height: pl.BlockSpec((height, LANES), lambda j: (0, j))
    q, k, kt, v, e, rl, rlb, attended, span_scale = pl.pallas_call(
        functools.partial(attend_kernel, gain_lane=experts, parts=reach + 1),
        grid=(parts,),
        in_specs=[
            place_spec,
            *[whole(block) for block in blocks],
            small_spec,
            columns_of(0),
            columns_of(1),
            columns_of(2),
            whole(cosine),
            whole(sine),
        ],
        out_specs=[
            wide_spec(rows),
            wide_spec(span),
            pl.BlockSpec((width, span), lambda j: (j, 0)),
            wide_spec(span),
            pl.BlockSpec((2 * at_a_time, span, rows), lambda j: (j, 0, 0)),
            pl.BlockSpec((at_a_time, 8, rows), lambda j: (j, 0, 0)),
            wide_spec(rows),
            wide_spec(rows),
            pl.BlockSpec((span, 1), lambda j: (0, 0)),
        ],
        out_shape=[
            jax.ShapeDtypeStruct((rows, model), BF),
            jax.ShapeDtypeStruct((span, model), BF),
            jax.ShapeDtypeStruct((model, span), BF),
            jax.ShapeDtypeStruct((span, model), BF),
            jax.ShapeDtypeStruct((HEADS, span, rows), BF),
            jax.ShapeDtypeStruct((pairs, 8, rows), F32),
            jax.ShapeDtypeStruct((rows, model), F32),
            jax.ShapeDtypeStruct((rows, model), BF),
            jax.ShapeDtypeStruct((span, 1), F32),
        ],
        scratch_shapes=[
            pltpu.VMEM((span, model), BF),
            pltpu.VMEM((2, span, rows), F32),
            pltpu.VMEM((width, span), BF),
            pltpu.VMEM((span, rows), F32),
        ],
        compiler_params=params(VMEM_MB),
        cost_estimate=cost(20),
        name="attend",
    )(place, *blocks, small_full, w_full, w_full, w_full, cosine, sine)

    out_spec = pl.BlockSpec((parts, model, width), lambda *_: (3, 0, 0))
    hidden, scale_two, normed, normed_t, outgoing, gates, gain_two = pl.pallas_call(
        functools.partial(middle_kernel, gain_lane=experts + 1),
        grid=(1,),
        in_specs=[
            whole(attended),
            out_spec,
            small_spec,
            whole(x),
            whole(picked),
            whole(put),
        ],
        out_specs=[
            pl.BlockSpec((rows, model), lambda *_: (0, 0)),
            pl.BlockSpec((rows, 1), lambda *_: (0, 0)),
            pl.BlockSpec((rows, model), lambda *_: (0, 0)),
            pl.BlockSpec((model, rows), lambda *_: (0, 0)),
            pl.BlockSpec((slots, model + LANES), lambda *_: (0, 0)),
            pl.BlockSpec((rows, LANES), lambda *_: (0, 0)),
            pl.BlockSpec((1, model), lambda *_: (0, 0)),
        ],
        out_shape=[
            jax.ShapeDtypeStruct((rows, model), F32),
            jax.ShapeDtypeStruct((rows, 1), F32),
            jax.ShapeDtypeStruct((rows, model), BF),
            jax.ShapeDtypeStruct((model, rows), BF),
            jax.ShapeDtypeStruct((slots, model + LANES), BF),
            jax.ShapeDtypeStruct((rows, LANES), F32),
            jax.ShapeDtypeStruct((1, model), F32),
        ],
        compiler_params=params(VMEM_MB),
        cost_estimate=cost(5),
        name="middle",
    )(attended, w_full, small_full, x, picked, put)
    normed_all = lax.all_gather(normed, "fsdp", axis=0)
    incoming = exchange(after(outgoing, slot_g))
    narrow = after(near, outgoing)
    shared_own_w = jnp.concatenate(
        [narrow[:, width + LANES : -TILE], narrow[:, -TILE:], down_own], axis=0
    )
    shared_full = to_ctx(after(shared_own_w, incoming))
    gain_one = small_full[:, experts : experts + 1].astype(F32)
    span_x = jnp.concatenate(
        [block[:rows] for block in lax.optimization_barrier((*blocks, outgoing))[:-1]], axis=0
    )
    first_t = (span_x.T.astype(F32) * span_scale.reshape(1, span) * gain_one).astype(BF)
    incoming = after(incoming, first_t)

    packed_rows = 3 * model

    steps = tiles // AT_ONCE
    expert_specs = [
        pl.BlockSpec((fsdp, AT_ONCE * in_rows, TILE), lambda t: (0, t, 0)),
        pl.BlockSpec((fsdp, AT_ONCE * in_rows, TILE), lambda t: (0, steps + t, 0)),
        pl.BlockSpec((AT_ONCE, model, TILE), lambda t: (t, 2 * in_rows * tiles // model, 0)),
    ]
    unit_spec = pl.BlockSpec((1, slots, AT_ONCE * TILE), lambda t: (t, 0, 0))
    expert_y, *units = pl.pallas_call(
        expert_kernel,
        grid=(steps,),
        in_specs=[whole(incoming), *expert_specs],
        out_specs=[
            pl.BlockSpec((slots, model), lambda t: (0, 0)),
            unit_spec,
            unit_spec,
            unit_spec,
        ],
        out_shape=[jax.ShapeDtypeStruct((slots, model), BF)]
        + [jax.ShapeDtypeStruct((steps, slots, AT_ONCE * TILE), BF)] * 3,
        scratch_shapes=[pltpu.VMEM((slots, model), F32)],
        compiler_params=params(VMEM_MB),
        cost_estimate=cost(60),
        name="expert",
    )(incoming, expert_full, expert_full, expert_full)
    returned_y = exchange(after(expert_y, shared_full))

    at_once = 2
    block = model // ctx
    shared_part, shared_pieces = pl.pallas_call(
        shared_kernel,
        grid=(fsdp // at_once,),
        in_specs=[
            pl.BlockSpec((at_once, rows, model), lambda t: (t, 0, 0)),
            pl.BlockSpec((at_once, rows, model), lambda t: (t, 0, 0)),
            whole(shared_full),
        ],
        out_specs=[
            pl.BlockSpec((at_once, rows, 2 * model), lambda t: (t, 0, 0)),
            whole(shared_full),
        ],
        out_shape=[
            jax.ShapeDtypeStruct((fsdp, rows, 2 * model), BF),
            jax.ShapeDtypeStruct(shared_full.shape, BF),
        ],
        scratch_shapes=[pltpu.VMEM((model, 2 * TILE), F32), pltpu.VMEM((TILE, model), F32)],
        compiler_params=params(VMEM_MB),
        cost_estimate=cost(18),
        name="shared",
    )(after(normed_all, expert_y), g_all, shared_full)
    shared_both = lax.psum_scatter(after(shared_part, returned_y), "fsdp", scatter_dimension=0)
    shared_own = jnp.sum(
        lax.all_to_all(
            after(shared_pieces, returned_y), "ctx", split_axis=0, concat_axis=0, tiled=True
        ).astype(F32),
        axis=0,
    )
    back, gexpert = pl.pallas_call(
        expert_back_kernel,
        grid=(steps,),
        in_specs=[
            whole(incoming),
            whole(slot_g),
            whole(own_lanes),
            *expert_specs,
            unit_spec,
            unit_spec,
            unit_spec,
        ],
        out_specs=[
            pl.BlockSpec((slots, model), lambda t: (0, 0)),
            pl.BlockSpec(memory_space=pl.ANY),
        ],
        out_shape=[
            jax.ShapeDtypeStruct((slots, model), BF),
            jax.ShapeDtypeStruct((fsdp, packed_rows, TILE), BF),
        ],
        scratch_shapes=[
            pltpu.VMEM((model, slots), BF),
            pltpu.VMEM((slots, model), BF),
            pltpu.VMEM((slots, model), F32),
            pltpu.VMEM((2, 2, fsdp, AT_ONCE * in_rows, TILE), BF),
            pltpu.VMEM((2, AT_ONCE, model, TILE), BF),
            pltpu.SemaphoreType.DMA((2, 3)),
        ],
        compiler_params=params(VMEM_MB),
        cost_estimate=cost(22),
        name="expert_back",
    )(after(incoming, shared_part, returned_y), slot_g, own_lanes, expert_full, expert_full, expert_full, *units)
    returned = exchange(after(back, shared_own))
    expert_sum = lax.psum_scatter(after(gexpert, shared_own), "fsdp", scatter_dimension=0)

    mixed, dgates = pl.pallas_call(
        combine_kernel,
        grid=(1,),
        in_specs=[
            pl.BlockSpec((slots, model), lambda *_: (0, 0)),
            pl.BlockSpec((rows, slots), lambda *_: (0, 0)),
            pl.BlockSpec((rows, slots), lambda *_: (0, 1)),
            whole(picked),
            whole(gates),
            whole(hidden),
            pl.BlockSpec((rows, model), lambda *_: (0, 0)),
            whole(g),
        ],
        out_specs=[
            pl.BlockSpec((1, rows, model), lambda *_: (0, 0, 0)),
            pl.BlockSpec((rows, LANES), lambda *_: (0, 0)),
        ],
        out_shape=[
            jax.ShapeDtypeStruct((1, rows, model), BF),
            jax.ShapeDtypeStruct((rows, LANES), F32),
        ],
        compiler_params=params(VMEM_MB),
        cost_estimate=cost(3),
        name="combine",
    )(returned_y, selector, selector, picked, gates, hidden, shared_both, g)

    returned = after(returned, dgates)

    dhidden, dhidden_low, dattended, dlogits, ggain_two = pl.pallas_call(
        middle_back_kernel,
        grid=(1,),
        in_specs=[
            whole(returned),
            whole(dgates),
            whole(take),
            whole(gates),
            small_spec,
            pl.BlockSpec((rows, model), lambda *_: (0, 1)),
            whole(g),
            whole(hidden),
            whole(scale_two),
            whole(gain_two),
            out_spec,
        ],
        out_specs=[
            pl.BlockSpec((rows, model), lambda *_: (0, 0)),
            pl.BlockSpec((rows, model), lambda *_: (0, 0)),
            pl.BlockSpec((rows, model), lambda *_: (0, 0)),
            pl.BlockSpec((rows, LANES), lambda *_: (0, 0)),
            pl.BlockSpec((1, model), lambda *_: (0, 0)),
        ],
        out_shape=[
            jax.ShapeDtypeStruct((rows, model), F32),
            jax.ShapeDtypeStruct((rows, model), BF),
            jax.ShapeDtypeStruct((rows, model), BF),
            jax.ShapeDtypeStruct((rows, LANES), BF),
            jax.ShapeDtypeStruct((1, model), F32),
        ],
        compiler_params=params(VMEM_MB),
        cost_estimate=cost(6),
        name="middle_back",
    )(
        returned, dgates, take, gates, small_full, shared_both, g, hidden, scale_two, gain_two, w_full
    )

    grouter = dot(normed_t, dlogits)
    small_grads = jnp.concatenate(
        [grouter[:, :experts], ggain_two.T, jnp.zeros((model, LANES - experts - 1), F32)], axis=1
    ).astype(BF)
    attended_t = attended.T
    core_scalar = core.astype(jnp.int32).reshape(1)

    def attend_back(first, count, down, *filled):
        pair_from = lambda height: pl.BlockSpec((height, LANES), lambda j: (0, first + j))
        operands = (
            core_scalar, q, k, kt, v, e, rl, rlb, down, cosine, sine, first_t, attended_t, dhidden_low, *filled,
        )
        return pl.pallas_call(
            attend_back_kernel,
            grid=(count,),
            in_specs=[
                place_spec,
                pair_from(rows),
                pair_from(span),
                pl.BlockSpec((LANES, span), lambda j: (first + j, 0)),
                pair_from(span),
                pl.BlockSpec((2, span, rows), lambda j: (first + j, 0, 0)),
                pl.BlockSpec((1, 8, rows), lambda j: (first + j, 0, 0)),
                pair_from(rows),
                pair_from(rows),
                whole(cosine),
                whole(sine),
                whole(first_t),
                whole(attended_t),
                pair_from(rows),
            ]
            + [pl.BlockSpec(memory_space=pl.ANY)] * len(filled),
            out_specs=[
                pair_from(rows),
                pair_from(span),
                pair_from(span),
                pl.BlockSpec((model, 2 * LANES), lambda j: (0, j)),
                pl.BlockSpec((model, 2 * LANES), lambda j: (0, j)),
            ],
            out_shape=[
                jax.ShapeDtypeStruct((rows, model), BF),
                jax.ShapeDtypeStruct((span, model), BF),
                jax.ShapeDtypeStruct((span, model), BF),
                jax.ShapeDtypeStruct((model, count * 2 * LANES), BF),
                jax.ShapeDtypeStruct((model, count * 2 * LANES), BF),
            ],
            input_output_aliases={
                len(operands) - len(filled) + index: index for index in range(len(filled))
            },
            scratch_shapes=[
                pltpu.VMEM((2, span, rows), F32),
                pltpu.VMEM((2, span, rows), BF),
                pltpu.VMEM((span, LANES), F32),
                pltpu.VMEM((span, LANES), F32),
            ],
            compiler_params=params(VMEM_MB),
            cost_estimate=cost(12 * count),
            name=f"attend_back_{first}",
        )(*operands)


    def paired_columns(kept, sent):
        partner = lax.ppermute(sent, "fsdp", [(i, i ^ 1) for i in range(fsdp)])
        return (kept.astype(F32) + partner.astype(F32)).astype(BF)

    def along_ctx(pieces):
        return lax.all_to_all(pieces, "ctx", split_axis=0, concat_axis=0, tiled=True)

    early_pairs = 2 * pairs // 3
    *grads_a, kept_a, sent_a = attend_back(0, early_pairs, dattended)
    paired_a = paired_columns(kept_a, sent_a)
    late_a = along_ctx(paired_a.reshape(ctx, block, -1))
    dq, dk, dv, kept_b, sent_b = attend_back(
        early_pairs, pairs - early_pairs, after(dattended, paired_a), *grads_a
    )
    paired_b = paired_columns(kept_b, sent_b)

    dspan, down = pl.pallas_call(
        project_back_kernel,
        grid=(2,),
        in_specs=[
            whole(dq),
            pl.BlockSpec((span // 2, model), lambda b: (b, 0)),
            pl.BlockSpec((span // 2, model), lambda b: (b, 0)),
            pl.BlockSpec((3 * parts, model, width), lambda b: (0, 0, 0)),
        ],
        out_specs=[
            pl.BlockSpec((span // 2, model), lambda b: (b, 0)),
            pl.BlockSpec((rows, model), lambda b: (0, 0)),
        ],
        out_shape=[
            jax.ShapeDtypeStruct((span, model), BF),
            jax.ShapeDtypeStruct((rows, model), F32),
        ],
        compiler_params=params(VMEM_MB),
        scratch_shapes=[pltpu.VMEM((model, 3 * model), BF)],
        cost_estimate=cost(8),
        name="project_back",
    )(dq, dk, dv, w_full)
    total, passed = down, dspan[:rows].astype(F32)
    for distance in range(1, reach):
        lower = (reach - distance) * rows
        moved = lax.ppermute(
            dspan[lower : lower + rows],
            "ctx",
            [(line + z, line + (z - distance) % ROW) for line in lines for z in range(ROW)],
        )
        moved = moved.astype(F32)
        here = place_z + distance < ROW
        total = total + jnp.where(here, moved, 0.0)
        passed = passed + jnp.where(here, 0.0, moved)
    grad_expert_in, grad_expert_down = pl.pallas_call(
        widen_kernel,
        grid=(1,),
        in_specs=[whole(expert_sum)],
        out_specs=[
            pl.BlockSpec((1, in_rows, 2 * ff), lambda *_: (0, 0, 0)),
            pl.BlockSpec((1, down_rows, model), lambda *_: (0, 0, 0)),
        ],
        out_shape=[
            jax.ShapeDtypeStruct((1, in_rows, 2 * ff), F32),
            jax.ShapeDtypeStruct((1, down_rows, model), F32),
        ],
        compiler_params=params(VMEM_MB),
        cost_estimate=cost(2),
        name="widen",
    )(expert_sum)
    late_a = jnp.sum(late_a.astype(F32), axis=0)
    quarter = paired_b.shape[1] // (fsdp // 2)
    late_b = lax.all_to_all(
        after(
            paired_b.reshape(model, fsdp // 2, quarter).transpose(1, 0, 2),
            down, late_a,
        ),
        "fsdp",
        split_axis=0,
        concat_axis=0,
        axis_index_groups=[list(range(start, fsdp, 2)) for start in range(2)],
        tiled=True,
    )
    late_b = jnp.sum(late_b.astype(F32), axis=0).astype(BF)
    received = shifted(after(passed.astype(BF), late_b), "ctx", -ROW)
    late_b = along_ctx(jnp.concatenate([late_b, small_grads], axis=1).reshape(ctx, block, -1))

    grad_shared_down = (
        shared_own[2 * block :]
        .reshape(columns, owned_down, TILE)
        .transpose(1, 0, 2)
        .reshape(owned_down, model)
    )
    packed_width = late_a.shape[1] + late_b.shape[2] + 2 * TILE
    last = pl.pallas_call(
        functools.partial(pack_kernel, block=block),
        grid=(1,),
        in_specs=[
            whole(late_a),
            whole(late_b),
            pl.BlockSpec((2 * block, TILE), lambda *_: (0, 0)),
        ],
        out_specs=pl.BlockSpec((fsdp, own, packed_width), lambda *_: (0, 0, 0)),
        out_shape=jax.ShapeDtypeStruct((fsdp, own, packed_width), BF),
        compiler_params=params(VMEM_MB),
        cost_estimate=cost(2),
        name="pack",
    )(late_a, late_b, shared_own)
    last = lax.all_to_all(last, "fsdp", split_axis=0, concat_axis=0, tiled=True)
    last = after(last, received, grad_expert_in, grad_expert_down)
    wanted = [
        jax.ShapeDtypeStruct((own, 3 * model), F32),
        jax.ShapeDtypeStruct((own, model), F32),
        jax.ShapeDtypeStruct((own, experts), F32),
        jax.ShapeDtypeStruct((1, own), F32),
        jax.ShapeDtypeStruct((1, own), F32),
        jax.ShapeDtypeStruct((own, 2 * ff), F32),
    ]
    gain_own = attn_gain.astype(F32)[:, None]
    grad_qkv, grad_out, grad_router, grad_gain_one, grad_gain_two, grad_shared_in = pl.pallas_call(
        functools.partial(unpack_kernel, piece=owned_down),
        grid=(1,),
        in_specs=[whole(last), whole(w_qkv), whole(gain_own)],
        out_specs=[whole(array) for array in wanted],
        out_shape=wanted,
        compiler_params=params(VMEM_MB),
        cost_estimate=cost(2),
        name="unpack",
    )(last, w_qkv, gain_own)

    total = total + received.astype(F32)
    input_rows = x.astype(F32)
    scale_one = span_scale[reach * rows :]
    weighted = total * gain_one.reshape(1, model)
    input_grad = (
        dhidden
        + scale_one * weighted
        - input_rows
        * scale_one**3
        * jnp.mean(weighted * input_rows, axis=-1, keepdims=True)
    )[None]

    return (
        mixed,
        input_grad,
        grad_qkv,
        grad_out,
        grad_router,
        grad_shared_in,
        grad_shared_down,
        grad_gain_one.reshape(own),
        grad_gain_two.reshape(own),
        grad_expert_in,
        grad_expert_down,
    )


def solution(mesh):
    placed = (
        P("fsdp", "ctx", None),
        P("fsdp", "ctx"),
        P("fsdp", "ctx", None),
        P(("ctx", "fsdp"), None),
        P(("ctx", "fsdp"), None),
        P(("ctx", "fsdp"), None),
        P(("ctx", "fsdp"), None),
        P(("ctx", "fsdp"), None),
        P(("ctx", "fsdp")),
        P(("ctx", "fsdp")),
        P("ctx", "fsdp", None),
        P("ctx", "fsdp", None),
        P("fsdp", "ctx", None),
    )
    return jax.shard_map(
        per_device,
        mesh=mesh,
        in_specs=placed,
        out_specs=(
            P("fsdp", "ctx", None),
            P("fsdp", "ctx", None),
            P(("ctx", "fsdp"), None),
            P(("ctx", "fsdp"), None),
            P(("ctx", "fsdp"), None),
            P(("ctx", "fsdp"), None),
            P(("ctx", "fsdp"), None),
            P(("ctx", "fsdp")),
            P(("ctx", "fsdp")),
            P("ctx", "fsdp", None),
            P("ctx", "fsdp", None),
        ),
        check_vma=False,
    )
```

```python
import functools

import jax
import jax.numpy as jnp
from jax import lax
from jax.experimental import pallas as pl
from jax.experimental.pallas import tpu as pltpu
from jax.sharding import PartitionSpec as P

HEADS = 12
HEAD_DIM = 64
TOPK = 2
WIN = 1024
EPSILON = 1e-06

BF = jnp.bfloat16
F32 = jnp.float32
TILE = 256
LANES = 128
IN_ROWS = 96
AT_ONCE = 2
KEY_BLOCK = 128
ROW = 4
VMEM_MB = 60


def dot(a, b):
    return jnp.dot(a, b, preferred_element_type=F32)


def dot_nt(a, b):
    return lax.dot_general(a, b, (((1,), (1,)), ((), ())), preferred_element_type=F32)


def dot_tn(a, b):
    return lax.dot_general(a, b, (((0,), (0,)), ((), ())), preferred_element_type=F32)


def params(megabytes):
    return pltpu.CompilerParams(vmem_limit_bytes=megabytes * 1024 * 1024)


def cost(microseconds):
    return pl.CostEstimate(
        flops=int(microseconds * 1.0e9), bytes_accessed=int(microseconds * 1.0e6), transcendentals=0
    )


def after(value, *others):
    return lax.optimization_barrier((value, *others))[0]


def whole(array):
    return pl.BlockSpec(array.shape, lambda *_: (0,) * array.ndim)


def shifted(value, axis, steps):
    count = lax.axis_size(axis)
    leading, last = (max(0, -steps), min(count, count - steps))
    return lax.ppermute(value, axis, [(source, source + steps) for source in range(leading, last)])


def split_high_low(values):
    high = values.astype(BF)
    return high, (values - high.astype(F32)).astype(BF)


def rotary_tables(rows, offset):
    half = HEAD_DIM // 2
    frequency = jnp.exp(-jnp.log(10000.0) * (2.0 * jnp.arange(half, dtype=F32) / HEAD_DIM))
    places = (offset + jnp.arange(rows, dtype=jnp.int32)).astype(F32)
    angles = places[:, None] * frequency[None, :]
    cosine, sine = jnp.cos(angles), jnp.sin(angles)
    return (
        jnp.concatenate([cosine] * 4, axis=1),
        jnp.concatenate([-sine, sine, -sine, sine], axis=1),
    )


def swapped_halves(values):
    width, half = values.shape[1], HEAD_DIM // 2
    lane = lax.broadcasted_iota(jnp.int32, (1, width), 1)
    return jnp.where(
        lane % HEAD_DIM < half,
        pltpu.roll(values, width - half, 1),
        pltpu.roll(values, half, 1),
    )


def head_lanes(values, head):
    lane = lax.broadcasted_iota(jnp.int32, (1, LANES), 1)
    return jnp.where(lane // HEAD_DIM == head, values, jnp.zeros_like(values))


def fold_rows(values, op):
    return op(values.reshape(values.shape[0] // 8, 8, values.shape[1]), axis=0)


def attend_kernel(
    place_ref, *refs, gain_lane, parts
):
    blocks, refs = refs[:parts], refs[parts:]
    (
        small_ref, wq_ref, wk_ref, wv_ref, cos_ref, sin_ref,
        q_ref, k_ref, kt_ref, v_ref, e_ref, rl_ref, rlb_ref, o_ref, scale_ref,
        normed, score, vt, bias_ref,
    ) = refs
    rows, model = q_ref.shape[0], normed.shape[1]
    span = parts * rows

    @pl.when(pl.program_id(0) == 0)
    def _():
        gain = small_ref[...].astype(F32).T[gain_lane : gain_lane + 1, :]
        query_segment = blocks[-1][rows : rows + 1, :rows].astype(F32)
        query_place = lax.broadcasted_iota(jnp.int32, (rows, rows), 1)
        key_place = lax.broadcasted_iota(jnp.int32, (rows, rows), 0)
        for index, block in enumerate(blocks):
            part = pl.ds(index * rows, rows)
            values = block[:rows, :].astype(F32)
            scale = lax.rsqrt(jnp.mean(values * values, axis=-1, keepdims=True) + EPSILON)
            scale_ref[part, :] = scale
            normed[part, :] = (values * scale * gain).astype(BF)
            key_segment = block[rows : rows + 16, :rows].astype(F32).T[:, :1]
            distance = query_place - key_place + (parts - 1 - index) * rows
            allowed = (distance >= 0) & (distance < WIN) & (key_segment == query_segment)
            allowed = allowed & (place_ref[0] >= parts - 1 - index)
            bias_ref[part, :] = jnp.where(allowed, 0.0, -1e30)

    wide = q_ref.shape[1]
    cosine = jnp.concatenate([cos_ref[...]] * (wide // LANES), axis=1)
    sine = jnp.concatenate([sin_ref[...]] * (wide // LANES), axis=1)
    pair = dot(normed[...], jnp.concatenate([wk_ref[0], wv_ref[0]], axis=1))
    keys = pair[:, :wide]
    keys = keys * cosine + swapped_halves(keys) * sine
    k_ref[...] = keys.astype(BF)
    kt_ref[...] = keys.T.astype(BF)
    queries = dot(normed[span - rows :, :], wq_ref[0])
    queries = queries * cosine[span - rows :] + swapped_halves(queries) * sine[span - rows :]
    queries = (queries.astype(BF).astype(F32) * HEAD_DIM**-0.5).astype(BF)
    q_ref[...] = queries
    heads = wide // HEAD_DIM

    def chunk(head):
        return slice(head // 2 * LANES, (head // 2 + 1) * LANES)

    own = [head_lanes(queries[:, chunk(head)], head % 2) for head in range(heads)]
    largest = [jnp.full((8, rows), -3e38, F32) for _ in range(heads)]
    total = [jnp.zeros((8, rows), F32) for _ in range(heads)]

    def scores(head, part):
        block = dot_nt(k_ref[part, chunk(head)], own[head]) + bias_ref[part, :]
        score[head % 2, part, :] = block
        largest[head] = jnp.maximum(largest[head], fold_rows(block, jnp.max))

    def weights(head, part):
        block = jnp.exp(score[head % 2, part, :] - largest[head])
        total[head] = total[head] + fold_rows(block, jnp.sum)
        e_ref[head, part, :] = block.astype(BF)

    blocks_of_keys = [pl.ds(start, KEY_BLOCK) for start in range(0, span, KEY_BLOCK)]
    for part in blocks_of_keys:
        scores(0, part)
    values = pair[:, wide:]
    v_ref[...] = values.astype(BF)
    vt[...] = values.T.astype(BF)
    outs, sums = [], []
    for head in range(heads):
        largest[head] = jnp.max(largest[head], axis=0, keepdims=True)
        for part in blocks_of_keys:
            weights(head, part)
            if head + 1 < heads:
                scores(head + 1, part)
        inverse = 1.0 / jnp.sum(total[head], axis=0, keepdims=True)
        rl_ref[head // 2, head % 2 : head % 2 + 1, :] = inverse
        outs.append(dot(vt[head * HEAD_DIM : (head + 1) * HEAD_DIM, :], e_ref[head]) * inverse)
        sums.append(jnp.broadcast_to(inverse, (HEAD_DIM, rows)))
    o_ref[...] = jnp.concatenate(outs, axis=0).T.astype(BF)
    rlb_ref[...] = jnp.concatenate(sums, axis=0).T


def attend_back_kernel(
    core_ref, q_ref, k_ref, kt_ref, v_ref, e_ref, rl_ref, rlb_ref, do_ref, cos_ref, sin_ref, xt_ref, ot_ref, dh_ref,
    *refs,
):
    dq_ref, dk_ref, dv_ref, kept_ref, sent_ref, dprob, dscore, dk, dv = refs[-9:]
    span, rows = k_ref.shape[0], q_ref.shape[0]
    scaled = do_ref[...].astype(F32) * rlb_ref[...]
    heads = range(2)
    down = [head_lanes(scaled, head).astype(BF) for head in heads]
    own = [head_lanes(q_ref[...], head) for head in heads]
    own_both, down_both = jnp.concatenate(own, axis=0), jnp.concatenate(down, axis=0)
    inner = [jnp.zeros((8, rows), F32) for _ in heads]
    for start in range(0, span, KEY_BLOCK):
        part = pl.ds(start, KEY_BLOCK)
        for head in heads:
            block = dot_nt(v_ref[part, :], down[head])
            dprob[head, part, :] = block
            inner[head] = inner[head] + fold_rows(block * e_ref[head, part, :].astype(F32), jnp.sum)
    inner = [
        jnp.sum(inner[head], axis=0, keepdims=True) * rl_ref[0, head : head + 1, :]
        for head in heads
    ]
    for start in range(0, span, KEY_BLOCK):
        part = pl.ds(start, KEY_BLOCK)
        for head in heads:
            weight = e_ref[head, part, :]
            block = (weight.astype(F32) * (dprob[head, part, :] - inner[head])).astype(BF)
            dscore[head, part, :] = block
        dk[part, :] = dot(
            jnp.concatenate([dscore[head, part, :] for head in heads], axis=1), own_both
        )
        dv[part, :] = dot(
            jnp.concatenate([e_ref[head, part, :] for head in heads], axis=1), down_both
        )
    dqs = [
        dot(kt_ref[head * HEAD_DIM : (head + 1) * HEAD_DIM, :], dscore[head]) for head in heads
    ]
    dquery = jnp.concatenate(dqs, axis=0).T * HEAD_DIM**-0.5
    dquery = dquery * cos_ref[span - rows :, :] - swapped_halves(dquery) * sin_ref[span - rows :, :]
    dquery = dquery.astype(BF)
    dq_ref[...] = dquery
    dkeys = dk[...]
    dkeys = (dkeys * cos_ref[...] - swapped_halves(dkeys) * sin_ref[...]).astype(BF)
    dvalues = dv[...].astype(BF)
    dk_ref[...] = dkeys
    dv_ref[...] = dvalues
    first = dot(xt_ref[...], jnp.concatenate([dkeys, dvalues], axis=1)).astype(BF)
    second = jnp.concatenate(
        [dot(xt_ref[:, span - rows :], dquery), dot(ot_ref[...], dh_ref[...])], axis=1
    ).astype(BF)
    kept_ref[...] = jnp.where(core_ref[0] == 0, first, second)
    sent_ref[...] = jnp.where(core_ref[0] == 0, second, first)


def middle_kernel(
    o_ref, w_ref, small_ref, x_ref, pick_ref, put_ref,
    h_ref, scale_ref, a_ref, at_ref, out_ref, gate_ref, gain_ref,
    *, gain_lane,
):
    projected = jnp.concatenate([dot(o_ref[...], w_ref[part]) for part in range(2)], axis=1)
    hidden = x_ref[...].astype(F32) + projected
    h_ref[...] = hidden
    scale = lax.rsqrt(jnp.mean(hidden * hidden, axis=-1, keepdims=True) + EPSILON)
    scale_ref[...] = scale
    small = small_ref[...]
    gain = small.astype(F32).T[gain_lane : gain_lane + 1, :]
    gain_ref[...] = gain
    low = (hidden * scale * gain).astype(BF)
    a_ref[...] = low
    at_ref[...] = low.astype(F32).T.astype(BF)
    logits = dot(low, small)
    first, second = pick_ref[0], pick_ref[1]
    chosen_first = jnp.sum(logits * first, axis=-1, keepdims=True)
    chosen_second = jnp.sum(logits * second, axis=-1, keepdims=True)
    largest = jnp.maximum(chosen_first, chosen_second)
    chosen_first = jnp.exp(chosen_first - largest)
    chosen_second = jnp.exp(chosen_second - largest)
    total = chosen_first + chosen_second
    table = (chosen_first / total) * first + (chosen_second / total) * second
    gate_ref[...] = table
    high, rest = split_high_low(table)
    extra = (high.astype(F32) + pltpu.roll(rest.astype(F32), LANES // 2, 1)).astype(BF)
    put = put_ref[...]
    width = a_ref.shape[1]
    out_ref[:, :width] = dot(put, low).astype(BF)
    out_ref[:, width:] = dot(put, extra).astype(BF)


def gated_forward(x, w_gate, w_lift):
    gate, lift = dot(x, w_gate), dot(x, w_lift)
    sigmoid = 1.0 / (1.0 + jnp.exp(-gate))
    act = gate * sigmoid
    slope = sigmoid + (act - act * sigmoid)
    return (act * lift).astype(BF), act, lift * slope


def add_up(total_ref, value):
    first = pl.program_id(0) == 0
    total_ref[...] = value + jnp.where(first, 0.0, total_ref[...])


def flush(step, steps, copies):
    @pl.when(step >= 2)
    def _():
        for copy in copies(step % 2, step):
            copy.wait()


def send(step, steps, copies):
    for copy in copies(step % 2, step):
        copy.start()

    @pl.when(step == steps - 1)
    def _():
        for copy in copies((step + 1) % 2, step):
            copy.wait()
        for copy in copies(step % 2, step):
            copy.wait()


def shared_kernel(
    x_ref, dy_ref, w_ref, out_ref, pieces_ref, gin_sum, gdown_sum
):
    count, rows, model = x_ref.shape
    block, columns = model // w_ref.shape[0], model // TILE
    piece = (w_ref.shape[1] - 2 * block) // columns
    x, dy = x_ref[...].reshape(count * rows, model), dy_ref[...].reshape(count * rows, model)
    w_gate = w_ref[:, :block, :].reshape(model, TILE)
    w_lift = w_ref[:, block : 2 * block, :].reshape(model, TILE)
    w_down = jnp.concatenate(
        [
            w_ref[:, start : start + piece, :].reshape(-1, TILE)
            for start in range(2 * block, w_ref.shape[1], piece)
        ],
        axis=1,
    )
    hidden, act, slope = gated_forward(x, w_gate, w_lift)
    out_ref[:, :, :model] = dot(hidden, w_down).astype(BF).reshape(count, rows, model)
    dhidden = dot_nt(dy, w_down)
    both = jnp.concatenate([dhidden * slope, dhidden * act], axis=1).astype(BF)
    dx = dot_nt(both, jnp.concatenate([w_gate, w_lift], axis=1))
    out_ref[:, :, model:] = dx.astype(BF).reshape(count, rows, model)
    add_up(gin_sum, dot_tn(x, both))
    add_up(gdown_sum, dot_tn(hidden, dy))

    @pl.when(pl.program_id(0) == pl.num_programs(0) - 1)
    def _():
        for owner in range(pieces_ref.shape[0]):
            rows_in = pl.ds(owner * block, block)
            for part in range(2):
                pieces_ref[owner, part * block : (part + 1) * block, :] = gin_sum[
                    rows_in, part * TILE : (part + 1) * TILE
                ].astype(BF)
            rows_down = pl.ds(owner * piece, piece)
            for column in range(columns):
                start = 2 * block + column * piece
                pieces_ref[owner, start : start + piece, :] = gdown_sum[
                    rows_down, column * TILE : (column + 1) * TILE
                ].astype(BF)


def side_by_side(blocks):
    count = blocks.shape[1] // IN_ROWS
    return jnp.concatenate(
        [
            blocks[:, part * IN_ROWS : (part + 1) * IN_ROWS].reshape(-1, TILE)
            for part in range(count)
        ],
        axis=1,
    )


def unpack_down(packed, model):
    return jnp.concatenate(
        [
            jnp.concatenate(
                [packed[tile, start : start + TILE] for start in range(0, model, TILE)], axis=1
            )
            for tile in range(packed.shape[0])
        ],
        axis=0,
    )


def expert_kernel(
    in_ref, wg_ref, wl_ref, wd_ref, y_ref, hidden_ref, act_ref, slope_ref, y_sum
):
    model = y_ref.shape[1]
    w_gate, w_lift = side_by_side(wg_ref[...]), side_by_side(wl_ref[...])
    hidden, act, slope = gated_forward(in_ref[:, :model], w_gate, w_lift)
    hidden_ref[0] = hidden
    act_ref[0] = act.astype(BF)
    slope_ref[0] = slope.astype(BF)
    add_up(y_sum, dot(hidden, unpack_down(wd_ref[...], model)))

    @pl.when(pl.program_id(0) == pl.num_programs(0) - 1)
    def _():
        y_ref[...] = y_sum[...].astype(BF)


def expert_back_kernel(
    in_ref, g_ref, own_ref, wg_ref, wl_ref, wd_ref, hidden_ref, act_ref, slope_ref,
    dx_ref, grads_ref,
    xt, dy, dx_sum, gin, gdown, sems,
):
    model = g_ref.shape[1]
    step, steps = pl.program_id(0), pl.num_programs(0)
    in_rows, tiles = gin.shape[3], gdown.shape[1]

    def copies(slot, now):
        for part in range(2):
            first = pl.multiple_of((part * steps + now) * in_rows, in_rows)
            yield pltpu.make_async_copy(
                gin.at[slot, part], grads_ref.at[:, pl.ds(first, in_rows)], sems.at[slot, part]
            )
        yield pltpu.make_async_copy(
            gdown.at[slot],
            grads_ref.at[pl.ds(now * tiles, tiles), pl.ds(2 * steps * in_rows, model)],
            sems.at[slot, 2],
        )

    @pl.when(step == 0)
    def _():
        xt[...] = in_ref[:, :model].astype(F32).T.astype(BF)
        gate = jnp.sum(in_ref[:, model:].astype(F32) * own_ref[...], axis=-1, keepdims=True)
        dy[...] = (g_ref[...].astype(F32) * gate).astype(BF)

    flush(step, steps, copies)
    slot = step % 2
    w_gate, w_lift = side_by_side(wg_ref[...]), side_by_side(wl_ref[...])
    dhidden = dot_nt(dy[...], unpack_down(wd_ref[...], model)).astype(BF)
    both = jnp.concatenate([dhidden * slope_ref[0], dhidden * act_ref[0]], axis=1)
    add_up(dx_sum, dot_nt(both, jnp.concatenate([w_gate, w_lift], axis=1)))
    into = dot(xt[...], both).astype(BF)
    shape = (gin.shape[2], IN_ROWS, TILE)
    for part in range(2):
        for tile in range(tiles):
            column = (part * tiles + tile) * TILE
            gin[slot, part, :, tile * IN_ROWS : (tile + 1) * IN_ROWS, :] = into[
                :, column : column + TILE
            ].reshape(shape)
    down = dot_tn(hidden_ref[0], dy[...]).astype(BF)
    for tile in range(tiles):
        for column in range(model // TILE):
            part = slice(column * TILE, (column + 1) * TILE)
            gdown[slot, tile, part, :] = down[tile * TILE : (tile + 1) * TILE, part]
    send(step, steps, copies)

    @pl.when(step == steps - 1)
    def _():
        dx_ref[...] = dx_sum[...].astype(BF)


def combine_kernel(
    y_ref, first_ref, second_ref, pick_ref, gate_ref, h_ref, shared_ref, g_ref, out_ref, dgate_ref
):
    table = gate_ref[...]
    y_first, y_second = dot(first_ref[...], y_ref[...]), dot(second_ref[...], y_ref[...])
    gate_first = jnp.sum(table * pick_ref[0], axis=-1, keepdims=True)
    gate_second = jnp.sum(table * pick_ref[1], axis=-1, keepdims=True)
    mixture = gate_first * y_first + gate_second * y_second
    out_ref[0] = (h_ref[...] + mixture + shared_ref[...].astype(F32)).astype(BF)
    g = g_ref[...].astype(F32)
    dgate_ref[...] = (
        jnp.sum(g * y_first, axis=-1, keepdims=True) * pick_ref[0]
        + jnp.sum(g * y_second, axis=-1, keepdims=True) * pick_ref[1]
    )


def middle_back_kernel(
    back_ref, dgate_ref, take_ref, gate_ref, small_ref, dshared_ref, g_ref, h_ref, scale_ref, gain_ref, w_ref,
    dh_ref, dhb_ref, do_ref, dlogits_ref, ggain_ref,
):
    take = take_ref[...]
    dgates = dgate_ref[...]
    table = gate_ref[...]
    gated = jnp.sum(table * dgates, axis=-1, keepdims=True)
    dlogits = (table * (dgates - gated)).astype(BF)
    dlogits_ref[...] = dlogits
    da = dshared_ref[...].astype(F32) + dot_nt(dlogits, small_ref[...]) + dot(take, back_ref[...])
    hidden, scale = h_ref[...], scale_ref[...]
    ggain_ref[...] = jnp.sum(da * hidden * scale, axis=0, keepdims=True)
    weighted = da * gain_ref[...]
    mean = jnp.mean(weighted * hidden, axis=-1, keepdims=True)
    dhidden = g_ref[...].astype(F32) + scale * weighted - hidden * (scale * scale * scale) * mean
    dh_ref[...] = dhidden
    low = dhidden.astype(BF)
    dhb_ref[...] = low
    width = w_ref.shape[2]
    do = dot_nt(low[:, :width], w_ref[0]) + dot_nt(low[:, width:], w_ref[1])
    do_ref[...] = do.astype(BF)


def project_back_kernel(dq_ref, dk_ref, dv_ref, w_ref, halo_ref, own_ref, w_back):
    width, model = w_ref.shape[2], w_ref.shape[1]
    parts = model // width
    rows = dq_ref.shape[0]

    @pl.when(pl.program_id(0) == 0)
    def _():
        for part in range(3 * parts):
            w_back[:, part * width : (part + 1) * width] = w_ref[part]

    da = dot_nt(
        jnp.concatenate([dk_ref[...], dv_ref[...]], axis=1), w_back[:, model:]
    )
    halo_ref[...] = da.astype(BF)

    @pl.when(pl.program_id(0) == pl.num_programs(0) - 1)
    def _():
        own_ref[...] = da[da.shape[0] - rows :] + dot_nt(dq_ref[...], w_back[:, :model])


def widen_kernel(in_ref, in_out_ref, down_out_ref):
    in_rows, down_rows = in_out_ref.shape[1], down_out_ref.shape[1]
    columns = in_out_ref.shape[2] // TILE
    for column in range(columns):
        in_out_ref[0, :, column * TILE : (column + 1) * TILE] = in_ref[
            column * in_rows : (column + 1) * in_rows, :
        ].astype(F32)
    for column in range(down_out_ref.shape[2] // TILE):
        first = columns * in_rows + column * down_rows
        down_out_ref[0, :, column * TILE : (column + 1) * TILE] = in_ref[
            first : first + down_rows, :
        ].astype(F32)


def pack_kernel(early_ref, late_ref, shared_ref, out_ref, *, block):
    late = late_ref[0].astype(F32)
    for source in range(1, late_ref.shape[0]):
        late = late + late_ref[source].astype(F32)
    early, own = early_ref[...], out_ref.shape[1]
    for owner in range(out_ref.shape[0]):
        part = slice(owner * own, (owner + 1) * own)
        first = early.shape[1]
        out_ref[owner, :, :first] = early[part].astype(BF)
        out_ref[owner, :, first : first + late.shape[1]] = late[part].astype(BF)
        first = first + late.shape[1]
        for half in range(2):
            out_ref[owner, :, first + half * TILE : first + (half + 1) * TILE] = shared_ref[
                half * block + owner * own : half * block + (owner + 1) * own, :
            ].astype(BF)


def unpack_kernel(
    in_ref, w_ref, gain_ref, qkv_ref, out_ref, small_ref, dgain_ref, second_ref, shared_ref, *, piece
):
    sources, own = in_ref.shape[0], in_ref.shape[1]
    model = out_ref.shape[1]

    def take(start, some):
        total = in_ref[some[0], :, start : start + LANES].astype(F32)
        for source in some[1:]:
            total = total + in_ref[source, :, start : start + LANES].astype(F32)
        return total

    dgain = jnp.zeros((own, LANES), F32)
    first_core, second_core = range(0, sources, 2), range(1, sources, 2)
    early = 2 * model - 2 * LANES * (sources // 4)
    for pair in range(model // LANES):
        start = pair * 2 * LANES
        if start < early:
            k, v = take(start, first_core), take(start + LANES, first_core)
            q, o = take(start, second_core), take(start + LANES, second_core)
        else:
            source = (start - early) // LANES * 2
            k, q = take(early, (source,)), take(early, (source + 1,))
            v, o = take(early, (source + 2,)), take(early, (source + 3,))
        for which, value in enumerate((q, k, v)):
            part = slice(which * model + pair * LANES, which * model + (pair + 1) * LANES)
            qkv_ref[:, part] = value
            dgain = dgain + value * w_ref[:, part].astype(F32)
        out_ref[:, pair * LANES : (pair + 1) * LANES] = o
    dgain = jnp.sum(dgain, axis=-1, keepdims=True) / gain_ref[...]
    lane = lax.broadcasted_iota(jnp.int32, (own, LANES), 1)
    row = lax.broadcasted_iota(jnp.int32, (own, LANES), 0)

    def as_row(column):
        return jnp.sum(jnp.where(lane == row, column, 0.0), axis=0, keepdims=True)[:, :own]

    dgain_ref[...] = as_row(dgain)
    small = take(early + LANES, range(sources))
    experts = small_ref.shape[1]
    small_ref[...] = small[:, :experts]
    second = jnp.sum(jnp.where(lane == experts, small, 0.0), axis=-1, keepdims=True)
    second_ref[...] = as_row(second)
    per = LANES // piece
    for column in range(shared_ref.shape[1] // LANES):
        start = early + 2 * LANES + column // per * LANES
        total = jnp.zeros((own, LANES), F32)
        for source in range(sources):
            turn = (source - column % per) * piece % LANES
            value = take(start, (source,))
            value = pltpu.roll(value, turn, 1) if turn else value
            total = jnp.where(lane // piece == source, value, total)
        shared_ref[:, column * LANES : (column + 1) * LANES] = total


def per_device(
    tokens,
    segments,
    routes,
    w_qkv,
    w_out,
    w_router,
    shared_in,
    shared_down,
    attn_gain,
    ffn_gain,
    expert_in,
    expert_down,
    cotangent,
):
    ctx, fsdp = lax.axis_size("ctx"), lax.axis_size("fsdp")
    ctx_index, core = lax.axis_index("ctx"), lax.axis_index("fsdp") % 2
    rows, model = tokens.shape[1], tokens.shape[2]
    reach = max(1, WIN // rows)
    span = (reach + 1) * rows
    capacity = max(2, 3 * rows * TOPK // (2 * ctx))
    slots = ctx * capacity
    own = w_qkv.shape[0]
    owned_down = shared_down.shape[0]
    experts = w_router.shape[1]
    ff = shared_in.shape[1] // 2
    tiles = ff // TILE

    x, g = tokens[0], cotangent[0]
    cosine, sine = rotary_tables(span, (ctx_index - reach) * rows)
    route_own = routes[0]
    expert_ids = jnp.arange(experts, dtype=jnp.int32)
    hits = route_own[:, :, None] == expert_ids[None, None, :]
    member = jnp.sum(hits.astype(jnp.int32), axis=1)
    ranking = jnp.cumsum(member, axis=0, dtype=jnp.int32) - 1
    slot_ids = jnp.arange(capacity, dtype=jnp.int32)
    placed = (member[:, :, None] > 0) & (ranking[:, :, None] == slot_ids[None, None, :])
    take = placed.astype(BF).reshape(rows, slots)
    put = take.T
    selector = (
        (hits[:, :, :, None] & placed[:, None, :, :]).astype(BF).reshape(rows, TOPK * slots)
    )
    picked = jnp.pad(
        hits.astype(F32).transpose(1, 0, 2), ((0, 0), (0, 0), (0, LANES - experts))
    )
    lane = jnp.arange(LANES, dtype=jnp.int32)[None, :]
    own_lanes = ((lane == ctx_index) | (lane == ctx_index + LANES // 2)).astype(F32)
    g_to_slots = dot(put, g).astype(BF)

    small = jnp.concatenate(
        [w_router, attn_gain[:, None], ffn_gain[:, None], jnp.zeros((own, LANES - experts - 2), BF)],
        axis=1,
    )
    projections = jnp.concatenate([w_qkv, w_out], axis=1)
    width = projections.shape[1] // fsdp
    near = lax.all_to_all(
        jnp.concatenate(
            [
                projections.reshape(own, fsdp, width).transpose(1, 0, 2),
                jnp.broadcast_to(small, (fsdp, own, LANES)),
                shared_in.reshape(own, 2, ctx, fsdp, owned_down)
                .transpose(3, 0, 1, 2, 4)
                .reshape(fsdp, own, 2 * TILE),
            ],
            axis=2,
        ),
        "fsdp",
        split_axis=0,
        concat_axis=0,
        tiled=True,
    ).reshape(fsdp * own, -1)

    segment_row = jnp.zeros((16, model), BF).at[0, :rows].set(segments[0].astype(BF))
    carried = jnp.concatenate([x, segment_row], axis=0)
    place_z = ctx_index % ROW
    lines = range(0, ctx, ROW)
    previous = shifted(after(carried, near), "ctx", ROW)
    arrived = [previous]
    for distance in range(reach - 1, 0, -1):
        arrived.append(
            lax.ppermute(
                jnp.where(place_z + distance < ROW, carried, previous),
                "ctx",
                [(line + z, line + (z + distance) % ROW) for line in lines for z in range(ROW)],
            )
        )

    def to_ctx(values):
        return lax.all_to_all(
            jnp.broadcast_to(values, (ctx, *values.shape)), "ctx", split_axis=0, concat_axis=0, tiled=True
        )

    g_all = lax.all_gather(g, "fsdp", axis=0)
    columns = model // TILE
    dense = to_ctx(near[:, :width]).reshape(model, width)
    w_full = lax.all_gather(after(dense, g_all, cosine, sine, g_to_slots, picked, previous), "fsdp", axis=0)
    small_full = to_ctx(after(near[:, width : width + LANES], dense)).reshape(model, LANES)
    down_own = shared_down.reshape(owned_down, columns, TILE).transpose(1, 0, 2).reshape(-1, TILE)
    place = ctx_index.astype(jnp.int32).reshape(1)
    place_spec = pl.BlockSpec(memory_space=pltpu.SMEM)
    in_rows, down_rows = expert_in.shape[1], expert_down.shape[1]
    expert_packed = jnp.concatenate(
        [
            expert_in[0].reshape(in_rows, 2 * tiles, TILE).transpose(1, 0, 2).reshape(-1, TILE),
            expert_down[0].reshape(down_rows, model // TILE, TILE).transpose(1, 0, 2).reshape(-1, TILE),
        ],
        axis=0,
    )
    expert_full = lax.all_gather(after(expert_packed, w_full, small_full, *arrived), "fsdp", axis=0)

    def exchange(values):
        return lax.all_to_all(
            values.reshape(ctx, values.shape[0] // ctx, values.shape[1]),
            "ctx",
            split_axis=0,
            concat_axis=0,
            tiled=True,
        ).reshape(values.shape)


    slot_g = exchange(after(g_to_slots, *arrived))

    pairs = model // LANES
    small_spec = whole(small_full)
    parts = model // width
    at_a_time = width // LANES

    def columns_of(which):
        return pl.BlockSpec((1, model, width), lambda j: (which * parts + j, 0, 0))

    def wide_spec(height):
        return pl.BlockSpec((height, width), lambda j: (0, j))

    blocks = [*arrived, carried]
    pair_spec = lambda height: pl.BlockSpec((height, LANES), lambda j: (0, j))
    q, k, kt, v, e, rl, rlb, attended, span_scale = pl.pallas_call(
        functools.partial(attend_kernel, gain_lane=experts, parts=reach + 1),
        grid=(parts,),
        in_specs=[
            place_spec,
            *[whole(block) for block in blocks],
            small_spec,
            columns_of(0),
            columns_of(1),
            columns_of(2),
            whole(cosine),
            whole(sine),
        ],
        out_specs=[
            wide_spec(rows),
            wide_spec(span),
            pl.BlockSpec((width, span), lambda j: (j, 0)),
            wide_spec(span),
            pl.BlockSpec((2 * at_a_time, span, rows), lambda j: (j, 0, 0)),
            pl.BlockSpec((at_a_time, 8, rows), lambda j: (j, 0, 0)),
            wide_spec(rows),
            wide_spec(rows),
            pl.BlockSpec((span, 1), lambda j: (0, 0)),
        ],
        out_shape=[
            jax.ShapeDtypeStruct((rows, model), BF),
            jax.ShapeDtypeStruct((span, model), BF),
            jax.ShapeDtypeStruct((model, span), BF),
            jax.ShapeDtypeStruct((span, model), BF),
            jax.ShapeDtypeStruct((HEADS, span, rows), BF),
            jax.ShapeDtypeStruct((pairs, 8, rows), F32),
            jax.ShapeDtypeStruct((rows, model), F32),
            jax.ShapeDtypeStruct((rows, model), BF),
            jax.ShapeDtypeStruct((span, 1), F32),
        ],
        scratch_shapes=[
            pltpu.VMEM((span, model), BF),
            pltpu.VMEM((2, span, rows), F32),
            pltpu.VMEM((width, span), BF),
            pltpu.VMEM((span, rows), F32),
        ],
        compiler_params=params(VMEM_MB),
        cost_estimate=cost(20),
        name="attend",
    )(place, *blocks, small_full, w_full, w_full, w_full, cosine, sine)

    out_spec = pl.BlockSpec((parts, model, width), lambda *_: (3, 0, 0))
    hidden, scale_two, normed, normed_t, outgoing, gates, gain_two = pl.pallas_call(
        functools.partial(middle_kernel, gain_lane=experts + 1),
        grid=(1,),
        in_specs=[
            whole(attended),
            out_spec,
            small_spec,
            whole(x),
            whole(picked),
            whole(put),
        ],
        out_specs=[
            pl.BlockSpec((rows, model), lambda *_: (0, 0)),
            pl.BlockSpec((rows, 1), lambda *_: (0, 0)),
            pl.BlockSpec((rows, model), lambda *_: (0, 0)),
            pl.BlockSpec((model, rows), lambda *_: (0, 0)),
            pl.BlockSpec((slots, model + LANES), lambda *_: (0, 0)),
            pl.BlockSpec((rows, LANES), lambda *_: (0, 0)),
            pl.BlockSpec((1, model), lambda *_: (0, 0)),
        ],
        out_shape=[
            jax.ShapeDtypeStruct((rows, model), F32),
            jax.ShapeDtypeStruct((rows, 1), F32),
            jax.ShapeDtypeStruct((rows, model), BF),
            jax.ShapeDtypeStruct((model, rows), BF),
            jax.ShapeDtypeStruct((slots, model + LANES), BF),
            jax.ShapeDtypeStruct((rows, LANES), F32),
            jax.ShapeDtypeStruct((1, model), F32),
        ],
        compiler_params=params(VMEM_MB),
        cost_estimate=cost(5),
        name="middle",
    )(attended, w_full, small_full, x, picked, put)
    normed_all = lax.all_gather(normed, "fsdp", axis=0)
    incoming = exchange(after(outgoing, slot_g))
    narrow = after(near, outgoing)
    shared_own_w = jnp.concatenate(
        [narrow[:, width + LANES : -TILE], narrow[:, -TILE:], down_own], axis=0
    )
    shared_full = to_ctx(after(shared_own_w, incoming))
    gain_one = small_full[:, experts : experts + 1].astype(F32)
    span_x = jnp.concatenate(
        [block[:rows] for block in lax.optimization_barrier((*blocks, outgoing))[:-1]], axis=0
    )
    first_t = (span_x.T.astype(F32) * span_scale.reshape(1, span) * gain_one).astype(BF)
    incoming = after(incoming, first_t)

    packed_rows = 3 * model

    steps = tiles // AT_ONCE
    expert_specs = [
        pl.BlockSpec((fsdp, AT_ONCE * in_rows, TILE), lambda t: (0, t, 0)),
        pl.BlockSpec((fsdp, AT_ONCE * in_rows, TILE), lambda t: (0, steps + t, 0)),
        pl.BlockSpec((AT_ONCE, model, TILE), lambda t: (t, 2 * in_rows * tiles // model, 0)),
    ]
    unit_spec = pl.BlockSpec((1, slots, AT_ONCE * TILE), lambda t: (t, 0, 0))
    expert_y, *units = pl.pallas_call(
        expert_kernel,
        grid=(steps,),
        in_specs=[whole(incoming), *expert_specs],
        out_specs=[
            pl.BlockSpec((slots, model), lambda t: (0, 0)),
            unit_spec,
            unit_spec,
            unit_spec,
        ],
        out_shape=[jax.ShapeDtypeStruct((slots, model), BF)]
        + [jax.ShapeDtypeStruct((steps, slots, AT_ONCE * TILE), BF)] * 3,
        scratch_shapes=[pltpu.VMEM((slots, model), F32)],
        compiler_params=params(VMEM_MB),
        cost_estimate=cost(60),
        name="expert",
    )(incoming, expert_full, expert_full, expert_full)
    returned_y = exchange(after(expert_y, shared_full))

    at_once = 2
    block = model // ctx
    shared_part, shared_pieces = pl.pallas_call(
        shared_kernel,
        grid=(fsdp // at_once,),
        in_specs=[
            pl.BlockSpec((at_once, rows, model), lambda t: (t, 0, 0)),
            pl.BlockSpec((at_once, rows, model), lambda t: (t, 0, 0)),
            whole(shared_full),
        ],
        out_specs=[
            pl.BlockSpec((at_once, rows, 2 * model), lambda t: (t, 0, 0)),
            whole(shared_full),
        ],
        out_shape=[
            jax.ShapeDtypeStruct((fsdp, rows, 2 * model), BF),
            jax.ShapeDtypeStruct(shared_full.shape, BF),
        ],
        scratch_shapes=[pltpu.VMEM((model, 2 * TILE), F32), pltpu.VMEM((TILE, model), F32)],
        compiler_params=params(VMEM_MB),
        cost_estimate=cost(18),
        name="shared",
    )(after(normed_all, expert_y), g_all, shared_full)
    shared_both = lax.psum_scatter(after(shared_part, returned_y), "fsdp", scatter_dimension=0)
    shared_own = jnp.sum(
        lax.all_to_all(
            after(shared_pieces, returned_y), "ctx", split_axis=0, concat_axis=0, tiled=True
        ).astype(F32),
        axis=0,
    )
    back, gexpert = pl.pallas_call(
        expert_back_kernel,
        grid=(steps,),
        in_specs=[
            whole(incoming),
            whole(slot_g),
            whole(own_lanes),
            *expert_specs,
            unit_spec,
            unit_spec,
            unit_spec,
        ],
        out_specs=[
            pl.BlockSpec((slots, model), lambda t: (0, 0)),
            pl.BlockSpec(memory_space=pl.ANY),
        ],
        out_shape=[
            jax.ShapeDtypeStruct((slots, model), BF),
            jax.ShapeDtypeStruct((fsdp, packed_rows, TILE), BF),
        ],
        scratch_shapes=[
            pltpu.VMEM((model, slots), BF),
            pltpu.VMEM((slots, model), BF),
            pltpu.VMEM((slots, model), F32),
            pltpu.VMEM((2, 2, fsdp, AT_ONCE * in_rows, TILE), BF),
            pltpu.VMEM((2, AT_ONCE, model, TILE), BF),
            pltpu.SemaphoreType.DMA((2, 3)),
        ],
        compiler_params=params(VMEM_MB),
        cost_estimate=cost(22),
        name="expert_back",
    )(after(incoming, shared_part, returned_y), slot_g, own_lanes, expert_full, expert_full, expert_full, *units)
    returned = exchange(after(back, shared_own))
    expert_sum = lax.psum_scatter(after(gexpert, shared_own), "fsdp", scatter_dimension=0)

    mixed, dgates = pl.pallas_call(
        combine_kernel,
        grid=(1,),
        in_specs=[
            pl.BlockSpec((slots, model), lambda *_: (0, 0)),
            pl.BlockSpec((rows, slots), lambda *_: (0, 0)),
            pl.BlockSpec((rows, slots), lambda *_: (0, 1)),
            whole(picked),
            whole(gates),
            whole(hidden),
            pl.BlockSpec((rows, model), lambda *_: (0, 0)),
            whole(g),
        ],
        out_specs=[
            pl.BlockSpec((1, rows, model), lambda *_: (0, 0, 0)),
            pl.BlockSpec((rows, LANES), lambda *_: (0, 0)),
        ],
        out_shape=[
            jax.ShapeDtypeStruct((1, rows, model), BF),
            jax.ShapeDtypeStruct((rows, LANES), F32),
        ],
        compiler_params=params(VMEM_MB),
        cost_estimate=cost(3),
        name="combine",
    )(returned_y, selector, selector, picked, gates, hidden, shared_both, g)

    returned = after(returned, dgates)

    dhidden, dhidden_low, dattended, dlogits, ggain_two = pl.pallas_call(
        middle_back_kernel,
        grid=(1,),
        in_specs=[
            whole(returned),
            whole(dgates),
            whole(take),
            whole(gates),
            small_spec,
            pl.BlockSpec((rows, model), lambda *_: (0, 1)),
            whole(g),
            whole(hidden),
            whole(scale_two),
            whole(gain_two),
            out_spec,
        ],
        out_specs=[
            pl.BlockSpec((rows, model), lambda *_: (0, 0)),
            pl.BlockSpec((rows, model), lambda *_: (0, 0)),
            pl.BlockSpec((rows, model), lambda *_: (0, 0)),
            pl.BlockSpec((rows, LANES), lambda *_: (0, 0)),
            pl.BlockSpec((1, model), lambda *_: (0, 0)),
        ],
        out_shape=[
            jax.ShapeDtypeStruct((rows, model), F32),
            jax.ShapeDtypeStruct((rows, model), BF),
            jax.ShapeDtypeStruct((rows, model), BF),
            jax.ShapeDtypeStruct((rows, LANES), BF),
            jax.ShapeDtypeStruct((1, model), F32),
        ],
        compiler_params=params(VMEM_MB),
        cost_estimate=cost(6),
        name="middle_back",
    )(
        returned, dgates, take, gates, small_full, shared_both, g, hidden, scale_two, gain_two, w_full
    )

    grouter = dot(normed_t, dlogits)
    small_grads = jnp.concatenate(
        [grouter[:, :experts], ggain_two.T, jnp.zeros((model, LANES - experts - 1), F32)], axis=1
    ).astype(BF)
    attended_t = attended.T
    core_scalar = core.astype(jnp.int32).reshape(1)

    def attend_back(first, count, down, *filled):
        pair_from = lambda height: pl.BlockSpec((height, LANES), lambda j: (0, first + j))
        operands = (
            core_scalar, q, k, kt, v, e, rl, rlb, down, cosine, sine, first_t, attended_t, dhidden_low, *filled,
        )
        return pl.pallas_call(
            attend_back_kernel,
            grid=(count,),
            in_specs=[
                place_spec,
                pair_from(rows),
                pair_from(span),
                pl.BlockSpec((LANES, span), lambda j: (first + j, 0)),
                pair_from(span),
                pl.BlockSpec((2, span, rows), lambda j: (first + j, 0, 0)),
                pl.BlockSpec((1, 8, rows), lambda j: (first + j, 0, 0)),
                pair_from(rows),
                pair_from(rows),
                whole(cosine),
                whole(sine),
                whole(first_t),
                whole(attended_t),
                pair_from(rows),
            ]
            + [pl.BlockSpec(memory_space=pl.ANY)] * len(filled),
            out_specs=[
                pair_from(rows),
                pair_from(span),
                pair_from(span),
                pl.BlockSpec((model, 2 * LANES), lambda j: (0, j)),
                pl.BlockSpec((model, 2 * LANES), lambda j: (0, j)),
            ],
            out_shape=[
                jax.ShapeDtypeStruct((rows, model), BF),
                jax.ShapeDtypeStruct((span, model), BF),
                jax.ShapeDtypeStruct((span, model), BF),
                jax.ShapeDtypeStruct((model, count * 2 * LANES), BF),
                jax.ShapeDtypeStruct((model, count * 2 * LANES), BF),
            ],
            input_output_aliases={
                len(operands) - len(filled) + index: index for index in range(len(filled))
            },
            scratch_shapes=[
                pltpu.VMEM((2, span, rows), F32),
                pltpu.VMEM((2, span, rows), BF),
                pltpu.VMEM((span, LANES), F32),
                pltpu.VMEM((span, LANES), F32),
            ],
            compiler_params=params(VMEM_MB),
            cost_estimate=cost(12 * count),
            name=f"attend_back_{first}",
        )(*operands)


    def paired_columns(kept, sent):
        partner = lax.ppermute(sent, "fsdp", [(i, i ^ 1) for i in range(fsdp)])
        return (kept.astype(F32) + partner.astype(F32)).astype(BF)

    def along_ctx(pieces):
        return lax.all_to_all(pieces, "ctx", split_axis=0, concat_axis=0, tiled=True)

    early_pairs = 2 * pairs // 3
    *grads_a, kept_a, sent_a = attend_back(0, early_pairs, dattended)
    paired_a = paired_columns(kept_a, sent_a)
    late_a = along_ctx(paired_a.reshape(ctx, block, -1))
    dq, dk, dv, kept_b, sent_b = attend_back(
        early_pairs, pairs - early_pairs, after(dattended, paired_a), *grads_a
    )
    paired_b = paired_columns(kept_b, sent_b)

    dspan, down = pl.pallas_call(
        project_back_kernel,
        grid=(2,),
        in_specs=[
            whole(dq),
            pl.BlockSpec((span // 2, model), lambda b: (b, 0)),
            pl.BlockSpec((span // 2, model), lambda b: (b, 0)),
            pl.BlockSpec((3 * parts, model, width), lambda b: (0, 0, 0)),
        ],
        out_specs=[
            pl.BlockSpec((span // 2, model), lambda b: (b, 0)),
            pl.BlockSpec((rows, model), lambda b: (0, 0)),
        ],
        out_shape=[
            jax.ShapeDtypeStruct((span, model), BF),
            jax.ShapeDtypeStruct((rows, model), F32),
        ],
        compiler_params=params(VMEM_MB),
        scratch_shapes=[pltpu.VMEM((model, 3 * model), BF)],
        cost_estimate=cost(8),
        name="project_back",
    )(dq, dk, dv, w_full)
    total, passed = down, dspan[:rows].astype(F32)
    for distance in range(1, reach):
        lower = (reach - distance) * rows
        moved = lax.ppermute(
            dspan[lower : lower + rows],
            "ctx",
            [(line + z, line + (z - distance) % ROW) for line in lines for z in range(ROW)],
        )
        moved = moved.astype(F32)
        here = place_z + distance < ROW
        total = total + jnp.where(here, moved, 0.0)
        passed = passed + jnp.where(here, 0.0, moved)
    grad_expert_in, grad_expert_down = pl.pallas_call(
        widen_kernel,
        grid=(1,),
        in_specs=[whole(expert_sum)],
        out_specs=[
            pl.BlockSpec((1, in_rows, 2 * ff), lambda *_: (0, 0, 0)),
            pl.BlockSpec((1, down_rows, model), lambda *_: (0, 0, 0)),
        ],
        out_shape=[
            jax.ShapeDtypeStruct((1, in_rows, 2 * ff), F32),
            jax.ShapeDtypeStruct((1, down_rows, model), F32),
        ],
        compiler_params=params(VMEM_MB),
        cost_estimate=cost(2),
        name="widen",
    )(expert_sum)
    late_a = jnp.sum(late_a.astype(F32), axis=0)
    quarter = paired_b.shape[1] // (fsdp // 2)
    late_b = lax.all_to_all(
        after(
            paired_b.reshape(model, fsdp // 2, quarter).transpose(1, 0, 2),
            down, late_a,
        ),
        "fsdp",
        split_axis=0,
        concat_axis=0,
        axis_index_groups=[list(range(start, fsdp, 2)) for start in range(2)],
        tiled=True,
    )
    late_b = jnp.sum(late_b.astype(F32), axis=0).astype(BF)
    received = shifted(after(passed.astype(BF), late_b), "ctx", -ROW)
    late_b = along_ctx(jnp.concatenate([late_b, small_grads], axis=1).reshape(ctx, block, -1))

    grad_shared_down = (
        shared_own[2 * block :]
        .reshape(columns, owned_down, TILE)
        .transpose(1, 0, 2)
        .reshape(owned_down, model)
    )
    packed_width = late_a.shape[1] + late_b.shape[2] + 2 * TILE
    last = pl.pallas_call(
        functools.partial(pack_kernel, block=block),
        grid=(1,),
        in_specs=[
            whole(late_a),
            whole(late_b),
            pl.BlockSpec((2 * block, TILE), lambda *_: (0, 0)),
        ],
        out_specs=pl.BlockSpec((fsdp, own, packed_width), lambda *_: (0, 0, 0)),
        out_shape=jax.ShapeDtypeStruct((fsdp, own, packed_width), BF),
        compiler_params=params(VMEM_MB),
        cost_estimate=cost(2),
        name="pack",
    )(late_a, late_b, shared_own)
    last = lax.all_to_all(last, "fsdp", split_axis=0, concat_axis=0, tiled=True)
    last = after(last, received, grad_expert_in, grad_expert_down)
    wanted = [
        jax.ShapeDtypeStruct((own, 3 * model), F32),
        jax.ShapeDtypeStruct((own, model), F32),
        jax.ShapeDtypeStruct((own, experts), F32),
        jax.ShapeDtypeStruct((1, own), F32),
        jax.ShapeDtypeStruct((1, own), F32),
        jax.ShapeDtypeStruct((own, 2 * ff), F32),
    ]
    gain_own = attn_gain.astype(F32)[:, None]
    grad_qkv, grad_out, grad_router, grad_gain_one, grad_gain_two, grad_shared_in = pl.pallas_call(
        functools.partial(unpack_kernel, piece=owned_down),
        grid=(1,),
        in_specs=[whole(last), whole(w_qkv), whole(gain_own)],
        out_specs=[whole(array) for array in wanted],
        out_shape=wanted,
        compiler_params=params(VMEM_MB),
        cost_estimate=cost(2),
        name="unpack",
    )(last, w_qkv, gain_own)

    total = total + received.astype(F32)
    input_rows = x.astype(F32)
    scale_one = span_scale[reach * rows :]
    weighted = total * gain_one.reshape(1, model)
    input_grad = (
        dhidden
        + scale_one * weighted
        - input_rows
        * scale_one**3
        * jnp.mean(weighted * input_rows, axis=-1, keepdims=True)
    )[None]

    return (
        mixed,
        input_grad,
        grad_qkv,
        grad_out,
        grad_router,
        grad_shared_in,
        grad_shared_down,
        grad_gain_one.reshape(own),
        grad_gain_two.reshape(own),
        grad_expert_in,
        grad_expert_down,
    )


def solution(mesh):
    placed = (
        P("fsdp", "ctx", None),
        P("fsdp", "ctx"),
        P("fsdp", "ctx", None),
        P(("ctx", "fsdp"), None),
        P(("ctx", "fsdp"), None),
        P(("ctx", "fsdp"), None),
        P(("ctx", "fsdp"), None),
        P(("ctx", "fsdp"), None),
        P(("ctx", "fsdp")),
        P(("ctx", "fsdp")),
        P("ctx", "fsdp", None),
        P("ctx", "fsdp", None),
        P("fsdp", "ctx", None),
    )
    return jax.shard_map(
        per_device,
        mesh=mesh,
        in_specs=placed,
        out_specs=(
            P("fsdp", "ctx", None),
            P("fsdp", "ctx", None),
            P(("ctx", "fsdp"), None),
            P(("ctx", "fsdp"), None),
            P(("ctx", "fsdp"), None),
            P(("ctx", "fsdp"), None),
            P(("ctx", "fsdp"), None),
            P(("ctx", "fsdp")),
            P(("ctx", "fsdp")),
            P("ctx", "fsdp", None),
            P("ctx", "fsdp", None),
        ),
        check_vma=False,
    )
```
